32 devices in a mesh: dp: 4 (over z), fsdp: 8 (over y, x, core).
Axes of the slice: x: 2, y: 2, z: 4, core: 2. Of those that a mesh axis runs over, the one named last changes fastest.
Arguments:
- tokens: bfloat16 [12288, 1024], P(('dp', 'fsdp')), may hold values from -6 to 6
- cotangent: bfloat16 [12288, 1024], P(('dp', 'fsdp')), may hold values from -6 to 6
- lengths: int32 [4, 4], P('dp'), may hold values from 1 to 2689, 3072 in all within a row
- adapter_index: int32 [4, 4], P('dp'), may hold values from 0 to 7
- routes: int32 [12288, 8], P(('dp', 'fsdp')), may hold values from 0 to 15, all different within a row; in each aligned block of 384 rows (0 to 383, 384 to 767, ...) at most 256 rows name the same one
- deal: int32 [4], replicated, may hold values from 0 to 3, as said below
- norm_gain_pair: bfloat16 [1024, 2], P(('dp', 'fsdp')), may hold values from 0.5 to 1.5
- query_weight: bfloat16 [1024, 1024], P(('dp', 'fsdp')), may hold values from -0.1875 to 0.1875
- key_weight: bfloat16 [1024, 512], P(('dp', 'fsdp')), may hold values from -0.1875 to 0.1875
- value_weight: bfloat16 [1024, 512], P(('dp', 'fsdp')), may hold values from -0.1875 to 0.1875
- output_weight_transposed: bfloat16 [1024, 1024], P(('dp', 'fsdp')), may hold values from -1.5 to 1.5
- router_weight: bfloat16 [1024, 16], P(('dp', 'fsdp')), may hold values from -0.09375 to 0.09375
- expert_input_weight: bfloat16 [1024, 16, 1024], P(None, 'fsdp'), may hold values from -0.1875 to 0.1875
- expert_output_weight: bfloat16 [1024, 16, 512], P(None, 'fsdp'), may hold values from -0.75 to 0.75
- adapter_input_factors: bfloat16 [7, 1024, 128], replicated, may hold values from -0.1875 to 0.1875
- adapter_down_first: bfloat16 [512, 128], replicated, may hold values from -0.75 to 0.75
- adapter_wide_second: bfloat16 [3, 128, 1024], replicated, may hold values from -0.75 to 0.75
- adapter_key_value_second: bfloat16 [2, 128, 512], replicated, may hold values from -0.75 to 0.75
- adapter_hidden_second: bfloat16 [2, 128, 512], replicated, may hold values from -0.75 to 0.75
- adapter_router_second: bfloat16 [128, 16], replicated, may hold values from -0.3125 to 0.3125
Outputs:
- layer_out: bfloat16 [12288, 1024], P(('dp', 'fsdp'))
- input_grad: float32 [12288, 1024], P(('dp', 'fsdp'))
- adapter_input_gradient: float32 [7, 1024, 128], replicated
- grad_lora_down_a: float32 [512, 128], replicated
- grad_lora_wide_b: float32 [3, 128, 1024], replicated
- grad_lora_kv_b: float32 [2, 128, 512], replicated
- grad_lora_ff_b: float32 [2, 128, 512], replicated
- grad_lora_route_b: float32 [128, 16], replicated
The draws below stay inside these ranges and needn't reach their ends.
Inputs may be any that keep to these rules, and one draw needn't show every extreme that they name: `lengths`: each row sums to 3072, and its largest entry is 2689. `routes`: each token names 8 different experts; among the rows of one device no expert is named more than 256 times. Each group number appears once; for some dealt group g, deal[g] is (g + 2) mod 4.
All inputs are finite; a program needn't handle non-finite values.
Results may differ from the reference program's by a relative error of at most 0.019.
Values may be sent and summed in bfloat16 or wider, within the bound.
A program may use at most 320 MiB of HBM per device.

```python
import math
import jax
import jax.numpy as jnp
import numpy as np
from jax import lax

MODEL_WIDTH = 1024
HEADS = 16
KEY_VALUE_HEADS = 8
HEAD_WIDTH = 64
HIDDEN_UNITS = 512
TOPK = 8
EXPERT_COUNT = 16
ADAPTER_COUNT = 8
ADAPTER_RANK = 16
NSEQ = 4
TOK_DEV = 384
GROUP_TOK = 3072
TOKENS = 12288
SEQ_MAX = 2689
CAP = 256
N_DP = 4


def draw_deal(key, part):
    key = jax.random.fold_in(key, 11)
    order_key, pick_key = jax.random.split(key)
    shuffled = jax.random.permutation(order_key, N_DP).astype(jnp.int32)
    chosen = jax.random.randint(pick_key, (), 0, N_DP).astype(jnp.int32)
    wanted = ((chosen + N_DP // 2) % N_DP).astype(jnp.int32)
    where_wanted = jnp.argmax(shuffled == wanted).astype(jnp.int32)
    displaced = shuffled[chosen]
    swapped = shuffled.at[where_wanted].set(displaced)
    return swapped.at[chosen].set(wanted).astype(jnp.int32)


def plant(drawn, own_key, low, top_value):
    index_at = [jax.random.randint(jax.random.fold_in(own_key, axis), (), 0, length) for axis, length in enumerate(drawn.shape)]
    main_axis = drawn.shape.index(max(drawn.shape))
    next_to = index_at[:main_axis] + [(index_at[main_axis] + 1) % drawn.shape[main_axis]] + index_at[main_axis + 1:]
    return drawn.at[tuple(index_at)].set(low).at[tuple(next_to)].set(top_value)


def block_levels(rng, shape, pieces, low, high):
    loudness = 1.0
    for axis_at, parts in pieces:
        draws = jax.random.uniform(jax.random.fold_in(jax.random.fold_in(rng, 6), axis_at), (parts,), jnp.float32, low / len(pieces), high / len(pieces))
        loudness = loudness * jnp.repeat(jnp.exp(draws), shape[axis_at] // parts).reshape((-1,) + (1,) * (len(shape) - 1 - axis_at))
    return loudness


def profile(amount, total, bound, lean):
    loads = [(1 << 20) // math.isqrt(grade ** lean) + 1 for grade in range(2, amount + 1)]
    spare, given = total - bound - (amount - 1), [1] * (amount - 1)
    while spare > 0:
        free = [i for i in range(amount - 1) if given[i] < bound]
        mass, remaining = sum([loads[i] for i in free]), spare
        for i in free:
            addition = min(bound - given[i], max(1, remaining * loads[i] // mass), spare)
            given[i] = given[i] + addition
            spare = spare - addition
    return np.array([bound] + given)


def uneven(key, amount, total, reach, skew):
    if amount == 2:
        one = jax.random.randint(key, (), max(1, total - reach), min(reach, total - 1) + 1)
        return jnp.stack([one, total - one])
    tallies = jnp.asarray(profile(amount, total, reach, skew), jnp.int32)
    couples = (amount - 1) // 2
    giver, sink = tallies[1:1 + 2 * couples:2], tallies[2:2 + 2 * couples:2]
    room = jnp.minimum(giver - 1, reach - sink)
    moved = jax.random.randint(jax.random.fold_in(key, 1), (couples,), 0, 1 << 20) % (room + 1)
    tallies = tallies.at[1:1 + 2 * couples:2].set(giver - moved).at[2:2 + 2 * couples:2].set(sink + moved)
    return tallies[jax.random.permutation(jax.random.fold_in(key, 2), amount)]


def shared_out(own_key, own, number, rows, amount, top, reach, lean):
    sequence = jax.random.permutation(own_key, amount)
    crowded, common = shares(amount, rows * top, reach, lean, True), shares(amount, rows * top, reach, lean, False)
    places = jnp.arange(amount)

    def named(sizes, offset_by):
        used = int((sizes > 0).sum())
        fixed = max(1, used // 4)
        moved = fixed + (places - fixed + offset_by * (used - fixed)) % max(1, amount - fixed)
        return jnp.zeros((amount,), jnp.int32).at[sequence[jnp.where(places < fixed, places, moved)]].set(jnp.asarray(sizes, jnp.int32))

    sizes = jnp.where(number % 4 == 0, named(crowded, number // 4), named(common, number - number // 4 - 1))
    mixed = jax.random.permutation(jax.random.fold_in(own, 3), amount)
    donor, sink = mixed[0:amount // 2 * 2:2], mixed[1:amount // 2 * 2:2]
    slack = jnp.minimum(sizes[donor] - 1, reach - sizes[sink]) // 2
    slack = jnp.where((donor == sequence[0]) | (sink == sequence[0]) | (sizes[sink] == 0), 0, jnp.maximum(slack, 0))
    moved = jax.random.randint(jax.random.fold_in(own, 4), (amount // 2,), 0, 1 << 20) % (slack + 1)
    sizes = sizes.at[donor].add(-moved).at[sink].add(moved)
    items = jnp.searchsorted(jnp.cumsum(sizes), jnp.arange(rows * top), side="right").astype(jnp.int32)
    table = items.reshape(top, rows).T
    table = table[jax.random.permutation(jax.random.fold_in(own, 1), rows)]
    offset_by = jax.random.randint(jax.random.fold_in(own, 2), (rows, 1), 0, top)
    return jnp.take_along_axis(table, (jnp.arange(top)[None, :] + offset_by) % top, axis=1)


def shares(amount, total, most, skew, full):
    portions = [(1 << 20) // math.isqrt(rank ** skew) + 1 for rank in range(1, amount + 1)]
    largest = most if full else min(most, max(-(-total // amount), total * portions[0] // sum(portions)))
    least = 1 if total - largest >= amount - 1 else 0
    holding, surplus = [largest] + [least] * (amount - 1), total - largest - least * (amount - 1)
    while surplus > 0:
        movable = [i for i in range(1, amount) if holding[i] < largest] or [i for i in range(1, amount) if holding[i] < most]
        pool, budget = sum([portions[i] for i in movable]), surplus
        for i in movable:
            extra = min(most - holding[i], max(1, budget * portions[i] // pool), surplus)
            holding[i] = holding[i] + extra
            surplus = surplus - extra
    return np.array(holding)


def gaussian(key, shape, spread, bound, cuts=(), kind=jnp.bfloat16):
    gain = block_levels(key, shape, cuts, -0.22, 0.18) if cuts else 1.0
    entries = jax.random.normal(key, shape, jnp.float32) * spread * gain
    return jnp.minimum(jnp.maximum(entries, -bound), bound).astype(kind)


def setup_inputs(seed: int = 0) -> dict:
    key_of = jax.random.split(jax.random.key(seed), 21)
    tokens = gaussian(key_of[0], (TOKENS, MODEL_WIDTH), 1.0, 6.0, ((0, 32),))
    cotangent = gaussian(key_of[1], (TOKENS, MODEL_WIDTH), 1.0, 6.0, ((0, 32),))
    lengths = jax.vmap(lambda own: uneven(own, NSEQ, GROUP_TOK, SEQ_MAX, 2))(jax.random.split(key_of[2], N_DP)).reshape((N_DP, NSEQ)).astype(jnp.int32)
    adapter_index = plant(jax.random.randint(key_of[3], (N_DP, NSEQ), 0, ADAPTER_COUNT), jax.random.fold_in(key_of[3], 1), 0, ADAPTER_COUNT - 1).astype(jnp.int32)
    routes_keys = jax.random.split(jax.random.fold_in(key_of[4], 1), TOKENS // TOK_DEV)
    routes_turns = jax.random.permutation(jax.random.fold_in(key_of[4], 3), TOKENS // TOK_DEV)
    routes = jax.vmap(lambda own, number: shared_out(jax.random.fold_in(key_of[4], 2), own, number, TOK_DEV, EXPERT_COUNT, TOPK, CAP, 1))(routes_keys, routes_turns).reshape((TOKENS, TOPK))
    deal = draw_deal(jax.random.fold_in(key_of[20], 71), 0)
    norm_gain_pair = jnp.clip(1.0 + 0.1 * jax.random.normal(key_of[6], (MODEL_WIDTH, 2), jnp.float32), 0.5, 1.5).astype(jnp.bfloat16)
    query_weight = gaussian(key_of[7], (MODEL_WIDTH, HEADS * HEAD_WIDTH), MODEL_WIDTH ** -0.5, 0.1875, ((0, 32),))
    key_weight = gaussian(key_of[8], (MODEL_WIDTH, KEY_VALUE_HEADS * HEAD_WIDTH), MODEL_WIDTH ** -0.5, 0.1875, ((0, 32),))
    value_weight = gaussian(key_of[9], (MODEL_WIDTH, KEY_VALUE_HEADS * HEAD_WIDTH), MODEL_WIDTH ** -0.5, 0.1875, ((0, 32),))
    output_weight_transposed = gaussian(key_of[10], (MODEL_WIDTH, HEADS * HEAD_WIDTH), (max(MODEL_WIDTH // 64, 1)) ** -0.5, 1.5, ((0, 32),))
    router_weight = gaussian(key_of[11], (MODEL_WIDTH, EXPERT_COUNT), (4 * MODEL_WIDTH) ** -0.5, 0.09375, ((0, 32),))
    expert_input_weight = gaussian(key_of[12], (MODEL_WIDTH, EXPERT_COUNT, 2 * HIDDEN_UNITS), MODEL_WIDTH ** -0.5, 0.1875, ((1, 8),))
    expert_output_weight = gaussian(key_of[13], (MODEL_WIDTH, EXPERT_COUNT, HIDDEN_UNITS), (HIDDEN_UNITS // 8) ** -0.5, 0.75, ((1, 8),))
    adapter_input_factors = gaussian(key_of[14], (7, MODEL_WIDTH, ADAPTER_COUNT * ADAPTER_RANK), MODEL_WIDTH ** -0.5, 0.1875)
    adapter_down_first = gaussian(key_of[15], (HIDDEN_UNITS, ADAPTER_COUNT * ADAPTER_RANK), (HIDDEN_UNITS // 8) ** -0.5, 0.75)
    adapter_wide_second = gaussian(key_of[16], (3, ADAPTER_COUNT * ADAPTER_RANK, MODEL_WIDTH), (4 * ADAPTER_RANK) ** -0.5, 0.75)
    adapter_key_value_second = gaussian(key_of[17], (2, ADAPTER_COUNT * ADAPTER_RANK, KEY_VALUE_HEADS * HEAD_WIDTH), (4 * ADAPTER_RANK) ** -0.5, 0.75)
    adapter_hidden_second = gaussian(key_of[18], (2, ADAPTER_COUNT * ADAPTER_RANK, HIDDEN_UNITS), (4 * ADAPTER_RANK) ** -0.5, 0.75)
    adapter_router_second = gaussian(key_of[19], (ADAPTER_COUNT * ADAPTER_RANK, EXPERT_COUNT), (25 * ADAPTER_RANK) ** -0.5, 0.3125)
    return {"tokens": tokens, "cotangent": cotangent, "lengths": lengths, "adapter_index": adapter_index, "routes": routes, "deal": deal, "norm_gain_pair": norm_gain_pair, "query_weight": query_weight, "key_weight": key_weight, "value_weight": value_weight, "output_weight_transposed": output_weight_transposed, "router_weight": router_weight, "expert_input_weight": expert_input_weight, "expert_output_weight": expert_output_weight, "adapter_input_factors": adapter_input_factors, "adapter_down_first": adapter_down_first, "adapter_wide_second": adapter_wide_second, "adapter_key_value_second": adapter_key_value_second, "adapter_hidden_second": adapter_hidden_second, "adapter_router_second": adapter_router_second}


@jax.custom_vjp
def lowrank_rows(v):
    return lax.optimization_barrier(v.astype(jnp.bfloat16)).astype(jnp.float32)

@jax.custom_vjp
def lowrank_backward(v):
    return v

def low_keep(v):
    return (lowrank_rows(v), None)

def low_pass(kept, grad):
    return (grad,)

def back_keep(v):
    return (v, None)

def back_low(kept, grad):
    return (lowrank_rows(grad),)
lowrank_rows.defvjp(low_keep, low_pass)
lowrank_backward.defvjp(back_keep, back_low)
EPSILON = 1e-06
ROPE_BASE = 10000.0
MASKED = -1e+30
PRECISE = lax.Precision.HIGHEST

def matrix_product_precise(first_op, second_op):
    return jnp.dot(first_op, second_op, precision=PRECISE, preferred_element_type=jnp.float32)

def token_meta(sequence_lengths, selected_experts, row_index):
    offsets = (jnp.cumsum(sequence_lengths) - sequence_lengths).astype(jnp.int32)
    seq_number = lax.optimization_barrier(jnp.sum((row_index[:, None] >= offsets[None, 1:]).astype(jnp.int32), axis=1))
    onehot = seq_number[:, None] == jnp.arange(sequence_lengths.shape[0], dtype=jnp.int32)[None, :]
    seq_start = lax.optimization_barrier(jnp.sum(jnp.where(onehot, offsets[None, :], 0), axis=1)).astype(jnp.int32)
    adapter_pick = lax.optimization_barrier(jnp.sum(jnp.where(onehot, selected_experts[None, :], 0), axis=1)).astype(jnp.int32)
    return (seq_start, adapter_pick)

def rope_tables(position):
    half_dim = HEAD_WIDTH // 2
    frequency = ROPE_BASE ** (-jnp.arange(half_dim, dtype=jnp.float32) / half_dim)
    angles = position.astype(jnp.float32)[:, None] * frequency[None, :]
    return (jnp.cos(angles), jnp.sin(angles))

def rotate(tensor, cosine_table, sine_table):
    rows_here = tensor.shape[0]
    head_view = tensor.reshape(rows_here, -1, HEAD_WIDTH)
    half_dim = HEAD_WIDTH // 2
    first_half = head_view[..., :half_dim]
    second_half = head_view[..., half_dim:]
    cos_view = cosine_table[:, None, :]
    sin_view = sine_table[:, None, :]
    turned = jnp.concatenate([first_half * cos_view - second_half * sin_view, second_half * cos_view + first_half * sin_view], axis=-1)
    return turned.reshape(rows_here, -1)

def adapter_contribution(inputs, factor, stacked_mask):
    return lowrank_rows(lowrank_backward(matrix_product_precise(inputs, factor) * stacked_mask))

def attend(query_rows, key_rows, value_rows, row_index, seq_start):
    rows_here = query_rows.shape[0]
    block_rows = math.gcd(rows_here, 512)
    group_heads = HEADS // KEY_VALUE_HEADS
    key_view = key_rows.reshape(rows_here, KEY_VALUE_HEADS, HEAD_WIDTH)
    value_view = value_rows.reshape(rows_here, KEY_VALUE_HEADS, HEAD_WIDTH)
    score_scale = HEAD_WIDTH ** (-0.5)

    def attend_block(block_item):
        query_blk, index_blk, start_blk = block_item
        head_view = query_blk.reshape(block_rows, KEY_VALUE_HEADS, group_heads, HEAD_WIDTH)
        scores = jnp.einsum('qkgd,nkd->kgqn', head_view, key_view, precision=PRECISE) * score_scale
        scores = lowrank_backward(scores)
        visible = (row_index[None, :] <= index_blk[:, None]) & (row_index[None, :] >= start_blk[:, None])
        scores = jnp.where(visible[None, None], scores, MASKED)
        probabilities = lowrank_rows(jax.nn.softmax(scores, axis=-1))
        mixed_out = jnp.einsum('kgqn,nkd->qkgd', probabilities, value_view, precision=PRECISE)
        return mixed_out.reshape(block_rows, -1)
    blocks = (query_rows.reshape(rows_here // block_rows, block_rows, -1), row_index.reshape(-1, block_rows), seq_start.reshape(-1, block_rows))
    return lax.map(jax.checkpoint(attend_block), blocks).reshape(rows_here, -1)

def group_layer_pass(input_value, adapter_input_factors, adapter_down_first, adapter_wide_second, adapter_key_value_second, adapter_hidden_second, adapter_router_second, frozen_weights, sequence_lengths, selected_experts, router_rows):
    norm_gain_pair, query_weight, key_weight, value_weight, output_weight_transposed, router_weight, expert_input_weight, expert_output_weight = frozen_weights
    rows_here = input_value.shape[0]
    row_index = jnp.arange(rows_here, dtype=jnp.int32)
    seq_start, adapter_pick = token_meta(sequence_lengths, selected_experts, row_index)
    stacked_mask = (jnp.arange(ADAPTER_COUNT * ADAPTER_RANK, dtype=jnp.int32)[None, :] // ADAPTER_RANK == adapter_pick[:, None]).astype(jnp.float32)
    cosine_table, sine_table = rope_tables(row_index - seq_start)
    inv_one = lax.rsqrt(lax.optimization_barrier(jnp.mean(input_value * input_value, axis=1, keepdims=True)) + EPSILON)
    normed_input = lowrank_rows(input_value * inv_one * norm_gain_pair[:, 0])
    query_rows = matrix_product_precise(normed_input, query_weight) + matrix_product_precise(adapter_contribution(normed_input, adapter_input_factors[0], stacked_mask), adapter_wide_second[0])
    key_rows = matrix_product_precise(normed_input, key_weight) + matrix_product_precise(adapter_contribution(normed_input, adapter_input_factors[1], stacked_mask), adapter_key_value_second[0])
    value_rows = matrix_product_precise(normed_input, value_weight) + matrix_product_precise(adapter_contribution(normed_input, adapter_input_factors[2], stacked_mask), adapter_key_value_second[1])
    query_rows = lowrank_rows(rotate(lowrank_backward(query_rows), cosine_table, sine_table))
    key_rows = lowrank_rows(rotate(lowrank_backward(key_rows), cosine_table, sine_table))
    value_rows = lowrank_rows(lowrank_backward(value_rows))
    attention_output = lowrank_rows(lowrank_backward(attend(query_rows, key_rows, value_rows, row_index, seq_start)))
    adapter_branch = matrix_product_precise(attention_output, output_weight_transposed.T) + matrix_product_precise(adapter_contribution(attention_output, adapter_input_factors[6], stacked_mask), adapter_wide_second[1])
    hidden_state = input_value + lowrank_backward(adapter_branch)
    inv_two = lax.rsqrt(lax.optimization_barrier(jnp.mean(hidden_state * hidden_state, axis=1, keepdims=True)) + EPSILON)
    second_normed_input = lowrank_rows(hidden_state * inv_two * norm_gain_pair[:, 1])
    router_logits = matrix_product_precise(second_normed_input, router_weight) + matrix_product_precise(adapter_contribution(second_normed_input, adapter_input_factors[3], stacked_mask), adapter_router_second)
    router_logits = lowrank_backward(router_logits)
    picks = router_rows[:, :, None] == jnp.arange(EXPERT_COUNT, dtype=jnp.int32)[None, None, :]
    picked = lax.optimization_barrier(jnp.sum(jnp.where(picks, router_logits[:, None, :], 0.0), axis=2))
    gates = jax.nn.softmax(picked, axis=1)
    expert_weight = lax.optimization_barrier(jnp.sum(jnp.where(picks, gates[:, :, None], 0.0), axis=1))
    gate_lifted = lowrank_rows(matrix_product_precise(adapter_contribution(second_normed_input, adapter_input_factors[4], stacked_mask), adapter_hidden_second[0]))
    upward_lifted = lowrank_rows(matrix_product_precise(adapter_contribution(second_normed_input, adapter_input_factors[5], stacked_mask), adapter_hidden_second[1]))
    lifted_rows = jnp.concatenate([gate_lifted, upward_lifted], axis=1)

    def expert_step(carry_in, expert_item):
        weight_in, weight_out, weight_now = expert_item
        expert_total, combined = carry_in
        inputs = lowrank_backward(second_normed_input)
        preactivation = matrix_product_precise(inputs, weight_in) + lifted_rows
        gate_part = lowrank_backward(preactivation[:, :HIDDEN_UNITS])
        up_part = lowrank_backward(preactivation[:, HIDDEN_UNITS:])
        inner_activation = lowrank_rows(jax.nn.silu(gate_part) * up_part)
        result = lowrank_rows(lowrank_backward(matrix_product_precise(inner_activation, weight_out.T)))
        reduced_output = lowrank_rows(lowrank_backward(matrix_product_precise(inner_activation, adapter_down_first)))
        return ((expert_total + weight_now[:, None] * result, combined + weight_now[:, None] * reduced_output), None)
    start_carry = (jnp.zeros((rows_here, MODEL_WIDTH), jnp.float32), jnp.zeros((rows_here, ADAPTER_COUNT * ADAPTER_RANK), jnp.float32))
    expert_items = (jnp.moveaxis(expert_input_weight, 1, 0), jnp.moveaxis(expert_output_weight, 1, 0), expert_weight.T)
    (experts_combined_sum, combined), _ = lax.scan(jax.checkpoint(expert_step), start_carry, expert_items)
    down_lowrank = lowrank_rows(lowrank_backward(combined * stacked_mask))
    return hidden_state + experts_combined_sum + matrix_product_precise(down_lowrank, adapter_wide_second[2])

def reference(tokens, cotangent, lengths, adapter_index, routes, deal, norm_gain_pair, query_weight, key_weight, value_weight, output_weight_transposed, router_weight, expert_input_weight, expert_output_weight, adapter_input_factors, adapter_down_first, adapter_wide_second, adapter_key_value_second, adapter_hidden_second, adapter_router_second):
    frozen_weights = tuple((weight.astype(jnp.float32) for weight in (norm_gain_pair, query_weight, key_weight, value_weight, output_weight_transposed, router_weight, expert_input_weight, expert_output_weight)))
    groups = lengths.shape[0]
    group_ids = jnp.arange(groups, dtype=jnp.int32)
    inverse = lax.optimization_barrier(jnp.sum(jnp.where(deal[:, None] == group_ids[None, :], group_ids[:, None], 0), axis=0)).astype(jnp.int32)

    def forward_pass(input_everything, adapter_first_factor, down_first_factor, wide_second_factor, key_value_second_factor, hidden_second_factor, router_second_factor):

        def one_group(group_item):
            input_group, sequence_lengths, selected_experts, router_rows = group_item
            return group_layer_pass(input_group, adapter_first_factor, down_first_factor, wide_second_factor, key_value_second_factor, hidden_second_factor, router_second_factor, frozen_weights, sequence_lengths, selected_experts, router_rows)
        dealt = jnp.take(input_everything.reshape(groups, -1, MODEL_WIDTH), deal, axis=0)
        shaped = (dealt, lengths, adapter_index, routes.reshape(groups, -1, TOPK))
        outs_dealt = lax.map(jax.checkpoint(one_group), shaped)
        return jnp.take(outs_dealt, inverse, axis=0).reshape(-1, MODEL_WIDTH)
    primal_inputs = (tokens.astype(jnp.float32), adapter_input_factors.astype(jnp.float32), adapter_down_first.astype(jnp.float32), adapter_wide_second.astype(jnp.float32), adapter_key_value_second.astype(jnp.float32), adapter_hidden_second.astype(jnp.float32), adapter_router_second.astype(jnp.float32))
    output, pullback = jax.vjp(forward_pass, *primal_inputs)
    gradients = pullback(cotangent.astype(jnp.float32))
    return (output.astype(jnp.bfloat16), gradients[0], gradients[1], gradients[2], gradients[3], gradients[4], gradients[5], gradients[6])
```

```python
import functools

import jax
import jax.numpy as jnp
from jax import lax
from jax.experimental import pallas as pl
from jax.experimental.pallas import tpu as pltpu
from jax.sharding import PartitionSpec as P

MODEL_WIDTH = 1024
HEADS = 16
KEY_VALUE_HEADS = 8
HEAD_WIDTH = 64
HIDDEN_UNITS = 512
TOPK = 8
EXPERT_COUNT = 16
ADAPTER_COUNT = 8
ADAPTER_RANK = 16
STACKED = ADAPTER_COUNT * ADAPTER_RANK

EPSILON = 1e-06
ROPE_BASE = 10000.0
MASKED = -1e30
BLOCK = 256
LANES = 128

BF = jnp.bfloat16
F32 = jnp.float32


def dot(a, b, ca=1, cb=0):
    return lax.dot_general(a, b, (((ca,), (cb,)), ((), ())), preferred_element_type=F32)


def splits(v):
    hi = v.astype(BF).astype(F32)
    rest = v - hi
    mid = rest.astype(BF).astype(F32)
    return hi, mid, rest - mid


def lane_of(shape):
    return lax.broadcasted_iota(jnp.int32, shape, len(shape) - 1)


def row_of(shape):
    return lax.broadcasted_iota(jnp.int32, shape, 0)


def attend_kernel(heads, lens_ref, qkv_ref, out_ref, q_ref, k_ref, v_ref):
    total = qkv_ref.shape[0]
    count = total // BLOCK
    rows = heads * BLOCK
    nseq = lens_ref.shape[1]
    half = HEAD_WIDTH

    def prepare(i, carry):
        at = pl.ds(pl.multiple_of(i * BLOCK, BLOCK), BLOCK)
        low = lane_of((BLOCK, LANES)) < half
        lane = lane_of((BLOCK, LANES))
        row = row_of((BLOCK, LANES)) + i * BLOCK
        first = jnp.int32(0)
        seq = jnp.zeros((BLOCK, LANES), jnp.bool_)
        for s in range(nseq):
            last = first + lens_ref[0, s]
            seq = seq | ((lane == s) & (row >= first) & (row < last))
            first = last
        queries = qkv_ref[at, 0:LANES].astype(F32) * (HEAD_WIDTH ** -0.5)
        pair = qkv_ref[at, LANES : 2 * LANES].astype(F32)
        turned = pltpu.roll(pair, half, 1)
        marks = jnp.where(seq, 1.0, 0.0).astype(BF)
        for h in range(heads):
            mine = jnp.where(low if h == 0 else ~low, queries, 0.0).astype(BF)
            base = pl.ds(pl.multiple_of(i * rows + h * BLOCK, BLOCK), BLOCK)
            q_ref[base, 0:LANES] = mine
            q_ref[base, LANES : 2 * LANES] = marks
        k_ref[at, 0:LANES] = jnp.where(low, pair, turned).astype(BF)
        far = jnp.where(lane < nseq, jnp.where(seq, 0.0, MASKED), 0.0)
        k_ref[at, LANES : 2 * LANES] = jnp.where(
            (lane >= nseq) & (lane < nseq + 3), 1.0, far
        ).astype(BF)
        v_ref[at, 0:LANES] = jnp.where(low, turned, pair).astype(BF)
        v_ref[at, LANES : 2 * LANES] = jnp.ones((BLOCK, LANES), BF)
        return carry

    lax.fori_loop(0, count, prepare, 0)

    def one_block(i, carry):
        at = pl.ds(pl.multiple_of(i * BLOCK, BLOCK), BLOCK)
        base = pl.ds(pl.multiple_of(i * rows, rows), rows)
        first = jnp.int32(0)
        start = jnp.int32(0)
        for s in range(nseq):
            start = jnp.where(i * BLOCK >= first, first, start)
            first = first + lens_ref[0, s]
        queries = q_ref[base, :]

        def step(j, state, diagonal):
            top, acc = state
            here = pl.ds(pl.multiple_of(j * BLOCK, BLOCK), BLOCK)
            scores = dot(queries, k_ref[here, :], 1, 1)
            if diagonal:
                row = jnp.concatenate([row_of((BLOCK, BLOCK))] * heads, axis=0)
                scores = jnp.where(lane_of((rows, BLOCK)) <= row, scores, MASKED)
            new_top = jnp.maximum(top, jnp.max(scores, axis=1, keepdims=True))
            weights = jnp.exp(scores - new_top).astype(BF)
            acc = acc * jnp.exp(top - new_top) + dot(weights, v_ref[here, :])
            return new_top, acc

        state = (jnp.full((rows, 1), MASKED, F32), jnp.zeros((rows, 2 * LANES), F32))
        state = lax.fori_loop(start // BLOCK, i, lambda j, s: step(j, s, False), state)
        top, acc = step(i, state, True)
        weight = acc[:, LANES:]
        mixed = acc[:, :LANES] / weight
        hi, mid, lo = splits(-(top + jnp.log(weight)))
        lane = lane_of((rows, LANES))
        marks = q_ref[base, LANES : 2 * LANES].astype(F32)
        marks = jnp.where(lane == nseq, hi, marks)
        marks = jnp.where(lane == nseq + 1, mid, marks)
        marks = jnp.where(lane == nseq + 2, lo, marks)
        q_ref[base, LANES : 2 * LANES] = marks.astype(BF)
        if heads == 1:
            out_ref[at, :] = mixed.astype(BF)
        else:
            low = lane_of((BLOCK, LANES)) < half
            out_ref[at, :] = jnp.where(low, mixed[:BLOCK], mixed[BLOCK:]).astype(BF)
        return carry

    lax.fori_loop(0, count, one_block, 0)


def attend(lens, qkv, heads):
    total = qkv.shape[0]
    vmem = pl.BlockSpec(memory_space=pltpu.VMEM)
    return pl.pallas_call(
        functools.partial(attend_kernel, heads),
        out_shape=(
            jax.ShapeDtypeStruct((total, LANES), BF),
            jax.ShapeDtypeStruct((heads * total, 2 * LANES), BF),
            jax.ShapeDtypeStruct((total, 2 * LANES), BF),
            jax.ShapeDtypeStruct((total, 2 * LANES), BF),
        ),
        in_specs=[pl.BlockSpec(memory_space=pltpu.SMEM), vmem],
        out_specs=(vmem,) * 4,
        compiler_params=pltpu.CompilerParams(vmem_limit_bytes=48 << 20),
        name="attend",
    )(lens, qkv)


def attend_back_kernel(
    heads, lens_ref, q_ref, k_ref, v_ref, out_ref, grad_ref, back_ref, g_ref, dq_ref
):
    total = out_ref.shape[0]
    count = total // BLOCK
    rows = heads * BLOCK
    nseq = lens_ref.shape[1]
    half = HEAD_WIDTH
    low = lane_of((BLOCK, LANES)) < half
    lane = lane_of((BLOCK, LANES))

    def prepare(i, carry):
        at = pl.ds(pl.multiple_of(i * BLOCK, BLOCK), BLOCK)
        grad = grad_ref[at, :].astype(F32)
        both = grad * out_ref[at, :].astype(F32)
        for h in range(heads):
            part = low if h == 0 else ~low
            delta = jnp.sum(jnp.where(part, both, 0.0), axis=1, keepdims=True)
            hi, mid, lo = splits(-delta)
            extra = jnp.where(lane == 0, hi, jnp.where(lane == 1, mid, jnp.where(lane == 2, lo, 0.0)))
            base = pl.ds(pl.multiple_of(i * rows + h * BLOCK, BLOCK), BLOCK)
            g_ref[base, 0:LANES] = jnp.where(part, grad, 0.0).astype(BF)
            g_ref[base, LANES : 2 * LANES] = extra.astype(BF)
            dq_ref[base, :] = jnp.zeros((BLOCK, LANES), F32)
        return carry

    lax.fori_loop(0, count, prepare, 0)

    def one_block(j, carry):
        here = pl.ds(pl.multiple_of(j * BLOCK, BLOCK), BLOCK)
        final = (j + 1) * BLOCK - 1
        first = jnp.int32(0)
        stop = jnp.int32(0)
        for s in range(nseq):
            last = first + lens_ref[0, s]
            stop = jnp.where(final >= first, last, stop)
            first = last
        keys = k_ref[here, :]
        values = v_ref[here, :]

        def step(i, state, diagonal):
            dk, dv = state
            base = pl.ds(pl.multiple_of(i * rows, rows), rows)
            queries = q_ref[base, :]
            grads = g_ref[base, :]
            weights = jnp.exp(dot(keys, queries, 1, 1))
            if diagonal:
                column = jnp.concatenate([lane_of((BLOCK, BLOCK))] * heads, axis=1)
                weights = jnp.where(row_of((BLOCK, rows)) <= column, weights, 0.0)
            slope = (weights * dot(values, grads, 1, 1)).astype(BF)
            dv = dv + dot(weights.astype(BF), grads[:, :LANES])
            dk = dk + dot(slope, queries[:, :LANES])
            dq_ref[base, :] += dot(slope, keys[:, :LANES], 0, 0)
            return dk, dv

        zero = jnp.zeros((BLOCK, LANES), F32)
        state = step(j, (zero, zero), True)
        dk, dv = lax.fori_loop(
            j + 1, (stop - 1) // BLOCK + 1, lambda i, s: step(i, s, False), state
        )
        back_ref[here, LANES : 2 * LANES] = jnp.where(
            low, dk + pltpu.roll(dk, half, 1), dv + pltpu.roll(dv, half, 1)
        ).astype(BF)
        return carry

    lax.fori_loop(0, count, one_block, 0)

    def finish(i, carry):
        at = pl.ds(pl.multiple_of(i * BLOCK, BLOCK), BLOCK)
        base = pl.multiple_of(i * rows, rows)
        mine = dq_ref[pl.ds(base, BLOCK), :]
        if heads == 2:
            mine = jnp.where(low, mine, dq_ref[pl.ds(base + BLOCK, BLOCK), :])
        back_ref[at, 0:LANES] = (mine * (HEAD_WIDTH ** -0.5)).astype(BF)
        return carry

    lax.fori_loop(0, count, finish, 0)


def attend_back(lens, q, k, v, out, grad, heads):
    total = out.shape[0]
    vmem = pl.BlockSpec(memory_space=pltpu.VMEM)
    return pl.pallas_call(
        functools.partial(attend_back_kernel, heads),
        out_shape=jax.ShapeDtypeStruct((total, 2 * LANES), BF),
        in_specs=[pl.BlockSpec(memory_space=pltpu.SMEM)] + [vmem] * 5,
        out_specs=vmem,
        scratch_shapes=[
            pltpu.VMEM((heads * total, 2 * LANES), BF),
            pltpu.VMEM((heads * total, LANES), F32),
        ],
        compiler_params=pltpu.CompilerParams(vmem_limit_bytes=56 << 20),
        name="attend_back",
    )(lens, q, k, v, out, grad)


def experts_kernel(
    first_expert_ref,
    n2_ref,
    grad_ref,
    mask_ref,
    win_ref,
    wout_ref,
    wide_ref,
    hid_ref,
    down_ref,
    spread_ref,
    fold_ref,
    out_ref,
    back_ref,
    gdown_ref,
    ghid_ref,
):
    local_experts = win_ref.shape[0]
    rows = n2_ref.shape[0]
    width = HIDDEN_UNITS
    step = pl.program_id(0)
    lane = lane_of((rows, LANES))
    n2 = n2_ref[:, :MODEL_WIDTH]
    side = n2_ref[:, MODEL_WIDTH:]
    grad = grad_ref[...]
    mask = mask_ref[...].astype(F32)
    lows = dot(side, spread_ref[...])
    low_gate = (lows[:, :STACKED] * mask).astype(BF)
    low_up = (lows[:, STACKED:] * mask).astype(BF)
    lift_gate = dot(low_gate, hid_ref[0])
    lift_up = dot(low_up, hid_ref[1])
    down_grad = (dot(grad, wide_ref[...], 1, 1) * mask).astype(BF)
    from_down = dot(down_grad, down_ref[...], 1, 1)
    side_full = side.astype(F32)
    total_inner = jnp.zeros((rows, width), F32)
    total_gate = jnp.zeros((rows, width), F32)
    total_up = jnp.zeros((rows, width), F32)
    out = jnp.zeros((rows, MODEL_WIDTH), F32)
    back = jnp.zeros((rows, MODEL_WIDTH), F32)
    extra = jnp.zeros((rows, LANES), F32)
    for e in range(local_experts):
        name = first_expert_ref[0] + e
        at_high, at_low = lane == name, lane == name + EXPERT_COUNT
        gate = jnp.sum(jnp.where(at_high | at_low, side_full, 0.0), axis=1, keepdims=True)
        pre_gate = dot(n2, win_ref[e, :, :width]) + lift_gate
        pre_up = dot(n2, win_ref[e, :, width:]) + lift_up
        pulled = dot(grad, wout_ref[e]) + from_down
        squashed = jax.nn.sigmoid(pre_gate)
        active = pre_gate * squashed
        inner = active * pre_up
        gate_grad = jnp.sum(inner * pulled, axis=1, keepdims=True)
        high = gate_grad.astype(BF).astype(F32)
        extra = extra + jnp.where(at_high, high, 0.0) + jnp.where(at_low, gate_grad - high, 0.0)
        gated = inner * gate
        pulled = pulled * gate
        grad_gate = pulled * pre_up * (squashed + active * (1.0 - squashed))
        grad_up = pulled * active
        gated_low = gated.astype(BF)
        gate_low = grad_gate.astype(BF)
        up_low = grad_up.astype(BF)
        out = out + dot(gated_low, wout_ref[e], 1, 1)
        back = (
            back
            + dot(gate_low, win_ref[e, :, :width], 1, 1)
            + dot(up_low, win_ref[e, :, width:], 1, 1)
        )
        total_inner = total_inner + gated
        total_gate = total_gate + grad_gate
        total_up = total_up + grad_up
    total_inner = total_inner.astype(BF)
    total_gate = total_gate.astype(BF)
    total_up = total_up.astype(BF)
    small = jnp.concatenate(
        [
            (dot(total_gate, hid_ref[0], 1, 1) * mask).astype(BF),
            (dot(total_up, hid_ref[1], 1, 1) * mask).astype(BF),
            (dot(total_inner, down_ref[...]) * mask).astype(BF),
        ],
        axis=1,
    )
    extra = extra + dot(small, fold_ref[...])
    out_ref[...] = out.astype(BF)
    back_ref[:, :MODEL_WIDTH] = back.astype(BF)
    back_ref[:, MODEL_WIDTH:] = extra.astype(BF)
    gdown = dot(total_inner, down_grad, 0, 0)
    ghid_gate = dot(low_gate, total_gate, 0, 0)
    ghid_up = dot(low_up, total_up, 0, 0)

    @pl.when(step == 0)
    def _():
        gdown_ref[...] = gdown
        ghid_ref[0] = ghid_gate
        ghid_ref[1] = ghid_up

    @pl.when(step != 0)
    def _():
        gdown_ref[...] += gdown
        ghid_ref[0] += ghid_gate
        ghid_ref[1] += ghid_up


def experts(first, n2, grad, mask, win, wout, wide, hid, down, rows):
    total = n2.shape[0]
    side = n2.shape[1]
    source = jnp.arange(LANES, dtype=jnp.int32)
    place = jnp.arange(STACKED, dtype=jnp.int32) % ADAPTER_RANK
    spread = jnp.concatenate(
        [(source[:, None] == offset + place[None, :]) for offset in (32, 48)], axis=1
    ).astype(BF)
    fold = jnp.concatenate(
        [(source[None, :] == offset + place[:, None]) for offset in (32, 48, 64)], axis=0
    ).astype(BF)

    def whole(array):
        return pl.BlockSpec(
            array.shape, lambda i: (0,) * array.ndim, pipeline_mode=pl.Buffered(1)
        )

    def block(columns):
        return pl.BlockSpec((rows, columns), lambda i: (i, 0))

    return pl.pallas_call(
        experts_kernel,
        grid=(total // rows,),
        out_shape=(
            jax.ShapeDtypeStruct((total, MODEL_WIDTH), BF),
            jax.ShapeDtypeStruct((total, side), BF),
            jax.ShapeDtypeStruct((HIDDEN_UNITS, STACKED), F32),
            jax.ShapeDtypeStruct((2, STACKED, HIDDEN_UNITS), F32),
        ),
        in_specs=[
            pl.BlockSpec(memory_space=pltpu.SMEM),
            block(side),
            block(MODEL_WIDTH),
            block(STACKED),
            whole(win),
            whole(wout),
            whole(wide),
            whole(hid),
            whole(down),
            whole(spread),
            whole(fold),
        ],
        out_specs=(
            block(MODEL_WIDTH),
            block(side),
            pl.BlockSpec((HIDDEN_UNITS, STACKED), lambda i: (0, 0)),
            pl.BlockSpec((2, STACKED, HIDDEN_UNITS), lambda i: (0, 0, 0)),
        ),
        compiler_params=pltpu.CompilerParams(vmem_limit_bytes=56 << 20),
        name="experts",
    )(first, n2, grad, mask, win, wout, wide, hid, down, spread, fold)


def plane_gather(rows):
    return lax.all_gather(rows, "fsdp", axis=0, tiled=True)


def plane_scatter(rows):
    return lax.psum_scatter(rows, "fsdp", scatter_dimension=0, tiled=True)


def plane_swap(blocks):
    return lax.all_to_all(blocks, "fsdp", split_axis=0, concat_axis=0, tiled=True)


def gather_all(rows):
    return lax.all_gather(rows, ("dp", "fsdp"), axis=0, tiled=True)


def rotate(tensor, cosine, sine):
    rows = tensor.shape[0]
    view = tensor.reshape(rows, -1, 2, HEAD_WIDTH // 2)
    first, second = view[:, :, 0], view[:, :, 1]
    c, s = cosine[:, None, :], sine[:, None, :]
    turned = jnp.stack([first * c - second * s, second * c + first * s], axis=2)
    return turned.reshape(rows, -1)


def local(
    tokens,
    cotangent,
    lengths,
    adapter_index,
    routes,
    deal,
    norm_gain_pair,
    query_weight,
    key_weight,
    value_weight,
    output_weight_transposed,
    router_weight,
    expert_input_weight,
    expert_output_weight,
    factors,
    down_first,
    wide,
    kv_second,
    hidden_second,
    router_second,
):
    shards = lax.axis_size("fsdp")
    groups = lax.axis_size("dp")
    rows = tokens.shape[0]
    total = rows * shards
    heads = HEADS // shards
    share = max(1, shards // KEY_VALUE_HEADS)
    me = lax.axis_index("fsdp")

    group_ids = jnp.arange(groups, dtype=jnp.int32)
    dealt = jnp.sum(jnp.where(deal == lax.axis_index("dp"), group_ids, 0))

    def of_group(array):
        everything = lax.all_gather(array, "dp", axis=0, tiled=False)
        return lax.dynamic_index_in_dim(everything, dealt, 0, keepdims=False)

    lens = of_group(lengths)
    chosen = of_group(adapter_index)[0]
    routes = of_group(routes)

    offsets = jnp.cumsum(lens[0]) - lens[0]
    index = jnp.arange(total, dtype=jnp.int32)
    ends = offsets + lens[0]
    inside = (index[:, None] >= offsets[None, :]) & (index[:, None] < ends[None, :])
    pick = jnp.sum(jnp.where(inside, chosen[None, :], 0), axis=1)
    begin = jnp.sum(jnp.where(inside, offsets[None, :], 0), axis=1)
    group_mask = (
        jnp.arange(STACKED, dtype=jnp.int32)[None, :] // ADAPTER_RANK == pick[:, None]
    ).astype(BF)
    mask_low = lax.dynamic_slice_in_dim(group_mask, me * rows, rows, 0)
    mask = mask_low.astype(F32)
    position = lax.dynamic_slice_in_dim(index - begin, me * rows, rows, 0)
    half = HEAD_WIDTH // 2
    frequency = ROPE_BASE ** (-jnp.arange(half, dtype=F32) / half)
    angles = position.astype(F32)[:, None] * frequency[None, :]
    cosine, sine = jnp.cos(angles), jnp.sin(angles)

    packed = jnp.concatenate(
        [
            query_weight,
            key_weight,
            value_weight,
            output_weight_transposed,
            router_weight,
            norm_gain_pair,
            jnp.zeros((router_weight.shape[0], LANES - EXPERT_COUNT - 2), BF),
        ],
        axis=1,
    )
    packed = gather_all(packed)
    in_width = 2 * MODEL_WIDTH
    in_weight = packed[:, :in_width]
    out_weight = packed[:, in_width : in_width + MODEL_WIDTH]
    router = packed[:, 3 * MODEL_WIDTH : 3 * MODEL_WIDTH + EXPERT_COUNT]
    gains = packed[:, 3 * MODEL_WIDTH + EXPERT_COUNT : 3 * MODEL_WIDTH + EXPERT_COUNT + 2].astype(F32)

    win = jnp.transpose(expert_input_weight, (1, 0, 2))
    wout = jnp.transpose(expert_output_weight, (1, 0, 2))
    all_grad = plane_gather(cotangent)

    x = tokens.astype(F32)
    r1 = lax.rsqrt(jnp.mean(x * x, axis=1, keepdims=True) + EPSILON)
    normed = (x * r1 * gains[:, 0]).astype(BF)
    first_low = [(dot(normed, factors[s]) * mask).astype(BF) for s in range(3)]
    mixed = dot(normed, in_weight)
    query = rotate(mixed[:, :MODEL_WIDTH] + dot(first_low[0], wide[0]), cosine, sine)
    split = MODEL_WIDTH + KEY_VALUE_HEADS * HEAD_WIDTH
    keys = rotate(mixed[:, MODEL_WIDTH:split] + dot(first_low[1], kv_second[0]), cosine, sine)
    values = mixed[:, split:] + dot(first_low[2], kv_second[1])

    def by_head(array, count, repeat):
        array = array.astype(BF).reshape(rows, count, -1).transpose(1, 0, 2)
        return jnp.repeat(array, repeat, axis=0) if repeat > 1 else array

    query = by_head(query, shards, 1)
    if query.shape[2] < LANES:
        query = jnp.pad(query, ((0, 0), (0, 0), (0, LANES - query.shape[2])))
    parts = jnp.concatenate(
        [query, by_head(keys, KEY_VALUE_HEADS, share), by_head(values, KEY_VALUE_HEADS, share)],
        axis=2,
    )
    qkv = plane_swap(parts).reshape(total, -1)
    attended, q_kept, k_kept, v_kept = attend(lens, qkv, heads)

    def home(array, columns):
        swapped = plane_swap(array.reshape(shards, rows, -1))
        return swapped[:, :, :columns].transpose(1, 0, 2).reshape(rows, -1)

    mine = home(attended, heads * HEAD_WIDTH)
    out_low = (dot(mine, factors[6]) * mask).astype(BF)
    hidden = x + dot(mine, out_weight, 1, 1) + dot(out_low, wide[1])
    r2 = lax.rsqrt(jnp.mean(hidden * hidden, axis=1, keepdims=True) + EPSILON)
    normed_two = (hidden * r2 * gains[:, 1]).astype(BF)
    second_low = [(dot(normed_two, factors[3 + s]) * mask).astype(BF) for s in range(3)]
    logits = dot(normed_two, router) + dot(second_low[0], router_second)
    chosen_experts = jnp.sum(
        (routes[:, :, None] == jnp.arange(EXPERT_COUNT, dtype=jnp.int32)).astype(F32), axis=1
    )
    picked = chosen_experts > 0
    peak = jnp.max(jnp.where(picked, logits, MASKED), axis=1, keepdims=True)
    lifted = jnp.where(picked, jnp.exp(logits - peak), 0.0)
    gates = lifted / jnp.sum(lifted, axis=1, keepdims=True)

    def compact(array):
        return jnp.sum(array.astype(F32).reshape(rows, ADAPTER_COUNT, ADAPTER_RANK), axis=1)

    def expand(array):
        return jnp.tile(array, (1, ADAPTER_COUNT))

    gate_high = gates.astype(BF).astype(F32)
    side = jnp.concatenate(
        [
            gate_high,
            gates - gate_high,
            compact(second_low[1]),
            compact(second_low[2]),
            jnp.zeros((rows, LANES - 64), F32),
        ],
        axis=1,
    ).astype(BF)
    everyone = plane_gather(jnp.concatenate([normed_two, side], axis=1))
    local_experts = win.shape[0]
    out_part, back_part, g_down_a, g_ff = experts(
        (me * local_experts).astype(jnp.int32)[None],
        everyone,
        all_grad,
        group_mask,
        win,
        wout,
        wide[2],
        hidden_second,
        down_first,
        rows,
    )
    out_sum = plane_scatter(out_part).astype(F32)
    back_sum = plane_scatter(back_part).astype(F32)

    grad = cotangent.astype(F32)
    extra = back_sum[:, MODEL_WIDTH:]
    gate_grad = extra[:, 0:16] + extra[:, 16:32]
    down_low = (expand(extra[:, 64:80]) * mask).astype(BF)
    layer_out = (hidden + out_sum + dot(down_low, wide[2])).astype(BF)
    g_wide_down = dot(down_low, cotangent, 0, 0)
    logit_grad = (
        gates * (gate_grad - jnp.sum(gates * gate_grad, axis=1, keepdims=True))
    ).astype(BF)
    g_route = dot(second_low[0], logit_grad, 0, 0)
    second_grad = [
        (dot(logit_grad, router_second, 1, 1) * mask).astype(BF),
        (expand(extra[:, 32:48]) * mask).astype(BF),
        (expand(extra[:, 48:64]) * mask).astype(BF),
    ]
    normed_two_grad = back_sum[:, :MODEL_WIDTH] + dot(logit_grad, router, 1, 1)
    for s in range(3):
        normed_two_grad = normed_two_grad + dot(second_grad[s], factors[3 + s], 1, 1)
    g_second = [dot(normed_two, second_grad[s], 0, 0) for s in range(3)]
    w2 = gains[:, 1] * normed_two_grad
    hidden_grad = grad + r2 * w2 - hidden * r2**3 * jnp.mean(w2 * hidden, axis=1, keepdims=True)
    out_grad = hidden_grad.astype(BF)
    g_wide_out = dot(out_low, out_grad, 0, 0)
    out_low_grad = (dot(out_grad, wide[1], 1, 1) * mask).astype(BF)
    g_factor_out = dot(mine, out_low_grad, 0, 0)
    attended_grad = (dot(out_grad, out_weight) + dot(out_low_grad, factors[6], 1, 1)).astype(BF)
    to_heads = by_head(attended_grad, shards, 1)
    if to_heads.shape[2] < LANES:
        to_heads = jnp.pad(to_heads, ((0, 0), (0, 0), (0, LANES - to_heads.shape[2])))
    head_grad = plane_swap(to_heads).reshape(total, -1)
    qkv_grad = attend_back(lens, q_kept, k_kept, v_kept, attended, head_grad, heads)
    qkv_grad = plane_swap(qkv_grad.reshape(shards, rows, -1)).astype(F32)

    def joined(array):
        array = array.reshape(shards // share, share, rows, -1).sum(1)
        return array.transpose(1, 0, 2).reshape(rows, -1)

    query_grad = qkv_grad[:, :, : heads * HEAD_WIDTH].transpose(1, 0, 2).reshape(rows, -1)
    query_grad = rotate(query_grad, cosine, -sine).astype(BF)
    keys_grad = rotate(joined(qkv_grad[:, :, LANES : LANES + 64]), cosine, -sine).astype(BF)
    values_grad = joined(qkv_grad[:, :, LANES + 64 :]).astype(BF)
    mixed_grad = jnp.concatenate([query_grad, keys_grad, values_grad], axis=1)
    normed_grad = dot(mixed_grad, in_weight, 1, 1)
    first_grad = [
        (dot(query_grad, wide[0], 1, 1) * mask).astype(BF),
        (dot(keys_grad, kv_second[0], 1, 1) * mask).astype(BF),
        (dot(values_grad, kv_second[1], 1, 1) * mask).astype(BF),
    ]
    for s in range(3):
        normed_grad = normed_grad + dot(first_grad[s], factors[s], 1, 1)
    g_first = [dot(normed, first_grad[s], 0, 0) for s in range(3)]
    g_wide_query = dot(first_low[0], query_grad, 0, 0)
    g_kv = [dot(first_low[1], keys_grad, 0, 0), dot(first_low[2], values_grad, 0, 0)]
    w1 = gains[:, 0] * normed_grad
    input_grad = hidden_grad + r1 * w1 - x * r1**3 * jnp.mean(w1 * x, axis=1, keepdims=True)

    sums = lax.psum(
        (
            jnp.stack(g_first + g_second + [g_factor_out]),
            g_down_a,
            jnp.stack([g_wide_query, g_wide_out, g_wide_down]),
            jnp.stack(g_kv),
            g_ff,
            g_route,
        ),
        ("dp", "fsdp"),
    )
    return (layer_out, input_grad) + tuple(sums)


def solution(mesh):
    rows = P(("dp", "fsdp"), None)
    placed = (
        (rows, rows, P("dp", None), P("dp", None), rows, P())
        + (rows,) * 6
        + (P(None, "fsdp", None),) * 2
        + (P(),) * 6
    )
    return jax.shard_map(
        local,
        mesh=mesh,
        in_specs=placed,
        out_specs=(rows, rows) + (P(),) * 6,
        check_vma=False,
    )
```

```python
import functools
import math

import jax
import jax.numpy as jnp
from jax import lax
from jax.experimental import pallas as pl
from jax.experimental.pallas import tpu as pltpu
from jax.sharding import PartitionSpec as P

MODEL_WIDTH = 1024
HEADS = 16
KEY_VALUE_HEADS = 8
HEAD_WIDTH = 64
HIDDEN_UNITS = 512
TOPK = 8
EXPERT_COUNT = 16
ADAPTER_COUNT = 8
ADAPTER_RANK = 16
STACKED = ADAPTER_COUNT * ADAPTER_RANK

EPSILON = 1e-06
ROPE_BASE = 10000.0
MASKED = -1e30
BLOCK = 256
LANES = 128

BF = jnp.bfloat16
F32 = jnp.float32
MESH = pl.DeviceIdType.MESH


def dot(a, b, ca=1, cb=0):
    return lax.dot_general(a, b, (((ca,), (cb,)), ((), ())), preferred_element_type=F32)


def splits(v):
    hi = v.astype(BF).astype(F32)
    rest = v - hi
    mid = rest.astype(BF).astype(F32)
    return hi, mid, rest - mid


def lane_of(shape):
    return lax.broadcasted_iota(jnp.int32, shape, len(shape) - 1)


def row_of(shape):
    return lax.broadcasted_iota(jnp.int32, shape, 0)


def attend_kernel(heads, lens_ref, qkv_ref, out_ref, q_ref, k_ref, v_ref):
    total = qkv_ref.shape[0]
    count = total // BLOCK
    rows = heads * BLOCK
    nseq = lens_ref.shape[1]
    half = HEAD_WIDTH

    def prepare(i, carry):
        at = pl.ds(pl.multiple_of(i * BLOCK, BLOCK), BLOCK)
        low = lane_of((BLOCK, LANES)) < half
        lane = lane_of((BLOCK, LANES))
        row = row_of((BLOCK, LANES)) + i * BLOCK
        first = jnp.int32(0)
        seq = jnp.zeros((BLOCK, LANES), jnp.bool_)
        for s in range(nseq):
            last = first + lens_ref[0, s]
            seq = seq | ((lane == s) & (row >= first) & (row < last))
            first = last
        queries = qkv_ref[at, 0:LANES].astype(F32) * (HEAD_WIDTH ** -0.5)
        pair = qkv_ref[at, LANES : 2 * LANES].astype(F32)
        turned = pltpu.roll(pair, half, 1)
        marks = jnp.where(seq, 1.0, 0.0).astype(BF)
        for h in range(heads):
            mine = jnp.where(low if h == 0 else ~low, queries, 0.0).astype(BF)
            base = pl.ds(pl.multiple_of(i * rows + h * BLOCK, BLOCK), BLOCK)
            q_ref[base, 0:LANES] = mine
            q_ref[base, LANES : 2 * LANES] = marks
        k_ref[at, 0:LANES] = jnp.where(low, pair, turned).astype(BF)
        far = jnp.where(lane < nseq, jnp.where(seq, 0.0, MASKED), 0.0)
        k_ref[at, LANES : 2 * LANES] = jnp.where(
            (lane >= nseq) & (lane < nseq + 3), 1.0, far
        ).astype(BF)
        v_ref[at, 0:LANES] = jnp.where(low, turned, pair).astype(BF)
        v_ref[at, LANES : 2 * LANES] = jnp.ones((BLOCK, LANES), BF)
        return carry

    lax.fori_loop(0, count, prepare, 0)

    def one_block(i, carry):
        at = pl.ds(pl.multiple_of(i * BLOCK, BLOCK), BLOCK)
        base = pl.ds(pl.multiple_of(i * rows, rows), rows)
        first = jnp.int32(0)
        start = jnp.int32(0)
        for s in range(nseq):
            start = jnp.where(i * BLOCK >= first, first, start)
            first = first + lens_ref[0, s]
        queries = q_ref[base, :]

        def step(j, state, diagonal):
            top, acc = state
            here = pl.ds(pl.multiple_of(j * BLOCK, BLOCK), BLOCK)
            scores = dot(queries, k_ref[here, :], 1, 1)
            if diagonal:
                row = jnp.concatenate([row_of((BLOCK, BLOCK))] * heads, axis=0)
                scores = jnp.where(lane_of((rows, BLOCK)) <= row, scores, MASKED)
            new_top = jnp.maximum(top, jnp.max(scores, axis=1, keepdims=True))
            weights = jnp.exp(scores - new_top).astype(BF)
            acc = acc * jnp.exp(top - new_top) + dot(weights, v_ref[here, :])
            return new_top, acc

        state = (jnp.full((rows, 1), MASKED, F32), jnp.zeros((rows, 2 * LANES), F32))
        state = lax.fori_loop(start // BLOCK, i, lambda j, s: step(j, s, False), state)
        top, acc = step(i, state, True)
        weight = acc[:, LANES:]
        mixed = acc[:, :LANES] / weight
        hi, mid, lo = splits(-(top + jnp.log(weight)))
        lane = lane_of((rows, LANES))
        marks = q_ref[base, LANES : 2 * LANES].astype(F32)
        marks = jnp.where(lane == nseq, hi, marks)
        marks = jnp.where(lane == nseq + 1, mid, marks)
        marks = jnp.where(lane == nseq + 2, lo, marks)
        q_ref[base, LANES : 2 * LANES] = marks.astype(BF)
        if heads == 1:
            out_ref[at, :] = mixed.astype(BF)
        else:
            low = lane_of((BLOCK, LANES)) < half
            out_ref[at, :] = jnp.where(low, mixed[:BLOCK], mixed[BLOCK:]).astype(BF)
        return carry

    lax.fori_loop(0, count, one_block, 0)


def attend(lens, qkv, heads):
    total = qkv.shape[0]
    vmem = pl.BlockSpec(memory_space=pltpu.VMEM)
    return pl.pallas_call(
        functools.partial(attend_kernel, heads),
        out_shape=(
            jax.ShapeDtypeStruct((total, LANES), BF),
            jax.ShapeDtypeStruct((heads * total, 2 * LANES), BF),
            jax.ShapeDtypeStruct((total, 2 * LANES), BF),
            jax.ShapeDtypeStruct((total, 2 * LANES), BF),
        ),
        in_specs=[pl.BlockSpec(memory_space=pltpu.SMEM), vmem],
        out_specs=(vmem,) * 4,
        compiler_params=pltpu.CompilerParams(vmem_limit_bytes=48 << 20),
        name="attend",
    )(lens, qkv)


def attend_back_kernel(
    heads, lens_ref, q_ref, k_ref, v_ref, out_ref, grad_ref, back_ref, g_ref, dq_ref
):
    total = out_ref.shape[0]
    count = total // BLOCK
    rows = heads * BLOCK
    nseq = lens_ref.shape[1]
    half = HEAD_WIDTH
    low = lane_of((BLOCK, LANES)) < half
    lane = lane_of((BLOCK, LANES))

    def prepare(i, carry):
        at = pl.ds(pl.multiple_of(i * BLOCK, BLOCK), BLOCK)
        grad = grad_ref[at, :].astype(F32)
        both = grad * out_ref[at, :].astype(F32)
        for h in range(heads):
            part = low if h == 0 else ~low
            delta = jnp.sum(jnp.where(part, both, 0.0), axis=1, keepdims=True)
            hi, mid, lo = splits(-delta)
            extra = jnp.where(lane == 0, hi, jnp.where(lane == 1, mid, jnp.where(lane == 2, lo, 0.0)))
            base = pl.ds(pl.multiple_of(i * rows + h * BLOCK, BLOCK), BLOCK)
            g_ref[base, 0:LANES] = jnp.where(part, grad, 0.0).astype(BF)
            g_ref[base, LANES : 2 * LANES] = extra.astype(BF)
            dq_ref[base, :] = jnp.zeros((BLOCK, LANES), F32)
        return carry

    lax.fori_loop(0, count, prepare, 0)

    def one_block(j, carry):
        here = pl.ds(pl.multiple_of(j * BLOCK, BLOCK), BLOCK)
        final = (j + 1) * BLOCK - 1
        first = jnp.int32(0)
        stop = jnp.int32(0)
        for s in range(nseq):
            last = first + lens_ref[0, s]
            stop = jnp.where(final >= first, last, stop)
            first = last
        keys = k_ref[here, :]
        values = v_ref[here, :]

        def step(i, state, diagonal):
            dk, dv = state
            base = pl.ds(pl.multiple_of(i * rows, rows), rows)
            queries = q_ref[base, :]
            grads = g_ref[base, :]
            weights = jnp.exp(dot(keys, queries, 1, 1))
            if diagonal:
                column = jnp.concatenate([lane_of((BLOCK, BLOCK))] * heads, axis=1)
                weights = jnp.where(row_of((BLOCK, rows)) <= column, weights, 0.0)
            slope = (weights * dot(values, grads, 1, 1)).astype(BF)
            dv = dv + dot(weights.astype(BF), grads[:, :LANES])
            dk = dk + dot(slope, queries[:, :LANES])
            dq_ref[base, :] += dot(slope, keys[:, :LANES], 0, 0)
            return dk, dv

        zero = jnp.zeros((BLOCK, LANES), F32)
        state = step(j, (zero, zero), True)
        dk, dv = lax.fori_loop(
            j + 1, (stop - 1) // BLOCK + 1, lambda i, s: step(i, s, False), state
        )
        back_ref[here, LANES : 2 * LANES] = jnp.where(
            low, dk + pltpu.roll(dk, half, 1), dv + pltpu.roll(dv, half, 1)
        ).astype(BF)
        return carry

    lax.fori_loop(0, count, one_block, 0)

    def finish(i, carry):
        at = pl.ds(pl.multiple_of(i * BLOCK, BLOCK), BLOCK)
        base = pl.multiple_of(i * rows, rows)
        mine = dq_ref[pl.ds(base, BLOCK), :]
        if heads == 2:
            mine = jnp.where(low, mine, dq_ref[pl.ds(base + BLOCK, BLOCK), :])
        back_ref[at, 0:LANES] = (mine * (HEAD_WIDTH ** -0.5)).astype(BF)
        return carry

    lax.fori_loop(0, count, finish, 0)


def attend_back(lens, q, k, v, out, grad, heads):
    total = out.shape[0]
    vmem = pl.BlockSpec(memory_space=pltpu.VMEM)
    return pl.pallas_call(
        functools.partial(attend_back_kernel, heads),
        out_shape=jax.ShapeDtypeStruct((total, 2 * LANES), BF),
        in_specs=[pl.BlockSpec(memory_space=pltpu.SMEM)] + [vmem] * 5,
        out_specs=vmem,
        scratch_shapes=[
            pltpu.VMEM((heads * total, 2 * LANES), BF),
            pltpu.VMEM((heads * total, LANES), F32),
        ],
        compiler_params=pltpu.CompilerParams(vmem_limit_bytes=56 << 20),
        name="attend_back",
    )(lens, q, k, v, out, grad)


def experts_kernel(
    first_expert_ref,
    n2_ref,
    grad_ref,
    mask_ref,
    win_ref,
    wout_ref,
    wide_ref,
    hid_ref,
    down_ref,
    spread_ref,
    fold_ref,
    out_ref,
    back_ref,
    gdown_ref,
    ghid_ref,
):
    local_experts = win_ref.shape[0]
    rows = n2_ref.shape[0]
    width = HIDDEN_UNITS
    step = pl.program_id(0)
    lane = lane_of((rows, LANES))
    n2 = n2_ref[:, :MODEL_WIDTH]
    side = n2_ref[:, MODEL_WIDTH:]
    grad = grad_ref[...]
    mask = mask_ref[...].astype(F32)
    lows = dot(side, spread_ref[...])
    low_gate = (lows[:, :STACKED] * mask).astype(BF)
    low_up = (lows[:, STACKED:] * mask).astype(BF)
    lift_gate = dot(low_gate, hid_ref[0])
    lift_up = dot(low_up, hid_ref[1])
    down_grad = (dot(grad, wide_ref[...], 1, 1) * mask).astype(BF)
    from_down = dot(down_grad, down_ref[...], 1, 1)
    side_full = side.astype(F32)
    total_inner = jnp.zeros((rows, width), F32)
    total_gate = jnp.zeros((rows, width), F32)
    total_up = jnp.zeros((rows, width), F32)
    out = jnp.zeros((rows, MODEL_WIDTH), F32)
    back = jnp.zeros((rows, MODEL_WIDTH), F32)
    extra = jnp.zeros((rows, LANES), F32)
    for e in range(local_experts):
        name = first_expert_ref[0] + e
        at_high, at_low = lane == name, lane == name + EXPERT_COUNT
        gate = jnp.sum(jnp.where(at_high | at_low, side_full, 0.0), axis=1, keepdims=True)
        pre_gate = dot(n2, win_ref[e, :, :width]) + lift_gate
        pre_up = dot(n2, win_ref[e, :, width:]) + lift_up
        pulled = dot(grad, wout_ref[e]) + from_down
        squashed = jax.nn.sigmoid(pre_gate)
        active = pre_gate * squashed
        inner = active * pre_up
        gate_grad = jnp.sum(inner * pulled, axis=1, keepdims=True)
        high = gate_grad.astype(BF).astype(F32)
        extra = extra + jnp.where(at_high, high, 0.0) + jnp.where(at_low, gate_grad - high, 0.0)
        gated = inner * gate
        pulled = pulled * gate
        grad_gate = pulled * pre_up * (squashed + active * (1.0 - squashed))
        grad_up = pulled * active
        gated_low = gated.astype(BF)
        gate_low = grad_gate.astype(BF)
        up_low = grad_up.astype(BF)
        out = out + dot(gated_low, wout_ref[e], 1, 1)
        back = (
            back
            + dot(gate_low, win_ref[e, :, :width], 1, 1)
            + dot(up_low, win_ref[e, :, width:], 1, 1)
        )
        total_inner = total_inner + gated
        total_gate = total_gate + grad_gate
        total_up = total_up + grad_up
    total_inner = total_inner.astype(BF)
    total_gate = total_gate.astype(BF)
    total_up = total_up.astype(BF)
    small = jnp.concatenate(
        [
            (dot(total_gate, hid_ref[0], 1, 1) * mask).astype(BF),
            (dot(total_up, hid_ref[1], 1, 1) * mask).astype(BF),
            (dot(total_inner, down_ref[...]) * mask).astype(BF),
        ],
        axis=1,
    )
    extra = extra + dot(small, fold_ref[...])
    out_ref[...] = out.astype(BF)
    back_ref[:, :MODEL_WIDTH] = back.astype(BF)
    back_ref[:, MODEL_WIDTH:] = extra.astype(BF)
    gdown = dot(total_inner, down_grad, 0, 0)
    ghid_gate = dot(low_gate, total_gate, 0, 0)
    ghid_up = dot(low_up, total_up, 0, 0)

    @pl.when(step == 0)
    def _():
        gdown_ref[...] = gdown
        ghid_ref[0] = ghid_gate
        ghid_ref[1] = ghid_up

    @pl.when(step != 0)
    def _():
        gdown_ref[...] += gdown
        ghid_ref[0] += ghid_gate
        ghid_ref[1] += ghid_up


def experts(first, n2, grad, mask, win, wout, wide, hid, down, rows):
    total = n2.shape[0]
    side = n2.shape[1]
    source = jnp.arange(LANES, dtype=jnp.int32)
    place = jnp.arange(STACKED, dtype=jnp.int32) % ADAPTER_RANK
    spread = jnp.concatenate(
        [(source[:, None] == offset + place[None, :]) for offset in (32, 48)], axis=1
    ).astype(BF)
    fold = jnp.concatenate(
        [(source[None, :] == offset + place[:, None]) for offset in (32, 48, 64)], axis=0
    ).astype(BF)

    def whole(array):
        return pl.BlockSpec(
            array.shape, lambda i: (0,) * array.ndim, pipeline_mode=pl.Buffered(1)
        )

    def block(columns):
        return pl.BlockSpec((rows, columns), lambda i: (i, 0))

    return pl.pallas_call(
        experts_kernel,
        grid=(total // rows,),
        out_shape=(
            jax.ShapeDtypeStruct((total, MODEL_WIDTH), BF),
            jax.ShapeDtypeStruct((total, side), BF),
            jax.ShapeDtypeStruct((HIDDEN_UNITS, STACKED), F32),
            jax.ShapeDtypeStruct((2, STACKED, HIDDEN_UNITS), F32),
        ),
        in_specs=[
            pl.BlockSpec(memory_space=pltpu.SMEM),
            block(side),
            block(MODEL_WIDTH),
            block(STACKED),
            whole(win),
            whole(wout),
            whole(wide),
            whole(hid),
            whole(down),
            whole(spread),
            whole(fold),
        ],
        out_specs=(
            block(MODEL_WIDTH),
            block(side),
            pl.BlockSpec((HIDDEN_UNITS, STACKED), lambda i: (0, 0)),
            pl.BlockSpec((2, STACKED, HIDDEN_UNITS), lambda i: (0, 0, 0)),
        ),
        compiler_params=pltpu.CompilerParams(vmem_limit_bytes=56 << 20),
        name="experts",
    )(first, n2, grad, mask, win, wout, wide, hid, down, spread, fold)


def bits_of(count):
    return [1 << k for k in range(count.bit_length() - 1)]


def orders_of(count):
    bits = bits_of(count)
    far = bits[1:]
    cut = (len(far) + 1) // 2
    return (far + bits[:1], far[cut:] + far[:cut] + bits[:1])


def span(bits):
    masks = [0]
    for bit in bits:
        masks = masks + [m ^ bit for m in masks]
    return masks


def greet(meetings):
    barrier = pltpu.get_barrier_semaphore()
    count = 0
    for axis, me, masks in meetings:
        for mask in masks:
            pl.semaphore_signal(
                barrier, inc=1, device_id={axis: me ^ mask}, device_id_type=MESH
            )
            count += 1
    pl.semaphore_wait(barrier, count)


class Gather:
    def __init__(self, axis, count, own, store, sems):
        self.axis, self.count, self.own, self.store = axis, count, own, store
        self.sends, self.recvs = sems
        self.me = lax.axis_index(axis)
        self.orders = orders_of(count)
        self.half = store.shape[1] // 2

    def copy(self, h, mask, bit):
        rows = pl.ds(h * self.half, self.half)
        there = self.store.at[self.me ^ mask, rows]
        return pltpu.make_async_remote_copy(
            src_ref=self.own.at[rows] if mask == 0 else there,
            dst_ref=there,
            send_sem=self.sends.at[h, mask ^ bit],
            recv_sem=self.recvs.at[h, mask ^ bit],
            device_id={self.axis: self.me ^ bit},
            device_id_type=MESH,
        )

    def incoming(self, h, mask):
        there = self.store.at[self.me ^ mask, pl.ds(h * self.half, self.half)]
        return pltpu.make_async_remote_copy(
            src_ref=there,
            dst_ref=there,
            send_sem=self.sends.at[h, mask],
            recv_sem=self.recvs.at[h, mask],
            device_id={self.axis: self.me ^ mask},
            device_id_type=MESH,
        )

    def start(self):
        for k in range(len(self.orders[0])):
            for h in range(2):
                self.copy(h, 0, self.orders[h][k]).start()

    def stage(self, k):
        for s in range(1 << k):
            for h in range(2):
                order = self.orders[h]
                mask = order[k] ^ span(order[:k])[s]
                self.incoming(h, mask).wait_recv()
                for bit in order[k + 1 :]:
                    self.copy(h, mask, bit).start()

    def stages(self):
        for k in range(len(self.orders[0])):
            self.stage(k)

    def finish(self):
        for h in range(2):
            for mask in range(1, self.count):
                self.incoming(h, mask).wait_send()


class Scatter:
    def __init__(self, axis, count, part, land, sems):
        self.axis, self.count, self.part, self.land = axis, count, part, land
        self.sends, self.recvs = sems
        self.me = lax.axis_index(axis)
        self.orders = [order[::-1] for order in orders_of(count)]
        self.half = part.shape[1] // 2

    def depth(self, h, mask):
        for k, bit in enumerate(self.orders[h]):
            if mask & bit:
                return k
        return len(self.orders[h])

    def copy(self, h, mask):
        bit = self.orders[h][self.depth(h, mask)]
        return pltpu.make_async_remote_copy(
            src_ref=self.part.at[self.me ^ mask, pl.ds(h * self.half, self.half)],
            dst_ref=self.land.at[h, mask],
            send_sem=self.sends.at[h, mask],
            recv_sem=self.recvs.at[h, mask],
            device_id={self.axis: self.me ^ bit},
            device_id_type=MESH,
        )

    def reduce(self, h, mask):
        depth = self.depth(h, mask)
        sources = [mask ^ bit for bit in self.orders[h][:depth]]
        for source in sources:
            self.copy(h, source).wait_recv()
        if sources:
            step = math.gcd(self.half, 64)
            mine = self.me ^ mask

            def add(c, carry):
                here = pl.ds(pl.multiple_of(c * step, step), step)
                at = pl.ds(pl.multiple_of(h * self.half + c * step, step), step)
                total = self.part[mine, at].astype(F32)
                for source in sources:
                    total = total + self.land[h, source, here].astype(F32)
                self.part[mine, at] = total.astype(BF)
                return carry

            lax.fori_loop(0, self.half // step, add, 0)
        if mask:
            self.copy(h, mask).start()

    def run(self):
        for k in range(len(self.orders[0]) + 1):
            for mask in range(self.count):
                for h in range(2):
                    if self.depth(h, mask) == k:
                        self.reduce(h, mask)

    def finish(self):
        for h in range(2):
            for mask in range(1, self.count):
                self.copy(h, mask).wait_send()


def pair_of_sems(count):
    return [pltpu.SemaphoreType.DMA((2, count)), pltpu.SemaphoreType.DMA((2, count))]


ANYWHERE = pl.BlockSpec(memory_space=pl.ANY)
IN_VMEM = pl.BlockSpec(memory_space=pltpu.VMEM)


def remote(identity, limit=48):
    return pltpu.CompilerParams(
        collective_id=identity, has_side_effects=True, vmem_limit_bytes=limit << 20
    )


def gather_kernel(axis, count, own, store, sends, recvs, local_sem):
    me = lax.axis_index(axis)
    keep = pltpu.make_async_copy(own, store.at[me], local_sem)
    keep.start()
    greet([(axis, me, bits_of(count))])
    moving = Gather(axis, count, own, store, (sends, recvs))
    moving.start()
    moving.stages()
    moving.finish()
    keep.wait()


def gather(rows, axis, identity):
    count = lax.axis_size(axis)
    return pl.pallas_call(
        functools.partial(gather_kernel, axis, count),
        out_shape=jax.ShapeDtypeStruct((count,) + rows.shape, rows.dtype),
        in_specs=[IN_VMEM],
        out_specs=IN_VMEM,
        scratch_shapes=pair_of_sems(count) + [pltpu.SemaphoreType.DMA(())],
        compiler_params=remote(identity),
        name="gather",
    )(rows)


def scatter_kernel(axis, count, given, total, part, land, sends, recvs, local_sem):
    me = lax.axis_index(axis)
    take = pltpu.make_async_copy(given, part, local_sem)
    take.start()
    greet([(axis, me, bits_of(count))])
    moving = Scatter(axis, count, part, land, (sends, recvs))
    take.wait()
    moving.run()
    total[...] = part[me]
    moving.finish()


def scatter(blocks, axis, identity):
    count, rows, columns = blocks.shape
    return pl.pallas_call(
        functools.partial(scatter_kernel, axis, count),
        out_shape=jax.ShapeDtypeStruct((rows, columns), BF),
        in_specs=[ANYWHERE],
        out_specs=IN_VMEM,
        scratch_shapes=[
            pltpu.VMEM(blocks.shape, BF),
            pltpu.VMEM((2, count, rows // 2, columns), BF),
        ]
        + pair_of_sems(count)
        + [pltpu.SemaphoreType.DMA(())],
        compiler_params=remote(identity, 56),
        name="scatter",
    )(blocks)


def swap_kernel(axis, count, given, taken, sends, recvs, local_sem):
    me = lax.axis_index(axis)
    keep = pltpu.make_async_copy(given.at[me], taken.at[me], local_sem)
    keep.start()
    greet([(axis, me, range(1, count))])

    def copy(mask):
        return pltpu.make_async_remote_copy(
            src_ref=given.at[me ^ mask],
            dst_ref=taken.at[me],
            send_sem=sends.at[mask],
            recv_sem=recvs.at[mask],
            device_id={axis: me ^ mask},
            device_id_type=MESH,
        )

    for mask in range(count - 1, 0, -1):
        copy(mask).start()
    for mask in range(1, count):
        copy(mask).wait()
    keep.wait()


def swap(blocks, axis, identity):
    count = lax.axis_size(axis)
    return pl.pallas_call(
        functools.partial(swap_kernel, axis, count),
        out_shape=jax.ShapeDtypeStruct(blocks.shape, blocks.dtype),
        in_specs=[IN_VMEM],
        out_specs=IN_VMEM,
        scratch_shapes=[pltpu.SemaphoreType.DMA((count,))] * 2 + [pltpu.SemaphoreType.DMA(())],
        compiler_params=remote(identity),
        name="swap",
    )(blocks)


def total_kernel(
    shards, groups, given, out, part, land, zpart, zland, zall, s1, r1, s2, r2, s3, r3, s4, r4, sem
):
    me, plane = lax.axis_index("fsdp"), lax.axis_index("dp")
    take = pltpu.make_async_copy(given, part, sem)
    take.start()
    greet([("fsdp", me, bits_of(shards)), ("dp", plane, bits_of(groups))])
    take.wait()
    down = Scatter("fsdp", shards, part, land, (s1, r1))
    down.run()
    piece = zpart.shape[1]
    for g in range(groups):
        zpart[g] = part[me, pl.ds(g * piece, piece)]
    across = Scatter("dp", groups, zpart, zland, (s2, r2))
    across.run()
    zall[plane] = zpart[plane]
    back = Gather("dp", groups, zall.at[plane], zall, (s3, r3))
    back.start()
    back.stages()
    for g in range(groups):
        out[me, pl.ds(g * piece, piece)] = zall[g]
    up = Gather("fsdp", shards, out.at[me], out, (s4, r4))
    up.start()
    up.stages()
    down.finish()
    across.finish()
    back.finish()
    up.finish()


def total_of(rows, identity):
    shards, groups = lax.axis_size("fsdp"), lax.axis_size("dp")
    unit = shards * groups * 2 * 16
    length = -(-rows.shape[0] // unit) * unit
    rows = jnp.pad(rows, ((0, length - rows.shape[0]), (0, 0)))
    share = length // shards
    piece = share // groups
    columns = rows.shape[1]
    out = pl.pallas_call(
        functools.partial(total_kernel, shards, groups),
        out_shape=jax.ShapeDtypeStruct((shards, share, columns), BF),
        in_specs=[ANYWHERE],
        out_specs=IN_VMEM,
        scratch_shapes=[
            pltpu.VMEM((shards, share, columns), BF),
            pltpu.VMEM((2, shards, share // 2, columns), BF),
            pltpu.VMEM((groups, piece, columns), BF),
            pltpu.VMEM((2, groups, piece // 2, columns), BF),
            pltpu.VMEM((groups, piece, columns), BF),
        ]
        + pair_of_sems(shards)
        + pair_of_sems(groups) * 2
        + pair_of_sems(shards)
        + [pltpu.SemaphoreType.DMA(())],
        compiler_params=remote(identity),
        name="total",
    )(rows.reshape(shards, share, columns))
    return out.reshape(length, columns)


def plane_gather(rows, identity):
    return gather(rows, "fsdp", identity).reshape(-1, rows.shape[1])


def plane_scatter(rows, identity):
    count = lax.axis_size("fsdp")
    return scatter(rows.reshape(count, -1, rows.shape[1]), "fsdp", identity)


def plane_swap(blocks, identity):
    return swap(blocks, "fsdp", identity)


def rotate(tensor, cosine, sine):
    rows = tensor.shape[0]
    view = tensor.reshape(rows, -1, 2, HEAD_WIDTH // 2)
    first, second = view[:, :, 0], view[:, :, 1]
    c, s = cosine[:, None, :], sine[:, None, :]
    turned = jnp.stack([first * c - second * s, second * c + first * s], axis=2)
    return turned.reshape(rows, -1)


def local(
    tokens,
    cotangent,
    lengths,
    adapter_index,
    routes,
    deal,
    norm_gain_pair,
    query_weight,
    key_weight,
    value_weight,
    output_weight_transposed,
    router_weight,
    expert_input_weight,
    expert_output_weight,
    factors,
    down_first,
    wide,
    kv_second,
    hidden_second,
    router_second,
):
    shards = lax.axis_size("fsdp")
    groups = lax.axis_size("dp")
    rows = tokens.shape[0]
    total = rows * shards
    heads = HEADS // shards
    share = max(1, shards // KEY_VALUE_HEADS)
    me = lax.axis_index("fsdp")

    group_ids = jnp.arange(groups, dtype=jnp.int32)
    dealt = jnp.sum(jnp.where(deal == lax.axis_index("dp"), group_ids, 0))

    def of_group(array):
        everything = lax.all_gather(array, "dp", axis=0, tiled=False)
        return lax.dynamic_index_in_dim(everything, dealt, 0, keepdims=False)

    lens = of_group(lengths)
    chosen = of_group(adapter_index)[0]
    routes = of_group(routes)

    offsets = jnp.cumsum(lens[0]) - lens[0]
    index = jnp.arange(total, dtype=jnp.int32)
    ends = offsets + lens[0]
    inside = (index[:, None] >= offsets[None, :]) & (index[:, None] < ends[None, :])
    pick = jnp.sum(jnp.where(inside, chosen[None, :], 0), axis=1)
    begin = jnp.sum(jnp.where(inside, offsets[None, :], 0), axis=1)
    group_mask = (
        jnp.arange(STACKED, dtype=jnp.int32)[None, :] // ADAPTER_RANK == pick[:, None]
    ).astype(BF)
    mask_low = lax.dynamic_slice_in_dim(group_mask, me * rows, rows, 0)
    mask = mask_low.astype(F32)
    position = lax.dynamic_slice_in_dim(index - begin, me * rows, rows, 0)
    half = HEAD_WIDTH // 2
    frequency = ROPE_BASE ** (-jnp.arange(half, dtype=F32) / half)
    angles = position.astype(F32)[:, None] * frequency[None, :]
    cosine, sine = jnp.cos(angles), jnp.sin(angles)

    packed = jnp.concatenate(
        [
            query_weight,
            key_weight,
            value_weight,
            output_weight_transposed,
            router_weight,
            norm_gain_pair,
            jnp.zeros((router_weight.shape[0], LANES - EXPERT_COUNT - 2), BF),
        ],
        axis=1,
    )
    packed = gather(packed, "dp", 1).reshape(-1, packed.shape[1])
    packed = gather(packed, "fsdp", 2)
    small = packed.shape[1] // groups
    packed = packed.reshape(shards, groups, small, -1).transpose(1, 0, 2, 3)
    packed = packed.reshape(MODEL_WIDTH, -1)
    in_width = 2 * MODEL_WIDTH
    in_weight = packed[:, :in_width]
    out_weight = packed[:, in_width : in_width + MODEL_WIDTH]
    router = packed[:, 3 * MODEL_WIDTH : 3 * MODEL_WIDTH + EXPERT_COUNT]
    gains = packed[:, 3 * MODEL_WIDTH + EXPERT_COUNT : 3 * MODEL_WIDTH + EXPERT_COUNT + 2].astype(F32)

    win = jnp.transpose(expert_input_weight, (1, 0, 2))
    wout = jnp.transpose(expert_output_weight, (1, 0, 2))
    all_grad = plane_gather(cotangent, 3)

    x = tokens.astype(F32)
    r1 = lax.rsqrt(jnp.mean(x * x, axis=1, keepdims=True) + EPSILON)
    normed = (x * r1 * gains[:, 0]).astype(BF)
    first_low = [(dot(normed, factors[s]) * mask).astype(BF) for s in range(3)]
    mixed = dot(normed, in_weight)
    query = rotate(mixed[:, :MODEL_WIDTH] + dot(first_low[0], wide[0]), cosine, sine)
    split = MODEL_WIDTH + KEY_VALUE_HEADS * HEAD_WIDTH
    keys = rotate(mixed[:, MODEL_WIDTH:split] + dot(first_low[1], kv_second[0]), cosine, sine)
    values = mixed[:, split:] + dot(first_low[2], kv_second[1])

    def by_head(array, count, repeat):
        array = array.astype(BF).reshape(rows, count, -1).transpose(1, 0, 2)
        return jnp.repeat(array, repeat, axis=0) if repeat > 1 else array

    query = by_head(query, shards, 1)
    if query.shape[2] < LANES:
        query = jnp.pad(query, ((0, 0), (0, 0), (0, LANES - query.shape[2])))
    parts = jnp.concatenate(
        [query, by_head(keys, KEY_VALUE_HEADS, share), by_head(values, KEY_VALUE_HEADS, share)],
        axis=2,
    )
    qkv = plane_swap(parts, 4).reshape(total, -1)
    attended, q_kept, k_kept, v_kept = attend(lens, qkv, heads)

    def home(array, columns):
        swapped = plane_swap(array.reshape(shards, rows, -1), 5)
        return swapped[:, :, :columns].transpose(1, 0, 2).reshape(rows, -1)

    mine = home(attended, heads * HEAD_WIDTH)
    out_low = (dot(mine, factors[6]) * mask).astype(BF)
    hidden = x + dot(mine, out_weight, 1, 1) + dot(out_low, wide[1])
    r2 = lax.rsqrt(jnp.mean(hidden * hidden, axis=1, keepdims=True) + EPSILON)
    normed_two = (hidden * r2 * gains[:, 1]).astype(BF)
    second_low = [(dot(normed_two, factors[3 + s]) * mask).astype(BF) for s in range(3)]
    logits = dot(normed_two, router) + dot(second_low[0], router_second)
    chosen_experts = jnp.sum(
        (routes[:, :, None] == jnp.arange(EXPERT_COUNT, dtype=jnp.int32)).astype(F32), axis=1
    )
    picked = chosen_experts > 0
    peak = jnp.max(jnp.where(picked, logits, MASKED), axis=1, keepdims=True)
    lifted = jnp.where(picked, jnp.exp(logits - peak), 0.0)
    gates = lifted / jnp.sum(lifted, axis=1, keepdims=True)

    def compact(array):
        return jnp.sum(array.astype(F32).reshape(rows, ADAPTER_COUNT, ADAPTER_RANK), axis=1)

    def expand(array):
        return jnp.tile(array, (1, ADAPTER_COUNT))

    gate_high = gates.astype(BF).astype(F32)
    side = jnp.concatenate(
        [
            gate_high,
            gates - gate_high,
            compact(second_low[1]),
            compact(second_low[2]),
            jnp.zeros((rows, LANES - 64), F32),
        ],
        axis=1,
    ).astype(BF)
    everyone = plane_gather(jnp.concatenate([normed_two, side], axis=1), 6)
    local_experts = win.shape[0]
    out_part, back_part, g_down_a, g_ff = experts(
        (me * local_experts).astype(jnp.int32)[None],
        everyone,
        all_grad,
        group_mask,
        win,
        wout,
        wide[2],
        hidden_second,
        down_first,
        rows,
    )
    out_sum = plane_scatter(out_part, 7).astype(F32)
    back_sum = plane_scatter(back_part, 8).astype(F32)

    grad = cotangent.astype(F32)
    extra = back_sum[:, MODEL_WIDTH:]
    gate_grad = extra[:, 0:16] + extra[:, 16:32]
    down_low = (expand(extra[:, 64:80]) * mask).astype(BF)
    layer_out = (hidden + out_sum + dot(down_low, wide[2])).astype(BF)
    g_wide_down = dot(down_low, cotangent, 0, 0)
    logit_grad = (
        gates * (gate_grad - jnp.sum(gates * gate_grad, axis=1, keepdims=True))
    ).astype(BF)
    g_route = dot(second_low[0], logit_grad, 0, 0)
    second_grad = [
        (dot(logit_grad, router_second, 1, 1) * mask).astype(BF),
        (expand(extra[:, 32:48]) * mask).astype(BF),
        (expand(extra[:, 48:64]) * mask).astype(BF),
    ]
    normed_two_grad = back_sum[:, :MODEL_WIDTH] + dot(logit_grad, router, 1, 1)
    for s in range(3):
        normed_two_grad = normed_two_grad + dot(second_grad[s], factors[3 + s], 1, 1)
    g_second = [dot(normed_two, second_grad[s], 0, 0) for s in range(3)]
    w2 = gains[:, 1] * normed_two_grad
    hidden_grad = grad + r2 * w2 - hidden * r2**3 * jnp.mean(w2 * hidden, axis=1, keepdims=True)
    out_grad = hidden_grad.astype(BF)
    g_wide_out = dot(out_low, out_grad, 0, 0)
    out_low_grad = (dot(out_grad, wide[1], 1, 1) * mask).astype(BF)
    g_factor_out = dot(mine, out_low_grad, 0, 0)
    attended_grad = (dot(out_grad, out_weight) + dot(out_low_grad, factors[6], 1, 1)).astype(BF)
    to_heads = by_head(attended_grad, shards, 1)
    if to_heads.shape[2] < LANES:
        to_heads = jnp.pad(to_heads, ((0, 0), (0, 0), (0, LANES - to_heads.shape[2])))
    head_grad = plane_swap(to_heads, 9).reshape(total, -1)
    qkv_grad = attend_back(lens, q_kept, k_kept, v_kept, attended, head_grad, heads)
    qkv_grad = plane_swap(qkv_grad.reshape(shards, rows, -1), 10).astype(F32)

    def joined(array):
        array = array.reshape(shards // share, share, rows, -1).sum(1)
        return array.transpose(1, 0, 2).reshape(rows, -1)

    query_grad = qkv_grad[:, :, : heads * HEAD_WIDTH].transpose(1, 0, 2).reshape(rows, -1)
    query_grad = rotate(query_grad, cosine, -sine).astype(BF)
    keys_grad = rotate(joined(qkv_grad[:, :, LANES : LANES + 64]), cosine, -sine).astype(BF)
    values_grad = joined(qkv_grad[:, :, LANES + 64 :]).astype(BF)
    mixed_grad = jnp.concatenate([query_grad, keys_grad, values_grad], axis=1)
    normed_grad = dot(mixed_grad, in_weight, 1, 1)
    first_grad = [
        (dot(query_grad, wide[0], 1, 1) * mask).astype(BF),
        (dot(keys_grad, kv_second[0], 1, 1) * mask).astype(BF),
        (dot(values_grad, kv_second[1], 1, 1) * mask).astype(BF),
    ]
    for s in range(3):
        normed_grad = normed_grad + dot(first_grad[s], factors[s], 1, 1)
    g_first = [dot(normed, first_grad[s], 0, 0) for s in range(3)]
    g_wide_query = dot(first_low[0], query_grad, 0, 0)
    g_kv = [dot(first_low[1], keys_grad, 0, 0), dot(first_low[2], values_grad, 0, 0)]
    w1 = gains[:, 0] * normed_grad
    input_grad = hidden_grad + r1 * w1 - x * r1**3 * jnp.mean(w1 * x, axis=1, keepdims=True)

    def tall(array):
        return [array[:, c : c + LANES] for c in range(0, array.shape[1], LANES)]

    pieces = g_first + g_second + [g_factor_out, g_down_a]
    for array in [g_wide_query, g_wide_out, g_wide_down] + g_kv + [g_ff[0], g_ff[1]]:
        pieces = pieces + tall(array)
    pieces = pieces + [jnp.pad(g_route, ((0, 0), (0, LANES - EXPERT_COUNT)))]
    sums = total_of(jnp.concatenate([p.astype(BF) for p in pieces], axis=0), 11).astype(F32)

    def wide_sum(start, count, parts):
        block = sums[start : start + count * parts * STACKED]
        block = block.reshape(count, parts, STACKED, LANES).transpose(0, 2, 1, 3)
        return block.reshape(count, STACKED, parts * LANES)

    edge = 7 * MODEL_WIDTH
    factor_sum = sums[:edge].reshape(7, MODEL_WIDTH, STACKED)
    down_sum = sums[edge : edge + HIDDEN_UNITS]
    edge += HIDDEN_UNITS
    wide_total = wide_sum(edge, 3, 8)
    edge += 24 * STACKED
    kv_total = wide_sum(edge, 2, 4)
    edge += 8 * STACKED
    ff_total = wide_sum(edge, 2, 4)
    edge += 8 * STACKED
    route_total = sums[edge : edge + STACKED, :EXPERT_COUNT]
    return (
        layer_out,
        input_grad,
        factor_sum,
        down_sum,
        wide_total,
        kv_total,
        ff_total,
        route_total,
    )


def solution(mesh):
    rows = P(("dp", "fsdp"), None)
    placed = (
        (rows, rows, P("dp", None), P("dp", None), rows, P())
        + (rows,) * 6
        + (P(None, "fsdp", None),) * 2
        + (P(),) * 6
    )
    return jax.shard_map(
        local,
        mesh=mesh,
        in_specs=placed,
        out_specs=(rows, rows) + (P(),) * 6,
        check_vma=False,
    )
```

```python
import functools
import math

import jax
import jax.numpy as jnp
import numpy as np
from jax import lax
from jax.experimental import pallas as pl
from jax.experimental.pallas import tpu as pltpu
from jax.sharding import PartitionSpec as P

MODEL_WIDTH = 1024
HEADS = 16
KEY_VALUE_HEADS = 8
HEAD_WIDTH = 64
HIDDEN_UNITS = 512
TOPK = 8
EXPERT_COUNT = 16
ADAPTER_COUNT = 8
ADAPTER_RANK = 16
STACKED = ADAPTER_COUNT * ADAPTER_RANK

EPSILON = 1e-06
ROPE_BASE = 10000.0
MASKED = -1e30
LANES = 128

BF = jnp.bfloat16
F32 = jnp.float32
MESH = pl.DeviceIdType.MESH


def dot(a, b, ca=1, cb=0):
    return lax.dot_general(a, b, (((ca,), (cb,)), ((), ())), preferred_element_type=F32)


def splits(v):
    hi = v.astype(BF).astype(F32)
    rest = v - hi
    mid = rest.astype(BF).astype(F32)
    return hi, mid, rest - mid


def lane_of(shape):
    return lax.broadcasted_iota(jnp.int32, shape, len(shape) - 1)


def row_of(shape):
    return lax.broadcasted_iota(jnp.int32, shape, 0)


def attend_kernel(heads, lens_ref, qkv_ref, out_ref, q_ref, k_ref, v_ref):
    total = qkv_ref.shape[0]
    nseq = lens_ref.shape[1]
    half = HEAD_WIDTH
    side = 256

    def prepare(i, carry):
        at = pl.ds(pl.multiple_of(i * side, side), side)
        low = lane_of((side, LANES)) < half
        lane = lane_of((side, LANES))
        row = row_of((side, LANES)) + i * side
        first = jnp.int32(0)
        seq = jnp.zeros((side, LANES), jnp.bool_)
        for s in range(nseq):
            last = first + lens_ref[0, s]
            seq = seq | ((lane == s) & (row >= first) & (row < last))
            first = last
        queries = qkv_ref[at, 0:LANES].astype(F32) * (HEAD_WIDTH ** -0.5)
        pair = qkv_ref[at, LANES : 2 * LANES].astype(F32)
        swapped = pltpu.roll(pair, half, 1)
        marks = jnp.where(seq, 1.0, 0.0).astype(BF)
        for h in range(heads):
            mine = jnp.where(low if h == 0 else ~low, queries, 0.0).astype(BF)
            q_ref[h, at, 0:LANES] = mine
            q_ref[h, at, LANES : 2 * LANES] = marks
        k_ref[at, 0:LANES] = jnp.where(low, pair, swapped).astype(BF)
        far = jnp.where(lane < nseq, jnp.where(seq, 0.0, MASKED), 0.0)
        k_ref[at, LANES : 2 * LANES] = jnp.where(
            (lane >= nseq) & (lane < nseq + 3), 1.0, far
        ).astype(BF)
        v_ref[at, 0:LANES] = jnp.where(low, swapped, pair).astype(BF)
        v_ref[at, LANES : 2 * LANES] = jnp.ones((side, LANES), BF)
        return carry

    lax.fori_loop(0, total // side, prepare, 0)

    rows = math.gcd(total, 384)
    block = rows
    low = lane_of((rows, LANES)) < half
    lane = lane_of((rows, LANES))
    for i in range(total // block):
        keys = (i + 1) * block

        def chunk(c, carry, i=i, keys=keys):
            first = i * block + c * rows
            at = pl.ds(pl.multiple_of(first, rows), rows)
            visible = lane_of((rows, block)) <= row_of((rows, block)) + c * rows
            mixed = []
            for h in range(heads):
                scores = dot(q_ref[h, at, :], k_ref[0:keys, :], 1, 1)
                final = jnp.where(visible, scores[:, keys - block :], MASKED)
                if i:
                    scores = jnp.concatenate([scores[:, : keys - block], final], axis=1)
                else:
                    scores = final
                top = jnp.max(scores, axis=1, keepdims=True)
                weights = jnp.exp(scores - top).astype(BF)
                acc = dot(weights, v_ref[0:keys, :])
                weight = acc[:, LANES:]
                mixed.append(acc[:, :LANES] / weight)
                hi, mid, lo = splits(-(top + jnp.log(weight)))
                marks = q_ref[h, at, LANES : 2 * LANES].astype(F32)
                marks = jnp.where(lane == nseq, hi, marks)
                marks = jnp.where(lane == nseq + 1, mid, marks)
                marks = jnp.where(lane == nseq + 2, lo, marks)
                q_ref[h, at, LANES : 2 * LANES] = marks.astype(BF)
            value = mixed[0] if heads == 1 else jnp.where(low, mixed[0], mixed[1])
            out_ref[at, :] = value.astype(BF)
            return carry

        lax.fori_loop(0, block // rows, chunk, 0)


def attend(lens, qkv, heads):
    total = qkv.shape[0]
    vmem = pl.BlockSpec(memory_space=pltpu.VMEM)
    return pl.pallas_call(
        functools.partial(attend_kernel, heads),
        out_shape=(
            jax.ShapeDtypeStruct((total, LANES), BF),
            jax.ShapeDtypeStruct((heads, total, 2 * LANES), BF),
            jax.ShapeDtypeStruct((total, 2 * LANES), BF),
            jax.ShapeDtypeStruct((total, 2 * LANES), BF),
        ),
        in_specs=[pl.BlockSpec(memory_space=pltpu.SMEM), vmem],
        out_specs=(vmem,) * 4,
        compiler_params=pltpu.CompilerParams(vmem_limit_bytes=56 << 20),
        name="attend",
    )(lens, qkv)


def attend_back_kernel(
    heads, lens_ref, q_ref, k_ref, v_ref, out_ref, grad_ref, back_ref, g_ref, dq_ref, dk_ref, dv_ref
):
    total = out_ref.shape[0]
    half = HEAD_WIDTH
    side = 256
    low = lane_of((side, LANES)) < half
    lane = lane_of((side, LANES))

    def prepare(i, carry):
        at = pl.ds(pl.multiple_of(i * side, side), side)
        grad = grad_ref[at, :].astype(F32)
        both = grad * out_ref[at, :].astype(F32)
        for h in range(heads):
            part = low if h == 0 else ~low
            delta = jnp.sum(jnp.where(part, both, 0.0), axis=1, keepdims=True)
            hi, mid, lo = splits(-delta)
            extra = jnp.where(lane == 0, hi, jnp.where(lane == 1, mid, jnp.where(lane == 2, lo, 0.0)))
            g_ref[h, at, 0:LANES] = jnp.where(part, grad, 0.0).astype(BF)
            g_ref[h, at, LANES : 2 * LANES] = extra.astype(BF)
            dq_ref[h, at, :] = jnp.zeros((side, LANES), F32)
        return carry

    lax.fori_loop(0, total // side, prepare, 0)
    cols = 256
    block = total
    count = 1

    def one_block(j, carry):
        here = pl.ds(pl.multiple_of(j * block, block), block)
        dk_ref[...] = jnp.zeros(dk_ref.shape, F32)
        dv_ref[...] = jnp.zeros(dv_ref.shape, F32)

        def step(i, state, diagonal):
            for h in range(heads):
                for c in range(block // cols):
                    at = pl.ds(pl.multiple_of(i * block + c * cols, cols), cols)
                    size = (c + 1) * cols if diagonal else block
                    mine = pl.ds(pl.multiple_of(j * block, block), size)
                    keys = k_ref[mine, :]
                    queries = q_ref[h, at, :]
                    grads = g_ref[h, at, :]
                    weights = jnp.exp(dot(keys, queries, 1, 1))
                    if diagonal:
                        seen = row_of((size, cols)) <= lane_of((size, cols)) + c * cols
                        weights = jnp.where(seen, weights, 0.0)
                    slope = (weights * dot(v_ref[mine, :], grads, 1, 1)).astype(BF)
                    dv_ref[:size, :] += dot(weights.astype(BF), grads[:, :LANES])
                    dk_ref[:size, :] += dot(slope, queries[:, :LANES])
                    dq_ref[h, at, :] += dot(slope, keys[:, :LANES], 0, 0)
            return state

        step(j, 0, True)
        lax.fori_loop(j + 1, count, lambda i, s: step(i, s, False), 0)
        dk, dv = dk_ref[...], dv_ref[...]
        back_ref[here, LANES : 2 * LANES] = jnp.where(
            lane_of((block, LANES)) < half, dk + pltpu.roll(dk, half, 1), dv + pltpu.roll(dv, half, 1)
        ).astype(BF)
        return carry

    lax.fori_loop(0, count, one_block, 0)

    def finish(i, carry):
        at = pl.ds(pl.multiple_of(i * side, side), side)
        mine = dq_ref[0, at, :]
        if heads == 2:
            mine = jnp.where(low, mine, dq_ref[1, at, :])
        back_ref[at, 0:LANES] = (mine * (HEAD_WIDTH ** -0.5)).astype(BF)
        return carry

    lax.fori_loop(0, total // side, finish, 0)


def attend_back(lens, q, k, v, out, grad, heads):
    total = out.shape[0]
    vmem = pl.BlockSpec(memory_space=pltpu.VMEM)
    return pl.pallas_call(
        functools.partial(attend_back_kernel, heads),
        out_shape=jax.ShapeDtypeStruct((total, 2 * LANES), BF),
        in_specs=[pl.BlockSpec(memory_space=pltpu.SMEM)] + [vmem] * 5,
        out_specs=vmem,
        scratch_shapes=[
            pltpu.VMEM((heads, total, 2 * LANES), BF),
            pltpu.VMEM((heads, total, LANES), F32),
            pltpu.VMEM((total, LANES), F32),
            pltpu.VMEM((total, LANES), F32),
        ],
        compiler_params=pltpu.CompilerParams(vmem_limit_bytes=56 << 20),
        name="attend_back",
    )(lens, q, k, v, out, grad)


def bits_of(count):
    return [1 << k for k in range(count.bit_length() - 1)]


def orders_of(count):
    bits = bits_of(count)
    far = bits[1:]
    cut = (len(far) + 1) // 2
    return (far + bits[:1], far[cut:] + far[:cut] + bits[:1])


def span(bits):
    masks = [0]
    for bit in bits:
        masks = masks + [m ^ bit for m in masks]
    return masks


def greet(meetings):
    barrier = pltpu.get_barrier_semaphore()
    count = 0
    for axis, me, masks in meetings:
        for mask in masks:
            pl.semaphore_signal(
                barrier, inc=1, device_id={axis: me ^ mask}, device_id_type=MESH
            )
            count += 1
    pl.semaphore_wait(barrier, count)


class Gather:
    def __init__(self, axis, count, own, store, sems):
        self.axis, self.count, self.own, self.store = axis, count, own, store
        self.sends, self.recvs = sems
        self.me = lax.axis_index(axis)
        self.orders = orders_of(count)
        self.half = store.shape[1] // 2

    def copy(self, h, mask, bit):
        rows = pl.ds(h * self.half, self.half)
        there = self.store.at[self.me ^ mask, rows]
        return pltpu.make_async_remote_copy(
            src_ref=self.own.at[rows] if mask == 0 else there,
            dst_ref=there,
            send_sem=self.sends.at[h, mask ^ bit],
            recv_sem=self.recvs.at[h, mask ^ bit],
            device_id={self.axis: self.me ^ bit},
            device_id_type=MESH,
        )

    def incoming(self, h, mask):
        there = self.store.at[self.me ^ mask, pl.ds(h * self.half, self.half)]
        return pltpu.make_async_remote_copy(
            src_ref=there,
            dst_ref=there,
            send_sem=self.sends.at[h, mask],
            recv_sem=self.recvs.at[h, mask],
            device_id={self.axis: self.me ^ mask},
            device_id_type=MESH,
        )

    def start(self):
        for k in range(len(self.orders[0])):
            for h in range(2):
                self.copy(h, 0, self.orders[h][k]).start()

    def take(self, h, mask):
        order = self.orders[h]
        self.incoming(h, mask).wait_recv()
        k = max(i for i, bit in enumerate(order) if mask & bit)
        for bit in order[k + 1 :]:
            self.copy(h, mask, bit).start()

    def stage(self, k):
        for s in range(1 << k):
            for h in range(2):
                order = self.orders[h]
                mask = order[k] ^ span(order[:k])[s]
                self.incoming(h, mask).wait_recv()
                for bit in order[k + 1 :]:
                    self.copy(h, mask, bit).start()

    def held(self, k):
        sets = [set(span(order[: k + 1])) for order in self.orders]
        return sets[0] & sets[1]

    def stages(self):
        for k in range(len(self.orders[0])):
            self.stage(k)

    def finish(self):
        for h in range(2):
            for mask in range(1, self.count):
                self.incoming(h, mask).wait_send()


class Scatter:
    def __init__(self, axis, count, part, land, sems):
        self.axis, self.count, self.part, self.land = axis, count, part, land
        self.sends, self.recvs = sems
        self.me = lax.axis_index(axis)
        self.orders = [order[::-1] for order in orders_of(count)]
        self.half = part.shape[1] // 2

    def depth(self, h, mask):
        for k, bit in enumerate(self.orders[h]):
            if mask & bit:
                return k
        return len(self.orders[h])

    def copy(self, h, mask):
        bit = self.orders[h][self.depth(h, mask)]
        return pltpu.make_async_remote_copy(
            src_ref=self.part.at[self.me ^ mask, pl.ds(h * self.half, self.half)],
            dst_ref=self.land.at[h, mask - 1],
            send_sem=self.sends.at[h, mask],
            recv_sem=self.recvs.at[h, mask],
            device_id={self.axis: self.me ^ bit},
            device_id_type=MESH,
        )

    def reduce(self, h, mask):
        depth = self.depth(h, mask)
        sources = [mask ^ bit for bit in self.orders[h][:depth]]
        for source in sources:
            self.copy(h, source).wait_recv()
        if sources:
            step = math.gcd(self.half, 64)
            mine = self.me ^ mask

            def add(c, carry):
                here = pl.ds(pl.multiple_of(c * step, step), step)
                at = pl.ds(pl.multiple_of(h * self.half + c * step, step), step)
                total = self.part[mine, at].astype(F32)
                for source in sources:
                    total = total + self.land[h, source - 1, here].astype(F32)
                self.part[mine, at] = total.astype(BF)
                return carry

            lax.fori_loop(0, self.half // step, add, 0)
        if mask:
            self.copy(h, mask).start()

    def run(self):
        for k in range(len(self.orders[0]) + 1):
            for mask in range(self.count):
                for h in range(2):
                    if self.depth(h, mask) == k:
                        self.reduce(h, mask)

    def finish(self):
        for h in range(2):
            for mask in range(1, self.count):
                self.copy(h, mask).wait_send()


def pair_of_sems(count):
    return [pltpu.SemaphoreType.DMA((2, count)), pltpu.SemaphoreType.DMA((2, count))]


ANYWHERE = pl.BlockSpec(memory_space=pl.ANY)
IN_VMEM = pl.BlockSpec(memory_space=pltpu.VMEM)


def remote(identity, limit=48):
    return pltpu.CompilerParams(
        collective_id=identity, has_side_effects=True, vmem_limit_bytes=limit << 20
    )


def gather_kernel(axis, count, own, store, sends, recvs, local_sem):
    me = lax.axis_index(axis)
    keep = pltpu.make_async_copy(own, store.at[me], local_sem)
    keep.start()
    greet([(axis, me, bits_of(count))])
    moving = Gather(axis, count, own, store, (sends, recvs))
    moving.start()
    moving.stages()
    moving.finish()
    keep.wait()


def gather(rows, axis, identity):
    count = lax.axis_size(axis)
    return pl.pallas_call(
        functools.partial(gather_kernel, axis, count),
        out_shape=jax.ShapeDtypeStruct((count,) + rows.shape, rows.dtype),
        in_specs=[IN_VMEM],
        out_specs=IN_VMEM,
        scratch_shapes=pair_of_sems(count) + [pltpu.SemaphoreType.DMA(())],
        compiler_params=remote(identity),
        name="gather",
    )(rows)


def scatter_kernel(axis, count, given, total, part, land, sends, recvs, local_sem):
    me = lax.axis_index(axis)
    take = pltpu.make_async_copy(given, part, local_sem)
    take.start()
    greet([(axis, me, bits_of(count))])
    moving = Scatter(axis, count, part, land, (sends, recvs))
    take.wait()
    moving.run()
    total[...] = part[me]
    moving.finish()


def scatter(blocks, axis, identity):
    count, rows, columns = blocks.shape
    return pl.pallas_call(
        functools.partial(scatter_kernel, axis, count),
        out_shape=jax.ShapeDtypeStruct((rows, columns), BF),
        in_specs=[ANYWHERE],
        out_specs=IN_VMEM,
        scratch_shapes=[
            pltpu.VMEM(blocks.shape, BF),
            pltpu.VMEM((2, count - 1, rows // 2, columns), BF),
        ]
        + pair_of_sems(count)
        + [pltpu.SemaphoreType.DMA(())],
        compiler_params=remote(identity, 56),
        name="scatter",
    )(blocks)


def swap_kernel(axis, count, given, taken, sends, recvs, local_sem):
    me = lax.axis_index(axis)
    keep = pltpu.make_async_copy(given.at[me], taken.at[me], local_sem)
    keep.start()
    greet([(axis, me, range(1, count))])

    def copy(mask):
        return pltpu.make_async_remote_copy(
            src_ref=given.at[me ^ mask],
            dst_ref=taken.at[me],
            send_sem=sends.at[mask],
            recv_sem=recvs.at[mask],
            device_id={axis: me ^ mask},
            device_id_type=MESH,
        )

    for mask in range(count - 1, 0, -1):
        copy(mask).start()
    for mask in range(1, count):
        copy(mask).wait()
    keep.wait()


def swap(blocks, axis, identity):
    count = lax.axis_size(axis)
    return pl.pallas_call(
        functools.partial(swap_kernel, axis, count),
        out_shape=jax.ShapeDtypeStruct(blocks.shape, blocks.dtype),
        in_specs=[IN_VMEM],
        out_specs=IN_VMEM,
        scratch_shapes=[pltpu.SemaphoreType.DMA((count,))] * 2 + [pltpu.SemaphoreType.DMA(())],
        compiler_params=remote(identity),
        name="swap",
    )(blocks)


def total_kernel(
    shards, groups, given, out, part, land, zpart, zland, zall, s1, r1, s2, r2, s3, r3, s4, r4, sem
):
    me, plane = lax.axis_index("fsdp"), lax.axis_index("dp")
    take = pltpu.make_async_copy(given, part, sem)
    take.start()
    greet([("fsdp", me, bits_of(shards)), ("dp", plane, bits_of(groups))])
    take.wait()
    down = Scatter("fsdp", shards, part, land, (s1, r1))
    down.run()
    piece = zpart.shape[1]
    for g in range(groups):
        zpart[g] = part[me, pl.ds(g * piece, piece)]
    across = Scatter("dp", groups, zpart, zland, (s2, r2))
    across.run()
    zall[plane] = zpart[plane]
    back = Gather("dp", groups, zall.at[plane], zall, (s3, r3))
    back.start()
    back.stages()
    for g in range(groups):
        out[me, pl.ds(g * piece, piece)] = zall[g]
    up = Gather("fsdp", shards, out.at[me], out, (s4, r4))
    up.start()
    up.stages()
    down.finish()
    across.finish()
    back.finish()
    up.finish()


def total_of(rows, identity):
    shards, groups = lax.axis_size("fsdp"), lax.axis_size("dp")
    unit = shards * groups * 2 * 16
    length = -(-rows.shape[0] // unit) * unit
    rows = jnp.pad(rows, ((0, length - rows.shape[0]), (0, 0)))
    share = length // shards
    piece = share // groups
    columns = rows.shape[1]
    out = pl.pallas_call(
        functools.partial(total_kernel, shards, groups),
        out_shape=jax.ShapeDtypeStruct((shards, share, columns), BF),
        in_specs=[ANYWHERE],
        out_specs=IN_VMEM,
        scratch_shapes=[
            pltpu.VMEM((shards, share, columns), BF),
            pltpu.VMEM((2, shards - 1, share // 2, columns), BF),
            pltpu.VMEM((groups, piece, columns), BF),
            pltpu.VMEM((2, groups - 1, piece // 2, columns), BF),
            pltpu.VMEM((groups, piece, columns), BF),
        ]
        + pair_of_sems(shards)
        + pair_of_sems(groups) * 2
        + pair_of_sems(shards)
        + [pltpu.SemaphoreType.DMA(())],
        compiler_params=remote(identity),
        name="total",
    )(rows.reshape(shards, share, columns))
    return out.reshape(length, columns)


def plane_gather(rows, identity):
    return gather(rows, "fsdp", identity).reshape(-1, rows.shape[1])


def plane_scatter(rows, identity):
    count = lax.axis_size("fsdp")
    return scatter(rows.reshape(count, -1, rows.shape[1]), "fsdp", identity)


def plane_swap(blocks, identity):
    return swap(blocks, "fsdp", identity)


def sequences(meta, first, rows, heads_of):
    row = row_of((rows, LANES)) + first
    start = jnp.zeros((1, 1), jnp.int32)
    picked = [jnp.zeros((rows, LANES), part[0].dtype) for part in heads_of]
    for s in range(len(heads_of[0])):
        inside = row >= start
        picked = [jnp.where(inside, part[s], value) for part, value in zip(heads_of, picked)]
        start = start + meta[8:9, s : s + 1]
    return picked


def turned(tensor, cosine, sine):
    lower = lane_of(tensor.shape) % HEAD_WIDTH < HEAD_WIDTH // 2
    other = jnp.where(lower, pltpu.roll(tensor, LANES - 32, 1), pltpu.roll(tensor, 32, 1))
    return tensor * cosine + other * sine


def head_columns(wide, narrow, pick_wide, pick_narrow, heads):
    low = lane_of((1, LANES)) < HEAD_WIDTH
    queries = wide
    if heads == 1:
        queries = jnp.where(low, jnp.where(pick_wide, pltpu.roll(wide, HEAD_WIDTH, 1), wide), 0.0)
    keys, values = narrow
    keys = jnp.where(pick_narrow, pltpu.roll(keys, HEAD_WIDTH, 1), keys)
    values = jnp.where(pick_narrow, values, pltpu.roll(values, HEAD_WIDTH, 1))
    return queries, jnp.where(low, keys, values)


def enter_kernel(
    shards,
    groups,
    deal_ref,
    x_ref,
    wq_ref,
    wk_ref,
    wv_ref,
    small_ref,
    meta_ref,
    factors_ref,
    wide_ref,
    kv_ref,
    cos_ref,
    sin_ref,
    freq_ref,
    qkv_ref,
    low_ref,
    mask_ref,
    small_out,
    meta_out,
    xs,
    slices,
    weights,
    metas,
    merged,
    second,
    xsend,
    xrecv,
    wsend,
    wrecv,
    zsend,
    zrecv,
    msend,
    mrecv,
):
    me, plane = lax.axis_index("fsdp"), lax.axis_index("dp")
    heads = HEADS // shards
    share = max(1, shards // KEY_VALUE_HEADS)
    rows = x_ref.shape[0]
    part = wq_ref.shape[0]
    order = [mask for mask in range(1, shards)]

    for f in range(shards):
        chunk = f * heads * HEAD_WIDTH // LANES
        head = f // share
        pair = head // 2
        queries, others = head_columns(
            wq_ref[:, chunk * LANES : (chunk + 1) * LANES].astype(F32),
            (
                wk_ref[:, pair * LANES : (pair + 1) * LANES].astype(F32),
                wv_ref[:, pair * LANES : (pair + 1) * LANES].astype(F32),
            ),
            f % 2 == 1,
            head % 2 == 1,
            heads,
        )
        slices[f, :, 0:LANES] = queries.astype(BF)
        slices[f, :, LANES : 2 * LANES] = others.astype(BF)
        slices[f, :, 2 * LANES :] = small_ref[...]
    metas[plane] = meta_ref[...]

    greet([("fsdp", me, order), ("dp", plane, range(1, groups))])

    moving = Gather("fsdp", shards, x_ref, xs, (xsend, xrecv))
    plane_rows = shards * part

    def column_copy(mask):
        return pltpu.make_async_remote_copy(
            src_ref=slices.at[me ^ mask],
            dst_ref=weights.at[plane, me],
            send_sem=wsend.at[mask],
            recv_sem=wrecv.at[mask],
            device_id={"fsdp": me ^ mask},
            device_id_type=MESH,
        )

    def plane_copy(mask):
        return pltpu.make_async_remote_copy(
            src_ref=weights.at[plane],
            dst_ref=weights.at[plane],
            send_sem=zsend.at[mask],
            recv_sem=zrecv.at[mask],
            device_id={"dp": plane ^ mask},
            device_id_type=MESH,
        )

    def meta_copy(mask):
        return pltpu.make_async_remote_copy(
            src_ref=meta_ref,
            dst_ref=metas.at[plane],
            send_sem=msend.at[mask],
            recv_sem=mrecv.at[mask],
            device_id={"dp": plane ^ mask},
            device_id_type=MESH,
        )

    for mask in order:
        column_copy(mask).start()
    for mask in range(1, groups):
        meta_copy(mask).start()
    moving.start()
    weights[plane, me] = slices[me]

    half = HEAD_WIDTH
    at = pl.ds(pl.multiple_of(me * heads * half // LANES * LANES, LANES), LANES)
    head = me // share
    pair_at = pl.ds(pl.multiple_of(head // 2 * LANES, LANES), LANES)
    queries, others = head_columns(
        wide_ref[:, at].astype(F32),
        (kv_ref[0, :, pair_at].astype(F32), kv_ref[1, :, pair_at].astype(F32)),
        me % 2 == 1,
        head % 2 == 1,
        heads,
    )
    low_lane = lane_of((STACKED, LANES)) < half
    second[...] = jnp.zeros(second.shape, BF)
    second[0:STACKED, 0:LANES] = queries.astype(BF)
    second[STACKED : 2 * STACKED, LANES:] = jnp.where(low_lane, others, 0.0).astype(BF)
    second[2 * STACKED :, LANES:] = jnp.where(low_lane, 0.0, others).astype(BF)

    for mask in order:
        column_copy(mask).wait_recv()
    for mask in range(1, groups):
        plane_copy(mask).start()
    for mask in range(1, groups):
        meta_copy(mask).wait_recv()
    dealt = jnp.int32(0)
    for g in range(groups):
        dealt = dealt + jnp.where(deal_ref[g] == plane, g, 0)
    meta = jnp.zeros(meta_ref.shape, jnp.int32)
    for g in range(groups):
        meta = jnp.where(dealt == g, metas[g], meta)
    meta_out[...] = meta
    moving.stage(0)
    for mask in range(1, groups):
        plane_copy(mask).wait_recv()

    for g in range(groups):
        for f in range(shards):
            here = pl.ds((g * shards + f) * part, part)
            block = weights[g, f]
            small_out[here, :] = block[:, 2 * LANES :]
            merged[here, 0 : 2 * LANES] = block[:, : 2 * LANES]
    for s in range(3):
        merged[:, (2 + s) * LANES : (3 + s) * LANES] = factors_ref[s]
    gain = gain_row(small_out[...], 16)

    nseq = 4
    lanes = lane_of((1, LANES))
    starts, first = [], jnp.zeros((1, 1), jnp.int32)
    for s in range(nseq):
        starts.append(first)
        first = first + meta[8:9, s : s + 1]
    angles = [start.astype(F32) * freq_ref[...] for start in starts]
    start_cos = [jnp.cos(angle) for angle in angles]
    start_sin = [jnp.sin(angle) for angle in angles]
    adapters = [jnp.broadcast_to(meta[9:10, s : s + 1], (1, LANES)) for s in range(nseq)]
    keyed = lanes < half
    sign = jnp.where(lanes % half < half // 2, -1.0, 1.0)

    def compute(mask):
        block = me ^ mask
        at = pl.ds(pl.multiple_of(block * rows, rows), rows)
        x = x_ref[...] if mask == 0 else xs[block]
        full = x.astype(F32)
        r1 = lax.rsqrt(jnp.mean(full * full, axis=1, keepdims=True) + EPSILON)
        product = dot((full * r1 * gain).astype(BF), merged[...])
        base_cos, base_sin, pick = sequences(
            meta, block * rows, rows, (start_cos, start_sin, adapters)
        )
        masked = lane_of((rows, LANES)) // ADAPTER_RANK == pick
        mask_ref[at, :] = jnp.where(masked, 1.0, 0.0).astype(BF)
        lows = [
            jnp.where(masked, product[:, (2 + s) * LANES : (3 + s) * LANES], 0.0).astype(BF)
            for s in range(3)
        ]
        lows = jnp.concatenate(lows, axis=1)
        low_ref[at, :] = lows
        product = product[:, : 2 * LANES] + dot(lows, second[...])
        row_cos, row_sin = cos_ref[at, :], sin_ref[at, :]
        cosine = row_cos * base_cos + row_sin * base_sin
        sine = (row_sin * base_cos - row_cos * base_sin) * sign
        qkv_ref[at, :LANES] = turned(product[:, :LANES], cosine, sine).astype(BF)
        others = product[:, LANES:]
        qkv_ref[at, LANES:] = turned(
            others, jnp.where(keyed, cosine, 1.0), jnp.where(keyed, sine, 0.0)
        ).astype(BF)

    compute(0)
    done = [0]
    for k in range(1, len(bits_of(shards))):
        moving.stage(k)
        for mask in range(1, shards):
            if mask not in done and mask in moving.held(k):
                compute(mask)
                done.append(mask)
    moving.finish()
    for mask in order:
        column_copy(mask).wait_send()
    for mask in range(1, groups):
        plane_copy(mask).wait_send()
        meta_copy(mask).wait_send()


def enter(deal, x, wq, wk, wv, small, meta, factors, wide, kv_second, identity):
    shards, groups = lax.axis_size("fsdp"), lax.axis_size("dp")
    rows, part = x.shape[0], wq.shape[0]
    total = rows * shards
    half = HEAD_WIDTH // 2
    frequency = ROPE_BASE ** (-np.arange(half, dtype=np.float64) / half)
    frequency = frequency.astype(np.float32)
    angles = np.arange(total, dtype=np.float64)[:, None] * frequency.astype(np.float64)[None, :]
    cosine = jnp.asarray(np.tile(np.cos(angles).astype(np.float32), (1, 4)))
    sine = jnp.asarray(np.tile(np.sin(angles).astype(np.float32), (1, 4)))
    frequency = jnp.asarray(np.tile(frequency, 4)[None, :])
    return pl.pallas_call(
        functools.partial(enter_kernel, shards, groups),
        out_shape=(
            jax.ShapeDtypeStruct((total, 2 * LANES), BF),
            jax.ShapeDtypeStruct((total, 3 * STACKED), BF),
            jax.ShapeDtypeStruct((total, STACKED), BF),
            jax.ShapeDtypeStruct((MODEL_WIDTH, LANES), BF),
            jax.ShapeDtypeStruct(meta.shape, jnp.int32),
        ),
        in_specs=[pl.BlockSpec(memory_space=pltpu.SMEM)] + [IN_VMEM] * 12,
        out_specs=(IN_VMEM,) * 5,
        scratch_shapes=[
            pltpu.VMEM((shards, rows, MODEL_WIDTH), BF),
            pltpu.VMEM((shards, part, 3 * LANES), BF),
            pltpu.VMEM((groups, shards, part, 3 * LANES), BF),
            pltpu.VMEM((groups,) + meta.shape, jnp.int32),
            pltpu.VMEM((MODEL_WIDTH, 2 * LANES + 3 * STACKED), BF),
            pltpu.VMEM((3 * STACKED, 2 * LANES), BF),
        ]
        + pair_of_sems(shards)
        + [pltpu.SemaphoreType.DMA((shards,))] * 2
        + [pltpu.SemaphoreType.DMA((groups,))] * 4,
        compiler_params=remote(identity, 60),
        name="enter",
    )(deal, x, wq, wk, wv, small, meta, factors, wide, kv_second, cosine, sine, frequency)


def gain_row(small, lane):
    pick = jnp.where(lane_of((8, LANES)) == lane, 1.0, 0.0).astype(BF)
    return dot(pick, small, 1, 1)[0:1, :]


def turn_of(step, shards):
    late = (step + shards - 4) // shards
    return step + late * (shards + 3 - 2 * step)


def scatter_plan(moving, shards):
    place = {turn_of(t, shards): t for t in range(shards)}
    sent, plan = {}, []
    for t in range(shards):
        now = []
        for mask in range(1, shards):
            for h in range(2):
                sources = [mask ^ bit for bit in moving.orders[h][: moving.depth(h, mask)]]
                ready = all((h, s) in sent and sent[h, s] < t for s in sources)
                if (h, mask) not in sent and place[mask] <= t and ready:
                    now.append((h, mask))
        for item in now:
            sent[item] = t
        plan.append(now)
    rest = [(h, m) for m in range(1, shards) for h in range(2) if (h, m) not in sent]
    rest.sort(key=lambda item: moving.depth(*item))
    return plan, rest + [(0, 0), (1, 0)]


def experts_block(first_expert, n2, side, grad, mask, win, wout, wide_down, hid, down, spread, fold):
    rows = n2.shape[0]
    width = HIDDEN_UNITS
    lane = lane_of((rows, LANES))
    lows = dot(side, spread[:, : 2 * STACKED])
    low_gate = (lows[:, :STACKED] * mask).astype(BF)
    low_up = (lows[:, STACKED:] * mask).astype(BF)
    lift_gate = dot(low_gate, hid[0])
    lift_up = dot(low_up, hid[1])
    down_grad = (dot(grad, wide_down, 1, 1) * mask).astype(BF)
    from_down = dot(down_grad, down[...], 1, 1)
    side_full = side.astype(F32)
    total_inner = jnp.zeros((rows, width), F32)
    total_gate = jnp.zeros((rows, width), F32)
    total_up = jnp.zeros((rows, width), F32)
    extra = jnp.zeros((rows, LANES), F32)
    gated_parts, slope_parts = [], []
    for e in range(win.shape[1] // (2 * width)):
        name = first_expert + e
        at_high, at_low = lane == name, lane == name + EXPERT_COUNT
        gate = jnp.sum(jnp.where(at_high | at_low, side_full, 0.0), axis=1, keepdims=True)
        first = 2 * e * width
        pre_gate = dot(n2, win[:, first : first + width]) + lift_gate
        pre_up = dot(n2, win[:, first + width : first + 2 * width]) + lift_up
        pulled = dot(grad, wout[:, e * width : (e + 1) * width]) + from_down
        squashed = jax.nn.sigmoid(pre_gate)
        active = pre_gate * squashed
        inner = active * pre_up
        gate_grad = jnp.sum(inner * pulled, axis=1, keepdims=True)
        high = gate_grad.astype(BF).astype(F32)
        extra = extra + jnp.where(at_high, high, 0.0) + jnp.where(at_low, gate_grad - high, 0.0)
        gated = inner * gate
        pulled = pulled * gate
        grad_gate = pulled * pre_up * (squashed + active * (1.0 - squashed))
        grad_up = pulled * active
        gated_parts.append(gated.astype(BF))
        slope_parts += [grad_gate.astype(BF), grad_up.astype(BF)]
        total_inner = total_inner + gated
        total_gate = total_gate + grad_gate
        total_up = total_up + grad_up
    out = dot(jnp.concatenate(gated_parts, axis=1), wout[...], 1, 1)
    back = dot(jnp.concatenate(slope_parts, axis=1), win[...], 1, 1)
    total_inner = total_inner.astype(BF)
    total_gate = total_gate.astype(BF)
    total_up = total_up.astype(BF)
    shrunk = jnp.concatenate(
        [
            (dot(total_gate, hid[0], 1, 1) * mask).astype(BF),
            (dot(total_up, hid[1], 1, 1) * mask).astype(BF),
            (dot(total_inner, down[...]) * mask).astype(BF),
        ],
        axis=1,
    )
    extra = extra + dot(shrunk, fold[...])
    sums = (
        dot(total_inner, down_grad, 0, 0),
        dot(low_gate, total_gate, 0, 0),
        dot(low_up, total_up, 0, 0),
    )
    return out.astype(BF), back.astype(BF), extra.astype(BF), sums


def middle_kernel(
    shards,
    mine_ref,
    x_ref,
    cot_ref,
    small_ref,
    meta_ref,
    mask_ref,
    wo_ref,
    factors_ref,
    wide_ref,
    router2_ref,
    hid_ref,
    down_ref,
    spread_ref,
    fold_ref,
    cots_ref,
    win_ref,
    wout_ref,
    outs_ref,
    base_ref,
    hgrad_ref,
    heads_ref,
    gdown_ref,
    ghid_ref,
    gsecond_ref,
    gfactor_ref,
    gwide_ref,
    groute_ref,
    *scratch,
):
    near = shards <= 8
    store, block_in, scratch = (scratch[0], None, scratch[1:]) if near else (scratch[0], scratch[1], scratch[2:])
    middle_body(
        shards,
        near,
        (
            mine_ref,
            x_ref,
            cot_ref,
            small_ref,
            meta_ref,
            mask_ref,
            wo_ref,
            factors_ref,
            wide_ref,
            router2_ref,
            hid_ref,
            down_ref,
            spread_ref,
            fold_ref,
            cots_ref,
            win_ref,
            wout_ref,
        ),
        (
            outs_ref,
            base_ref,
            hgrad_ref,
            heads_ref,
            gdown_ref,
            ghid_ref,
            gsecond_ref,
            gfactor_ref,
            gwide_ref,
            groute_ref,
        ),
        store,
        block_in,
        *scratch,
    )


def middle_body(
    shards,
    near,
    given,
    results,
    store,
    block_in,
    own_in,
    part,
    land,
    win,
    wout,
    cots,
    outs,
    attended,
    gsend,
    grecv,
    ssend,
    srecv,
    wsem,
    csem,
    osem,
    bsem,
):
    (
        mine_ref,
        x_ref,
        cot_ref,
        small_ref,
        meta_ref,
        mask_ref,
        wo_ref,
        factors_ref,
        wide_ref,
        router2_ref,
        hid_ref,
        down_ref,
        spread_ref,
        fold_ref,
        cots_ref,
        win_ref,
        wout_ref,
    ) = given
    (
        outs_ref,
        base_ref,
        hgrad_ref,
        heads_ref,
        gdown_ref,
        ghid_ref,
        gsecond_ref,
        gfactor_ref,
        gwide_ref,
        groute_ref,
    ) = results
    me = lax.axis_index("fsdp")
    rows = x_ref.shape[0]
    if near:
        own_in = store.at[me]
    width = MODEL_WIDTH
    heads = HEADS // shards
    lane = lane_of((rows, LANES))
    loads = [
        pltpu.make_async_copy(win_ref, win, wsem.at[0]),
        pltpu.make_async_copy(wout_ref, wout, wsem.at[1]),
    ]
    for load in loads:
        load.start()

    def cot_copy(step):
        return pltpu.make_async_copy(
            cots_ref.at[me ^ turn_of(step, shards)], cots.at[step % 2], csem.at[step % 2]
        )

    cot_copy(0).start()
    greet([("fsdp", me, bits_of(shards))])

    for s in range(shards):
        if heads == 2:
            attended[:, s * LANES : (s + 1) * LANES] = mine_ref[s]
        elif s % 2 == 0:
            second = pltpu.roll(mine_ref[s + 1].astype(F32), HEAD_WIDTH, 1)
            both = jnp.where(lane < HEAD_WIDTH, mine_ref[s].astype(F32), second)
            attended[:, s // 2 * LANES : (s // 2 + 1) * LANES] = both.astype(BF)
    own = pl.ds(pl.multiple_of(me * rows, rows), rows)
    mask = mask_ref[own, :].astype(F32)
    small = small_ref[...]
    gain = gain_row(small, 17)
    out_low = (dot(attended[...], factors_ref[3]) * mask).astype(BF)
    hidden = (
        x_ref[...].astype(F32) + dot(attended[...], wo_ref[...], 1, 1) + dot(out_low, wide_ref[1])
    )
    base_ref[...] = hidden
    r2 = lax.rsqrt(jnp.mean(hidden * hidden, axis=1, keepdims=True) + EPSILON)
    n2 = (hidden * r2 * gain).astype(BF)
    own_in[:, :width] = n2
    lows = [(dot(n2, factors_ref[s]) * mask).astype(BF) for s in range(3)]
    logits = dot(n2, small) + dot(lows[0], router2_ref[...])
    named = jnp.zeros((LANES, rows), jnp.bool_)
    for k in range(TOPK):
        named = named | (row_of((LANES, rows)) == meta_ref[k : k + 1, :])
    eye = jnp.where(row_of((LANES, LANES)) == lane_of((LANES, LANES)), 1.0, 0.0).astype(BF)
    picked = dot(jnp.where(named, 1.0, 0.0).astype(BF), eye, 0, 0) > 0.5
    peak = jnp.max(jnp.where(picked, logits, MASKED), axis=1, keepdims=True)
    lifted = jnp.where(picked, jnp.exp(jnp.where(picked, logits, peak) - peak), 0.0)
    gates = lifted / jnp.sum(lifted, axis=1, keepdims=True)
    high = gates.astype(BF).astype(F32)
    shrunk = dot(jnp.concatenate(lows[1:], axis=1), fold_ref[: 2 * STACKED, :])
    side = high + pltpu.roll(gates - high, EXPERT_COUNT, 1) + shrunk
    own_in[:, width:] = side.astype(BF)

    going = Gather("fsdp", shards, own_in, store, (gsend, grecv))
    coming = Scatter("fsdp", shards, part, land, (ssend, srecv))
    going.start()
    for load in loads:
        load.wait()

    last = len(bits_of(shards)) - 1
    early, late = [], []
    for k in range(last):
        for s in range(1 << k):
            for h in range(2):
                order = going.orders[h]
                (late if shards == 8 and k == 1 and s else early).append(
                    (h, order[k] ^ span(order[:k])[s])
                )
    plan, rest = scatter_plan(coming, shards)
    first_expert = me * (EXPERT_COUNT // shards)

    def step(t, carry):
        turn = turn_of(t, shards)
        block = me ^ turn
        slot = t % 2

        @pl.when(t == 2)
        def _():
            for h, m in early:
                going.take(h, m)

        @pl.when(t == 3)
        def _():
            for h, m in late:
                going.take(h, m)

        for k in range(1, shards):
            m = turn_of(k, shards)
            if m % 2:

                @pl.when(t == k)
                def _(m=m):
                    for h in range(2):
                        going.take(h, m)

        @pl.when(t + 1 < shards)
        def _():
            cot_copy(t + 1).start()

        cot_copy(t).wait()

        def out_copy(at):
            return pltpu.make_async_copy(
                outs.at[at % 2], outs_ref.at[me ^ turn_of(at, shards)], osem.at[at % 2]
            )

        @pl.when(t >= 2)
        def _():
            out_copy(t - 2).wait()

        block_rows = pl.ds(pl.multiple_of(block * rows, rows), rows)
        if near:
            here = store.at[block]
        else:
            here = block_in

            @pl.when(t == 0)
            def _():
                block_in[...] = own_in[...]

            @pl.when(t != 0)
            def _():
                fetch = pltpu.make_async_copy(store.at[block], block_in, bsem)
                fetch.start()
                fetch.wait()

        out, back, extra, sums = experts_block(
            first_expert,
            here[:, :width],
            here[:, width:],
            cots[slot],
            mask_ref[block_rows, :].astype(F32),
            win,
            wout,
            wide_ref[2],
            hid_ref,
            down_ref,
            spread_ref,
            fold_ref,
        )
        outs[slot] = out
        out_copy(t).start()
        part[block, :, :width] = back
        part[block, :, width:] = extra

        @pl.when(t == 0)
        def _():
            gdown_ref[...] = sums[0]
            ghid_ref[0] = sums[1]
            ghid_ref[1] = sums[2]

        @pl.when(t != 0)
        def _():
            gdown_ref[...] += sums[0]
            ghid_ref[0] += sums[1]
            ghid_ref[1] += sums[2]

        for k in range(shards):
            if plan[k]:

                @pl.when(t == k)
                def _(k=k):
                    for h, m in plan[k]:
                        coming.reduce(h, m)

        @pl.when(t == shards - 1)
        def _():
            out_copy(shards - 2).wait()
            out_copy(shards - 1).wait()

        return carry

    lax.fori_loop(0, shards, step, 0)
    for h, m in rest:
        coming.reduce(h, m)

    hidden = base_ref[...]
    mask = mask_ref[own, :].astype(F32)
    r2 = lax.rsqrt(jnp.mean(hidden * hidden, axis=1, keepdims=True) + EPSILON)
    n2 = own_in[:, :width]
    cot = cot_ref[...]
    grad = cot.astype(F32)
    extra = part[me, :, width:]
    extra_full = extra.astype(F32)
    gate_grad = extra_full + pltpu.roll(extra_full, LANES - EXPERT_COUNT, 1)
    logit_grad = gates * (gate_grad - jnp.sum(gates * gate_grad, axis=1, keepdims=True))
    logit_grad = jnp.where(lane < EXPERT_COUNT, logit_grad, 0.0).astype(BF)
    wider = dot(extra, spread_ref[...])
    second_grad = [
        (dot(logit_grad, router2_ref[...], 1, 1) * mask).astype(BF),
        (wider[:, :STACKED] * mask).astype(BF),
        (wider[:, STACKED : 2 * STACKED] * mask).astype(BF),
    ]
    down_low = (wider[:, 2 * STACKED :] * mask).astype(BF)
    base_ref[...] = hidden + dot(down_low, wide_ref[2])
    gwide_ref[1] = dot(down_low, cot, 0, 0)
    groute_ref[...] = dot(lows[0], logit_grad, 0, 0)
    n2_grad = part[me, :, :width].astype(F32) + dot(logit_grad, small, 1, 1)
    for s in range(3):
        n2_grad = n2_grad + dot(second_grad[s], factors_ref[s], 1, 1)
    gsecond_ref[...] = dot(n2, jnp.concatenate(second_grad, axis=1), 0, 0)
    w2 = gain * n2_grad
    hidden_grad = grad + r2 * w2 - hidden * (r2 * r2 * r2) * jnp.mean(w2 * hidden, axis=1, keepdims=True)
    hgrad_ref[...] = hidden_grad
    out_grad = hidden_grad.astype(BF)
    gwide_ref[0] = dot(out_low, out_grad, 0, 0)
    out_low_grad = (dot(out_grad, wide_ref[1], 1, 1) * mask).astype(BF)
    gfactor_ref[...] = dot(attended[...], out_low_grad, 0, 0)
    attended_grad = dot(out_grad, wo_ref[...]) + dot(out_low_grad, factors_ref[3], 1, 1)
    for s in range(shards):
        if heads == 2:
            heads_ref[s] = attended_grad[:, s * LANES : (s + 1) * LANES].astype(BF)
        else:
            pair = attended_grad[:, s // 2 * LANES : (s // 2 + 1) * LANES]
            if s % 2:
                pair = pltpu.roll(pair, HEAD_WIDTH, 1)
            heads_ref[s] = jnp.where(lane < HEAD_WIDTH, pair, 0.0).astype(BF)
    going.finish()
    coming.finish()


def middle(mine, x, cot, small, meta, mask, wo, factors, wide, router2, hid, down, cots, win, wout, identity):
    shards = lax.axis_size("fsdp")
    rows = x.shape[0]
    side = MODEL_WIDTH + LANES
    source = np.arange(LANES)
    place = np.arange(STACKED) % ADAPTER_RANK
    spread = np.concatenate([source[:, None] == o + place[None, :] for o in (32, 48, 64)], axis=1)
    fold = np.concatenate([source[None, :] == o + place[:, None] for o in (32, 48, 64)], axis=0)
    spread, fold = jnp.asarray(spread, BF), jnp.asarray(fold, BF)
    gathered = (shards, rows, side)
    near = shards <= 8
    results = pl.pallas_call(
        functools.partial(middle_kernel, shards),
        out_shape=(
            jax.ShapeDtypeStruct((shards, rows, MODEL_WIDTH), BF),
            jax.ShapeDtypeStruct((rows, MODEL_WIDTH), F32),
            jax.ShapeDtypeStruct((rows, MODEL_WIDTH), F32),
            jax.ShapeDtypeStruct((shards, rows, LANES), BF),
            jax.ShapeDtypeStruct((HIDDEN_UNITS, STACKED), F32),
            jax.ShapeDtypeStruct((2, STACKED, HIDDEN_UNITS), F32),
            jax.ShapeDtypeStruct((MODEL_WIDTH, 3 * STACKED), F32),
            jax.ShapeDtypeStruct((MODEL_WIDTH, STACKED), F32),
            jax.ShapeDtypeStruct((2, STACKED, MODEL_WIDTH), F32),
            jax.ShapeDtypeStruct((STACKED, LANES), F32),
        )
        + (() if near else (jax.ShapeDtypeStruct(gathered, BF),)),
        in_specs=[IN_VMEM] * 14 + [ANYWHERE] * 3,
        out_specs=(ANYWHERE,) + (IN_VMEM,) * 9 + (() if near else (ANYWHERE,)),
        scratch_shapes=[
            pltpu.VMEM(gathered if near else gathered[1:], BF),
            pltpu.VMEM((16, LANES) if near else gathered[1:], BF),
            pltpu.VMEM((shards, rows, side), BF),
            pltpu.VMEM((2, shards - 1, rows // 2, side), BF),
            pltpu.VMEM(win.shape, BF),
            pltpu.VMEM(wout.shape, BF),
            pltpu.VMEM((2, rows, MODEL_WIDTH), BF),
            pltpu.VMEM((2, rows, MODEL_WIDTH), BF),
            pltpu.VMEM((rows, MODEL_WIDTH), BF),
        ]
        + pair_of_sems(shards) * 2
        + [pltpu.SemaphoreType.DMA((2,))] * 3
        + [pltpu.SemaphoreType.DMA(())],
        compiler_params=remote(identity, 62),
        name="middle",
    )(mine, x, cot, small, meta, mask, wo, factors, wide, router2, hid, down, spread, fold, cots, win, wout)
    return results[:10]


def rotate(tensor, cosine, sine):
    rows = tensor.shape[0]
    view = tensor.reshape(rows, -1, 2, HEAD_WIDTH // 2)
    first, second = view[:, :, 0], view[:, :, 1]
    c, s = cosine[:, None, :], sine[:, None, :]
    turned = jnp.stack([first * c - second * s, second * c + first * s], axis=2)
    return turned.reshape(rows, -1)


def local(
    tokens,
    cotangent,
    lengths,
    adapter_index,
    routes,
    deal,
    norm_gain_pair,
    query_weight,
    key_weight,
    value_weight,
    output_weight_transposed,
    router_weight,
    expert_input_weight,
    expert_output_weight,
    factors,
    down_first,
    wide,
    kv_second,
    hidden_second,
    router_second,
):
    shards = lax.axis_size("fsdp")
    groups = lax.axis_size("dp")
    rows = tokens.shape[0]
    total = rows * shards
    heads = HEADS // shards
    share = max(1, shards // KEY_VALUE_HEADS)
    me = lax.axis_index("fsdp")

    padded = ((0, 0), (0, rows - lengths.shape[1]))
    meta = jnp.concatenate(
        [
            routes.T,
            jnp.pad(lengths, padded),
            jnp.pad(adapter_index, padded),
            jnp.zeros((6, rows), jnp.int32),
        ],
        axis=0,
    )
    small = jnp.concatenate(
        [
            router_weight,
            norm_gain_pair,
            jnp.zeros((router_weight.shape[0], LANES - EXPERT_COUNT - 2), BF),
        ],
        axis=1,
    )
    qkv, low_all, group_mask, small, meta = enter(
        deal,
        tokens,
        query_weight,
        key_weight,
        value_weight,
        small,
        meta,
        factors[0:3],
        wide[0],
        kv_second,
        1,
    )
    lens = meta[8:9, : lengths.shape[1]]
    gains = small[:, EXPERT_COUNT : EXPERT_COUNT + 2].astype(F32)
    mask_low = lax.dynamic_slice_in_dim(group_mask, me * rows, rows, 0)
    mask = mask_low.astype(F32)
    win = expert_input_weight.reshape(MODEL_WIDTH, -1)
    wout = expert_output_weight.reshape(MODEL_WIDTH, -1)
    all_grad = lax.all_gather(cotangent, "fsdp", axis=0, tiled=True)
    out_weight = lax.all_gather(output_weight_transposed, ("dp", "fsdp"), axis=0, tiled=True)

    x = tokens.astype(F32)
    r1 = lax.rsqrt(jnp.mean(x * x, axis=1, keepdims=True) + EPSILON)
    normed = (x * r1 * gains[:, 0]).astype(BF)
    first_low = lax.dynamic_slice_in_dim(low_all, me * rows, rows, 0)
    first_low = [first_low[:, s * STACKED : (s + 1) * STACKED] for s in range(3)]

    def by_head(array, count, repeat):
        array = array.astype(BF).reshape(rows, count, -1).transpose(1, 0, 2)
        return jnp.repeat(array, repeat, axis=0) if repeat > 1 else array

    in_weight = lax.all_gather(
        jnp.concatenate([query_weight, key_weight, value_weight], axis=1),
        ("dp", "fsdp"),
        axis=0,
        tiled=True,
    )
    offsets = jnp.cumsum(lens[0]) - lens[0]
    index = me * rows + jnp.arange(rows, dtype=jnp.int32)
    inside = (index[:, None] >= offsets[None, :]) & (index[:, None] < (offsets + lens[0])[None, :])
    begin = jnp.sum(jnp.where(inside, offsets[None, :], 0), axis=1)
    half = HEAD_WIDTH // 2
    frequency = ROPE_BASE ** (-jnp.arange(half, dtype=F32) / half)
    angles = (index - begin).astype(F32)[:, None] * frequency[None, :]
    cosine, sine = jnp.cos(angles), jnp.sin(angles)
    attended, q_kept, k_kept, v_kept = attend(lens, qkv, heads)

    mine = plane_swap(attended.reshape(shards, rows, -1), 5)
    router2 = jnp.pad(router_second, ((0, 0), (0, LANES - EXPERT_COUNT)))
    (
        out_part,
        base,
        hidden_grad,
        to_heads,
        g_down_a,
        g_ff,
        g_second,
        g_factor_out,
        g_wide,
        g_route,
    ) = middle(
        mine,
        tokens,
        cotangent,
        small,
        meta,
        group_mask,
        out_weight,
        factors[3:7],
        wide,
        router2,
        hidden_second,
        down_first,
        all_grad.reshape(shards, rows, -1),
        win,
        wout,
        6,
    )
    layer_out = (base + scatter(out_part, "fsdp", 7).astype(F32)).astype(BF)
    g_second = [g_second[:, s * STACKED : (s + 1) * STACKED] for s in range(3)]
    g_wide_out, g_wide_down = g_wide[0], g_wide[1]
    head_grad = plane_swap(to_heads, 9).reshape(total, -1)
    qkv_grad = attend_back(lens, q_kept, k_kept, v_kept, attended, head_grad, heads)
    qkv_grad = plane_swap(qkv_grad.reshape(shards, rows, -1), 10).astype(F32)

    def joined(array):
        array = array.reshape(shards // share, share, rows, -1).sum(1)
        return array.transpose(1, 0, 2).reshape(rows, -1)

    query_grad = qkv_grad[:, :, : heads * HEAD_WIDTH].transpose(1, 0, 2).reshape(rows, -1)
    query_grad = rotate(query_grad, cosine, -sine).astype(BF)
    keys_grad = rotate(joined(qkv_grad[:, :, LANES : LANES + 64]), cosine, -sine).astype(BF)
    values_grad = joined(qkv_grad[:, :, LANES + 64 :]).astype(BF)
    mixed_grad = jnp.concatenate([query_grad, keys_grad, values_grad], axis=1)
    normed_grad = dot(mixed_grad, in_weight, 1, 1)
    first_grad = [
        (dot(query_grad, wide[0], 1, 1) * mask).astype(BF),
        (dot(keys_grad, kv_second[0], 1, 1) * mask).astype(BF),
        (dot(values_grad, kv_second[1], 1, 1) * mask).astype(BF),
    ]
    for s in range(3):
        normed_grad = normed_grad + dot(first_grad[s], factors[s], 1, 1)
    g_first = [dot(normed, first_grad[s], 0, 0) for s in range(3)]
    g_wide_query = dot(first_low[0], query_grad, 0, 0)
    g_kv = [dot(first_low[1], keys_grad, 0, 0), dot(first_low[2], values_grad, 0, 0)]
    w1 = gains[:, 0] * normed_grad
    input_grad = hidden_grad + r1 * w1 - x * r1**3 * jnp.mean(w1 * x, axis=1, keepdims=True)

    def tall(array):
        return [array[:, c : c + LANES] for c in range(0, array.shape[1], LANES)]

    pieces = g_first + g_second + [g_factor_out, g_down_a]
    for array in [g_wide_query, g_wide_out, g_wide_down] + g_kv + [g_ff[0], g_ff[1]]:
        pieces = pieces + tall(array)
    pieces = pieces + [g_route]
    sums = total_of(jnp.concatenate([p.astype(BF) for p in pieces], axis=0), 11).astype(F32)

    def wide_sum(start, count, parts):
        block = sums[start : start + count * parts * STACKED]
        block = block.reshape(count, parts, STACKED, LANES).transpose(0, 2, 1, 3)
        return block.reshape(count, STACKED, parts * LANES)

    edge = 7 * MODEL_WIDTH
    factor_sum = sums[:edge].reshape(7, MODEL_WIDTH, STACKED)
    down_sum = sums[edge : edge + HIDDEN_UNITS]
    edge += HIDDEN_UNITS
    wide_total = wide_sum(edge, 3, 8)
    edge += 24 * STACKED
    kv_total = wide_sum(edge, 2, 4)
    edge += 8 * STACKED
    ff_total = wide_sum(edge, 2, 4)
    edge += 8 * STACKED
    route_total = sums[edge : edge + STACKED, :EXPERT_COUNT]
    return (
        layer_out,
        input_grad,
        factor_sum,
        down_sum,
        wide_total,
        kv_total,
        ff_total,
        route_total,
    )


def solution(mesh):
    rows = P(("dp", "fsdp"), None)
    placed = (
        (rows, rows, P("dp", None), P("dp", None), rows, P())
        + (rows,) * 6
        + (P(None, "fsdp", None),) * 2
        + (P(),) * 6
    )
    return jax.shard_map(
        local,
        mesh=mesh,
        in_specs=placed,
        out_specs=(rows, rows) + (P(),) * 6,
        check_vma=False,
    )
```

```python
import functools
import math

import jax
import jax.numpy as jnp
import numpy as np
from jax import lax
from jax.experimental import pallas as pl
from jax.experimental.pallas import tpu as pltpu
from jax.sharding import PartitionSpec as P

MODEL_WIDTH = 1024
HEADS = 16
KEY_VALUE_HEADS = 8
HEAD_WIDTH = 64
HIDDEN_UNITS = 512
TOPK = 8
EXPERT_COUNT = 16
ADAPTER_COUNT = 8
ADAPTER_RANK = 16
STACKED = ADAPTER_COUNT * ADAPTER_RANK

EPSILON = 1e-06
ROPE_BASE = 10000.0
MASKED = -1e30
LANES = 128
PART = 128
NSEQ = 4

BF = jnp.bfloat16
F32 = jnp.float32
MESH = pl.DeviceIdType.MESH


def dot(a, b, ca=1, cb=0):
    return lax.dot_general(a, b, (((ca,), (cb,)), ((), ())), preferred_element_type=F32)


def splits(v):
    hi = v.astype(BF).astype(F32)
    rest = v - hi
    mid = rest.astype(BF).astype(F32)
    return hi, mid, rest - mid


def lane_of(shape):
    return lax.broadcasted_iota(jnp.int32, shape, len(shape) - 1)


def row_of(shape):
    return lax.broadcasted_iota(jnp.int32, shape, 0)


def bits_of(count):
    return [1 << k for k in range(count.bit_length() - 1)]


def orders_of(count):
    bits = bits_of(count)
    far = bits[1:]
    cut = (len(far) + 1) // 2
    return (far + bits[:1], far[cut:] + far[:cut] + bits[:1])


def span(bits):
    masks = [0]
    for bit in bits:
        masks = masks + [m ^ bit for m in masks]
    return masks


def greet(meetings):
    barrier = pltpu.get_barrier_semaphore()
    count = 0
    for axis, me, masks in meetings:
        for mask in masks:
            pl.semaphore_signal(
                barrier, inc=1, device_id={axis: me ^ mask}, device_id_type=MESH
            )
            count += 1
    pl.semaphore_wait(barrier, count)


class Gather:
    def __init__(self, axis, count, own, store, sems):
        self.axis, self.count, self.own, self.store = axis, count, own, store
        self.sends, self.recvs = sems
        self.me = lax.axis_index(axis)
        self.orders = orders_of(count)
        self.half = store.shape[1] // 2

    def copy(self, h, mask, bit):
        rows = pl.ds(h * self.half, self.half)
        there = self.store.at[self.me ^ mask, rows]
        return pltpu.make_async_remote_copy(
            src_ref=self.own.at[rows] if mask == 0 else there,
            dst_ref=there,
            send_sem=self.sends.at[h, mask ^ bit],
            recv_sem=self.recvs.at[h, mask ^ bit],
            device_id={self.axis: self.me ^ bit},
            device_id_type=MESH,
        )

    def incoming(self, h, mask):
        there = self.store.at[self.me ^ mask, pl.ds(h * self.half, self.half)]
        return pltpu.make_async_remote_copy(
            src_ref=there,
            dst_ref=there,
            send_sem=self.sends.at[h, mask],
            recv_sem=self.recvs.at[h, mask],
            device_id={self.axis: self.me ^ mask},
            device_id_type=MESH,
        )

    def start(self):
        for k in range(len(self.orders[0])):
            for h in range(2):
                self.copy(h, 0, self.orders[h][k]).start()

    def take(self, h, mask):
        order = self.orders[h]
        self.incoming(h, mask).wait_recv()
        k = max(i for i, bit in enumerate(order) if mask & bit)
        for bit in order[k + 1 :]:
            self.copy(h, mask, bit).start()

    def halves(self):
        early, late = [], []
        for k in range(len(self.orders[0]) - 1):
            for s in range(1 << k):
                for h in range(2):
                    mask = self.orders[h][k] ^ span(self.orders[h][:k])[s]
                    (late if self.count == 8 and k == 1 and s else early).append((h, mask))
        return early, late

    def stage(self, k):
        for s in range(1 << k):
            for h in range(2):
                order = self.orders[h]
                mask = order[k] ^ span(order[:k])[s]
                self.incoming(h, mask).wait_recv()
                for bit in order[k + 1 :]:
                    self.copy(h, mask, bit).start()

    def held(self, k):
        sets = [set(span(order[: k + 1])) for order in self.orders]
        return sets[0] & sets[1]

    def stages(self):
        for k in range(len(self.orders[0])):
            self.stage(k)

    def finish(self):
        for h in range(2):
            for mask in range(1, self.count):
                self.incoming(h, mask).wait_send()


class Scatter:
    def __init__(self, axis, count, part, land, sems):
        self.axis, self.count, self.part, self.land = axis, count, part, land
        self.sends, self.recvs = sems
        self.me = lax.axis_index(axis)
        self.orders = [order[::-1] for order in orders_of(count)]
        self.half = part.shape[1] // 2

    def depth(self, h, mask):
        for k, bit in enumerate(self.orders[h]):
            if mask & bit:
                return k
        return len(self.orders[h])

    def copy(self, h, mask):
        bit = self.orders[h][self.depth(h, mask)]
        return pltpu.make_async_remote_copy(
            src_ref=self.part.at[self.me ^ mask, pl.ds(h * self.half, self.half)],
            dst_ref=self.land.at[h, mask - 1],
            send_sem=self.sends.at[h, mask],
            recv_sem=self.recvs.at[h, mask],
            device_id={self.axis: self.me ^ bit},
            device_id_type=MESH,
        )

    def reduce(self, h, mask):
        depth = self.depth(h, mask)
        sources = [mask ^ bit for bit in self.orders[h][:depth]]
        for source in sources:
            self.copy(h, source).wait_recv()
        if sources:
            step = math.gcd(self.half, 64)
            mine = self.me ^ mask

            def add(c, carry):
                here = pl.ds(pl.multiple_of(c * step, step), step)
                at = pl.ds(pl.multiple_of(h * self.half + c * step, step), step)
                total = self.part[mine, at].astype(F32)
                for source in sources:
                    total = total + self.land[h, source - 1, here].astype(F32)
                self.part[mine, at] = total.astype(BF)
                return carry

            lax.fori_loop(0, self.half // step, add, 0)
        if mask:
            self.copy(h, mask).start()

    def run(self):
        for k in range(len(self.orders[0]) + 1):
            for mask in range(self.count):
                for h in range(2):
                    if self.depth(h, mask) == k:
                        self.reduce(h, mask)

    def finish(self):
        for h in range(2):
            for mask in range(1, self.count):
                self.copy(h, mask).wait_send()


def pair_of_sems(count):
    return [pltpu.SemaphoreType.DMA((2, count)), pltpu.SemaphoreType.DMA((2, count))]


ANYWHERE = pl.BlockSpec(memory_space=pl.ANY)
IN_VMEM = pl.BlockSpec(memory_space=pltpu.VMEM)


def remote(identity, limit=48):
    return pltpu.CompilerParams(
        collective_id=identity, has_side_effects=True, vmem_limit_bytes=limit << 20
    )


def scatter_kernel(axis, count, given, total, part, land, sends, recvs, local_sem):
    me = lax.axis_index(axis)
    take = pltpu.make_async_copy(given, part, local_sem)
    take.start()
    greet([(axis, me, bits_of(count))])
    moving = Scatter(axis, count, part, land, (sends, recvs))
    take.wait()
    moving.run()
    total[...] = part[me]
    moving.finish()


def scatter(blocks, axis, identity):
    count, rows, columns = blocks.shape
    return pl.pallas_call(
        functools.partial(scatter_kernel, axis, count),
        out_shape=jax.ShapeDtypeStruct((rows, columns), BF),
        in_specs=[ANYWHERE],
        out_specs=IN_VMEM,
        scratch_shapes=[
            pltpu.VMEM(blocks.shape, BF),
            pltpu.VMEM((2, count - 1, rows // 2, columns), BF),
        ]
        + pair_of_sems(count)
        + [pltpu.SemaphoreType.DMA(())],
        compiler_params=remote(identity, 56),
        name="scatter",
    )(blocks)


def attend_kernel(
    shards,
    near,
    heads,
    meta_ref,
    qkv_ref,
    cot_ref,
    mine_ref,
    out_ref,
    q_ref,
    k_ref,
    v_ref,
    cots_ref,
    gsend,
    grecv,
    asend,
    arecv,
    keep_sem,
):
    me = lax.axis_index("fsdp")
    total = qkv_ref.shape[0]
    nseq = NSEQ
    keep = pltpu.make_async_copy(cot_ref, cots_ref.at[me], keep_sem)
    keep.start()
    greet([("fsdp", me, range(1, shards))])
    going = Gather("fsdp", shards, cot_ref, cots_ref, (gsend, grecv))
    going.start()
    early, late = going.halves()
    edges = [jnp.zeros((1, 1), jnp.int32)]
    for s in range(nseq):
        edges.append(edges[-1] + meta_ref[8:9, s : s + 1])
    half = HEAD_WIDTH
    side = PART

    def prepare(i, carry):
        at = pl.ds(pl.multiple_of(i * side, side), side)
        low = lane_of((side, LANES)) < half
        lane = lane_of((side, LANES))
        row = row_of((side, LANES)) + i * side
        seq = jnp.zeros((side, LANES), jnp.bool_)
        for s in range(nseq):
            seq = seq | ((lane == s) & (row >= edges[s]) & (row < edges[s + 1]))
        queries = qkv_ref[at, 0:LANES].astype(F32) * (HEAD_WIDTH ** -0.5)
        pair = qkv_ref[at, LANES : 2 * LANES].astype(F32)
        swapped = pltpu.roll(pair, half, 1)
        marks = jnp.where(seq, 1.0, 0.0).astype(BF)
        for h in range(heads):
            mine = jnp.where(low if h == 0 else ~low, queries, 0.0).astype(BF)
            q_ref[i, h * side : (h + 1) * side, 0:LANES] = mine
            q_ref[i, h * side : (h + 1) * side, LANES : 2 * LANES] = marks
        k_ref[at, 0:LANES] = jnp.where(low, pair, swapped).astype(BF)
        far = jnp.where(lane < nseq, jnp.where(seq, 0.0, MASKED), 0.0)
        k_ref[at, LANES : 2 * LANES] = jnp.where(
            (lane >= nseq) & (lane < nseq + 3), 1.0, far
        ).astype(BF)
        v_ref[at, 0:LANES] = jnp.where(low, swapped, pair).astype(BF)
        v_ref[at, LANES : 2 * LANES] = jnp.ones((side, LANES), BF)
        return carry

    lax.fori_loop(0, total // side, prepare, 0)

    rows = 3 * side

    def place(ref, source):
        if near:
            return ref.at[:, pl.ds(pl.multiple_of(source * LANES, LANES), LANES)]
        return ref.at[source]

    def home_copy(target):
        return pltpu.make_async_remote_copy(
            src_ref=out_ref.at[pl.ds(target * rows, rows)],
            dst_ref=place(mine_ref, me),
            send_sem=asend.at[target],
            recv_sem=arecv.at[me],
            device_id={"fsdp": target},
            device_id_type=MESH,
        )

    low = lane_of((rows, LANES)) < half
    lane = lane_of((rows, LANES))
    visible = lane_of((rows, rows)) <= row_of((rows, rows))
    for i in range(total // rows):
        keys = (i + 1) * rows
        at = pl.ds(i * rows, rows)
        mixed = []
        for h in range(heads):
            mine = pl.ds(h * side, side)
            queries = jnp.concatenate([q_ref[3 * i + u, mine, :] for u in range(3)], axis=0)
            scores = dot(queries, k_ref[0:keys, :], 1, 1)
            final = jnp.where(visible, scores[:, keys - rows :], MASKED)
            if i:
                scores = jnp.concatenate([scores[:, : keys - rows], final], axis=1)
            else:
                scores = final
            top = jnp.max(scores, axis=1, keepdims=True)
            weights = jnp.exp(scores - top).astype(BF)
            acc = dot(weights, v_ref[0:keys, :])
            weight = acc[:, LANES:]
            mixed.append(acc[:, :LANES] / weight)
            hi, mid, lo = splits(-(top + jnp.log(weight)))
            marks = queries[:, LANES:].astype(F32)
            marks = jnp.where(lane == nseq, hi, marks)
            marks = jnp.where(lane == nseq + 1, mid, marks)
            marks = jnp.where(lane == nseq + 2, lo, marks).astype(BF)
            for u in range(3):
                q_ref[3 * i + u, mine, LANES:] = marks[u * side : (u + 1) * side]
        value = mixed[0] if heads == 1 else jnp.where(low, mixed[0], mixed[1])
        out_ref[at, :] = value.astype(BF)

        @pl.when(me != i)
        def _(i=i):
            home_copy(i).start()

        if i == shards - 2:
            for h, m in early:
                going.take(h, m)

    place(mine_ref, me)[...] = out_ref[pl.ds(pl.multiple_of(me * rows, rows), rows), :]
    for h, m in late:
        going.take(h, m)
    for m in range(1, shards):
        pltpu.make_async_remote_copy(
            src_ref=out_ref.at[pl.ds(0, rows)],
            dst_ref=place(mine_ref, me ^ m),
            send_sem=asend.at[0],
            recv_sem=arecv.at[me ^ m],
            device_id={"fsdp": me ^ m},
            device_id_type=MESH,
        ).wait_recv()
    for i in range(shards):

        @pl.when(me != i)
        def _(i=i):
            home_copy(i).wait_send()

    for h in range(2):
        for m in span(going.orders[h][:-1]):
            going.incoming(h, m ^ going.orders[h][-1]).wait_recv()
    going.finish()
    keep.wait()


def attend(meta, qkv, cot, heads, identity):
    shards = lax.axis_size("fsdp")
    near = shards <= 8
    total = qkv.shape[0]
    rows = total // shards
    return pl.pallas_call(
        functools.partial(attend_kernel, shards, near, heads),
        out_shape=(
            jax.ShapeDtypeStruct((rows, MODEL_WIDTH) if near else (shards, rows, LANES), BF),
            jax.ShapeDtypeStruct((total, LANES), BF),
            jax.ShapeDtypeStruct((total // PART, heads * PART, 2 * LANES), BF),
            jax.ShapeDtypeStruct((total, 2 * LANES), BF),
            jax.ShapeDtypeStruct((total, 2 * LANES), BF),
            jax.ShapeDtypeStruct((shards,) + cot.shape, BF),
        ),
        in_specs=[IN_VMEM, IN_VMEM, ANYWHERE],
        out_specs=(IN_VMEM,) * 5 + (ANYWHERE,),
        scratch_shapes=pair_of_sems(shards)
        + [pltpu.SemaphoreType.DMA((shards,))] * 2
        + [pltpu.SemaphoreType.DMA(())],
        compiler_params=remote(identity, 60),
        name="attend",
    )(meta, qkv, cot)


def sequences(meta, first, rows, heads_of):
    row = row_of((rows, LANES)) + first
    start = jnp.zeros((1, 1), jnp.int32)
    picked = [jnp.zeros((rows, LANES), part[0].dtype) for part in heads_of]
    for s in range(len(heads_of[0])):
        inside = row >= start
        picked = [jnp.where(inside, part[s], value) for part, value in zip(heads_of, picked)]
        start = start + meta[8:9, s : s + 1]
    return picked


def turned(tensor, cosine, sine):
    lower = lane_of(tensor.shape) % HEAD_WIDTH < HEAD_WIDTH // 2
    other = jnp.where(lower, pltpu.roll(tensor, LANES - 32, 1), pltpu.roll(tensor, 32, 1))
    return tensor * cosine + other * sine


def head_columns(wide, narrow, pick_wide, pick_narrow, heads):
    low = lane_of((1, LANES)) < HEAD_WIDTH
    queries = wide
    if heads == 1:
        queries = jnp.where(low, jnp.where(pick_wide, pltpu.roll(wide, HEAD_WIDTH, 1), wide), 0.0)
    keys, values = narrow
    keys = jnp.where(pick_narrow, pltpu.roll(keys, HEAD_WIDTH, 1), keys)
    values = jnp.where(pick_narrow, values, pltpu.roll(values, HEAD_WIDTH, 1))
    return queries, jnp.where(low, keys, values)


def enter_kernel(
    shards,
    groups,
    deal_ref,
    x_ref,
    wq_ref,
    wk_ref,
    wv_ref,
    small_ref,
    meta_ref,
    factors_ref,
    wide_ref,
    kv_ref,
    cos_ref,
    sin_ref,
    freq_ref,
    qkv_ref,
    low_ref,
    mask_ref,
    small_out,
    meta_out,
    columns_out,
    turn_ref,
    xs,
    slices,
    weights,
    metas,
    merged,
    second,
    xsend,
    xrecv,
    wsend,
    wrecv,
    zsend,
    zrecv,
    msend,
    mrecv,
):
    me, plane = lax.axis_index("fsdp"), lax.axis_index("dp")
    heads = HEADS // shards
    share = max(1, shards // KEY_VALUE_HEADS)
    rows = x_ref.shape[0]
    part = wq_ref.shape[0]
    order = [mask for mask in range(1, shards)]

    for f in range(shards):
        chunk = f * heads * HEAD_WIDTH // LANES
        head = f // share
        pair = head // 2
        queries, others = head_columns(
            wq_ref[:, chunk * LANES : (chunk + 1) * LANES].astype(F32),
            (
                wk_ref[:, pair * LANES : (pair + 1) * LANES].astype(F32),
                wv_ref[:, pair * LANES : (pair + 1) * LANES].astype(F32),
            ),
            f % 2 == 1,
            head % 2 == 1,
            heads,
        )
        slices[f, :, 0:LANES] = queries.astype(BF)
        slices[f, :, LANES : 2 * LANES] = others.astype(BF)
        slices[f, :, 2 * LANES :] = small_ref[...]
    metas[plane] = meta_ref[...]

    greet([("fsdp", me, order), ("dp", plane, range(1, groups))])

    moving = Gather("fsdp", shards, x_ref, xs, (xsend, xrecv))
    plane_rows = shards * part

    def column_copy(mask):
        return pltpu.make_async_remote_copy(
            src_ref=slices.at[me ^ mask],
            dst_ref=weights.at[plane, me],
            send_sem=wsend.at[mask],
            recv_sem=wrecv.at[mask],
            device_id={"fsdp": me ^ mask},
            device_id_type=MESH,
        )

    def plane_copy(mask):
        return pltpu.make_async_remote_copy(
            src_ref=weights.at[plane],
            dst_ref=weights.at[plane],
            send_sem=zsend.at[mask],
            recv_sem=zrecv.at[mask],
            device_id={"dp": plane ^ mask},
            device_id_type=MESH,
        )

    def meta_copy(mask):
        return pltpu.make_async_remote_copy(
            src_ref=meta_ref,
            dst_ref=metas.at[plane],
            send_sem=msend.at[mask],
            recv_sem=mrecv.at[mask],
            device_id={"dp": plane ^ mask},
            device_id_type=MESH,
        )

    for mask in order:
        column_copy(mask).start()
    for mask in range(1, groups):
        meta_copy(mask).start()
    moving.start()
    weights[plane, me] = slices[me]

    half = HEAD_WIDTH
    at = pl.ds(pl.multiple_of(me * heads * half // LANES * LANES, LANES), LANES)
    head = me // share
    pair_at = pl.ds(pl.multiple_of(head // 2 * LANES, LANES), LANES)
    queries, others = head_columns(
        wide_ref[0, :, at].astype(F32),
        (kv_ref[0, :, pair_at].astype(F32), kv_ref[1, :, pair_at].astype(F32)),
        me % 2 == 1,
        head % 2 == 1,
        heads,
    )
    low_lane = lane_of((STACKED, LANES)) < half
    second[...] = jnp.zeros(second.shape, BF)
    second[0:STACKED, 0:LANES] = queries.astype(BF)
    second[STACKED : 2 * STACKED, LANES:] = jnp.where(low_lane, others, 0.0).astype(BF)
    second[2 * STACKED :, LANES:] = jnp.where(low_lane, 0.0, others).astype(BF)

    for mask in order:
        column_copy(mask).wait_recv()
    for mask in range(1, groups):
        plane_copy(mask).start()
    for mask in range(1, groups):
        meta_copy(mask).wait_recv()
    dealt = jnp.int32(0)
    for g in range(groups):
        dealt = dealt + jnp.where(deal_ref[g] == plane, g, 0)
    meta = jnp.zeros(meta_ref.shape, jnp.int32)
    for g in range(groups):
        meta = jnp.where(dealt == g, metas[g], meta)
    meta_out[...] = meta
    moving.stage(0)
    for mask in range(1, groups):
        plane_copy(mask).wait_recv()

    for g in range(groups):
        for f in range(shards):
            here = pl.ds((g * shards + f) * part, part)
            block = weights[g, f]
            small_out[here, :] = block[:, 2 * LANES :]
            merged[here, 0 : 2 * LANES] = block[:, : 2 * LANES]
            columns_out[here, :] = block[:, : 2 * LANES]
    for s in range(3):
        merged[:, (2 + s) * LANES : (3 + s) * LANES] = factors_ref[s]
    gain = gain_row(small_out[...], 16)

    nseq = NSEQ
    lanes = lane_of((1, LANES))
    starts, first = [], jnp.zeros((1, 1), jnp.int32)
    for s in range(nseq):
        starts.append(first)
        first = first + meta[8:9, s : s + 1]
    angles = [start.astype(F32) * freq_ref[...] for start in starts]
    start_cos = [jnp.cos(angle) for angle in angles]
    start_sin = [jnp.sin(angle) for angle in angles]
    adapters = [jnp.broadcast_to(meta[9:10, s : s + 1], (1, LANES)) for s in range(nseq)]
    keyed = lanes < half
    sign = jnp.where(lanes % half < half // 2, -1.0, 1.0)

    def compute(mask):
        block = me ^ mask
        at = pl.ds(pl.multiple_of(block * rows, rows), rows)
        x = x_ref[...] if mask == 0 else xs[block]
        full = x.astype(F32)
        r1 = lax.rsqrt(jnp.mean(full * full, axis=1, keepdims=True) + EPSILON)
        product = dot((full * r1 * gain).astype(BF), merged[...])
        base_cos, base_sin, pick = sequences(
            meta, block * rows, rows, (start_cos, start_sin, adapters)
        )
        masked = lane_of((rows, LANES)) // ADAPTER_RANK == pick
        mask_ref[at, :] = jnp.where(masked, 1.0, 0.0).astype(BF)
        lows = [
            jnp.where(masked, product[:, (2 + s) * LANES : (3 + s) * LANES], 0.0).astype(BF)
            for s in range(3)
        ]
        lows = jnp.concatenate(lows, axis=1)
        low_ref[at, :] = lows
        product = product[:, : 2 * LANES] + dot(lows, second[...])
        row_cos, row_sin = cos_ref[at, :], sin_ref[at, :]
        cosine = row_cos * base_cos + row_sin * base_sin
        sine = (row_sin * base_cos - row_cos * base_sin) * sign
        turn_ref[at, :LANES] = cosine
        turn_ref[at, LANES:] = sine
        qkv_ref[at, :LANES] = turned(product[:, :LANES], cosine, sine).astype(BF)
        others = product[:, LANES:]
        qkv_ref[at, LANES:] = turned(
            others, jnp.where(keyed, cosine, 1.0), jnp.where(keyed, sine, 0.0)
        ).astype(BF)

    compute(0)
    for h in range(2):
        moving.take(h, 1)
    compute(1)
    early, late = moving.halves()
    for h, m in early:
        if m not in (moving.orders[h][0],):
            moving.take(h, m)
    whole = [m for m in range(2, shards, 2) if all((h, m) in early for h in range(2))]
    for m in whole:
        compute(m)
    for h, m in late:
        moving.take(h, m)
    for m in range(2, shards, 2):
        if m not in whole:
            compute(m)
    for m in range(3, shards, 2):
        for h in range(2):
            moving.take(h, m)
        compute(m)
    moving.finish()
    for mask in order:
        column_copy(mask).wait_send()
    for mask in range(1, groups):
        plane_copy(mask).wait_send()
        meta_copy(mask).wait_send()


def enter(deal, x, wq, wk, wv, small, meta, factors, wide, kv_second, identity):
    shards, groups = lax.axis_size("fsdp"), lax.axis_size("dp")
    rows, part = x.shape[0], wq.shape[0]
    total = rows * shards
    half = HEAD_WIDTH // 2
    frequency = ROPE_BASE ** (-np.arange(half, dtype=np.float64) / half)
    frequency = frequency.astype(np.float32)
    angles = np.arange(total, dtype=np.float64)[:, None] * frequency.astype(np.float64)[None, :]
    cosine = jnp.asarray(np.tile(np.cos(angles).astype(np.float32), (1, 4)))
    sine = jnp.asarray(np.tile(np.sin(angles).astype(np.float32), (1, 4)))
    frequency = jnp.asarray(np.tile(frequency, 4)[None, :])
    return pl.pallas_call(
        functools.partial(enter_kernel, shards, groups),
        out_shape=(
            jax.ShapeDtypeStruct((total, 2 * LANES), BF),
            jax.ShapeDtypeStruct((total, 3 * STACKED), BF),
            jax.ShapeDtypeStruct((total, STACKED), BF),
            jax.ShapeDtypeStruct((MODEL_WIDTH, LANES), BF),
            jax.ShapeDtypeStruct(meta.shape, jnp.int32),
            jax.ShapeDtypeStruct((MODEL_WIDTH, 2 * LANES), BF),
            jax.ShapeDtypeStruct((total, 2 * LANES), F32),
        ),
        in_specs=[pl.BlockSpec(memory_space=pltpu.SMEM)] + [IN_VMEM] * 12,
        out_specs=(IN_VMEM,) * 7,
        scratch_shapes=[
            pltpu.VMEM((shards, rows, MODEL_WIDTH), BF),
            pltpu.VMEM((shards, part, 3 * LANES), BF),
            pltpu.VMEM((groups, shards, part, 3 * LANES), BF),
            pltpu.VMEM((groups,) + meta.shape, jnp.int32),
            pltpu.VMEM((MODEL_WIDTH, 2 * LANES + 3 * STACKED), BF),
            pltpu.VMEM((3 * STACKED, 2 * LANES), BF),
        ]
        + pair_of_sems(shards)
        + [pltpu.SemaphoreType.DMA((shards,))] * 2
        + [pltpu.SemaphoreType.DMA((groups,))] * 4,
        compiler_params=remote(identity, 60),
        name="enter",
    )(deal, x, wq, wk, wv, small, meta, factors, wide, kv_second, cosine, sine, frequency)


def gain_row(small, lane):
    pick = jnp.where(lane_of((8, LANES)) == lane, 1.0, 0.0).astype(BF)
    return dot(pick, small, 1, 1)[0:1, :]


def turn_of(step, shards):
    late = (step + shards - 4) // shards
    if shards == 8:
        u = step - 4
        then = 5 + 2 * u - 3 * (u * (u - 1)) // 2 + (u * (u - 1) * (u - 2)) // 3
        return step + late * (then - step)
    return step + late * (shards + 3 - 2 * step)


def scatter_plan(moving, shards):
    place = {turn_of(t, shards): t for t in range(shards)}
    sent, plan = {}, []
    for t in range(shards):
        now = []
        for mask in range(1, shards):
            for h in range(2):
                sources = [mask ^ bit for bit in moving.orders[h][: moving.depth(h, mask)]]
                ready = all((h, s) in sent and sent[h, s] < t for s in sources)
                if (h, mask) not in sent and place[mask] <= t and ready:
                    now.append((h, mask))
        for item in now:
            sent[item] = t
        plan.append(now)
    rest = [(h, m) for m in range(1, shards) for h in range(2) if (h, m) not in sent]
    rest.sort(key=lambda item: moving.depth(*item))
    return plan, rest + [(0, 0), (1, 0)]


def out_plan(moving, shards):
    place = {turn_of(t, shards): t for t in range(shards)}
    sends = [[] for _ in range(shards + 1)]
    items = [[] for _ in range(shards + 1)]
    sent = {}
    for mask in range(1, shards, 2):
        for h in range(2):
            sent[h, mask] = place[mask] + 1
            sends[place[mask] + 1].append((h, mask))
    for t in range(1, shards + 1):
        for h in range(2):
            for mask in range(2, shards, 2):
                sources = [mask ^ bit for bit in moving.orders[h][: moving.depth(h, mask)]]
                ready = all(sent.get((h, s), 99) < t for s in sources) and place[mask] < t
                if ready and (h, mask) not in sent:
                    if not [item for item in items[t] if item[0] == h]:
                        items[t].append((h, mask))
                        sent[h, mask] = t + 1
                        if t < shards:
                            sends[t + 1].append((h, mask))
    last = [(h, m) for m in range(2, shards, 2) for h in range(2) if (h, m) not in sent]
    return sends, items, last


def experts_block(first_expert, n2, side, grad, mask, win, wout, wide_down, hid, down, spread, fold):
    rows = n2.shape[0]
    width = HIDDEN_UNITS
    lane = lane_of((rows, LANES))
    lows = dot(side, spread[:, : 2 * STACKED])
    low_gate = (lows[:, :STACKED] * mask).astype(BF)
    low_up = (lows[:, STACKED:] * mask).astype(BF)
    lift_gate = dot(low_gate, hid[0])
    lift_up = dot(low_up, hid[1])
    down_grad = (dot(grad, wide_down, 1, 1) * mask).astype(BF)
    from_down = dot(down_grad, down[...], 1, 1)
    side_full = side.astype(F32)
    total_inner = jnp.zeros((rows, width), F32)
    total_gate = jnp.zeros((rows, width), F32)
    total_up = jnp.zeros((rows, width), F32)
    extra = jnp.zeros((rows, LANES), F32)
    gated_parts, slope_parts = [], []
    for e in range(win.shape[1] // (2 * width)):
        name = first_expert + e
        at_high, at_low = lane == name, lane == name + EXPERT_COUNT
        gate = jnp.sum(jnp.where(at_high | at_low, side_full, 0.0), axis=1, keepdims=True)
        first = 2 * e * width
        pre_gate = dot(n2, win[:, first : first + width]) + lift_gate
        pre_up = dot(n2, win[:, first + width : first + 2 * width]) + lift_up
        pulled = dot(grad, wout[:, e * width : (e + 1) * width]) + from_down
        squashed = jax.nn.sigmoid(pre_gate)
        active = pre_gate * squashed
        inner = active * pre_up
        gate_grad = jnp.sum(inner * pulled, axis=1, keepdims=True)
        high = gate_grad.astype(BF).astype(F32)
        extra = extra + jnp.where(at_high, high, 0.0) + jnp.where(at_low, gate_grad - high, 0.0)
        gated = inner * gate
        pulled = pulled * gate
        grad_gate = pulled * pre_up * (squashed + active * (1.0 - squashed))
        grad_up = pulled * active
        gated_parts.append(gated.astype(BF))
        slope_parts += [grad_gate.astype(BF), grad_up.astype(BF)]
        total_inner = total_inner + gated
        total_gate = total_gate + grad_gate
        total_up = total_up + grad_up
    out = dot(jnp.concatenate(gated_parts, axis=1), wout[...], 1, 1)
    back = dot(jnp.concatenate(slope_parts, axis=1), win[...], 1, 1)
    total_inner = total_inner.astype(BF)
    total_gate = total_gate.astype(BF)
    total_up = total_up.astype(BF)
    shrunk = jnp.concatenate(
        [
            (dot(total_gate, hid[0], 1, 1) * mask).astype(BF),
            (dot(total_up, hid[1], 1, 1) * mask).astype(BF),
            (dot(total_inner, down[...]) * mask).astype(BF),
        ],
        axis=1,
    )
    extra = extra + dot(shrunk, fold[...])
    sums = (
        dot(total_inner, down_grad, 0, 0),
        dot(low_gate, total_gate, 0, 0),
        dot(low_up, total_up, 0, 0),
    )
    return out.astype(BF), back.astype(BF), extra.astype(BF), sums


def middle_kernel(
    shards,
    mine_ref,
    x_ref,
    small_ref,
    meta_ref,
    mask_ref,
    wo_ref,
    factors_ref,
    wide_ref,
    router2_ref,
    hid_ref,
    down_ref,
    spread_ref,
    fold_ref,
    cots_ref,
    win_ref,
    wout_ref,
    layer_ref,
    outs_ref,
    hgrad_ref,
    heads_ref,
    early_ref,
    oland_ref,
    *scratch,
):
    near = shards <= 8
    store, block_in, scratch = (scratch[0], None, scratch[1:]) if near else (scratch[0], scratch[1], scratch[2:])
    middle_body(
        shards,
        near,
        (
            mine_ref,
            x_ref,
                    small_ref,
            meta_ref,
            mask_ref,
            wo_ref,
            factors_ref,
            wide_ref,
            router2_ref,
            hid_ref,
            down_ref,
            spread_ref,
            fold_ref,
            cots_ref,
            win_ref,
            wout_ref,
        ),
        (
            layer_ref,
            outs_ref,
            hgrad_ref,
            heads_ref,
            early_ref,
            oland_ref,
        ),
        store,
        block_in,
        *scratch,
    )


def middle_body(
    shards,
    near,
    given,
    results,
    store,
    block_in,
    own_in,
    part,
    land,
    win,
    wout,
    cots,
    outs,
    attended,
    base_ref,
    factors,
    staged,
    gdown_ref,
    ghid_ref,
    gsend,
    grecv,
    ssend,
    srecv,
    wsem,
    csem,
    osem,
    bsem,
    osend,
    orecv,
    lsem,
    tsem,
):
    (
        mine_ref,
        x_ref,
            small_ref,
        meta_ref,
        mask_ref,
        wo_ref,
        factors_ref,
        wide_ref,
        router2_ref,
        hid_ref,
        down_ref,
        spread_ref,
        fold_ref,
        cots_ref,
        win_ref,
        wout_ref,
    ) = given
    (
        layer_ref,
        outs_ref,
        hgrad_ref,
        heads_ref,
        early_ref,
        oland_ref,
    ) = results
    me = lax.axis_index("fsdp")
    rows = x_ref.shape[0]
    if near:
        own_in = store.at[me]
    width = MODEL_WIDTH
    heads = HEADS // shards
    lane = lane_of((rows, LANES))
    loads = [
        pltpu.make_async_copy(win_ref, win, wsem.at[0]),
        pltpu.make_async_copy(wout_ref, wout, wsem.at[1]),
    ]
    fetch_factors = pltpu.make_async_copy(factors_ref.at[pl.ds(3, 4)], factors, wsem.at[2])
    fetch_factors.start()
    for load in loads:
        load.start()

    def cot_copy(step):
        return pltpu.make_async_copy(
            cots_ref.at[me ^ turn_of(step, shards)], cots.at[step % 2], csem.at[step % 2]
        )

    cot_copy(0).start()
    greet([("fsdp", me, bits_of(shards))])

    if near:
        attended = mine_ref
    else:
        for s in range(0, shards, 2):
            second = pltpu.roll(mine_ref[s + 1].astype(F32), HEAD_WIDTH, 1)
            both = jnp.where(lane < HEAD_WIDTH, mine_ref[s].astype(F32), second)
            attended[:, s // 2 * LANES : (s // 2 + 1) * LANES] = both.astype(BF)
    own = pl.ds(pl.multiple_of(me * rows, rows), rows)
    mask = mask_ref[own, :].astype(F32)
    small = small_ref[...]
    gain = gain_row(small, 17)
    fetch_factors.wait()
    out_low = (dot(attended[...], factors[3]) * mask).astype(BF)
    hidden = (
        x_ref[...].astype(F32) + dot(attended[...], wo_ref[...], 1, 1) + dot(out_low, wide_ref[1])
    )
    base_ref[...] = hidden
    r2 = lax.rsqrt(jnp.mean(hidden * hidden, axis=1, keepdims=True) + EPSILON)
    n2 = (hidden * r2 * gain).astype(BF)
    own_in[:, :width] = n2
    lows = [(dot(n2, factors[s]) * mask).astype(BF) for s in range(3)]
    logits = dot(n2, small) + dot(lows[0], router2_ref[...])
    named = jnp.zeros((LANES, rows), jnp.bool_)
    for k in range(TOPK):
        named = named | (row_of((LANES, rows)) == meta_ref[k : k + 1, :])
    eye = jnp.where(row_of((LANES, LANES)) == lane_of((LANES, LANES)), 1.0, 0.0).astype(BF)
    picked = dot(jnp.where(named, 1.0, 0.0).astype(BF), eye, 0, 0) > 0.5
    peak = jnp.max(jnp.where(picked, logits, MASKED), axis=1, keepdims=True)
    lifted = jnp.where(picked, jnp.exp(jnp.where(picked, logits, peak) - peak), 0.0)
    gates = lifted / jnp.sum(lifted, axis=1, keepdims=True)
    high = gates.astype(BF).astype(F32)
    shrunk = dot(jnp.concatenate(lows[1:], axis=1), fold_ref[: 2 * STACKED, :])
    side = high + pltpu.roll(gates - high, EXPERT_COUNT, 1) + shrunk
    own_in[:, width:] = side.astype(BF)

    going = Gather("fsdp", shards, own_in, store, (gsend, grecv))
    coming = Scatter("fsdp", shards, part, land, (ssend, srecv))
    going.start()
    for load in loads:
        load.wait()

    early, late = going.halves()
    plan, rest = scatter_plan(coming, shards)
    first_expert = me * (EXPERT_COUNT // shards)

    def out_copy(at):
        return pltpu.make_async_copy(outs, outs_ref.at[me ^ turn_of(at, shards)], osem.at[0])

    if near:
        leaving = Scatter("fsdp", shards, outs_ref, oland_ref, (osend, orecv))
        half_rows = rows // 2
        out_sends, out_items, out_last = out_plan(leaving, shards)

        def out_half(h, k_mask):
            return outs_ref.at[me ^ k_mask, pl.ds(h * half_rows, half_rows)]

        def sources_of(h, k_mask):
            return [k_mask ^ bit for bit in leaving.orders[h][: leaving.depth(h, k_mask)]]

        def item_loads(h, k_mask):
            refs = [out_half(h, k_mask)] + [oland_ref.at[h, s - 1] for s in sources_of(h, k_mask)]
            return [
                pltpu.make_async_copy(ref, staged.at[h, n], lsem.at[h, n])
                for n, ref in enumerate(refs)
            ]

        def load_item(h, k_mask):
            for s in sources_of(h, k_mask):
                leaving.copy(h, s).wait_recv()
            for load in item_loads(h, k_mask):
                load.start()

        def item_sum(h, k_mask):
            loads = item_loads(h, k_mask)
            for load in loads:
                load.wait()
            total = staged[h, 0].astype(F32)
            for n in range(1, len(loads)):
                total = total + staged[h, n].astype(F32)
            return total

        def item_store(h, k_mask):
            return pltpu.make_async_copy(staged.at[h, 0], out_half(h, k_mask), tsem.at[h])

        def add_item(h, k_mask):
            staged[h, 0] = item_sum(h, k_mask).astype(BF)
            item_store(h, k_mask).start()

        def send_item(h, k_mask):
            if leaving.depth(h, k_mask):
                item_store(h, k_mask).wait()
            leaving.copy(h, k_mask).start()


    def step(t, carry):
        turn = turn_of(t, shards)
        block = me ^ turn
        slot = t % 2

        @pl.when(t == 2)
        def _():
            for h, m in early:
                going.take(h, m)

        @pl.when(t == 4)
        def _():
            for h, m in late:
                going.take(h, m)

        for k in range(1, shards):
            m = turn_of(k, shards)
            if m % 2:

                @pl.when(t == k)
                def _(m=m):
                    for h in range(2):
                        going.take(h, m)

        @pl.when(t + 1 < shards)
        def _():
            cot_copy(t + 1).start()

        cot_copy(t).wait()

        @pl.when(t >= 1)
        def _():
            out_copy(t - 1).wait()

        if near:
            for k in range(1, shards):
                for h, k_mask in out_sends[k]:

                    @pl.when(t == k)
                    def _(h=h, k_mask=k_mask):
                        send_item(h, k_mask)

                for h, k_mask in out_items[k]:

                    @pl.when(t == k)
                    def _(h=h, k_mask=k_mask):
                        load_item(h, k_mask)

        block_rows = pl.ds(pl.multiple_of(block * rows, rows), rows)
        if near:
            here = store.at[block]
        else:
            here = block_in

            @pl.when(t == 0)
            def _():
                block_in[...] = own_in[...]

            @pl.when(t != 0)
            def _():
                fetch = pltpu.make_async_copy(store.at[block], block_in, bsem)
                fetch.start()
                fetch.wait()

        out, back, extra, sums = experts_block(
            first_expert,
            here[:, :width],
            here[:, width:],
            cots[slot],
            mask_ref[block_rows, :].astype(F32),
            win,
            wout,
            wide_ref[2],
            hid_ref,
            down_ref,
            spread_ref,
            fold_ref,
        )
        outs[...] = out
        out_copy(t).start()
        part[block, :, :width] = back
        part[block, :, width:] = extra

        @pl.when(t == 0)
        def _():
            gdown_ref[...] = sums[0]
            ghid_ref[0] = sums[1]
            ghid_ref[1] = sums[2]

        @pl.when(t != 0)
        def _():
            gdown_ref[...] += sums[0]
            ghid_ref[0] += sums[1]
            ghid_ref[1] += sums[2]

        for k in range(shards):
            if plan[k]:

                @pl.when(t == k)
                def _(k=k):
                    for h, m in plan[k]:
                        coming.reduce(h, m)

        if near:
            for k in range(1, shards):
                for h, k_mask in out_items[k]:

                    @pl.when(t == k)
                    def _(h=h, k_mask=k_mask):
                        add_item(h, k_mask)

        return carry

    lax.fori_loop(0, shards, step, 0)
    out_copy(shards - 1).wait()
    cot_load = pltpu.make_async_copy(cots_ref.at[me], cots.at[0], csem.at[0])
    cot_load.start()
    tail = [rest[:-2], rest[-2:]]
    if near:
        for h, k_mask in out_sends[shards]:
            send_item(h, k_mask)
        for h, k_mask in out_items[shards]:
            load_item(h, k_mask)
    for h, m in tail[0]:
        coming.reduce(h, m)
    if near:
        for h, k_mask in out_items[shards]:
            add_item(h, k_mask)
            send_item(h, k_mask)
    for h, m in tail[1]:
        coming.reduce(h, m)
    cot_load.wait()

    hidden = base_ref[...]
    mask = mask_ref[own, :].astype(F32)
    r2 = lax.rsqrt(jnp.mean(hidden * hidden, axis=1, keepdims=True) + EPSILON)
    n2 = own_in[:, :width]
    cot = cots[0]
    grad = cot.astype(F32)
    extra = part[me, :, width:]
    extra_full = extra.astype(F32)
    gate_grad = extra_full + pltpu.roll(extra_full, LANES - EXPERT_COUNT, 1)
    logit_grad = gates * (gate_grad - jnp.sum(gates * gate_grad, axis=1, keepdims=True))
    logit_grad = jnp.where(lane < EXPERT_COUNT, logit_grad, 0.0).astype(BF)
    wider = dot(extra, spread_ref[...])
    second_grad = [
        (dot(logit_grad, router2_ref[...], 1, 1) * mask).astype(BF),
        (wider[:, :STACKED] * mask).astype(BF),
        (wider[:, STACKED : 2 * STACKED] * mask).astype(BF),
    ]
    down_low = (wider[:, 2 * STACKED :] * mask).astype(BF)
    base_ref[...] = hidden + dot(down_low, wide_ref[2])
    if near:
        for h, k_mask in out_last:
            load_item(h, k_mask)
    n2_grad = part[me, :, :width].astype(F32) + dot(logit_grad, small, 1, 1)
    for s in range(3):
        n2_grad = n2_grad + dot(second_grad[s], factors[s], 1, 1)
    w2 = gain * n2_grad
    hidden_grad = grad + r2 * w2 - hidden * (r2 * r2 * r2) * jnp.mean(w2 * hidden, axis=1, keepdims=True)
    hgrad_ref[...] = hidden_grad
    out_grad = hidden_grad.astype(BF)
    out_low_grad = (dot(out_grad, wide_ref[1], 1, 1) * mask).astype(BF)
    if near:
        for h, k_mask in out_last:
            add_item(h, k_mask)
            send_item(h, k_mask)
    attended_grad = dot(out_grad, wo_ref[...]) + dot(out_low_grad, factors[3], 1, 1)
    for s in range(shards):
        if heads == 2:
            heads_ref[s] = attended_grad[:, s * LANES : (s + 1) * LANES].astype(BF)
        else:
            pair = attended_grad[:, s // 2 * LANES : (s // 2 + 1) * LANES]
            if s % 2:
                pair = pltpu.roll(pair, HEAD_WIDTH, 1)
            heads_ref[s] = jnp.where(lane < HEAD_WIDTH, pair, 0.0).astype(BF)
    gsecond = dot(n2, jnp.concatenate(second_grad, axis=1), 0, 0).astype(BF)
    packed = [gsecond[:, s * LANES : (s + 1) * LANES] for s in range(3)]
    packed.append(dot(attended[...], out_low_grad, 0, 0).astype(BF))
    packed.append(gdown_ref[...].astype(BF))
    for s in range(2):
        packed += [ghid_ref[s, :, j : j + LANES].astype(BF) for j in range(0, HIDDEN_UNITS, LANES)]
    for one, two in ((out_low, out_grad), (down_low, cot)):
        product = dot(one, two, 0, 0).astype(BF)
        packed += [product[:, j : j + LANES] for j in range(0, MODEL_WIDTH, LANES)]
    packed.append(dot(lows[0], logit_grad, 0, 0).astype(BF))
    pack(early_ref, packed, early_ref.shape[1])
    if near:
        for h in range(2):
            load_item(h, 0)
            half = pl.ds(h * half_rows, half_rows)
            layer_ref[half, :] = (base_ref[half, :] + item_sum(h, 0)).astype(BF)
        leaving.finish()
    else:
        layer_ref[...] = base_ref[...]
    going.finish()
    coming.finish()


def middle(mine, x, small, meta, mask, wo, factors, wide, router2, hid, down, cots, win, wout, identity):
    shards = lax.axis_size("fsdp")
    rows = x.shape[0]
    side = MODEL_WIDTH + LANES
    source = np.arange(LANES)
    place = np.arange(STACKED) % ADAPTER_RANK
    spread = np.concatenate([source[:, None] == o + place[None, :] for o in (32, 48, 64)], axis=1)
    fold = np.concatenate([source[None, :] == o + place[:, None] for o in (32, 48, 64)], axis=0)
    spread, fold = jnp.asarray(spread, BF), jnp.asarray(fold, BF)
    gathered = (shards, rows, side)
    near = shards <= 8
    results = pl.pallas_call(
        functools.partial(middle_kernel, shards),
        out_shape=(
            jax.ShapeDtypeStruct((rows, MODEL_WIDTH), BF if near else F32),
            jax.ShapeDtypeStruct((shards, rows, MODEL_WIDTH), BF),
            jax.ShapeDtypeStruct((rows, MODEL_WIDTH), F32),
            jax.ShapeDtypeStruct((shards, rows, LANES), BF),
            jax.ShapeDtypeStruct((shards, total_length(EARLY) // shards, LANES), BF),
            jax.ShapeDtypeStruct((2, shards - 1, rows // 2, MODEL_WIDTH) if near else (2, 1, 16, LANES), BF),
        )
        + (() if near else (jax.ShapeDtypeStruct(gathered, BF),)),
        in_specs=[IN_VMEM] * 6 + [ANYWHERE] + [IN_VMEM] * 6 + [ANYWHERE] * 3,
        out_specs=(IN_VMEM, ANYWHERE) + (IN_VMEM,) * 3 + (ANYWHERE,) + (() if near else (ANYWHERE,)),
        scratch_shapes=[
            pltpu.VMEM(gathered if near else gathered[1:], BF),
            pltpu.VMEM((16, LANES) if near else gathered[1:], BF),
            pltpu.VMEM((shards, rows, side), BF),
            pltpu.VMEM((2, shards - 1, rows // 2, side), BF),
            pltpu.VMEM(win.shape, BF),
            pltpu.VMEM(wout.shape, BF),
            pltpu.VMEM((2, rows, MODEL_WIDTH), BF),
            pltpu.VMEM((rows, MODEL_WIDTH), BF),
            pltpu.VMEM((16, LANES) if near else (rows, MODEL_WIDTH), BF),
            pltpu.VMEM((rows, MODEL_WIDTH), F32),
            pltpu.VMEM((4, MODEL_WIDTH, STACKED), BF),
            pltpu.VMEM((2, 4, rows // 2, MODEL_WIDTH) if near else (2, 1, 16, LANES), BF),
            pltpu.VMEM((HIDDEN_UNITS, STACKED), F32),
            pltpu.VMEM((2, STACKED, HIDDEN_UNITS), F32),
        ]
        + pair_of_sems(shards) * 2
        + [pltpu.SemaphoreType.DMA((3,))] * 3
        + [pltpu.SemaphoreType.DMA(())]
        + pair_of_sems(shards)
        + [pltpu.SemaphoreType.DMA((2, 4)), pltpu.SemaphoreType.DMA((2,))],
        compiler_params=remote(identity, 62),
        name="middle",
    )(mine, x, small, meta, mask, wo, factors, wide, router2, hid, down, spread, fold, cots, win, wout)
    return results[:5]


class Total:
    def __init__(self, shards, groups, out, part, land, zpart, zland, zall, sems):
        self.me, self.plane = lax.axis_index("fsdp"), lax.axis_index("dp")
        self.groups, self.out, self.part, self.zpart, self.zall = groups, out, part, zpart, zall
        self.down = Scatter("fsdp", shards, part, land, sems[0:2])
        self.across = Scatter("dp", groups, zpart, zland, sems[2:4])
        self.back = Gather("dp", groups, zall.at[self.plane], zall, sems[4:6])
        self.up = Gather("fsdp", shards, out.at[self.me], out, sems[6:8])
        self.steps = [lambda k=k: self.level(self.down, k) for k in range(len(bits_of(shards)))]
        self.steps.append(self.turn)
        self.steps += [lambda k=k: self.level(self.across, k) for k in range(1, len(bits_of(groups)))]
        self.steps.append(self.turn_back)
        for k in range(len(bits_of(groups)) - 1):
            self.steps.append(lambda k=k: self.back.stage(k))
        self.steps.append(self.rise)
        for k in range(len(bits_of(shards))):
            self.steps.append(lambda k=k: self.up.stage(k))
        self.steps.append(self.finish)

    def level(self, moving, k):
        for mask in range(moving.count):
            for h in range(2):
                if moving.depth(h, mask) == k:
                    moving.reduce(h, mask)

    def turn(self):
        self.level(self.down, len(self.down.orders[0]))
        piece = self.zpart.shape[1]
        for g in range(self.groups):
            self.zpart[g] = self.part[self.me, pl.ds(g * piece, piece)]
        self.level(self.across, 0)

    def turn_back(self):
        self.level(self.across, len(self.across.orders[0]))
        self.zall[self.plane] = self.zpart[self.plane]
        self.back.start()

    def rise(self):
        self.back.stage(len(bits_of(self.groups)) - 1)
        piece = self.zpart.shape[1]
        for g in range(self.groups):
            self.out[self.me, pl.ds(g * piece, piece)] = self.zall[g]
        self.up.start()

    def finish(self):
        self.down.finish()
        self.across.finish()
        self.back.finish()
        self.up.finish()

    def next(self, count=1):
        for _ in range(count):
            if self.steps:
                self.steps.pop(0)()


def total_scratch(shards, groups, length):
    share = length // shards
    piece = share // groups
    return [
        pltpu.VMEM((shards, share, LANES), BF),
        pltpu.VMEM((shards, share, LANES), BF),
        pltpu.VMEM((2, shards - 1, share // 2, LANES), BF),
        pltpu.VMEM((groups, piece, LANES), BF),
        pltpu.VMEM((2, groups - 1, piece // 2, LANES), BF),
        pltpu.VMEM((groups, piece, LANES), BF),
    ] + pair_of_sems(shards) + pair_of_sems(groups) * 2 + pair_of_sems(shards)


def total_length(length):
    unit = lax.axis_size("fsdp") * lax.axis_size("dp") * 2 * 16
    return -(-length // unit) * unit


EARLY = 5 * MODEL_WIDTH + HIDDEN_UNITS + 2 * MODEL_WIDTH + STACKED
LATE = 5 * MODEL_WIDTH


def leave_kernel(
    shards,
    groups,
    heads_ref,
    q_ref,
    k_ref,
    v_ref,
    att_ref,
    columns_ref,
    x_ref,
    small_ref,
    factors_ref,
    wide_ref,
    kv_ref,
    hgrad_ref,
    low_ref,
    turn_ref,
    mask_ref,
    xgrad_ref,
    late_out,
    columns,
    grads,
    dk_ref,
    dv_ref,
    dq_ref,
    mixes,
    landed,
    near_columns,
    low,
    turn,
    own_mask_ref,
    asend,
    arecv,
    msend,
    mrecv,
    gsend,
    grecv,
    isem,
    *sums,
):
    me, plane = lax.axis_index("fsdp"), lax.axis_index("dp")
    rows = x_ref.shape[0]
    heads = HEADS // shards
    share = max(1, shards // KEY_VALUE_HEADS)
    side = PART
    cols = heads * side
    nparts = rows // side
    late_part = sums[0]
    near = shards <= 8
    columns = near_columns if near else columns
    own_rows = pl.ds(pl.multiple_of(me * rows, rows), rows)
    takes = [
        pltpu.make_async_copy(mask_ref.at[own_rows], own_mask_ref, isem.at[1]),
        pltpu.make_async_copy(low_ref.at[own_rows], low, isem.at[2]),
    ]
    for take in takes:
        take.start()
    greet([("fsdp", me, range(1, shards)), ("dp", plane, bits_of(groups))])

    def head_copy(mask):
        return pltpu.make_async_remote_copy(
            src_ref=heads_ref.at[me ^ mask],
            dst_ref=grads.at[me],
            send_sem=asend.at[mask],
            recv_sem=arecv.at[me],
            device_id={"fsdp": me ^ mask},
            device_id_type=MESH,
        )

    def home_copy(target):
        return pltpu.make_async_remote_copy(
            src_ref=mixes.at[target],
            dst_ref=landed.at[me],
            send_sem=msend.at[target],
            recv_sem=mrecv.at[me],
            device_id={"fsdp": target},
            device_id_type=MESH,
        )

    for m in range(shards - 1, 0, -1):
        head_copy(m).start()
    grads[me] = heads_ref[me]
    dk_ref[...] = jnp.zeros(dk_ref.shape, F32)
    dv_ref[...] = jnp.zeros(dv_ref.shape, F32)

    going = Gather("fsdp", shards, columns_ref, columns, (gsend, grecv))
    late = Total(shards, groups, late_out, *sums[:5], sums[5:])

    low_lane = lane_of((side, LANES)) < HEAD_WIDTH
    lane = lane_of((side, LANES))
    keyed = lane_of((rows, LANES)) < HEAD_WIDTH
    first_takes, late_takes = going.halves()

    for c in reversed(range(shards)):
        take_turn = pltpu.make_async_copy(turn_ref.at[pl.ds(c * rows, rows)], turn, isem.at[0])
        take_turn.start()

        @pl.when(me != c)
        def _(c=c):
            pltpu.make_async_remote_copy(
                src_ref=heads_ref.at[c],
                dst_ref=grads.at[c],
                send_sem=asend.at[0],
                recv_sem=arecv.at[c],
                device_id={"fsdp": c},
                device_id_type=MESH,
            ).wait_recv()

        if c == shards - 1:
            going.start()
        if c == shards - 4:
            for h, m in first_takes:
                going.take(h, m)
        if c == shards - 6:
            for h, m in late_takes:
                going.take(h, m)
        keys = (c + 1) * rows

        def step(u, carry, c=c, keys=keys):
            at = pl.ds(pl.multiple_of(u * side, side), side)
            grad = grads[c, at, :].astype(F32)
            both = grad * att_ref[pl.ds(pl.multiple_of(c * rows + u * side, side), side), :].astype(F32)
            stack = []
            for h in range(heads):
                mine = low_lane if h == 0 else ~low_lane
                delta = jnp.sum(jnp.where(mine, both, 0.0), axis=1, keepdims=True)
                hi, mid, lo = splits(-delta)
                extra = jnp.where(lane == 0, hi, jnp.where(lane == 1, mid, jnp.where(lane == 2, lo, 0.0)))
                stack.append(
                    jnp.concatenate([jnp.where(mine, grad, 0.0).astype(BF), extra.astype(BF)], axis=1)
                )
            do = jnp.concatenate(stack, axis=0) if heads > 1 else stack[0]
            queries = q_ref[c * nparts + u]
            weights = jnp.exp(dot(k_ref[0:keys, :], queries, 1, 1))
            seen = row_of((rows, cols)) <= lane_of((rows, cols)) % side + u * side
            final = jnp.where(seen, weights[keys - rows :], 0.0)
            weights = jnp.concatenate([weights[: keys - rows], final], axis=0) if c else final
            slope = (weights * dot(v_ref[0:keys, :], do, 1, 1)).astype(BF)
            dv_ref[0:keys, :] += dot(weights.astype(BF), do[:, :LANES])
            dk_ref[0:keys, :] += dot(slope, queries[:, :LANES])
            dq = dot(slope, k_ref[0:keys, :LANES], 0, 0)
            dq = dq if heads == 1 else jnp.where(low_lane, dq[:side], dq[side:])
            dq_ref[at, :] = dq * (HEAD_WIDTH ** -0.5)
            return carry

        lax.fori_loop(0, nparts, step, 0)

        block = pl.ds(c * rows, rows)
        dk, dv = dk_ref[block, :], dv_ref[block, :]
        other = jnp.where(
            keyed, dk + pltpu.roll(dk, HEAD_WIDTH, 1), dv + pltpu.roll(dv, HEAD_WIDTH, 1)
        )
        take_turn.wait()
        cosine, sine = turn[:, :LANES], turn[:, LANES:]
        mixes[c, :, :LANES] = turned(dq_ref[...], cosine, -sine).astype(BF)
        mixes[c, :, LANES:] = turned(
            other, jnp.where(keyed, cosine, 1.0), jnp.where(keyed, -sine, 0.0)
        ).astype(BF)

        @pl.when(me != c)
        def _(c=c):
            home_copy(c).start()

    if shards < 8:
        for h, m in first_takes + late_takes:
            going.take(h, m)
    for h in range(2):
        for m in span(going.orders[h][:-1]):
            going.incoming(h, m ^ going.orders[h][-1]).wait_recv()

    landed[me] = mixes[me]
    if near:
        columns[me] = columns_ref[...]
    else:
        keep = pltpu.make_async_copy(columns_ref, columns.at[me], isem.at[3])
        keep.start()
        keep.wait()
    for take in takes:
        take.wait()
    own_mask = own_mask_ref[...].astype(F32)
    x = x_ref[...].astype(F32)
    r1 = lax.rsqrt(jnp.mean(x * x, axis=1, keepdims=True) + EPSILON)
    gain = gain_row(small_ref[...], 16)
    normed = (x * r1 * gain).astype(BF)
    for m in range(1, shards):
        pltpu.make_async_remote_copy(
            src_ref=mixes.at[0],
            dst_ref=landed.at[me ^ m],
            send_sem=msend.at[0],
            recv_sem=mrecv.at[me ^ m],
            device_id={"fsdp": me ^ m},
            device_id_type=MESH,
        ).wait_recv()
    query_grad, normed_grad = [], jnp.zeros((rows, MODEL_WIDTH), F32)
    for s in range(shards):
        if near:
            weight = columns[s]
        else:
            fetch = pltpu.make_async_copy(columns.at[s], near_columns, isem.at[3])
            fetch.start()
            fetch.wait()
            weight = near_columns[...]
        normed_grad = normed_grad + dot(landed[s], weight, 1, 1)
        query = landed[s, :, :LANES]
        if heads == 2:
            query_grad.append(query)
        elif s % 2 == 0:
            then = pltpu.roll(landed[s + 1, :, :LANES].astype(F32), HEAD_WIDTH, 1)
            query_grad.append(jnp.where(keyed, query.astype(F32), then).astype(BF))

    def pair_of(head):
        pair = jnp.zeros((rows, LANES), F32)
        for s in range(head * share, (head + 1) * share):
            pair = pair + landed[s, :, LANES:].astype(F32)
        return pair

    keys_grad, values_grad = [], []
    for head in range(0, KEY_VALUE_HEADS, 2):
        one, two = pair_of(head), pair_of(head + 1)
        keys_grad.append(jnp.where(keyed, one, pltpu.roll(two, HEAD_WIDTH, 1)).astype(BF))
        values_grad.append(jnp.where(keyed, pltpu.roll(one, HEAD_WIDTH, 1), two).astype(BF))
    whole = [jnp.concatenate(part, axis=1) for part in (query_grad, keys_grad, values_grad)]
    seconds = (wide_ref[0], kv_ref[0], kv_ref[1])
    firsts = []
    for s in range(3):
        firsts.append((dot(whole[s], seconds[s], 1, 1) * own_mask).astype(BF))
        normed_grad = normed_grad + dot(firsts[s], factors_ref[s], 1, 1)

    packed, share_rows = [], late_part.shape[1]
    gfirst = dot(normed, jnp.concatenate(firsts, axis=1), 0, 0).astype(BF)
    packed += [gfirst[:, s * LANES : (s + 1) * LANES] for s in range(3)]
    for s in range(3):
        second = dot(low[:, s * LANES : (s + 1) * LANES], whole[s], 0, 0).astype(BF)
        packed += [second[:, j : j + LANES] for j in range(0, second.shape[1], LANES)]
    pack(late_part, packed, share_rows)
    late.next()
    w1 = gain * normed_grad
    xgrad_ref[...] = (
        hgrad_ref[...] + r1 * w1 - x * (r1 * r1 * r1) * jnp.mean(w1 * x, axis=1, keepdims=True)
    )
    late.next(2)
    late.next(99)

    for m in range(1, shards):
        head_copy(m).wait_send()
    for c in range(shards):

        @pl.when(me != c)
        def _(c=c):
            home_copy(c).wait_send()

    going.finish()


def pieces_of(first, size, share):
    parts, done = [], 0
    while done < size:
        block, row = divmod(first + done, share)
        length = min(size - done, share - row)
        parts.append((block, row, done, length))
        done += length
    return parts


def pack(target, arrays, share):
    first = 0
    for array in arrays:
        for block, row, done, length in pieces_of(first, array.shape[0], share):
            target[block, row : row + length, :] = array[done : done + length]
        first += array.shape[0]
    total = target.shape[0] * share
    for block, row, _, length in pieces_of(first, total - first, share):
        target[block, row : row + length, :] = jnp.zeros((length, LANES), BF)


def unpack(source, first, size):
    parts = pieces_of(first, size, source.shape[1])
    parts = [source[block, row : row + length, :] for block, row, _, length in parts]
    return parts[0] if len(parts) == 1 else jnp.concatenate(parts, axis=0)


def unpack_kernel(late_out, early_out, gfactor_ref, gdown_ref, gwide_ref, gkv_ref, gff_ref, groute_ref):
    def read(source, first, size):
        return unpack(source, first, size).astype(F32)

    for s in range(3):
        gfactor_ref[s] = read(late_out, s * MODEL_WIDTH, MODEL_WIDTH)
        gfactor_ref[3 + s] = read(early_out, s * MODEL_WIDTH, MODEL_WIDTH)
    gfactor_ref[6] = read(early_out, 3 * MODEL_WIDTH, MODEL_WIDTH)
    edge = 4 * MODEL_WIDTH
    gdown_ref[...] = read(early_out, edge, HIDDEN_UNITS)
    edge += HIDDEN_UNITS
    for s in range(2):
        for j in range(4):
            gff_ref[s, :, j * LANES : (j + 1) * LANES] = read(early_out, edge, STACKED)
            edge += STACKED
    for s in range(2):
        for j in range(8):
            gwide_ref[1 + s, :, j * LANES : (j + 1) * LANES] = read(early_out, edge, STACKED)
            edge += STACKED
    groute_ref[...] = read(early_out, edge, STACKED)
    edge = 3 * MODEL_WIDTH
    for j in range(8):
        gwide_ref[0, :, j * LANES : (j + 1) * LANES] = read(late_out, edge, STACKED)
        edge += STACKED
    for s in range(2):
        for j in range(4):
            gkv_ref[s, :, j * LANES : (j + 1) * LANES] = read(late_out, edge, STACKED)
            edge += STACKED

def unpack_all(late, early):
    return pl.pallas_call(
        unpack_kernel,
        out_shape=(
            jax.ShapeDtypeStruct((7, MODEL_WIDTH, STACKED), F32),
            jax.ShapeDtypeStruct((HIDDEN_UNITS, STACKED), F32),
            jax.ShapeDtypeStruct((3, STACKED, MODEL_WIDTH), F32),
            jax.ShapeDtypeStruct((2, STACKED, HIDDEN_UNITS), F32),
            jax.ShapeDtypeStruct((2, STACKED, HIDDEN_UNITS), F32),
            jax.ShapeDtypeStruct((STACKED, LANES), F32),
        ),
        in_specs=[IN_VMEM] * 2,
        out_specs=(IN_VMEM,) * 6,
        compiler_params=pltpu.CompilerParams(vmem_limit_bytes=40 << 20),
        name="unpack_all",
    )(late, early)


def leave(to_heads, q, k, v, att, columns, x, small, factors, wide, kv_second, hgrad, low, turn, mask, identity):
    shards, groups = lax.axis_size("fsdp"), lax.axis_size("dp")
    rows = x.shape[0]
    near = shards <= 8
    total = shards * rows
    return pl.pallas_call(
        functools.partial(leave_kernel, shards, groups),
        out_shape=(
            jax.ShapeDtypeStruct((rows, MODEL_WIDTH), F32),
            jax.ShapeDtypeStruct((shards, total_length(LATE) // shards, LANES), BF),
            jax.ShapeDtypeStruct((16, LANES) if near else (shards, MODEL_WIDTH, 2 * LANES), BF),
        ),
        in_specs=[IN_VMEM] * 12 + [ANYWHERE] * 3,
        out_specs=(IN_VMEM, IN_VMEM, ANYWHERE),
        scratch_shapes=[
            pltpu.VMEM((shards, rows, LANES), BF),
            pltpu.VMEM((total, LANES), F32),
            pltpu.VMEM((total, LANES), F32),
            pltpu.VMEM((rows, LANES), F32),
            pltpu.VMEM((shards, rows, 2 * LANES), BF),
            pltpu.VMEM((shards, rows, 2 * LANES), BF),
            pltpu.VMEM((shards, MODEL_WIDTH, 2 * LANES) if near else (MODEL_WIDTH, 2 * LANES), BF),
            pltpu.VMEM((rows, 3 * STACKED), BF),
            pltpu.VMEM((rows, 2 * LANES), F32),
            pltpu.VMEM((rows, STACKED), BF),
        ]
        + [pltpu.SemaphoreType.DMA((shards,))] * 4
        + pair_of_sems(shards)
        + [pltpu.SemaphoreType.DMA((4,))]
        + total_scratch(shards, groups, total_length(LATE))[1:],
        compiler_params=remote(identity, 62),
        name="leave",
    )(to_heads, q, k, v, att, columns, x, small, factors, wide, kv_second, hgrad, low, turn, mask)


def local(
    tokens,
    cotangent,
    lengths,
    adapter_index,
    routes,
    deal,
    norm_gain_pair,
    query_weight,
    key_weight,
    value_weight,
    output_weight_transposed,
    router_weight,
    expert_input_weight,
    expert_output_weight,
    factors,
    down_first,
    wide,
    kv_second,
    hidden_second,
    router_second,
):
    shards = lax.axis_size("fsdp")
    groups = lax.axis_size("dp")
    rows = tokens.shape[0]
    total = rows * shards
    heads = HEADS // shards
    share = max(1, shards // KEY_VALUE_HEADS)
    me = lax.axis_index("fsdp")

    padded = ((0, 0), (0, rows - lengths.shape[1]))
    meta = jnp.concatenate(
        [
            routes.T,
            jnp.pad(lengths, padded),
            jnp.pad(adapter_index, padded),
            jnp.zeros((6, rows), jnp.int32),
        ],
        axis=0,
    )
    small = jnp.concatenate(
        [
            router_weight,
            norm_gain_pair,
            jnp.zeros((router_weight.shape[0], LANES - EXPERT_COUNT - 2), BF),
        ],
        axis=1,
    )
    qkv, low_all, group_mask, small, meta, columns, turn = enter(
        deal,
        tokens,
        query_weight,
        key_weight,
        value_weight,
        small,
        meta,
        factors,
        wide,
        kv_second,
        1,
    )
    win = expert_input_weight.reshape(MODEL_WIDTH, -1)
    wout = expert_output_weight.reshape(MODEL_WIDTH, -1)
    out_weight = lax.all_gather(output_weight_transposed, ("dp", "fsdp"), axis=0, tiled=True)
    mine, attended, q_kept, k_kept, v_kept, all_grad = attend(meta, qkv, cotangent, heads, 5)
    router2 = jnp.pad(router_second, ((0, 0), (0, LANES - EXPERT_COUNT)))
    (
        layer_out,
        out_part,
        hidden_grad,
        to_heads,
        early,
    ) = middle(
        mine,
        tokens,
        small,
        meta,
        group_mask,
        out_weight,
        factors,
        wide,
        router2,
        hidden_second,
        down_first,
        all_grad,
        win,
        wout,
        6,
    )
    if shards > 8:
        layer_out = (layer_out + scatter(out_part, "fsdp", 8).astype(F32)).astype(BF)
    early_sum = lax.psum(early, ("dp", "fsdp"))
    input_grad, late, _ = leave(
        to_heads,
        q_kept,
        k_kept,
        v_kept,
        attended,
        columns,
        tokens,
        small,
        factors,
        wide,
        kv_second,
        hidden_grad,
        low_all,
        turn,
        group_mask,
        7,
    )
    g_factors, g_down, g_wide, g_kv, g_ff, g_route = unpack_all(late, early_sum)
    return (
        layer_out,
        input_grad,
        g_factors,
        g_down,
        g_wide,
        g_kv,
        g_ff,
        g_route[:, :EXPERT_COUNT],
    )


def solution(mesh):
    rows = P(("dp", "fsdp"), None)
    placed = (
        (rows, rows, P("dp", None), P("dp", None), rows, P())
        + (rows,) * 6
        + (P(None, "fsdp", None),) * 2
        + (P(),) * 6
    )
    return jax.shard_map(
        local,
        mesh=mesh,
        in_specs=placed,
        out_specs=(rows, rows) + (P(),) * 6,
        check_vma=False,
    )
```

```python
import functools
import math

import jax
import jax.numpy as jnp
import numpy as np
from jax import lax
from jax.experimental import pallas as pl
from jax.experimental.pallas import tpu as pltpu
from jax.sharding import PartitionSpec as P

MODEL_WIDTH = 1024
HEADS = 16
KEY_VALUE_HEADS = 8
HEAD_WIDTH = 64
HIDDEN_UNITS = 512
TOPK = 8
EXPERT_COUNT = 16
ADAPTER_COUNT = 8
ADAPTER_RANK = 16
STACKED = ADAPTER_COUNT * ADAPTER_RANK

EPSILON = 1e-06
ROPE_BASE = 10000.0
MASKED = -1e30
LANES = 128
PART = 128
NSEQ = 4

BF = jnp.bfloat16
F32 = jnp.float32
MESH = pl.DeviceIdType.MESH


def dot(a, b, ca=1, cb=0):
    return lax.dot_general(a, b, (((ca,), (cb,)), ((), ())), preferred_element_type=F32)


def splits(v):
    hi = v.astype(BF).astype(F32)
    rest = v - hi
    mid = rest.astype(BF).astype(F32)
    return hi, mid, rest - mid


def lane_of(shape):
    return lax.broadcasted_iota(jnp.int32, shape, len(shape) - 1)


def row_of(shape):
    return lax.broadcasted_iota(jnp.int32, shape, 0)


def bits_of(count):
    return [1 << k for k in range(count.bit_length() - 1)]


def orders_of(count):
    bits = bits_of(count)
    far = bits[1:]
    cut = (len(far) + 1) // 2
    return (far + bits[:1], far[cut:] + far[:cut] + bits[:1])


def span(bits):
    masks = [0]
    for bit in bits:
        masks = masks + [m ^ bit for m in masks]
    return masks


def greet(meetings):
    barrier = pltpu.get_barrier_semaphore()
    count = 0
    for axis, me, masks in meetings:
        for mask in masks:
            pl.semaphore_signal(
                barrier, inc=1, device_id={axis: me ^ mask}, device_id_type=MESH
            )
            count += 1
    pl.semaphore_wait(barrier, count)


class Gather:
    def __init__(self, axis, count, own, store, sems):
        self.axis, self.count, self.own, self.store = axis, count, own, store
        self.sends, self.recvs = sems
        self.me = lax.axis_index(axis)
        self.orders = orders_of(count)
        self.half = store.shape[1] // 2

    def copy(self, h, mask, bit):
        rows = pl.ds(h * self.half, self.half)
        there = self.store.at[self.me ^ mask, rows]
        return pltpu.make_async_remote_copy(
            src_ref=self.own.at[rows] if mask == 0 else there,
            dst_ref=there,
            send_sem=self.sends.at[h, mask ^ bit],
            recv_sem=self.recvs.at[h, mask ^ bit],
            device_id={self.axis: self.me ^ bit},
            device_id_type=MESH,
        )

    def incoming(self, h, mask):
        there = self.store.at[self.me ^ mask, pl.ds(h * self.half, self.half)]
        return pltpu.make_async_remote_copy(
            src_ref=there,
            dst_ref=there,
            send_sem=self.sends.at[h, mask],
            recv_sem=self.recvs.at[h, mask],
            device_id={self.axis: self.me ^ mask},
            device_id_type=MESH,
        )

    def start(self):
        for k in range(len(self.orders[0])):
            for h in range(2):
                self.copy(h, 0, self.orders[h][k]).start()

    def take(self, h, mask):
        order = self.orders[h]
        self.incoming(h, mask).wait_recv()
        k = max(i for i, bit in enumerate(order) if mask & bit)
        for bit in order[k + 1 :]:
            self.copy(h, mask, bit).start()

    def halves(self):
        early, late = [], []
        for k in range(len(self.orders[0]) - 1):
            for s in range(1 << k):
                for h in range(2):
                    mask = self.orders[h][k] ^ span(self.orders[h][:k])[s]
                    (late if self.count == 8 and k == 1 and s else early).append((h, mask))
        return early, late

    def stage(self, k):
        for s in range(1 << k):
            for h in range(2):
                order = self.orders[h]
                mask = order[k] ^ span(order[:k])[s]
                self.incoming(h, mask).wait_recv()
                for bit in order[k + 1 :]:
                    self.copy(h, mask, bit).start()

    def held(self, k):
        sets = [set(span(order[: k + 1])) for order in self.orders]
        return sets[0] & sets[1]

    def stages(self):
        for k in range(len(self.orders[0])):
            self.stage(k)

    def finish(self):
        for h in range(2):
            for mask in range(1, self.count):
                self.incoming(h, mask).wait_send()


class Scatter:
    def __init__(self, axis, count, part, land, sems):
        self.axis, self.count, self.part, self.land = axis, count, part, land
        self.sends, self.recvs = sems
        self.me = lax.axis_index(axis)
        self.orders = [order[::-1] for order in orders_of(count)]
        self.half = part.shape[1] // 2

    def depth(self, h, mask):
        for k, bit in enumerate(self.orders[h]):
            if mask & bit:
                return k
        return len(self.orders[h])

    def copy(self, h, mask):
        bit = self.orders[h][self.depth(h, mask)]
        return pltpu.make_async_remote_copy(
            src_ref=self.part.at[self.me ^ mask, pl.ds(h * self.half, self.half)],
            dst_ref=self.land.at[h, mask - 1],
            send_sem=self.sends.at[h, mask],
            recv_sem=self.recvs.at[h, mask],
            device_id={self.axis: self.me ^ bit},
            device_id_type=MESH,
        )

    def reduce(self, h, mask):
        depth = self.depth(h, mask)
        sources = [mask ^ bit for bit in self.orders[h][:depth]]
        for source in sources:
            self.copy(h, source).wait_recv()
        if sources:
            step = math.gcd(self.half, 64)
            mine = self.me ^ mask

            def add(c, carry):
                here = pl.ds(pl.multiple_of(c * step, step), step)
                at = pl.ds(pl.multiple_of(h * self.half + c * step, step), step)
                total = self.part[mine, at].astype(F32)
                for source in sources:
                    total = total + self.land[h, source - 1, here].astype(F32)
                self.part[mine, at] = total.astype(BF)
                return carry

            lax.fori_loop(0, self.half // step, add, 0)
        if mask:
            self.copy(h, mask).start()

    def run(self):
        for k in range(len(self.orders[0]) + 1):
            for mask in range(self.count):
                for h in range(2):
                    if self.depth(h, mask) == k:
                        self.reduce(h, mask)

    def finish(self):
        for h in range(2):
            for mask in range(1, self.count):
                self.copy(h, mask).wait_send()


def pair_of_sems(count):
    return [pltpu.SemaphoreType.DMA((2, count)), pltpu.SemaphoreType.DMA((2, count))]


ANYWHERE = pl.BlockSpec(memory_space=pl.ANY)
IN_VMEM = pl.BlockSpec(memory_space=pltpu.VMEM)


def remote(identity, limit=48):
    return pltpu.CompilerParams(
        collective_id=identity, has_side_effects=True, vmem_limit_bytes=limit << 20
    )


def scatter_kernel(axis, count, given, total, part, land, sends, recvs, local_sem):
    me = lax.axis_index(axis)
    take = pltpu.make_async_copy(given, part, local_sem)
    take.start()
    greet([(axis, me, bits_of(count))])
    moving = Scatter(axis, count, part, land, (sends, recvs))
    take.wait()
    moving.run()
    total[...] = part[me]
    moving.finish()


def scatter(blocks, axis, identity):
    count, rows, columns = blocks.shape
    return pl.pallas_call(
        functools.partial(scatter_kernel, axis, count),
        out_shape=jax.ShapeDtypeStruct((rows, columns), BF),
        in_specs=[ANYWHERE],
        out_specs=IN_VMEM,
        scratch_shapes=[
            pltpu.VMEM(blocks.shape, BF),
            pltpu.VMEM((2, count - 1, rows // 2, columns), BF),
        ]
        + pair_of_sems(count)
        + [pltpu.SemaphoreType.DMA(())],
        compiler_params=remote(identity, 56),
        name="scatter",
    )(blocks)


def attend_kernel(
    shards,
    near,
    heads,
    meta_ref,
    qkv_ref,
    cot_ref,
    mine_ref,
    out_ref,
    q_ref,
    k_ref,
    v_ref,
    cots_ref,
    gsend,
    grecv,
    asend,
    arecv,
    keep_sem,
):
    me = lax.axis_index("fsdp")
    total = qkv_ref.shape[0]
    nseq = NSEQ
    keep = pltpu.make_async_copy(cot_ref, cots_ref.at[me], keep_sem)
    keep.start()
    greet([("fsdp", me, range(1, shards))])
    going = Gather("fsdp", shards, cot_ref, cots_ref, (gsend, grecv))
    going.start()
    early, late = going.halves()
    edges = [jnp.zeros((1, 1), jnp.int32)]
    for s in range(nseq):
        edges.append(edges[-1] + meta_ref[8:9, s : s + 1])
    half = HEAD_WIDTH
    side = PART

    def prepare(i, carry):
        at = pl.ds(pl.multiple_of(i * side, side), side)
        low = lane_of((side, LANES)) < half
        lane = lane_of((side, LANES))
        row = row_of((side, LANES)) + i * side
        seq = jnp.zeros((side, LANES), jnp.bool_)
        for s in range(nseq):
            seq = seq | ((lane == s) & (row >= edges[s]) & (row < edges[s + 1]))
        queries = qkv_ref[at, 0:LANES].astype(F32) * (HEAD_WIDTH ** -0.5)
        pair = qkv_ref[at, LANES : 2 * LANES].astype(F32)
        swapped = pltpu.roll(pair, half, 1)
        marks = jnp.where(seq, 1.0, 0.0).astype(BF)
        for h in range(heads):
            mine = jnp.where(low if h == 0 else ~low, queries, 0.0).astype(BF)
            q_ref[i, h * side : (h + 1) * side, 0:LANES] = mine
            q_ref[i, h * side : (h + 1) * side, LANES : 2 * LANES] = marks
        k_ref[at, 0:LANES] = jnp.where(low, pair, swapped).astype(BF)
        far = jnp.where(lane < nseq, jnp.where(seq, 0.0, MASKED), 0.0)
        k_ref[at, LANES : 2 * LANES] = jnp.where(
            (lane >= nseq) & (lane < nseq + 3), 1.0, far
        ).astype(BF)
        v_ref[at, 0:LANES] = jnp.where(low, swapped, pair).astype(BF)
        v_ref[at, LANES : 2 * LANES] = jnp.ones((side, LANES), BF)
        return carry

    lax.fori_loop(0, total // side, prepare, 0)

    rows = 3 * side

    def place(ref, source):
        if near:
            return ref.at[:, pl.ds(pl.multiple_of(source * LANES, LANES), LANES)]
        return ref.at[source]

    def home_copy(target):
        return pltpu.make_async_remote_copy(
            src_ref=out_ref.at[pl.ds(target * rows, rows)],
            dst_ref=place(mine_ref, me),
            send_sem=asend.at[target],
            recv_sem=arecv.at[me],
            device_id={"fsdp": target},
            device_id_type=MESH,
        )

    low = lane_of((rows, LANES)) < half
    lane = lane_of((rows, LANES))
    visible = lane_of((rows, rows)) <= row_of((rows, rows))
    for i in range(total // rows):
        keys = (i + 1) * rows
        at = pl.ds(i * rows, rows)
        mixed = []
        for h in range(heads):
            mine = pl.ds(h * side, side)
            queries = jnp.concatenate([q_ref[3 * i + u, mine, :] for u in range(3)], axis=0)
            scores = dot(queries, k_ref[0:keys, :], 1, 1)
            final = jnp.where(visible, scores[:, keys - rows :], MASKED)
            if i:
                scores = jnp.concatenate([scores[:, : keys - rows], final], axis=1)
            else:
                scores = final
            top = jnp.max(scores, axis=1, keepdims=True)
            weights = jnp.exp(scores - top).astype(BF)
            acc = dot(weights, v_ref[0:keys, :])
            weight = acc[:, LANES:]
            mixed.append(acc[:, :LANES] / weight)
            hi, mid, lo = splits(-(top + jnp.log(weight)))
            marks = queries[:, LANES:].astype(F32)
            marks = jnp.where(lane == nseq, hi, marks)
            marks = jnp.where(lane == nseq + 1, mid, marks)
            marks = jnp.where(lane == nseq + 2, lo, marks).astype(BF)
            for u in range(3):
                q_ref[3 * i + u, mine, LANES:] = marks[u * side : (u + 1) * side]
        value = mixed[0] if heads == 1 else jnp.where(low, mixed[0], mixed[1])
        out_ref[at, :] = value.astype(BF)

        @pl.when(me != i)
        def _(i=i):
            home_copy(i).start()

        if i == shards - 2:
            for h, m in early:
                going.take(h, m)

    place(mine_ref, me)[...] = out_ref[pl.ds(pl.multiple_of(me * rows, rows), rows), :]
    for h, m in late:
        going.take(h, m)
    for m in range(1, shards):
        pltpu.make_async_remote_copy(
            src_ref=out_ref.at[pl.ds(0, rows)],
            dst_ref=place(mine_ref, me ^ m),
            send_sem=asend.at[0],
            recv_sem=arecv.at[me ^ m],
            device_id={"fsdp": me ^ m},
            device_id_type=MESH,
        ).wait_recv()
    for i in range(shards):

        @pl.when(me != i)
        def _(i=i):
            home_copy(i).wait_send()

    for h in range(2):
        for m in span(going.orders[h][:-1]):
            going.incoming(h, m ^ going.orders[h][-1]).wait_recv()
    going.finish()
    keep.wait()


def attend(meta, qkv, cot, heads, identity):
    shards = lax.axis_size("fsdp")
    near = shards <= 8
    total = qkv.shape[0]
    rows = total // shards
    return pl.pallas_call(
        functools.partial(attend_kernel, shards, near, heads),
        out_shape=(
            jax.ShapeDtypeStruct((rows, MODEL_WIDTH) if near else (shards, rows, LANES), BF),
            jax.ShapeDtypeStruct((total, LANES), BF),
            jax.ShapeDtypeStruct((total // PART, heads * PART, 2 * LANES), BF),
            jax.ShapeDtypeStruct((total, 2 * LANES), BF),
            jax.ShapeDtypeStruct((total, 2 * LANES), BF),
            jax.ShapeDtypeStruct((shards,) + cot.shape, BF),
        ),
        in_specs=[IN_VMEM, IN_VMEM, ANYWHERE],
        out_specs=(IN_VMEM,) * 5 + (ANYWHERE,),
        scratch_shapes=pair_of_sems(shards)
        + [pltpu.SemaphoreType.DMA((shards,))] * 2
        + [pltpu.SemaphoreType.DMA(())],
        compiler_params=remote(identity, 60),
        name="attend",
    )(meta, qkv, cot)


def sequences(meta, first, rows, heads_of):
    row = row_of((rows, LANES)) + first
    start = jnp.zeros((1, 1), jnp.int32)
    picked = [jnp.zeros((rows, LANES), part[0].dtype) for part in heads_of]
    for s in range(len(heads_of[0])):
        inside = row >= start
        picked = [jnp.where(inside, part[s], value) for part, value in zip(heads_of, picked)]
        start = start + meta[8:9, s : s + 1]
    return picked


def turned(tensor, cosine, sine):
    lower = lane_of(tensor.shape) % HEAD_WIDTH < HEAD_WIDTH // 2
    other = jnp.where(lower, pltpu.roll(tensor, LANES - 32, 1), pltpu.roll(tensor, 32, 1))
    return tensor * cosine + other * sine


def head_columns(wide, narrow, pick_wide, pick_narrow, heads):
    low = lane_of((1, LANES)) < HEAD_WIDTH
    queries = wide
    if heads == 1:
        queries = jnp.where(low, jnp.where(pick_wide, pltpu.roll(wide, HEAD_WIDTH, 1), wide), 0.0)
    keys, values = narrow
    keys = jnp.where(pick_narrow, pltpu.roll(keys, HEAD_WIDTH, 1), keys)
    values = jnp.where(pick_narrow, values, pltpu.roll(values, HEAD_WIDTH, 1))
    return queries, jnp.where(low, keys, values)


def enter_kernel(
    shards,
    groups,
    deal_ref,
    x_ref,
    wq_ref,
    wk_ref,
    wv_ref,
    small_ref,
    meta_ref,
    factors_ref,
    wide_ref,
    kv_ref,
    cos_ref,
    sin_ref,
    freq_ref,
    qkv_ref,
    low_ref,
    mask_ref,
    small_out,
    meta_out,
    columns_out,
    turn_ref,
    xs,
    slices,
    weights,
    metas,
    merged,
    second,
    xsend,
    xrecv,
    wsend,
    wrecv,
    zsend,
    zrecv,
    msend,
    mrecv,
):
    me, plane = lax.axis_index("fsdp"), lax.axis_index("dp")
    heads = HEADS // shards
    share = max(1, shards // KEY_VALUE_HEADS)
    rows = x_ref.shape[0]
    part = wq_ref.shape[0]
    order = [mask for mask in range(1, shards)]

    for f in range(shards):
        chunk = f * heads * HEAD_WIDTH // LANES
        head = f // share
        pair = head // 2
        queries, others = head_columns(
            wq_ref[:, chunk * LANES : (chunk + 1) * LANES].astype(F32),
            (
                wk_ref[:, pair * LANES : (pair + 1) * LANES].astype(F32),
                wv_ref[:, pair * LANES : (pair + 1) * LANES].astype(F32),
            ),
            f % 2 == 1,
            head % 2 == 1,
            heads,
        )
        slices[f, :, 0:LANES] = queries.astype(BF)
        slices[f, :, LANES : 2 * LANES] = others.astype(BF)
        slices[f, :, 2 * LANES :] = small_ref[...]
    metas[plane] = meta_ref[...]

    greet([("fsdp", me, order), ("dp", plane, range(1, groups))])

    moving = Gather("fsdp", shards, x_ref, xs, (xsend, xrecv))
    plane_rows = shards * part

    def column_copy(mask):
        return pltpu.make_async_remote_copy(
            src_ref=slices.at[me ^ mask],
            dst_ref=weights.at[plane, me],
            send_sem=wsend.at[mask],
            recv_sem=wrecv.at[mask],
            device_id={"fsdp": me ^ mask},
            device_id_type=MESH,
        )

    def plane_copy(mask):
        return pltpu.make_async_remote_copy(
            src_ref=weights.at[plane],
            dst_ref=weights.at[plane],
            send_sem=zsend.at[mask],
            recv_sem=zrecv.at[mask],
            device_id={"dp": plane ^ mask},
            device_id_type=MESH,
        )

    def meta_copy(mask):
        return pltpu.make_async_remote_copy(
            src_ref=meta_ref,
            dst_ref=metas.at[plane],
            send_sem=msend.at[mask],
            recv_sem=mrecv.at[mask],
            device_id={"dp": plane ^ mask},
            device_id_type=MESH,
        )

    for mask in order:
        column_copy(mask).start()
    for mask in range(1, groups):
        meta_copy(mask).start()
    moving.start()
    weights[plane, me] = slices[me]

    half = HEAD_WIDTH
    at = pl.ds(pl.multiple_of(me * heads * half // LANES * LANES, LANES), LANES)
    head = me // share
    pair_at = pl.ds(pl.multiple_of(head // 2 * LANES, LANES), LANES)
    queries, others = head_columns(
        wide_ref[0, :, at].astype(F32),
        (kv_ref[0, :, pair_at].astype(F32), kv_ref[1, :, pair_at].astype(F32)),
        me % 2 == 1,
        head % 2 == 1,
        heads,
    )
    low_lane = lane_of((STACKED, LANES)) < half
    second[...] = jnp.zeros(second.shape, BF)
    second[0:STACKED, 0:LANES] = queries.astype(BF)
    second[STACKED : 2 * STACKED, LANES:] = jnp.where(low_lane, others, 0.0).astype(BF)
    second[2 * STACKED :, LANES:] = jnp.where(low_lane, 0.0, others).astype(BF)

    for mask in order:
        column_copy(mask).wait_recv()
    for mask in range(1, groups):
        plane_copy(mask).start()
    for mask in range(1, groups):
        meta_copy(mask).wait_recv()
    dealt = jnp.int32(0)
    for g in range(groups):
        dealt = dealt + jnp.where(deal_ref[g] == plane, g, 0)
    meta = jnp.zeros(meta_ref.shape, jnp.int32)
    for g in range(groups):
        meta = jnp.where(dealt == g, metas[g], meta)
    meta_out[...] = meta
    moving.stage(0)
    for mask in range(1, groups):
        plane_copy(mask).wait_recv()

    for g in range(groups):
        for f in range(shards):
            here = pl.ds((g * shards + f) * part, part)
            block = weights[g, f]
            small_out[here, :] = block[:, 2 * LANES :]
            merged[here, 0 : 2 * LANES] = block[:, : 2 * LANES]
            columns_out[here, :] = block[:, : 2 * LANES]
    for s in range(3):
        merged[:, (2 + s) * LANES : (3 + s) * LANES] = factors_ref[s]
    gain = gain_row(small_out[...], 16)

    nseq = NSEQ
    lanes = lane_of((1, LANES))
    starts, first = [], jnp.zeros((1, 1), jnp.int32)
    for s in range(nseq):
        starts.append(first)
        first = first + meta[8:9, s : s + 1]
    angles = [start.astype(F32) * freq_ref[...] for start in starts]
    start_cos = [jnp.cos(angle) for angle in angles]
    start_sin = [jnp.sin(angle) for angle in angles]
    adapters = [jnp.broadcast_to(meta[9:10, s : s + 1], (1, LANES)) for s in range(nseq)]
    keyed = lanes < half
    sign = jnp.where(lanes % half < half // 2, -1.0, 1.0)

    def compute(mask):
        block = me ^ mask
        at = pl.ds(pl.multiple_of(block * rows, rows), rows)
        x = x_ref[...] if mask == 0 else xs[block]
        full = x.astype(F32)
        r1 = lax.rsqrt(jnp.mean(full * full, axis=1, keepdims=True) + EPSILON)
        product = dot((full * r1 * gain).astype(BF), merged[...])
        base_cos, base_sin, pick = sequences(
            meta, block * rows, rows, (start_cos, start_sin, adapters)
        )
        masked = lane_of((rows, LANES)) // ADAPTER_RANK == pick
        mask_ref[at, :] = jnp.where(masked, 1.0, 0.0).astype(BF)
        lows = [
            jnp.where(masked, product[:, (2 + s) * LANES : (3 + s) * LANES], 0.0).astype(BF)
            for s in range(3)
        ]
        lows = jnp.concatenate(lows, axis=1)
        low_ref[at, :] = lows
        product = product[:, : 2 * LANES] + dot(lows, second[...])
        row_cos, row_sin = cos_ref[at, :], sin_ref[at, :]
        cosine = row_cos * base_cos + row_sin * base_sin
        sine = (row_sin * base_cos - row_cos * base_sin) * sign
        turn_ref[at, :LANES] = cosine
        turn_ref[at, LANES:] = sine
        qkv_ref[at, :LANES] = turned(product[:, :LANES], cosine, sine).astype(BF)
        others = product[:, LANES:]
        qkv_ref[at, LANES:] = turned(
            others, jnp.where(keyed, cosine, 1.0), jnp.where(keyed, sine, 0.0)
        ).astype(BF)

    compute(0)
    for h in range(2):
        moving.take(h, 1)
    compute(1)
    early, late = moving.halves()
    for h, m in early:
        if m not in (moving.orders[h][0],):
            moving.take(h, m)
    whole = [m for m in range(2, shards, 2) if all((h, m) in early for h in range(2))]
    for m in whole:
        compute(m)
    for h, m in late:
        moving.take(h, m)
    for m in range(2, shards, 2):
        if m not in whole:
            compute(m)
    for m in range(3, shards, 2):
        for h in range(2):
            moving.take(h, m)
        compute(m)
    moving.finish()
    for mask in order:
        column_copy(mask).wait_send()
    for mask in range(1, groups):
        plane_copy(mask).wait_send()
        meta_copy(mask).wait_send()


def enter(deal, x, wq, wk, wv, small, meta, factors, wide, kv_second, identity):
    shards, groups = lax.axis_size("fsdp"), lax.axis_size("dp")
    rows, part = x.shape[0], wq.shape[0]
    total = rows * shards
    half = HEAD_WIDTH // 2
    frequency = ROPE_BASE ** (-np.arange(half, dtype=np.float64) / half)
    frequency = frequency.astype(np.float32)
    angles = np.arange(total, dtype=np.float64)[:, None] * frequency.astype(np.float64)[None, :]
    cosine = jnp.asarray(np.tile(np.cos(angles).astype(np.float32), (1, 4)))
    sine = jnp.asarray(np.tile(np.sin(angles).astype(np.float32), (1, 4)))
    frequency = jnp.asarray(np.tile(frequency, 4)[None, :])
    return pl.pallas_call(
        functools.partial(enter_kernel, shards, groups),
        out_shape=(
            jax.ShapeDtypeStruct((total, 2 * LANES), BF),
            jax.ShapeDtypeStruct((total, 3 * STACKED), BF),
            jax.ShapeDtypeStruct((total, STACKED), BF),
            jax.ShapeDtypeStruct((MODEL_WIDTH, LANES), BF),
            jax.ShapeDtypeStruct(meta.shape, jnp.int32),
            jax.ShapeDtypeStruct((MODEL_WIDTH, 2 * LANES), BF),
            jax.ShapeDtypeStruct((total, 2 * LANES), F32),
        ),
        in_specs=[pl.BlockSpec(memory_space=pltpu.SMEM)] + [IN_VMEM] * 12,
        out_specs=(IN_VMEM,) * 7,
        scratch_shapes=[
            pltpu.VMEM((shards, rows, MODEL_WIDTH), BF),
            pltpu.VMEM((shards, part, 3 * LANES), BF),
            pltpu.VMEM((groups, shards, part, 3 * LANES), BF),
            pltpu.VMEM((groups,) + meta.shape, jnp.int32),
            pltpu.VMEM((MODEL_WIDTH, 2 * LANES + 3 * STACKED), BF),
            pltpu.VMEM((3 * STACKED, 2 * LANES), BF),
        ]
        + pair_of_sems(shards)
        + [pltpu.SemaphoreType.DMA((shards,))] * 2
        + [pltpu.SemaphoreType.DMA((groups,))] * 4,
        compiler_params=remote(identity, 60),
        name="enter",
    )(deal, x, wq, wk, wv, small, meta, factors, wide, kv_second, cosine, sine, frequency)


def gain_row(small, lane):
    pick = jnp.where(lane_of((8, LANES)) == lane, 1.0, 0.0).astype(BF)
    return dot(pick, small, 1, 1)[0:1, :]


def turn_of(step, shards):
    if shards == 8:
        return step + step // 4 * (1 - 2 * (step % 2))
    late = (step + shards - 4) // shards
    return step + late * (shards + 3 - 2 * step)


def scatter_plan(moving, shards):
    place = {turn_of(t, shards): t for t in range(shards)}
    sent, plan = {}, []
    for t in range(shards):
        now = []
        for mask in range(1, shards):
            for h in range(2):
                sources = [mask ^ bit for bit in moving.orders[h][: moving.depth(h, mask)]]
                ready = all((h, s) in sent and sent[h, s] < t for s in sources)
                if (h, mask) not in sent and place[mask] <= t and ready:
                    now.append((h, mask))
        for item in now:
            sent[item] = t
        plan.append(now)
    rest = [(h, m) for m in range(1, shards) for h in range(2) if (h, m) not in sent]
    rest.sort(key=lambda item: moving.depth(*item))
    return plan, rest + [(0, 0), (1, 0)]


def experts_block(first_expert, n2, side, grad, mask, win, wout, wide_down, hid, down, spread, fold):
    rows = n2.shape[0]
    width = HIDDEN_UNITS
    lane = lane_of((rows, LANES))
    lows = dot(side, spread[:, : 2 * STACKED])
    low_gate = (lows[:, :STACKED] * mask).astype(BF)
    low_up = (lows[:, STACKED:] * mask).astype(BF)
    lift_gate = dot(low_gate, hid[0])
    lift_up = dot(low_up, hid[1])
    down_grad = (dot(grad, wide_down, 1, 1) * mask).astype(BF)
    from_down = dot(down_grad, down[...], 1, 1)
    side_full = side.astype(F32)
    total_inner = jnp.zeros((rows, width), F32)
    total_gate = jnp.zeros((rows, width), F32)
    total_up = jnp.zeros((rows, width), F32)
    extra = jnp.zeros((rows, LANES), F32)
    gated_parts, slope_parts = [], []
    for e in range(win.shape[1] // (2 * width)):
        name = first_expert + e
        at_high, at_low = lane == name, lane == name + EXPERT_COUNT
        gate = jnp.sum(jnp.where(at_high | at_low, side_full, 0.0), axis=1, keepdims=True)
        first = 2 * e * width
        pre_gate = dot(n2, win[:, first : first + width]) + lift_gate
        pre_up = dot(n2, win[:, first + width : first + 2 * width]) + lift_up
        pulled = dot(grad, wout[:, e * width : (e + 1) * width]) + from_down
        squashed = jax.nn.sigmoid(pre_gate)
        active = pre_gate * squashed
        inner = active * pre_up
        gate_grad = jnp.sum(inner * pulled, axis=1, keepdims=True)
        high = gate_grad.astype(BF).astype(F32)
        extra = extra + jnp.where(at_high, high, 0.0) + jnp.where(at_low, gate_grad - high, 0.0)
        gated = inner * gate
        pulled = pulled * gate
        grad_gate = pulled * pre_up * (squashed + active * (1.0 - squashed))
        grad_up = pulled * active
        gated_parts.append(gated.astype(BF))
        slope_parts += [grad_gate.astype(BF), grad_up.astype(BF)]
        total_inner = total_inner + gated
        total_gate = total_gate + grad_gate
        total_up = total_up + grad_up
    out = dot(jnp.concatenate(gated_parts, axis=1), wout[...], 1, 1)
    back = dot(jnp.concatenate(slope_parts, axis=1), win[...], 1, 1)
    total_inner = total_inner.astype(BF)
    total_gate = total_gate.astype(BF)
    total_up = total_up.astype(BF)
    shrunk = jnp.concatenate(
        [
            (dot(total_gate, hid[0], 1, 1) * mask).astype(BF),
            (dot(total_up, hid[1], 1, 1) * mask).astype(BF),
            (dot(total_inner, down[...]) * mask).astype(BF),
        ],
        axis=1,
    )
    extra = extra + dot(shrunk, fold[...])
    sums = (
        dot(total_inner, down_grad, 0, 0),
        dot(low_gate, total_gate, 0, 0),
        dot(low_up, total_up, 0, 0),
    )
    return out.astype(BF), back.astype(BF), extra.astype(BF), sums


def middle_kernel(
    shards,
    mine_ref,
    x_ref,
    small_ref,
    meta_ref,
    mask_ref,
    wo_ref,
    factors_ref,
    wide_ref,
    router2_ref,
    hid_ref,
    down_ref,
    spread_ref,
    fold_ref,
    cots_ref,
    win_ref,
    wout_ref,
    base_ref,
    outs_ref,
    hgrad_ref,
    heads_ref,
    early_ref,
    *scratch,
):
    near = shards <= 8
    store, block_in, scratch = (scratch[0], None, scratch[1:]) if near else (scratch[0], scratch[1], scratch[2:])
    middle_body(
        shards,
        near,
        (
            mine_ref,
            x_ref,
                    small_ref,
            meta_ref,
            mask_ref,
            wo_ref,
            factors_ref,
            wide_ref,
            router2_ref,
            hid_ref,
            down_ref,
            spread_ref,
            fold_ref,
            cots_ref,
            win_ref,
            wout_ref,
        ),
        (
            base_ref,
            outs_ref,
            hgrad_ref,
            heads_ref,
            early_ref,
        ),
        store,
        block_in,
        *scratch,
    )


def middle_body(
    shards,
    near,
    given,
    results,
    store,
    block_in,
    own_in,
    part,
    land,
    win,
    wout,
    cots,
    outs,
    attended,
    factors,
    gdown_ref,
    ghid_ref,
    gsend,
    grecv,
    ssend,
    srecv,
    wsem,
    csem,
    osem,
    bsem,
):
    (
        mine_ref,
        x_ref,
            small_ref,
        meta_ref,
        mask_ref,
        wo_ref,
        factors_ref,
        wide_ref,
        router2_ref,
        hid_ref,
        down_ref,
        spread_ref,
        fold_ref,
        cots_ref,
        win_ref,
        wout_ref,
    ) = given
    (
        base_ref,
        outs_ref,
        hgrad_ref,
        heads_ref,
        early_ref,
    ) = results
    me = lax.axis_index("fsdp")
    rows = x_ref.shape[0]
    if near:
        own_in = store.at[me]
    width = MODEL_WIDTH
    heads = HEADS // shards
    lane = lane_of((rows, LANES))
    loads = [
        pltpu.make_async_copy(win_ref, win, wsem.at[0]),
        pltpu.make_async_copy(wout_ref, wout, wsem.at[1]),
    ]
    fetch_factors = pltpu.make_async_copy(factors_ref.at[pl.ds(3, 4)], factors, wsem.at[2])
    fetch_factors.start()
    for load in loads:
        load.start()

    def cot_copy(step):
        return pltpu.make_async_copy(
            cots_ref.at[me ^ turn_of(step, shards)], cots.at[step % 2], csem.at[step % 2]
        )

    cot_copy(0).start()
    greet([("fsdp", me, bits_of(shards))])

    if near:
        attended = mine_ref
    else:
        for s in range(0, shards, 2):
            second = pltpu.roll(mine_ref[s + 1].astype(F32), HEAD_WIDTH, 1)
            both = jnp.where(lane < HEAD_WIDTH, mine_ref[s].astype(F32), second)
            attended[:, s // 2 * LANES : (s // 2 + 1) * LANES] = both.astype(BF)
    own = pl.ds(pl.multiple_of(me * rows, rows), rows)
    mask = mask_ref[own, :].astype(F32)
    small = small_ref[...]
    gain = gain_row(small, 17)
    fetch_factors.wait()
    out_low = (dot(attended[...], factors[3]) * mask).astype(BF)
    hidden = (
        x_ref[...].astype(F32) + dot(attended[...], wo_ref[...], 1, 1) + dot(out_low, wide_ref[1])
    )
    base_ref[...] = hidden
    r2 = lax.rsqrt(jnp.mean(hidden * hidden, axis=1, keepdims=True) + EPSILON)
    n2 = (hidden * r2 * gain).astype(BF)
    own_in[:, :width] = n2
    lows = [(dot(n2, factors[s]) * mask).astype(BF) for s in range(3)]
    logits = dot(n2, small) + dot(lows[0], router2_ref[...])
    named = jnp.zeros((LANES, rows), jnp.bool_)
    for k in range(TOPK):
        named = named | (row_of((LANES, rows)) == meta_ref[k : k + 1, :])
    eye = jnp.where(row_of((LANES, LANES)) == lane_of((LANES, LANES)), 1.0, 0.0).astype(BF)
    picked = dot(jnp.where(named, 1.0, 0.0).astype(BF), eye, 0, 0) > 0.5
    peak = jnp.max(jnp.where(picked, logits, MASKED), axis=1, keepdims=True)
    lifted = jnp.where(picked, jnp.exp(jnp.where(picked, logits, peak) - peak), 0.0)
    gates = lifted / jnp.sum(lifted, axis=1, keepdims=True)
    high = gates.astype(BF).astype(F32)
    shrunk = dot(jnp.concatenate(lows[1:], axis=1), fold_ref[: 2 * STACKED, :])
    side = high + pltpu.roll(gates - high, EXPERT_COUNT, 1) + shrunk
    own_in[:, width:] = side.astype(BF)

    going = Gather("fsdp", shards, own_in, store, (gsend, grecv))
    coming = Scatter("fsdp", shards, part, land, (ssend, srecv))
    going.start()
    for load in loads:
        load.wait()

    early, late = going.halves()
    plan, rest = scatter_plan(coming, shards)
    first_expert = me * (EXPERT_COUNT // shards)

    def out_copy(at):
        return pltpu.make_async_copy(outs, outs_ref.at[me ^ turn_of(at, shards)], osem.at[0])

    def step(t, carry):
        turn = turn_of(t, shards)
        block = me ^ turn
        slot = t % 2

        @pl.when(t == 2)
        def _():
            for h, m in early:
                going.take(h, m)

        @pl.when(t == 4)
        def _():
            for h, m in late:
                going.take(h, m)

        for k in range(shards):
            m = turn_of(k, shards)
            if m % 2:

                @pl.when(t == k)
                def _(m=m):
                    for h in range(2):
                        going.take(h, m)

        @pl.when(t + 1 < shards)
        def _():
            cot_copy(t + 1).start()

        cot_copy(t).wait()

        @pl.when(t >= 1)
        def _():
            out_copy(t - 1).wait()

        block_rows = pl.ds(pl.multiple_of(block * rows, rows), rows)
        if near:
            here = store.at[block]
        else:
            here = block_in

            @pl.when(t == 0)
            def _():
                block_in[...] = own_in[...]

            @pl.when(t != 0)
            def _():
                fetch = pltpu.make_async_copy(store.at[block], block_in, bsem)
                fetch.start()
                fetch.wait()

        out, back, extra, sums = experts_block(
            first_expert,
            here[:, :width],
            here[:, width:],
            cots[slot],
            mask_ref[block_rows, :].astype(F32),
            win,
            wout,
            wide_ref[2],
            hid_ref,
            down_ref,
            spread_ref,
            fold_ref,
        )
        outs[...] = out
        out_copy(t).start()
        part[block, :, :width] = back
        part[block, :, width:] = extra

        @pl.when(t == 0)
        def _():
            gdown_ref[...] = sums[0]
            ghid_ref[0] = sums[1]
            ghid_ref[1] = sums[2]

        @pl.when(t != 0)
        def _():
            gdown_ref[...] += sums[0]
            ghid_ref[0] += sums[1]
            ghid_ref[1] += sums[2]

        for k in range(shards):
            if plan[k]:

                @pl.when(t == k)
                def _(k=k):
                    for h, m in plan[k]:
                        coming.reduce(h, m)

        return carry

    lax.fori_loop(0, shards, step, 0)
    out_copy(shards - 1).wait()
    cot_load = pltpu.make_async_copy(cots_ref.at[me], cots.at[0], csem.at[0])
    cot_load.start()
    for h, m in rest:
        coming.reduce(h, m)
    cot_load.wait()

    hidden = base_ref[...]
    mask = mask_ref[own, :].astype(F32)
    r2 = lax.rsqrt(jnp.mean(hidden * hidden, axis=1, keepdims=True) + EPSILON)
    n2 = own_in[:, :width]
    cot = cots[0]
    grad = cot.astype(F32)
    extra = part[me, :, width:]
    extra_full = extra.astype(F32)
    gate_grad = extra_full + pltpu.roll(extra_full, LANES - EXPERT_COUNT, 1)
    logit_grad = gates * (gate_grad - jnp.sum(gates * gate_grad, axis=1, keepdims=True))
    logit_grad = jnp.where(lane < EXPERT_COUNT, logit_grad, 0.0).astype(BF)
    wider = dot(extra, spread_ref[...])
    second_grad = [
        (dot(logit_grad, router2_ref[...], 1, 1) * mask).astype(BF),
        (wider[:, :STACKED] * mask).astype(BF),
        (wider[:, STACKED : 2 * STACKED] * mask).astype(BF),
    ]
    down_low = (wider[:, 2 * STACKED :] * mask).astype(BF)
    base_ref[...] = hidden + dot(down_low, wide_ref[2])
    n2_grad = part[me, :, :width].astype(F32) + dot(logit_grad, small, 1, 1)
    for s in range(3):
        n2_grad = n2_grad + dot(second_grad[s], factors[s], 1, 1)
    w2 = gain * n2_grad
    hidden_grad = grad + r2 * w2 - hidden * (r2 * r2 * r2) * jnp.mean(w2 * hidden, axis=1, keepdims=True)
    hgrad_ref[...] = hidden_grad
    out_grad = hidden_grad.astype(BF)
    out_low_grad = (dot(out_grad, wide_ref[1], 1, 1) * mask).astype(BF)
    attended_grad = dot(out_grad, wo_ref[...]) + dot(out_low_grad, factors[3], 1, 1)
    for s in range(shards):
        if heads == 2:
            heads_ref[s] = attended_grad[:, s * LANES : (s + 1) * LANES].astype(BF)
        else:
            pair = attended_grad[:, s // 2 * LANES : (s // 2 + 1) * LANES]
            if s % 2:
                pair = pltpu.roll(pair, HEAD_WIDTH, 1)
            heads_ref[s] = jnp.where(lane < HEAD_WIDTH, pair, 0.0).astype(BF)
    gsecond = dot(n2, jnp.concatenate(second_grad, axis=1), 0, 0).astype(BF)
    packed = [gsecond[:, s * LANES : (s + 1) * LANES] for s in range(3)]
    packed.append(dot(attended[...], out_low_grad, 0, 0).astype(BF))
    packed.append(gdown_ref[...].astype(BF))
    for s in range(2):
        packed += [ghid_ref[s, :, j : j + LANES].astype(BF) for j in range(0, HIDDEN_UNITS, LANES)]
    for one, two in ((out_low, out_grad), (down_low, cot)):
        product = dot(one, two, 0, 0).astype(BF)
        packed += [product[:, j : j + LANES] for j in range(0, MODEL_WIDTH, LANES)]
    packed.append(dot(lows[0], logit_grad, 0, 0).astype(BF))
    pack(early_ref, packed, early_ref.shape[1])
    going.finish()
    coming.finish()


def middle(mine, x, small, meta, mask, wo, factors, wide, router2, hid, down, cots, win, wout, identity):
    shards = lax.axis_size("fsdp")
    rows = x.shape[0]
    side = MODEL_WIDTH + LANES
    source = np.arange(LANES)
    place = np.arange(STACKED) % ADAPTER_RANK
    spread = np.concatenate([source[:, None] == o + place[None, :] for o in (32, 48, 64)], axis=1)
    fold = np.concatenate([source[None, :] == o + place[:, None] for o in (32, 48, 64)], axis=0)
    spread, fold = jnp.asarray(spread, BF), jnp.asarray(fold, BF)
    gathered = (shards, rows, side)
    near = shards <= 8
    results = pl.pallas_call(
        functools.partial(middle_kernel, shards),
        out_shape=(
            jax.ShapeDtypeStruct((rows, MODEL_WIDTH), F32),
            jax.ShapeDtypeStruct((shards, rows, MODEL_WIDTH), BF),
            jax.ShapeDtypeStruct((rows, MODEL_WIDTH), F32),
            jax.ShapeDtypeStruct((shards, rows, LANES), BF),
            jax.ShapeDtypeStruct((shards, total_length(EARLY) // shards, LANES), BF),
        )
        + (() if near else (jax.ShapeDtypeStruct(gathered, BF),)),
        in_specs=[IN_VMEM] * 6 + [ANYWHERE] + [IN_VMEM] * 6 + [ANYWHERE] * 3,
        out_specs=(IN_VMEM, ANYWHERE) + (IN_VMEM,) * 3 + (() if near else (ANYWHERE,)),
        scratch_shapes=[
            pltpu.VMEM(gathered if near else gathered[1:], BF),
            pltpu.VMEM((16, LANES) if near else gathered[1:], BF),
            pltpu.VMEM((shards, rows, side), BF),
            pltpu.VMEM((2, shards - 1, rows // 2, side), BF),
            pltpu.VMEM(win.shape, BF),
            pltpu.VMEM(wout.shape, BF),
            pltpu.VMEM((2, rows, MODEL_WIDTH), BF),
            pltpu.VMEM((rows, MODEL_WIDTH), BF),
            pltpu.VMEM((16, LANES) if near else (rows, MODEL_WIDTH), BF),
            pltpu.VMEM((4, MODEL_WIDTH, STACKED), BF),
            pltpu.VMEM((HIDDEN_UNITS, STACKED), F32),
            pltpu.VMEM((2, STACKED, HIDDEN_UNITS), F32),
        ]
        + pair_of_sems(shards) * 2
        + [pltpu.SemaphoreType.DMA((3,))] * 3
        + [pltpu.SemaphoreType.DMA(())],
        compiler_params=remote(identity, 62),
        name="middle",
    )(mine, x, small, meta, mask, wo, factors, wide, router2, hid, down, spread, fold, cots, win, wout)
    return results[:5]


class Total:
    def __init__(self, shards, groups, out, part, land, zpart, zland, zall, sems):
        self.me, self.plane = lax.axis_index("fsdp"), lax.axis_index("dp")
        self.groups, self.out, self.part, self.zpart, self.zall = groups, out, part, zpart, zall
        self.down = Scatter("fsdp", shards, part, land, sems[0:2])
        self.across = Scatter("dp", groups, zpart, zland, sems[2:4])
        self.back = Gather("dp", groups, zall.at[self.plane], zall, sems[4:6])
        self.up = Gather("fsdp", shards, out.at[self.me], out, sems[6:8])
        self.steps = [lambda k=k: self.level(self.down, k) for k in range(len(bits_of(shards)))]
        self.steps.append(self.turn)
        self.steps += [lambda k=k: self.level(self.across, k) for k in range(1, len(bits_of(groups)))]
        self.steps.append(self.turn_back)
        for k in range(len(bits_of(groups)) - 1):
            self.steps.append(lambda k=k: self.back.stage(k))
        self.steps.append(self.rise)
        for k in range(len(bits_of(shards))):
            self.steps.append(lambda k=k: self.up.stage(k))
        self.steps.append(self.finish)

    def level(self, moving, k):
        for mask in range(moving.count):
            for h in range(2):
                if moving.depth(h, mask) == k:
                    moving.reduce(h, mask)

    def turn(self):
        self.level(self.down, len(self.down.orders[0]))
        piece = self.zpart.shape[1]
        for g in range(self.groups):
            self.zpart[g] = self.part[self.me, pl.ds(g * piece, piece)]
        self.level(self.across, 0)

    def turn_back(self):
        self.level(self.across, len(self.across.orders[0]))
        self.zall[self.plane] = self.zpart[self.plane]
        self.back.start()

    def rise(self):
        self.back.stage(len(bits_of(self.groups)) - 1)
        piece = self.zpart.shape[1]
        for g in range(self.groups):
            self.out[self.me, pl.ds(g * piece, piece)] = self.zall[g]
        self.up.start()

    def finish(self):
        self.down.finish()
        self.across.finish()
        self.back.finish()
        self.up.finish()

    def next(self, count=1):
        for _ in range(count):
            if self.steps:
                self.steps.pop(0)()


def total_scratch(shards, groups, length):
    share = length // shards
    piece = share // groups
    return [
        pltpu.VMEM((shards, share, LANES), BF),
        pltpu.VMEM((shards, share, LANES), BF),
        pltpu.VMEM((2, shards - 1, share // 2, LANES), BF),
        pltpu.VMEM((groups, piece, LANES), BF),
        pltpu.VMEM((2, groups - 1, piece // 2, LANES), BF),
        pltpu.VMEM((groups, piece, LANES), BF),
    ] + pair_of_sems(shards) + pair_of_sems(groups) * 2 + pair_of_sems(shards)


def total_length(length):
    unit = lax.axis_size("fsdp") * lax.axis_size("dp") * 2 * 16
    return -(-length // unit) * unit


EARLY = 5 * MODEL_WIDTH + HIDDEN_UNITS + 2 * MODEL_WIDTH + STACKED
LATE = 5 * MODEL_WIDTH


def leave_kernel(
    shards,
    groups,
    heads_ref,
    q_ref,
    k_ref,
    v_ref,
    att_ref,
    columns_ref,
    x_ref,
    small_ref,
    factors_ref,
    wide_ref,
    kv_ref,
    hgrad_ref,
    base_ref,
    low_ref,
    turn_ref,
    mask_ref,
    outs_ref,
    layer_ref,
    xgrad_ref,
    late_out,
    columns,
    grads,
    dk_ref,
    dv_ref,
    dq_ref,
    mixes,
    landed,
    near_columns,
    low,
    turn,
    own_mask_ref,
    outs,
    out_land,
    asend,
    arecv,
    msend,
    mrecv,
    gsend,
    grecv,
    osend,
    orecv,
    isem,
    *sums,
):
    me, plane = lax.axis_index("fsdp"), lax.axis_index("dp")
    rows = x_ref.shape[0]
    heads = HEADS // shards
    share = max(1, shards // KEY_VALUE_HEADS)
    side = PART
    cols = heads * side
    nparts = rows // side
    late_part = sums[0]
    near = shards <= 8
    columns = near_columns if near else columns
    own_rows = pl.ds(pl.multiple_of(me * rows, rows), rows)
    takes = [
        pltpu.make_async_copy(mask_ref.at[own_rows], own_mask_ref, isem.at[1]),
        pltpu.make_async_copy(low_ref.at[own_rows], low, isem.at[2]),
    ]
    for take in takes:
        take.start()
    if near:
        take_outs = pltpu.make_async_copy(outs_ref, outs, isem.at[3])
        take_outs.start()
    greet([("fsdp", me, range(1, shards)), ("dp", plane, bits_of(groups))])

    def head_copy(mask):
        return pltpu.make_async_remote_copy(
            src_ref=heads_ref.at[me ^ mask],
            dst_ref=grads.at[me],
            send_sem=asend.at[mask],
            recv_sem=arecv.at[me],
            device_id={"fsdp": me ^ mask},
            device_id_type=MESH,
        )

    def home_copy(target):
        return pltpu.make_async_remote_copy(
            src_ref=mixes.at[target],
            dst_ref=landed.at[me],
            send_sem=msend.at[target],
            recv_sem=mrecv.at[me],
            device_id={"fsdp": target},
            device_id_type=MESH,
        )

    for m in range(shards - 1, 0, -1):
        head_copy(m).start()
    grads[me] = heads_ref[me]
    dk_ref[...] = jnp.zeros(dk_ref.shape, F32)
    dv_ref[...] = jnp.zeros(dv_ref.shape, F32)

    going = Gather("fsdp", shards, columns_ref, columns, (gsend, grecv))
    late = Total(shards, groups, late_out, *sums[:5], sums[5:])

    if near:
        leaving = Scatter("fsdp", shards, outs, out_land, (osend, orecv))
        levels = len(leaving.orders[0])

        def out_level(k):
            for m in range(shards):
                for h in range(2):
                    if leaving.depth(h, m) == k:
                        leaving.reduce(h, m)

        take_outs.wait()
        out_level(0)

    low_lane = lane_of((side, LANES)) < HEAD_WIDTH
    lane = lane_of((side, LANES))
    keyed = lane_of((rows, LANES)) < HEAD_WIDTH
    first_takes, late_takes = going.halves()

    for c in reversed(range(shards)):
        take_turn = pltpu.make_async_copy(turn_ref.at[pl.ds(c * rows, rows)], turn, isem.at[0])
        take_turn.start()

        @pl.when(me != c)
        def _(c=c):
            pltpu.make_async_remote_copy(
                src_ref=heads_ref.at[c],
                dst_ref=grads.at[c],
                send_sem=asend.at[0],
                recv_sem=arecv.at[c],
                device_id={"fsdp": c},
                device_id_type=MESH,
            ).wait_recv()

        if c == shards - 1:
            going.start()
        if c == shards - 4:
            for h, m in first_takes:
                going.take(h, m)
        if c == shards - 6:
            for h, m in late_takes:
                going.take(h, m)
        if near and shards - 1 - c in (2, 4):
            out_level((shards - 1 - c) // 2)
        keys = (c + 1) * rows

        def step(u, carry, c=c, keys=keys):
            at = pl.ds(pl.multiple_of(u * side, side), side)
            grad = grads[c, at, :].astype(F32)
            both = grad * att_ref[pl.ds(pl.multiple_of(c * rows + u * side, side), side), :].astype(F32)
            stack = []
            for h in range(heads):
                mine = low_lane if h == 0 else ~low_lane
                delta = jnp.sum(jnp.where(mine, both, 0.0), axis=1, keepdims=True)
                hi, mid, lo = splits(-delta)
                extra = jnp.where(lane == 0, hi, jnp.where(lane == 1, mid, jnp.where(lane == 2, lo, 0.0)))
                stack.append(
                    jnp.concatenate([jnp.where(mine, grad, 0.0).astype(BF), extra.astype(BF)], axis=1)
                )
            do = jnp.concatenate(stack, axis=0) if heads > 1 else stack[0]
            queries = q_ref[c * nparts + u]
            weights = jnp.exp(dot(k_ref[0:keys, :], queries, 1, 1))
            seen = row_of((rows, cols)) <= lane_of((rows, cols)) % side + u * side
            final = jnp.where(seen, weights[keys - rows :], 0.0)
            weights = jnp.concatenate([weights[: keys - rows], final], axis=0) if c else final
            slope = (weights * dot(v_ref[0:keys, :], do, 1, 1)).astype(BF)
            dv_ref[0:keys, :] += dot(weights.astype(BF), do[:, :LANES])
            dk_ref[0:keys, :] += dot(slope, queries[:, :LANES])
            dq = dot(slope, k_ref[0:keys, :LANES], 0, 0)
            dq = dq if heads == 1 else jnp.where(low_lane, dq[:side], dq[side:])
            dq_ref[at, :] = dq * (HEAD_WIDTH ** -0.5)
            return carry

        lax.fori_loop(0, nparts, step, 0)

        block = pl.ds(c * rows, rows)
        dk, dv = dk_ref[block, :], dv_ref[block, :]
        other = jnp.where(
            keyed, dk + pltpu.roll(dk, HEAD_WIDTH, 1), dv + pltpu.roll(dv, HEAD_WIDTH, 1)
        )
        take_turn.wait()
        cosine, sine = turn[:, :LANES], turn[:, LANES:]
        mixes[c, :, :LANES] = turned(dq_ref[...], cosine, -sine).astype(BF)
        mixes[c, :, LANES:] = turned(
            other, jnp.where(keyed, cosine, 1.0), jnp.where(keyed, -sine, 0.0)
        ).astype(BF)

        @pl.when(me != c)
        def _(c=c):
            home_copy(c).start()

    if shards < 8:
        for h, m in first_takes + late_takes:
            going.take(h, m)
    for h in range(2):
        for m in span(going.orders[h][:-1]):
            going.incoming(h, m ^ going.orders[h][-1]).wait_recv()

    landed[me] = mixes[me]
    if near:
        columns[me] = columns_ref[...]
    else:
        keep = pltpu.make_async_copy(columns_ref, columns.at[me], isem.at[3])
        keep.start()
        keep.wait()
    for take in takes:
        take.wait()
    own_mask = own_mask_ref[...].astype(F32)
    x = x_ref[...].astype(F32)
    r1 = lax.rsqrt(jnp.mean(x * x, axis=1, keepdims=True) + EPSILON)
    gain = gain_row(small_ref[...], 16)
    normed = (x * r1 * gain).astype(BF)
    for m in range(1, shards):
        pltpu.make_async_remote_copy(
            src_ref=mixes.at[0],
            dst_ref=landed.at[me ^ m],
            send_sem=msend.at[0],
            recv_sem=mrecv.at[me ^ m],
            device_id={"fsdp": me ^ m},
            device_id_type=MESH,
        ).wait_recv()
    query_grad, normed_grad = [], jnp.zeros((rows, MODEL_WIDTH), F32)
    for s in range(shards):
        if near:
            weight = columns[s]
        else:
            fetch = pltpu.make_async_copy(columns.at[s], near_columns, isem.at[3])
            fetch.start()
            fetch.wait()
            weight = near_columns[...]
        normed_grad = normed_grad + dot(landed[s], weight, 1, 1)
        query = landed[s, :, :LANES]
        if heads == 2:
            query_grad.append(query)
        elif s % 2 == 0:
            then = pltpu.roll(landed[s + 1, :, :LANES].astype(F32), HEAD_WIDTH, 1)
            query_grad.append(jnp.where(keyed, query.astype(F32), then).astype(BF))

    def pair_of(head):
        pair = jnp.zeros((rows, LANES), F32)
        for s in range(head * share, (head + 1) * share):
            pair = pair + landed[s, :, LANES:].astype(F32)
        return pair

    keys_grad, values_grad = [], []
    for head in range(0, KEY_VALUE_HEADS, 2):
        one, two = pair_of(head), pair_of(head + 1)
        keys_grad.append(jnp.where(keyed, one, pltpu.roll(two, HEAD_WIDTH, 1)).astype(BF))
        values_grad.append(jnp.where(keyed, pltpu.roll(one, HEAD_WIDTH, 1), two).astype(BF))
    whole = [jnp.concatenate(part, axis=1) for part in (query_grad, keys_grad, values_grad)]
    seconds = (wide_ref[0], kv_ref[0], kv_ref[1])
    firsts = []
    for s in range(3):
        firsts.append((dot(whole[s], seconds[s], 1, 1) * own_mask).astype(BF))
        normed_grad = normed_grad + dot(firsts[s], factors_ref[s], 1, 1)

    packed, share_rows = [], late_part.shape[1]
    gfirst = dot(normed, jnp.concatenate(firsts, axis=1), 0, 0).astype(BF)
    packed += [gfirst[:, s * LANES : (s + 1) * LANES] for s in range(3)]
    for s in range(3):
        second = dot(low[:, s * LANES : (s + 1) * LANES], whole[s], 0, 0).astype(BF)
        packed += [second[:, j : j + LANES] for j in range(0, second.shape[1], LANES)]
    pack(late_part, packed, share_rows)
    late.next()
    w1 = gain * normed_grad
    xgrad_ref[...] = (
        hgrad_ref[...] + r1 * w1 - x * (r1 * r1 * r1) * jnp.mean(w1 * x, axis=1, keepdims=True)
    )
    late.next(2)
    layer = base_ref[...]
    if near:
        for k in range(3, levels + 1):
            out_level(k)
        layer = layer + outs[me].astype(F32)
    layer_ref[...] = layer.astype(layer_ref.dtype)
    late.next(99)

    for m in range(1, shards):
        head_copy(m).wait_send()
    for c in range(shards):

        @pl.when(me != c)
        def _(c=c):
            home_copy(c).wait_send()

    going.finish()
    if near:
        leaving.finish()


def pieces_of(first, size, share):
    parts, done = [], 0
    while done < size:
        block, row = divmod(first + done, share)
        length = min(size - done, share - row)
        parts.append((block, row, done, length))
        done += length
    return parts


def pack(target, arrays, share):
    first = 0
    for array in arrays:
        for block, row, done, length in pieces_of(first, array.shape[0], share):
            target[block, row : row + length, :] = array[done : done + length]
        first += array.shape[0]
    total = target.shape[0] * share
    for block, row, _, length in pieces_of(first, total - first, share):
        target[block, row : row + length, :] = jnp.zeros((length, LANES), BF)


def unpack(source, first, size):
    parts = pieces_of(first, size, source.shape[1])
    parts = [source[block, row : row + length, :] for block, row, _, length in parts]
    return parts[0] if len(parts) == 1 else jnp.concatenate(parts, axis=0)


def unpack_kernel(late_out, early_out, gfactor_ref, gdown_ref, gwide_ref, gkv_ref, gff_ref, groute_ref):
    def read(source, first, size):
        return unpack(source, first, size).astype(F32)

    for s in range(3):
        gfactor_ref[s] = read(late_out, s * MODEL_WIDTH, MODEL_WIDTH)
        gfactor_ref[3 + s] = read(early_out, s * MODEL_WIDTH, MODEL_WIDTH)
    gfactor_ref[6] = read(early_out, 3 * MODEL_WIDTH, MODEL_WIDTH)
    edge = 4 * MODEL_WIDTH
    gdown_ref[...] = read(early_out, edge, HIDDEN_UNITS)
    edge += HIDDEN_UNITS
    for s in range(2):
        for j in range(4):
            gff_ref[s, :, j * LANES : (j + 1) * LANES] = read(early_out, edge, STACKED)
            edge += STACKED
    for s in range(2):
        for j in range(8):
            gwide_ref[1 + s, :, j * LANES : (j + 1) * LANES] = read(early_out, edge, STACKED)
            edge += STACKED
    groute_ref[...] = read(early_out, edge, STACKED)
    edge = 3 * MODEL_WIDTH
    for j in range(8):
        gwide_ref[0, :, j * LANES : (j + 1) * LANES] = read(late_out, edge, STACKED)
        edge += STACKED
    for s in range(2):
        for j in range(4):
            gkv_ref[s, :, j * LANES : (j + 1) * LANES] = read(late_out, edge, STACKED)
            edge += STACKED

def unpack_all(late, early):
    return pl.pallas_call(
        unpack_kernel,
        out_shape=(
            jax.ShapeDtypeStruct((7, MODEL_WIDTH, STACKED), F32),
            jax.ShapeDtypeStruct((HIDDEN_UNITS, STACKED), F32),
            jax.ShapeDtypeStruct((3, STACKED, MODEL_WIDTH), F32),
            jax.ShapeDtypeStruct((2, STACKED, HIDDEN_UNITS), F32),
            jax.ShapeDtypeStruct((2, STACKED, HIDDEN_UNITS), F32),
            jax.ShapeDtypeStruct((STACKED, LANES), F32),
        ),
        in_specs=[IN_VMEM] * 2,
        out_specs=(IN_VMEM,) * 6,
        compiler_params=pltpu.CompilerParams(vmem_limit_bytes=40 << 20),
        name="unpack_all",
    )(late, early)


def leave(to_heads, q, k, v, att, columns, x, small, factors, wide, kv_second, hgrad, base, low, turn, mask, outs, identity):
    shards, groups = lax.axis_size("fsdp"), lax.axis_size("dp")
    rows = x.shape[0]
    near = shards <= 8
    total = shards * rows
    return pl.pallas_call(
        functools.partial(leave_kernel, shards, groups),
        out_shape=(
            jax.ShapeDtypeStruct((rows, MODEL_WIDTH), BF if near else F32),
            jax.ShapeDtypeStruct((rows, MODEL_WIDTH), F32),
            jax.ShapeDtypeStruct((shards, total_length(LATE) // shards, LANES), BF),
            jax.ShapeDtypeStruct((16, LANES) if near else (shards, MODEL_WIDTH, 2 * LANES), BF),
        ),
        in_specs=[IN_VMEM] * 13 + [ANYWHERE] * 4,
        out_specs=(IN_VMEM, IN_VMEM, IN_VMEM, ANYWHERE),
        scratch_shapes=[
            pltpu.VMEM((shards, rows, LANES), BF),
            pltpu.VMEM((total, LANES), F32),
            pltpu.VMEM((total, LANES), F32),
            pltpu.VMEM((rows, LANES), F32),
            pltpu.VMEM((shards, rows, 2 * LANES), BF),
            pltpu.VMEM((shards, rows, 2 * LANES), BF),
            pltpu.VMEM((shards, MODEL_WIDTH, 2 * LANES) if near else (MODEL_WIDTH, 2 * LANES), BF),
            pltpu.VMEM((rows, 3 * STACKED), BF),
            pltpu.VMEM((rows, 2 * LANES), F32),
            pltpu.VMEM((rows, STACKED), BF),
            pltpu.VMEM((shards, rows, MODEL_WIDTH) if near else (2, 32, LANES), BF),
            pltpu.VMEM((2, shards - 1, rows // 2, MODEL_WIDTH) if near else (2, 2, 32, LANES), BF),
        ]
        + [pltpu.SemaphoreType.DMA((shards,))] * 4
        + pair_of_sems(shards) * 2
        + [pltpu.SemaphoreType.DMA((4,))]
        + total_scratch(shards, groups, total_length(LATE))[1:],
        compiler_params=remote(identity, 62),
        name="leave",
    )(to_heads, q, k, v, att, columns, x, small, factors, wide, kv_second, hgrad, base, low, turn, mask, outs)


def local(
    tokens,
    cotangent,
    lengths,
    adapter_index,
    routes,
    deal,
    norm_gain_pair,
    query_weight,
    key_weight,
    value_weight,
    output_weight_transposed,
    router_weight,
    expert_input_weight,
    expert_output_weight,
    factors,
    down_first,
    wide,
    kv_second,
    hidden_second,
    router_second,
):
    shards = lax.axis_size("fsdp")
    groups = lax.axis_size("dp")
    rows = tokens.shape[0]
    total = rows * shards
    heads = HEADS // shards
    share = max(1, shards // KEY_VALUE_HEADS)
    me = lax.axis_index("fsdp")

    padded = ((0, 0), (0, rows - lengths.shape[1]))
    meta = jnp.concatenate(
        [
            routes.T,
            jnp.pad(lengths, padded),
            jnp.pad(adapter_index, padded),
            jnp.zeros((6, rows), jnp.int32),
        ],
        axis=0,
    )
    small = jnp.concatenate(
        [
            router_weight,
            norm_gain_pair,
            jnp.zeros((router_weight.shape[0], LANES - EXPERT_COUNT - 2), BF),
        ],
        axis=1,
    )
    qkv, low_all, group_mask, small, meta, columns, turn = enter(
        deal,
        tokens,
        query_weight,
        key_weight,
        value_weight,
        small,
        meta,
        factors,
        wide,
        kv_second,
        1,
    )
    win = expert_input_weight.reshape(MODEL_WIDTH, -1)
    wout = expert_output_weight.reshape(MODEL_WIDTH, -1)
    out_weight = lax.all_gather(output_weight_transposed, ("dp", "fsdp"), axis=0, tiled=True)
    mine, attended, q_kept, k_kept, v_kept, all_grad = attend(meta, qkv, cotangent, heads, 5)
    router2 = jnp.pad(router_second, ((0, 0), (0, LANES - EXPERT_COUNT)))
    (
        base,
        out_part,
        hidden_grad,
        to_heads,
        early,
    ) = middle(
        mine,
        tokens,
        small,
        meta,
        group_mask,
        out_weight,
        factors,
        wide,
        router2,
        hidden_second,
        down_first,
        all_grad,
        win,
        wout,
        6,
    )
    early_sum = lax.psum(early, ("dp", "fsdp"))
    layer_out, input_grad, late, _ = leave(
        to_heads,
        q_kept,
        k_kept,
        v_kept,
        attended,
        columns,
        tokens,
        small,
        factors,
        wide,
        kv_second,
        hidden_grad,
        base,
        low_all,
        turn,
        group_mask,
        out_part,
        7,
    )
    if shards > 8:
        layer_out = (layer_out + scatter(out_part, "fsdp", 8).astype(F32)).astype(BF)
    g_factors, g_down, g_wide, g_kv, g_ff, g_route = unpack_all(late, early_sum)
    return (
        layer_out,
        input_grad,
        g_factors,
        g_down,
        g_wide,
        g_kv,
        g_ff,
        g_route[:, :EXPERT_COUNT],
    )


def solution(mesh):
    rows = P(("dp", "fsdp"), None)
    placed = (
        (rows, rows, P("dp", None), P("dp", None), rows, P())
        + (rows,) * 6
        + (P(None, "fsdp", None),) * 2
        + (P(),) * 6
    )
    return jax.shard_map(
        local,
        mesh=mesh,
        in_specs=placed,
        out_specs=(rows, rows) + (P(),) * 6,
        check_vma=False,
    )
```

```python
import functools
import math

import jax
import jax.numpy as jnp
import numpy as np
from jax import lax
from jax.experimental import pallas as pl
from jax.experimental.pallas import tpu as pltpu
from jax.sharding import PartitionSpec as P

MODEL_WIDTH = 1024
HEADS = 16
KEY_VALUE_HEADS = 8
HEAD_WIDTH = 64
HIDDEN_UNITS = 512
TOPK = 8
EXPERT_COUNT = 16
ADAPTER_COUNT = 8
ADAPTER_RANK = 16
STACKED = ADAPTER_COUNT * ADAPTER_RANK

EPSILON = 1e-06
ROPE_BASE = 10000.0
MASKED = -1e30
LANES = 128
PART = 128
NSEQ = 4

BF = jnp.bfloat16
F32 = jnp.float32
MESH = pl.DeviceIdType.MESH


def dot(a, b, ca=1, cb=0):
    return lax.dot_general(a, b, (((ca,), (cb,)), ((), ())), preferred_element_type=F32)


def splits(v):
    hi = v.astype(BF).astype(F32)
    rest = v - hi
    mid = rest.astype(BF).astype(F32)
    return hi, mid, rest - mid


def lane_of(shape):
    return lax.broadcasted_iota(jnp.int32, shape, len(shape) - 1)


def row_of(shape):
    return lax.broadcasted_iota(jnp.int32, shape, 0)


def bits_of(count):
    return [1 << k for k in range(count.bit_length() - 1)]


def orders_of(count):
    bits = bits_of(count)
    far = bits[1:]
    cut = (len(far) + 1) // 2
    return (far + bits[:1], far[cut:] + far[:cut] + bits[:1])


def span(bits):
    masks = [0]
    for bit in bits:
        masks = masks + [m ^ bit for m in masks]
    return masks


def greet(meetings):
    barrier = pltpu.get_barrier_semaphore()
    count = 0
    for axis, me, masks in meetings:
        for mask in masks:
            pl.semaphore_signal(
                barrier, inc=1, device_id={axis: me ^ mask}, device_id_type=MESH
            )
            count += 1
    pl.semaphore_wait(barrier, count)


class Gather:
    def __init__(self, axis, count, own, store, sems):
        self.axis, self.count, self.own, self.store = axis, count, own, store
        self.sends, self.recvs = sems
        self.me = lax.axis_index(axis)
        self.orders = orders_of(count)
        self.half = store.shape[1] // 2

    def copy(self, h, mask, bit):
        rows = pl.ds(h * self.half, self.half)
        there = self.store.at[self.me ^ mask, rows]
        return pltpu.make_async_remote_copy(
            src_ref=self.own.at[rows] if mask == 0 else there,
            dst_ref=there,
            send_sem=self.sends.at[h, mask ^ bit],
            recv_sem=self.recvs.at[h, mask ^ bit],
            device_id={self.axis: self.me ^ bit},
            device_id_type=MESH,
        )

    def incoming(self, h, mask):
        there = self.store.at[self.me ^ mask, pl.ds(h * self.half, self.half)]
        return pltpu.make_async_remote_copy(
            src_ref=there,
            dst_ref=there,
            send_sem=self.sends.at[h, mask],
            recv_sem=self.recvs.at[h, mask],
            device_id={self.axis: self.me ^ mask},
            device_id_type=MESH,
        )

    def start(self):
        for k in range(len(self.orders[0])):
            for h in range(2):
                self.copy(h, 0, self.orders[h][k]).start()

    def take(self, h, mask):
        order = self.orders[h]
        self.incoming(h, mask).wait_recv()
        k = max(i for i, bit in enumerate(order) if mask & bit)
        for bit in order[k + 1 :]:
            self.copy(h, mask, bit).start()

    def halves(self):
        early, late = [], []
        for k in range(len(self.orders[0]) - 1):
            for s in range(1 << k):
                for h in range(2):
                    mask = self.orders[h][k] ^ span(self.orders[h][:k])[s]
                    (late if self.count == 8 and k == 1 and s else early).append((h, mask))
        return early, late

    def stage(self, k):
        for s in range(1 << k):
            for h in range(2):
                order = self.orders[h]
                mask = order[k] ^ span(order[:k])[s]
                self.incoming(h, mask).wait_recv()
                for bit in order[k + 1 :]:
                    self.copy(h, mask, bit).start()

    def held(self, k):
        sets = [set(span(order[: k + 1])) for order in self.orders]
        return sets[0] & sets[1]

    def stages(self):
        for k in range(len(self.orders[0])):
            self.stage(k)

    def finish(self):
        for h in range(2):
            for mask in range(1, self.count):
                self.incoming(h, mask).wait_send()


class Scatter:
    def __init__(self, axis, count, part, land, sems):
        self.axis, self.count, self.part, self.land = axis, count, part, land
        self.sends, self.recvs = sems
        self.me = lax.axis_index(axis)
        self.orders = [order[::-1] for order in orders_of(count)]
        self.half = part.shape[1] // 2

    def depth(self, h, mask):
        for k, bit in enumerate(self.orders[h]):
            if mask & bit:
                return k
        return len(self.orders[h])

    def copy(self, h, mask):
        bit = self.orders[h][self.depth(h, mask)]
        return pltpu.make_async_remote_copy(
            src_ref=self.part.at[self.me ^ mask, pl.ds(h * self.half, self.half)],
            dst_ref=self.land.at[h, mask - 1],
            send_sem=self.sends.at[h, mask],
            recv_sem=self.recvs.at[h, mask],
            device_id={self.axis: self.me ^ bit},
            device_id_type=MESH,
        )

    def reduce(self, h, mask):
        depth = self.depth(h, mask)
        sources = [mask ^ bit for bit in self.orders[h][:depth]]
        for source in sources:
            self.copy(h, source).wait_recv()
        if sources:
            step = math.gcd(self.half, 64)
            mine = self.me ^ mask

            def add(c, carry):
                here = pl.ds(pl.multiple_of(c * step, step), step)
                at = pl.ds(pl.multiple_of(h * self.half + c * step, step), step)
                total = self.part[mine, at].astype(F32)
                for source in sources:
                    total = total + self.land[h, source - 1, here].astype(F32)
                self.part[mine, at] = total.astype(BF)
                return carry

            lax.fori_loop(0, self.half // step, add, 0)
        if mask:
            self.copy(h, mask).start()

    def run(self):
        for k in range(len(self.orders[0]) + 1):
            for mask in range(self.count):
                for h in range(2):
                    if self.depth(h, mask) == k:
                        self.reduce(h, mask)

    def finish(self):
        for h in range(2):
            for mask in range(1, self.count):
                self.copy(h, mask).wait_send()


def pair_of_sems(count):
    return [pltpu.SemaphoreType.DMA((2, count)), pltpu.SemaphoreType.DMA((2, count))]


ANYWHERE = pl.BlockSpec(memory_space=pl.ANY)
IN_VMEM = pl.BlockSpec(memory_space=pltpu.VMEM)


def remote(identity, limit=48):
    return pltpu.CompilerParams(
        collective_id=identity, has_side_effects=True, vmem_limit_bytes=limit << 20
    )


def scatter_kernel(axis, count, given, total, part, land, sends, recvs, local_sem):
    me = lax.axis_index(axis)
    take = pltpu.make_async_copy(given, part, local_sem)
    take.start()
    greet([(axis, me, bits_of(count))])
    moving = Scatter(axis, count, part, land, (sends, recvs))
    take.wait()
    moving.run()
    total[...] = part[me]
    moving.finish()


def scatter(blocks, axis, identity):
    count, rows, columns = blocks.shape
    return pl.pallas_call(
        functools.partial(scatter_kernel, axis, count),
        out_shape=jax.ShapeDtypeStruct((rows, columns), BF),
        in_specs=[ANYWHERE],
        out_specs=IN_VMEM,
        scratch_shapes=[
            pltpu.VMEM(blocks.shape, BF),
            pltpu.VMEM((2, count - 1, rows // 2, columns), BF),
        ]
        + pair_of_sems(count)
        + [pltpu.SemaphoreType.DMA(())],
        compiler_params=remote(identity, 56),
        name="scatter",
    )(blocks)


def attend_kernel(
    shards,
    near,
    heads,
    meta_ref,
    qkv_ref,
    cot_ref,
    mine_ref,
    out_ref,
    q_ref,
    k_ref,
    v_ref,
    cots_ref,
    gsend,
    grecv,
    asend,
    arecv,
    keep_sem,
):
    me = lax.axis_index("fsdp")
    total = qkv_ref.shape[0]
    nseq = NSEQ
    keep = pltpu.make_async_copy(cot_ref, cots_ref.at[me], keep_sem)
    keep.start()
    greet([("fsdp", me, range(1, shards))])
    going = Gather("fsdp", shards, cot_ref, cots_ref, (gsend, grecv))
    going.start()
    early, late = going.halves()
    edges = [jnp.zeros((1, 1), jnp.int32)]
    for s in range(nseq):
        edges.append(edges[-1] + meta_ref[8:9, s : s + 1])
    half = HEAD_WIDTH
    side = PART

    def prepare(i, carry):
        at = pl.ds(pl.multiple_of(i * side, side), side)
        low = lane_of((side, LANES)) < half
        lane = lane_of((side, LANES))
        row = row_of((side, LANES)) + i * side
        seq = jnp.zeros((side, LANES), jnp.bool_)
        for s in range(nseq):
            seq = seq | ((lane == s) & (row >= edges[s]) & (row < edges[s + 1]))
        queries = qkv_ref[at, 0:LANES].astype(F32) * (HEAD_WIDTH ** -0.5)
        pair = qkv_ref[at, LANES : 2 * LANES].astype(F32)
        swapped = pltpu.roll(pair, half, 1)
        marks = jnp.where(seq, 1.0, 0.0).astype(BF)
        for h in range(heads):
            mine = jnp.where(low if h == 0 else ~low, queries, 0.0).astype(BF)
            q_ref[i, h * side : (h + 1) * side, 0:LANES] = mine
            q_ref[i, h * side : (h + 1) * side, LANES : 2 * LANES] = marks
        k_ref[at, 0:LANES] = jnp.where(low, pair, swapped).astype(BF)
        far = jnp.where(lane < nseq, jnp.where(seq, 0.0, MASKED), 0.0)
        k_ref[at, LANES : 2 * LANES] = jnp.where(
            (lane >= nseq) & (lane < nseq + 3), 1.0, far
        ).astype(BF)
        v_ref[at, 0:LANES] = jnp.where(low, swapped, pair).astype(BF)
        v_ref[at, LANES : 2 * LANES] = jnp.ones((side, LANES), BF)
        return carry

    lax.fori_loop(0, total // side, prepare, 0)

    rows = 3 * side

    def place(ref, source):
        if near:
            return ref.at[:, pl.ds(pl.multiple_of(source * LANES, LANES), LANES)]
        return ref.at[source]

    def home_copy(target):
        return pltpu.make_async_remote_copy(
            src_ref=out_ref.at[pl.ds(target * rows, rows)],
            dst_ref=place(mine_ref, me),
            send_sem=asend.at[target],
            recv_sem=arecv.at[me],
            device_id={"fsdp": target},
            device_id_type=MESH,
        )

    low = lane_of((rows, LANES)) < half
    lane = lane_of((rows, LANES))
    visible = lane_of((rows, rows)) <= row_of((rows, rows))
    for i in range(total // rows):
        keys = (i + 1) * rows
        at = pl.ds(i * rows, rows)
        mixed = []
        for h in range(heads):
            mine = pl.ds(h * side, side)
            queries = jnp.concatenate([q_ref[3 * i + u, mine, :] for u in range(3)], axis=0)
            scores = dot(queries, k_ref[0:keys, :], 1, 1)
            final = jnp.where(visible, scores[:, keys - rows :], MASKED)
            if i:
                scores = jnp.concatenate([scores[:, : keys - rows], final], axis=1)
            else:
                scores = final
            top = jnp.max(scores, axis=1, keepdims=True)
            weights = jnp.exp(scores - top).astype(BF)
            acc = dot(weights, v_ref[0:keys, :])
            weight = acc[:, LANES:]
            mixed.append(acc[:, :LANES] / weight)
            hi, mid, lo = splits(-(top + jnp.log(weight)))
            marks = queries[:, LANES:].astype(F32)
            marks = jnp.where(lane == nseq, hi, marks)
            marks = jnp.where(lane == nseq + 1, mid, marks)
            marks = jnp.where(lane == nseq + 2, lo, marks).astype(BF)
            for u in range(3):
                q_ref[3 * i + u, mine, LANES:] = marks[u * side : (u + 1) * side]
        value = mixed[0] if heads == 1 else jnp.where(low, mixed[0], mixed[1])
        out_ref[at, :] = value.astype(BF)

        @pl.when(me != i)
        def _(i=i):
            home_copy(i).start()

        if i == shards - 2:
            for h, m in early:
                going.take(h, m)

    place(mine_ref, me)[...] = out_ref[pl.ds(pl.multiple_of(me * rows, rows), rows), :]
    for h, m in late:
        going.take(h, m)
    for m in range(1, shards):
        pltpu.make_async_remote_copy(
            src_ref=out_ref.at[pl.ds(0, rows)],
            dst_ref=place(mine_ref, me ^ m),
            send_sem=asend.at[0],
            recv_sem=arecv.at[me ^ m],
            device_id={"fsdp": me ^ m},
            device_id_type=MESH,
        ).wait_recv()
    for i in range(shards):

        @pl.when(me != i)
        def _(i=i):
            home_copy(i).wait_send()

    for h in range(2):
        for m in span(going.orders[h][:-1]):
            going.incoming(h, m ^ going.orders[h][-1]).wait_recv()
    going.finish()
    keep.wait()


def attend(meta, qkv, cot, heads, identity):
    shards = lax.axis_size("fsdp")
    near = shards <= 8
    total = qkv.shape[0]
    rows = total // shards
    return pl.pallas_call(
        functools.partial(attend_kernel, shards, near, heads),
        out_shape=(
            jax.ShapeDtypeStruct((rows, MODEL_WIDTH) if near else (shards, rows, LANES), BF),
            jax.ShapeDtypeStruct((total, LANES), BF),
            jax.ShapeDtypeStruct((total // PART, heads * PART, 2 * LANES), BF),
            jax.ShapeDtypeStruct((total, 2 * LANES), BF),
            jax.ShapeDtypeStruct((total, 2 * LANES), BF),
            jax.ShapeDtypeStruct((shards,) + cot.shape, BF),
        ),
        in_specs=[IN_VMEM, IN_VMEM, ANYWHERE],
        out_specs=(IN_VMEM,) * 5 + (ANYWHERE,),
        scratch_shapes=pair_of_sems(shards)
        + [pltpu.SemaphoreType.DMA((shards,))] * 2
        + [pltpu.SemaphoreType.DMA(())],
        compiler_params=remote(identity, 60),
        name="attend",
    )(meta, qkv, cot)


def sequences(meta, first, rows, heads_of):
    row = row_of((rows, LANES)) + first
    start = jnp.zeros((1, 1), jnp.int32)
    picked = [jnp.zeros((rows, LANES), part[0].dtype) for part in heads_of]
    for s in range(len(heads_of[0])):
        inside = row >= start
        picked = [jnp.where(inside, part[s], value) for part, value in zip(heads_of, picked)]
        start = start + meta[8:9, s : s + 1]
    return picked


def turned(tensor, cosine, sine):
    lower = lane_of(tensor.shape) % HEAD_WIDTH < HEAD_WIDTH // 2
    other = jnp.where(lower, pltpu.roll(tensor, LANES - 32, 1), pltpu.roll(tensor, 32, 1))
    return tensor * cosine + other * sine


def head_columns(wide, narrow, pick_wide, pick_narrow, heads):
    low = lane_of((1, LANES)) < HEAD_WIDTH
    queries = wide
    if heads == 1:
        queries = jnp.where(low, jnp.where(pick_wide, pltpu.roll(wide, HEAD_WIDTH, 1), wide), 0.0)
    keys, values = narrow
    keys = jnp.where(pick_narrow, pltpu.roll(keys, HEAD_WIDTH, 1), keys)
    values = jnp.where(pick_narrow, values, pltpu.roll(values, HEAD_WIDTH, 1))
    return queries, jnp.where(low, keys, values)


def enter_kernel(
    shards,
    groups,
    deal_ref,
    x_ref,
    wq_ref,
    wk_ref,
    wv_ref,
    small_ref,
    meta_ref,
    factors_ref,
    wide_ref,
    kv_ref,
    cos_ref,
    sin_ref,
    freq_ref,
    qkv_ref,
    low_ref,
    mask_ref,
    small_out,
    meta_out,
    columns_out,
    turn_ref,
    xs,
    slices,
    weights,
    metas,
    merged,
    second,
    xsend,
    xrecv,
    wsend,
    wrecv,
    zsend,
    zrecv,
    msend,
    mrecv,
):
    me, plane = lax.axis_index("fsdp"), lax.axis_index("dp")
    heads = HEADS // shards
    share = max(1, shards // KEY_VALUE_HEADS)
    rows = x_ref.shape[0]
    part = wq_ref.shape[0]
    order = [mask for mask in range(1, shards)]

    for f in range(shards):
        chunk = f * heads * HEAD_WIDTH // LANES
        head = f // share
        pair = head // 2
        queries, others = head_columns(
            wq_ref[:, chunk * LANES : (chunk + 1) * LANES].astype(F32),
            (
                wk_ref[:, pair * LANES : (pair + 1) * LANES].astype(F32),
                wv_ref[:, pair * LANES : (pair + 1) * LANES].astype(F32),
            ),
            f % 2 == 1,
            head % 2 == 1,
            heads,
        )
        slices[f, :, 0:LANES] = queries.astype(BF)
        slices[f, :, LANES : 2 * LANES] = others.astype(BF)
        slices[f, :, 2 * LANES :] = small_ref[...]
    metas[plane] = meta_ref[...]

    greet([("fsdp", me, order), ("dp", plane, range(1, groups))])

    moving = Gather("fsdp", shards, x_ref, xs, (xsend, xrecv))
    plane_rows = shards * part

    def column_copy(mask):
        return pltpu.make_async_remote_copy(
            src_ref=slices.at[me ^ mask],
            dst_ref=weights.at[plane, me],
            send_sem=wsend.at[mask],
            recv_sem=wrecv.at[mask],
            device_id={"fsdp": me ^ mask},
            device_id_type=MESH,
        )

    def plane_copy(mask):
        return pltpu.make_async_remote_copy(
            src_ref=weights.at[plane],
            dst_ref=weights.at[plane],
            send_sem=zsend.at[mask],
            recv_sem=zrecv.at[mask],
            device_id={"dp": plane ^ mask},
            device_id_type=MESH,
        )

    def meta_copy(mask):
        return pltpu.make_async_remote_copy(
            src_ref=meta_ref,
            dst_ref=metas.at[plane],
            send_sem=msend.at[mask],
            recv_sem=mrecv.at[mask],
            device_id={"dp": plane ^ mask},
            device_id_type=MESH,
        )

    for mask in order:
        column_copy(mask).start()
    for mask in range(1, groups):
        meta_copy(mask).start()
    moving.start()
    weights[plane, me] = slices[me]

    half = HEAD_WIDTH
    at = pl.ds(pl.multiple_of(me * heads * half // LANES * LANES, LANES), LANES)
    head = me // share
    pair_at = pl.ds(pl.multiple_of(head // 2 * LANES, LANES), LANES)
    queries, others = head_columns(
        wide_ref[0, :, at].astype(F32),
        (kv_ref[0, :, pair_at].astype(F32), kv_ref[1, :, pair_at].astype(F32)),
        me % 2 == 1,
        head % 2 == 1,
        heads,
    )
    low_lane = lane_of((STACKED, LANES)) < half
    second[...] = jnp.zeros(second.shape, BF)
    second[0:STACKED, 0:LANES] = queries.astype(BF)
    second[STACKED : 2 * STACKED, LANES:] = jnp.where(low_lane, others, 0.0).astype(BF)
    second[2 * STACKED :, LANES:] = jnp.where(low_lane, 0.0, others).astype(BF)

    for mask in order:
        column_copy(mask).wait_recv()
    for mask in range(1, groups):
        plane_copy(mask).start()
    for mask in range(1, groups):
        meta_copy(mask).wait_recv()
    dealt = jnp.int32(0)
    for g in range(groups):
        dealt = dealt + jnp.where(deal_ref[g] == plane, g, 0)
    meta = jnp.zeros(meta_ref.shape, jnp.int32)
    for g in range(groups):
        meta = jnp.where(dealt == g, metas[g], meta)
    meta_out[...] = meta
    moving.stage(0)
    for mask in range(1, groups):
        plane_copy(mask).wait_recv()

    for g in range(groups):
        for f in range(shards):
            here = pl.ds((g * shards + f) * part, part)
            block = weights[g, f]
            small_out[here, :] = block[:, 2 * LANES :]
            merged[here, 0 : 2 * LANES] = block[:, : 2 * LANES]
            columns_out[here, :] = block[:, : 2 * LANES]
    for s in range(3):
        merged[:, (2 + s) * LANES : (3 + s) * LANES] = factors_ref[s]
    gain = gain_row(small_out[...], 16)

    nseq = NSEQ
    lanes = lane_of((1, LANES))
    starts, first = [], jnp.zeros((1, 1), jnp.int32)
    for s in range(nseq):
        starts.append(first)
        first = first + meta[8:9, s : s + 1]
    angles = [start.astype(F32) * freq_ref[...] for start in starts]
    start_cos = [jnp.cos(angle) for angle in angles]
    start_sin = [jnp.sin(angle) for angle in angles]
    adapters = [jnp.broadcast_to(meta[9:10, s : s + 1], (1, LANES)) for s in range(nseq)]
    keyed = lanes < half
    sign = jnp.where(lanes % half < half // 2, -1.0, 1.0)

    def compute(mask):
        block = me ^ mask
        at = pl.ds(pl.multiple_of(block * rows, rows), rows)
        x = x_ref[...] if mask == 0 else xs[block]
        full = x.astype(F32)
        r1 = lax.rsqrt(jnp.mean(full * full, axis=1, keepdims=True) + EPSILON)
        product = dot((full * r1 * gain).astype(BF), merged[...])
        base_cos, base_sin, pick = sequences(
            meta, block * rows, rows, (start_cos, start_sin, adapters)
        )
        masked = lane_of((rows, LANES)) // ADAPTER_RANK == pick
        mask_ref[at, :] = jnp.where(masked, 1.0, 0.0).astype(BF)
        lows = [
            jnp.where(masked, product[:, (2 + s) * LANES : (3 + s) * LANES], 0.0).astype(BF)
            for s in range(3)
        ]
        lows = jnp.concatenate(lows, axis=1)
        low_ref[at, :] = lows
        product = product[:, : 2 * LANES] + dot(lows, second[...])
        row_cos, row_sin = cos_ref[at, :], sin_ref[at, :]
        cosine = row_cos * base_cos + row_sin * base_sin
        sine = (row_sin * base_cos - row_cos * base_sin) * sign
        turn_ref[at, :LANES] = cosine
        turn_ref[at, LANES:] = sine
        qkv_ref[at, :LANES] = turned(product[:, :LANES], cosine, sine).astype(BF)
        others = product[:, LANES:]
        qkv_ref[at, LANES:] = turned(
            others, jnp.where(keyed, cosine, 1.0), jnp.where(keyed, sine, 0.0)
        ).astype(BF)

    compute(0)
    for h in range(2):
        moving.take(h, 1)
    compute(1)
    early, late = moving.halves()
    for h, m in early:
        if m not in (moving.orders[h][0],):
            moving.take(h, m)
    whole = [m for m in range(2, shards, 2) if all((h, m) in early for h in range(2))]
    for m in whole:
        compute(m)
    for m in whole:
        for h in range(2):
            moving.take(h, m + 1)
        compute(m + 1)
    for h, m in late:
        moving.take(h, m)
    rest = [m for m in range(2, shards, 2) if m not in whole]
    for m in rest:
        compute(m)
    for m in rest:
        for h in range(2):
            moving.take(h, m + 1)
        compute(m + 1)
    moving.finish()
    for mask in order:
        column_copy(mask).wait_send()
    for mask in range(1, groups):
        plane_copy(mask).wait_send()
        meta_copy(mask).wait_send()


def enter(deal, x, wq, wk, wv, small, meta, factors, wide, kv_second, identity):
    shards, groups = lax.axis_size("fsdp"), lax.axis_size("dp")
    rows, part = x.shape[0], wq.shape[0]
    total = rows * shards
    half = HEAD_WIDTH // 2
    frequency = ROPE_BASE ** (-np.arange(half, dtype=np.float64) / half)
    frequency = frequency.astype(np.float32)
    angles = np.arange(total, dtype=np.float64)[:, None] * frequency.astype(np.float64)[None, :]
    cosine = jnp.asarray(np.tile(np.cos(angles).astype(np.float32), (1, 4)))
    sine = jnp.asarray(np.tile(np.sin(angles).astype(np.float32), (1, 4)))
    frequency = jnp.asarray(np.tile(frequency, 4)[None, :])
    return pl.pallas_call(
        functools.partial(enter_kernel, shards, groups),
        out_shape=(
            jax.ShapeDtypeStruct((total, 2 * LANES), BF),
            jax.ShapeDtypeStruct((total, 3 * STACKED), BF),
            jax.ShapeDtypeStruct((total, STACKED), BF),
            jax.ShapeDtypeStruct((MODEL_WIDTH, LANES), BF),
            jax.ShapeDtypeStruct(meta.shape, jnp.int32),
            jax.ShapeDtypeStruct((MODEL_WIDTH, 2 * LANES), BF),
            jax.ShapeDtypeStruct((total, 2 * LANES), F32),
        ),
        in_specs=[pl.BlockSpec(memory_space=pltpu.SMEM)] + [IN_VMEM] * 12,
        out_specs=(IN_VMEM,) * 7,
        scratch_shapes=[
            pltpu.VMEM((shards, rows, MODEL_WIDTH), BF),
            pltpu.VMEM((shards, part, 3 * LANES), BF),
            pltpu.VMEM((groups, shards, part, 3 * LANES), BF),
            pltpu.VMEM((groups,) + meta.shape, jnp.int32),
            pltpu.VMEM((MODEL_WIDTH, 2 * LANES + 3 * STACKED), BF),
            pltpu.VMEM((3 * STACKED, 2 * LANES), BF),
        ]
        + pair_of_sems(shards)
        + [pltpu.SemaphoreType.DMA((shards,))] * 2
        + [pltpu.SemaphoreType.DMA((groups,))] * 4,
        compiler_params=remote(identity, 60),
        name="enter",
    )(deal, x, wq, wk, wv, small, meta, factors, wide, kv_second, cosine, sine, frequency)


def gain_row(small, lane):
    pick = jnp.where(lane_of((8, LANES)) == lane, 1.0, 0.0).astype(BF)
    return dot(pick, small, 1, 1)[0:1, :]


def turn_of(step, shards):
    if shards == 8:
        return step + step // 4 * (1 - 2 * (step % 2))
    late = (step + shards - 4) // shards
    return step + late * (shards + 3 - 2 * step)


def scatter_plan(moving, shards):
    place = {turn_of(t, shards): t for t in range(shards)}
    sent, plan = {}, []
    for t in range(shards):
        now = []
        for mask in range(1, shards):
            for h in range(2):
                sources = [mask ^ bit for bit in moving.orders[h][: moving.depth(h, mask)]]
                ready = all((h, s) in sent and sent[h, s] < t for s in sources)
                if (h, mask) not in sent and place[mask] <= t and ready:
                    now.append((h, mask))
        for item in now:
            sent[item] = t
        plan.append(now)
    rest = [(h, m) for m in range(1, shards) for h in range(2) if (h, m) not in sent]
    rest.sort(key=lambda item: moving.depth(*item))
    return plan, rest + [(0, 0), (1, 0)]


def experts_block(first_expert, n2, side, grad, mask, win, wout, wide_down, hid, down, spread, fold):
    rows = n2.shape[0]
    width = HIDDEN_UNITS
    lane = lane_of((rows, LANES))
    lows = dot(side, spread[:, : 2 * STACKED])
    low_gate = (lows[:, :STACKED] * mask).astype(BF)
    low_up = (lows[:, STACKED:] * mask).astype(BF)
    lift_gate = dot(low_gate, hid[0])
    lift_up = dot(low_up, hid[1])
    down_grad = (dot(grad, wide_down, 1, 1) * mask).astype(BF)
    from_down = dot(down_grad, down[...], 1, 1)
    side_full = side.astype(F32)
    total_inner = jnp.zeros((rows, width), F32)
    total_gate = jnp.zeros((rows, width), F32)
    total_up = jnp.zeros((rows, width), F32)
    extra = jnp.zeros((rows, LANES), F32)
    gated_parts, slope_parts = [], []
    for e in range(win.shape[1] // (2 * width)):
        name = first_expert + e
        at_high, at_low = lane == name, lane == name + EXPERT_COUNT
        gate = jnp.sum(jnp.where(at_high | at_low, side_full, 0.0), axis=1, keepdims=True)
        first = 2 * e * width
        pre_gate = dot(n2, win[:, first : first + width]) + lift_gate
        pre_up = dot(n2, win[:, first + width : first + 2 * width]) + lift_up
        pulled = dot(grad, wout[:, e * width : (e + 1) * width]) + from_down
        squashed = jax.nn.sigmoid(pre_gate)
        active = pre_gate * squashed
        inner = active * pre_up
        gate_grad = jnp.sum(inner * pulled, axis=1, keepdims=True)
        high = gate_grad.astype(BF).astype(F32)
        extra = extra + jnp.where(at_high, high, 0.0) + jnp.where(at_low, gate_grad - high, 0.0)
        gated = inner * gate
        pulled = pulled * gate
        grad_gate = pulled * pre_up * (squashed + active * (1.0 - squashed))
        grad_up = pulled * active
        gated_parts.append(gated.astype(BF))
        slope_parts += [grad_gate.astype(BF), grad_up.astype(BF)]
        total_inner = total_inner + gated
        total_gate = total_gate + grad_gate
        total_up = total_up + grad_up
    out = dot(jnp.concatenate(gated_parts, axis=1), wout[...], 1, 1)
    back = dot(jnp.concatenate(slope_parts, axis=1), win[...], 1, 1)
    total_inner = total_inner.astype(BF)
    total_gate = total_gate.astype(BF)
    total_up = total_up.astype(BF)
    shrunk = jnp.concatenate(
        [
            (dot(total_gate, hid[0], 1, 1) * mask).astype(BF),
            (dot(total_up, hid[1], 1, 1) * mask).astype(BF),
            (dot(total_inner, down[...]) * mask).astype(BF),
        ],
        axis=1,
    )
    extra = extra + dot(shrunk, fold[...])
    sums = (
        dot(total_inner, down_grad, 0, 0),
        dot(low_gate, total_gate, 0, 0),
        dot(low_up, total_up, 0, 0),
    )
    return out.astype(BF), back.astype(BF), extra.astype(BF), sums


def middle_kernel(
    shards,
    mine_ref,
    x_ref,
    small_ref,
    meta_ref,
    mask_ref,
    wo_ref,
    factors_ref,
    wide_ref,
    router2_ref,
    hid_ref,
    down_ref,
    spread_ref,
    fold_ref,
    cots_ref,
    win_ref,
    wout_ref,
    base_ref,
    outs_ref,
    hgrad_ref,
    heads_ref,
    early_ref,
    *scratch,
):
    near = shards <= 8
    store, block_in, scratch = (scratch[0], None, scratch[1:]) if near else (scratch[0], scratch[1], scratch[2:])
    middle_body(
        shards,
        near,
        (
            mine_ref,
            x_ref,
                    small_ref,
            meta_ref,
            mask_ref,
            wo_ref,
            factors_ref,
            wide_ref,
            router2_ref,
            hid_ref,
            down_ref,
            spread_ref,
            fold_ref,
            cots_ref,
            win_ref,
            wout_ref,
        ),
        (
            base_ref,
            outs_ref,
            hgrad_ref,
            heads_ref,
            early_ref,
        ),
        store,
        block_in,
        *scratch,
    )


def middle_body(
    shards,
    near,
    given,
    results,
    store,
    block_in,
    own_in,
    part,
    land,
    win,
    wout,
    cots,
    outs,
    attended,
    factors,
    gdown_ref,
    ghid_ref,
    gsend,
    grecv,
    ssend,
    srecv,
    wsem,
    csem,
    osem,
    bsem,
):
    (
        mine_ref,
        x_ref,
            small_ref,
        meta_ref,
        mask_ref,
        wo_ref,
        factors_ref,
        wide_ref,
        router2_ref,
        hid_ref,
        down_ref,
        spread_ref,
        fold_ref,
        cots_ref,
        win_ref,
        wout_ref,
    ) = given
    (
        base_ref,
        outs_ref,
        hgrad_ref,
        heads_ref,
        early_ref,
    ) = results
    me = lax.axis_index("fsdp")
    rows = x_ref.shape[0]
    if near:
        own_in = store.at[me]
    width = MODEL_WIDTH
    heads = HEADS // shards
    lane = lane_of((rows, LANES))
    loads = [
        pltpu.make_async_copy(win_ref, win, wsem.at[0]),
        pltpu.make_async_copy(wout_ref, wout, wsem.at[1]),
    ]
    fetch_factors = pltpu.make_async_copy(factors_ref.at[pl.ds(3, 4)], factors, wsem.at[2])
    fetch_factors.start()
    for load in loads:
        load.start()

    def cot_copy(step):
        return pltpu.make_async_copy(
            cots_ref.at[me ^ turn_of(step, shards)], cots.at[step % 2], csem.at[step % 2]
        )

    cot_copy(0).start()
    greet([("fsdp", me, bits_of(shards))])

    if near:
        attended = mine_ref
    else:
        for s in range(0, shards, 2):
            second = pltpu.roll(mine_ref[s + 1].astype(F32), HEAD_WIDTH, 1)
            both = jnp.where(lane < HEAD_WIDTH, mine_ref[s].astype(F32), second)
            attended[:, s // 2 * LANES : (s // 2 + 1) * LANES] = both.astype(BF)
    own = pl.ds(pl.multiple_of(me * rows, rows), rows)
    mask = mask_ref[own, :].astype(F32)
    small = small_ref[...]
    gain = gain_row(small, 17)
    fetch_factors.wait()
    out_low = (dot(attended[...], factors[3]) * mask).astype(BF)
    hidden = (
        x_ref[...].astype(F32) + dot(attended[...], wo_ref[...], 1, 1) + dot(out_low, wide_ref[1])
    )
    base_ref[...] = hidden
    r2 = lax.rsqrt(jnp.mean(hidden * hidden, axis=1, keepdims=True) + EPSILON)
    n2 = (hidden * r2 * gain).astype(BF)
    own_in[:, :width] = n2
    lows = [(dot(n2, factors[s]) * mask).astype(BF) for s in range(3)]
    logits = dot(n2, small) + dot(lows[0], router2_ref[...])
    named = jnp.zeros((LANES, rows), jnp.bool_)
    for k in range(TOPK):
        named = named | (row_of((LANES, rows)) == meta_ref[k : k + 1, :])
    eye = jnp.where(row_of((LANES, LANES)) == lane_of((LANES, LANES)), 1.0, 0.0).astype(BF)
    picked = dot(jnp.where(named, 1.0, 0.0).astype(BF), eye, 0, 0) > 0.5
    peak = jnp.max(jnp.where(picked, logits, MASKED), axis=1, keepdims=True)
    lifted = jnp.where(picked, jnp.exp(jnp.where(picked, logits, peak) - peak), 0.0)
    gates = lifted / jnp.sum(lifted, axis=1, keepdims=True)
    high = gates.astype(BF).astype(F32)
    shrunk = dot(jnp.concatenate(lows[1:], axis=1), fold_ref[: 2 * STACKED, :])
    side = high + pltpu.roll(gates - high, EXPERT_COUNT, 1) + shrunk
    own_in[:, width:] = side.astype(BF)

    going = Gather("fsdp", shards, own_in, store, (gsend, grecv))
    coming = Scatter("fsdp", shards, part, land, (ssend, srecv))
    going.start()
    for load in loads:
        load.wait()

    early, late = going.halves()
    plan, rest = scatter_plan(coming, shards)
    first_expert = me * (EXPERT_COUNT // shards)

    def out_copy(at):
        return pltpu.make_async_copy(outs, outs_ref.at[me ^ turn_of(at, shards)], osem.at[0])

    def step(t, carry):
        turn = turn_of(t, shards)
        block = me ^ turn
        slot = t % 2

        @pl.when(t == 2)
        def _():
            for h, m in early:
                going.take(h, m)

        @pl.when(t == 4)
        def _():
            for h, m in late:
                going.take(h, m)

        for k in range(shards):
            m = turn_of(k, shards)
            if m % 2:

                @pl.when(t == k)
                def _(m=m):
                    for h in range(2):
                        going.take(h, m)

        @pl.when(t + 1 < shards)
        def _():
            cot_copy(t + 1).start()

        cot_copy(t).wait()

        @pl.when(t >= 1)
        def _():
            out_copy(t - 1).wait()

        block_rows = pl.ds(pl.multiple_of(block * rows, rows), rows)
        if near:
            here = store.at[block]
        else:
            here = block_in

            @pl.when(t == 0)
            def _():
                block_in[...] = own_in[...]

            @pl.when(t != 0)
            def _():
                fetch = pltpu.make_async_copy(store.at[block], block_in, bsem)
                fetch.start()
                fetch.wait()

        out, back, extra, sums = experts_block(
            first_expert,
            here[:, :width],
            here[:, width:],
            cots[slot],
            mask_ref[block_rows, :].astype(F32),
            win,
            wout,
            wide_ref[2],
            hid_ref,
            down_ref,
            spread_ref,
            fold_ref,
        )
        outs[...] = out
        out_copy(t).start()
        part[block, :, :width] = back
        part[block, :, width:] = extra

        @pl.when(t == 0)
        def _():
            gdown_ref[...] = sums[0]
            ghid_ref[0] = sums[1]
            ghid_ref[1] = sums[2]

        @pl.when(t != 0)
        def _():
            gdown_ref[...] += sums[0]
            ghid_ref[0] += sums[1]
            ghid_ref[1] += sums[2]

        for k in range(shards):
            if plan[k]:

                @pl.when(t == k)
                def _(k=k):
                    for h, m in plan[k]:
                        coming.reduce(h, m)

        return carry

    lax.fori_loop(0, shards, step, 0)
    out_copy(shards - 1).wait()
    cot_load = pltpu.make_async_copy(cots_ref.at[me], cots.at[0], csem.at[0])
    cot_load.start()
    for h, m in rest:
        coming.reduce(h, m)
    cot_load.wait()

    hidden = base_ref[...]
    mask = mask_ref[own, :].astype(F32)
    r2 = lax.rsqrt(jnp.mean(hidden * hidden, axis=1, keepdims=True) + EPSILON)
    n2 = own_in[:, :width]
    cot = cots[0]
    grad = cot.astype(F32)
    extra = part[me, :, width:]
    extra_full = extra.astype(F32)
    gate_grad = extra_full + pltpu.roll(extra_full, LANES - EXPERT_COUNT, 1)
    logit_grad = gates * (gate_grad - jnp.sum(gates * gate_grad, axis=1, keepdims=True))
    logit_grad = jnp.where(lane < EXPERT_COUNT, logit_grad, 0.0).astype(BF)
    wider = dot(extra, spread_ref[...])
    second_grad = [
        (dot(logit_grad, router2_ref[...], 1, 1) * mask).astype(BF),
        (wider[:, :STACKED] * mask).astype(BF),
        (wider[:, STACKED : 2 * STACKED] * mask).astype(BF),
    ]
    down_low = (wider[:, 2 * STACKED :] * mask).astype(BF)
    base_ref[...] = hidden + dot(down_low, wide_ref[2])
    n2_grad = part[me, :, :width].astype(F32) + dot(logit_grad, small, 1, 1)
    for s in range(3):
        n2_grad = n2_grad + dot(second_grad[s], factors[s], 1, 1)
    w2 = gain * n2_grad
    hidden_grad = grad + r2 * w2 - hidden * (r2 * r2 * r2) * jnp.mean(w2 * hidden, axis=1, keepdims=True)
    hgrad_ref[...] = hidden_grad
    out_grad = hidden_grad.astype(BF)
    out_low_grad = (dot(out_grad, wide_ref[1], 1, 1) * mask).astype(BF)
    attended_grad = dot(out_grad, wo_ref[...]) + dot(out_low_grad, factors[3], 1, 1)
    for s in range(shards):
        if heads == 2:
            heads_ref[s] = attended_grad[:, s * LANES : (s + 1) * LANES].astype(BF)
        else:
            pair = attended_grad[:, s // 2 * LANES : (s // 2 + 1) * LANES]
            if s % 2:
                pair = pltpu.roll(pair, HEAD_WIDTH, 1)
            heads_ref[s] = jnp.where(lane < HEAD_WIDTH, pair, 0.0).astype(BF)
    gsecond = dot(n2, jnp.concatenate(second_grad, axis=1), 0, 0).astype(BF)
    packed = [gsecond[:, s * LANES : (s + 1) * LANES] for s in range(3)]
    packed.append(dot(attended[...], out_low_grad, 0, 0).astype(BF))
    packed.append(gdown_ref[...].astype(BF))
    for s in range(2):
        packed += [ghid_ref[s, :, j : j + LANES].astype(BF) for j in range(0, HIDDEN_UNITS, LANES)]
    for one, two in ((out_low, out_grad), (down_low, cot)):
        product = dot(one, two, 0, 0).astype(BF)
        packed += [product[:, j : j + LANES] for j in range(0, MODEL_WIDTH, LANES)]
    packed.append(dot(lows[0], logit_grad, 0, 0).astype(BF))
    pack(early_ref, packed, early_ref.shape[1])
    going.finish()
    coming.finish()


def middle(mine, x, small, meta, mask, wo, factors, wide, router2, hid, down, cots, win, wout, identity):
    shards = lax.axis_size("fsdp")
    rows = x.shape[0]
    side = MODEL_WIDTH + LANES
    source = np.arange(LANES)
    place = np.arange(STACKED) % ADAPTER_RANK
    spread = np.concatenate([source[:, None] == o + place[None, :] for o in (32, 48, 64)], axis=1)
    fold = np.concatenate([source[None, :] == o + place[:, None] for o in (32, 48, 64)], axis=0)
    spread, fold = jnp.asarray(spread, BF), jnp.asarray(fold, BF)
    gathered = (shards, rows, side)
    near = shards <= 8
    results = pl.pallas_call(
        functools.partial(middle_kernel, shards),
        out_shape=(
            jax.ShapeDtypeStruct((rows, MODEL_WIDTH), F32),
            jax.ShapeDtypeStruct((shards, rows, MODEL_WIDTH), BF),
            jax.ShapeDtypeStruct((rows, MODEL_WIDTH), F32),
            jax.ShapeDtypeStruct((shards, rows, LANES), BF),
            jax.ShapeDtypeStruct((shards, total_length(EARLY) // shards, LANES), BF),
        )
        + (() if near else (jax.ShapeDtypeStruct(gathered, BF),)),
        in_specs=[IN_VMEM] * 6 + [ANYWHERE] + [IN_VMEM] * 6 + [ANYWHERE] * 3,
        out_specs=(IN_VMEM, ANYWHERE) + (IN_VMEM,) * 3 + (() if near else (ANYWHERE,)),
        scratch_shapes=[
            pltpu.VMEM(gathered if near else gathered[1:], BF),
            pltpu.VMEM((16, LANES) if near else gathered[1:], BF),
            pltpu.VMEM((shards, rows, side), BF),
            pltpu.VMEM((2, shards - 1, rows // 2, side), BF),
            pltpu.VMEM(win.shape, BF),
            pltpu.VMEM(wout.shape, BF),
            pltpu.VMEM((2, rows, MODEL_WIDTH), BF),
            pltpu.VMEM((rows, MODEL_WIDTH), BF),
            pltpu.VMEM((16, LANES) if near else (rows, MODEL_WIDTH), BF),
            pltpu.VMEM((4, MODEL_WIDTH, STACKED), BF),
            pltpu.VMEM((HIDDEN_UNITS, STACKED), F32),
            pltpu.VMEM((2, STACKED, HIDDEN_UNITS), F32),
        ]
        + pair_of_sems(shards) * 2
        + [pltpu.SemaphoreType.DMA((3,))] * 3
        + [pltpu.SemaphoreType.DMA(())],
        compiler_params=remote(identity, 62),
        name="middle",
    )(mine, x, small, meta, mask, wo, factors, wide, router2, hid, down, spread, fold, cots, win, wout)
    return results[:5]


class Total:
    def __init__(self, shards, groups, out, part, land, zpart, zland, zall, sems):
        self.me, self.plane = lax.axis_index("fsdp"), lax.axis_index("dp")
        self.groups, self.out, self.part, self.zpart, self.zall = groups, out, part, zpart, zall
        self.zland, self.zsems = zland, sems[2:6]
        self.down = Scatter("fsdp", shards, part, land, sems[0:2])
        self.up = Gather("fsdp", shards, out.at[self.me], out, sems[6:8])
        self.steps = [lambda k=k: self.level(self.down, k) for k in range(len(bits_of(shards)))]
        self.steps.append(self.turn)
        self.steps += [self.turn_back, self.rise]
        for k in range(len(bits_of(shards))):
            self.steps.append(lambda k=k: self.up.stage(k))
        self.steps.append(self.finish)

    def level(self, moving, k):
        for mask in range(moving.count):
            for h in range(2):
                if moving.depth(h, mask) == k:
                    moving.reduce(h, mask)

    def turn(self):
        self.level(self.down, len(self.down.orders[0]))
        piece = self.zpart.shape[1]
        for g in range(self.groups):
            self.zpart[g] = self.part[self.me, pl.ds(g * piece, piece)]
        for mask in range(1, self.groups):
            self.piece(mask).start()

    def piece(self, mask):
        return pltpu.make_async_remote_copy(
            src_ref=self.zpart.at[self.plane ^ mask],
            dst_ref=self.zland.at[mask - 1],
            send_sem=self.zsems[0].at[mask],
            recv_sem=self.zsems[1].at[mask],
            device_id={"dp": self.plane ^ mask},
            device_id_type=MESH,
        )

    def added(self, mask, owner):
        return pltpu.make_async_remote_copy(
            src_ref=self.zall.at[owner],
            dst_ref=self.zall.at[owner],
            send_sem=self.zsems[2].at[mask],
            recv_sem=self.zsems[3].at[mask],
            device_id={"dp": self.plane ^ mask},
            device_id_type=MESH,
        )

    def turn_back(self):
        total = self.zpart[self.plane].astype(F32)
        for mask in range(1, self.groups):
            self.piece(mask).wait_recv()
            total = total + self.zland[mask - 1].astype(F32)
        self.zall[self.plane] = total.astype(BF)
        for mask in range(1, self.groups):
            self.added(mask, self.plane).start()

    def rise(self):
        for mask in range(1, self.groups):
            self.added(mask, self.plane ^ mask).wait_recv()
        piece = self.zpart.shape[1]
        for g in range(self.groups):
            self.out[self.me, pl.ds(g * piece, piece)] = self.zall[g]
        self.up.start()

    def finish(self):
        self.down.finish()
        for mask in range(1, self.groups):
            self.piece(mask).wait_send()
            self.added(mask, self.plane).wait_send()
        self.up.finish()

    def next(self, count=1):
        for _ in range(count):
            if self.steps:
                self.steps.pop(0)()


def total_scratch(shards, groups, length):
    share = length // shards
    piece = share // groups
    return [
        pltpu.VMEM((shards, share, LANES), BF),
        pltpu.VMEM((shards, share, LANES), BF),
        pltpu.VMEM((2, shards - 1, share // 2, LANES), BF),
        pltpu.VMEM((groups, piece, LANES), BF),
        pltpu.VMEM((groups - 1, piece, LANES), BF),
        pltpu.VMEM((groups, piece, LANES), BF),
    ] + pair_of_sems(shards) + [pltpu.SemaphoreType.DMA((groups,))] * 4 + pair_of_sems(shards)


def total_length(length):
    unit = lax.axis_size("fsdp") * lax.axis_size("dp") * 2 * 16
    return -(-length // unit) * unit


EARLY = 5 * MODEL_WIDTH + HIDDEN_UNITS + 2 * MODEL_WIDTH + STACKED
LATE = 5 * MODEL_WIDTH


def leave_kernel(
    shards,
    groups,
    heads_ref,
    q_ref,
    k_ref,
    v_ref,
    att_ref,
    columns_ref,
    x_ref,
    small_ref,
    factors_ref,
    wide_ref,
    kv_ref,
    hgrad_ref,
    base_ref,
    low_ref,
    turn_ref,
    mask_ref,
    outs_ref,
    layer_ref,
    xgrad_ref,
    late_out,
    columns,
    grads,
    dk_ref,
    dv_ref,
    dq_ref,
    mixes,
    landed,
    near_columns,
    low,
    turn,
    own_mask_ref,
    outs,
    out_land,
    asend,
    arecv,
    msend,
    mrecv,
    gsend,
    grecv,
    osend,
    orecv,
    isem,
    *sums,
):
    me, plane = lax.axis_index("fsdp"), lax.axis_index("dp")
    rows = x_ref.shape[0]
    heads = HEADS // shards
    share = max(1, shards // KEY_VALUE_HEADS)
    side = PART
    cols = heads * side
    nparts = rows // side
    late_part = sums[0]
    near = shards <= 8
    columns = near_columns if near else columns
    own_rows = pl.ds(pl.multiple_of(me * rows, rows), rows)
    takes = [
        pltpu.make_async_copy(mask_ref.at[own_rows], own_mask_ref, isem.at[1]),
        pltpu.make_async_copy(low_ref.at[own_rows], low, isem.at[2]),
    ]
    for take in takes:
        take.start()
    if near:
        take_outs = pltpu.make_async_copy(outs_ref, outs, isem.at[3])
        take_outs.start()
    greet([("fsdp", me, range(1, shards)), ("dp", plane, range(1, groups))])

    def head_copy(mask):
        return pltpu.make_async_remote_copy(
            src_ref=heads_ref.at[me ^ mask],
            dst_ref=grads.at[me],
            send_sem=asend.at[mask],
            recv_sem=arecv.at[me],
            device_id={"fsdp": me ^ mask},
            device_id_type=MESH,
        )

    def home_copy(target):
        return pltpu.make_async_remote_copy(
            src_ref=mixes.at[target],
            dst_ref=landed.at[me],
            send_sem=msend.at[target],
            recv_sem=mrecv.at[me],
            device_id={"fsdp": target},
            device_id_type=MESH,
        )

    for m in range(shards - 1, 0, -1):
        head_copy(m).start()
    grads[me] = heads_ref[me]
    dk_ref[...] = jnp.zeros(dk_ref.shape, F32)
    dv_ref[...] = jnp.zeros(dv_ref.shape, F32)

    going = Gather("fsdp", shards, columns_ref, columns, (gsend, grecv))
    late = Total(shards, groups, late_out, *sums[:5], sums[5:])

    if near:
        leaving = Scatter("fsdp", shards, outs, out_land, (osend, orecv))
        levels = len(leaving.orders[0])

        def out_level(k):
            for m in range(shards):
                for h in range(2):
                    if leaving.depth(h, m) == k:
                        leaving.reduce(h, m)

        take_outs.wait()
        out_level(0)

    low_lane = lane_of((side, LANES)) < HEAD_WIDTH
    lane = lane_of((side, LANES))
    keyed = lane_of((rows, LANES)) < HEAD_WIDTH
    first_takes, late_takes = going.halves()

    for c in reversed(range(shards)):
        take_turn = pltpu.make_async_copy(turn_ref.at[pl.ds(c * rows, rows)], turn, isem.at[0])
        take_turn.start()

        @pl.when(me != c)
        def _(c=c):
            pltpu.make_async_remote_copy(
                src_ref=heads_ref.at[c],
                dst_ref=grads.at[c],
                send_sem=asend.at[0],
                recv_sem=arecv.at[c],
                device_id={"fsdp": c},
                device_id_type=MESH,
            ).wait_recv()

        if c == shards - 1:
            going.start()
        if c == shards - 4:
            for h, m in first_takes:
                going.take(h, m)
        if c == shards - 6:
            for h, m in late_takes:
                going.take(h, m)
        if near and shards - 1 - c in (2, 4):
            out_level((shards - 1 - c) // 2)
        keys = (c + 1) * rows

        def step(u, carry, c=c, keys=keys):
            at = pl.ds(pl.multiple_of(u * side, side), side)
            grad = grads[c, at, :].astype(F32)
            both = grad * att_ref[pl.ds(pl.multiple_of(c * rows + u * side, side), side), :].astype(F32)
            stack = []
            for h in range(heads):
                mine = low_lane if h == 0 else ~low_lane
                delta = jnp.sum(jnp.where(mine, both, 0.0), axis=1, keepdims=True)
                hi, mid, lo = splits(-delta)
                extra = jnp.where(lane == 0, hi, jnp.where(lane == 1, mid, jnp.where(lane == 2, lo, 0.0)))
                stack.append(
                    jnp.concatenate([jnp.where(mine, grad, 0.0).astype(BF), extra.astype(BF)], axis=1)
                )
            do = jnp.concatenate(stack, axis=0) if heads > 1 else stack[0]
            queries = q_ref[c * nparts + u]
            weights = jnp.exp(dot(k_ref[0:keys, :], queries, 1, 1))
            seen = row_of((rows, cols)) <= lane_of((rows, cols)) % side + u * side
            final = jnp.where(seen, weights[keys - rows :], 0.0)
            weights = jnp.concatenate([weights[: keys - rows], final], axis=0) if c else final
            slope = (weights * dot(v_ref[0:keys, :], do, 1, 1)).astype(BF)
            dv_ref[0:keys, :] += dot(weights.astype(BF), do[:, :LANES])
            dk_ref[0:keys, :] += dot(slope, queries[:, :LANES])
            dq = dot(slope, k_ref[0:keys, :LANES], 0, 0)
            dq = dq if heads == 1 else jnp.where(low_lane, dq[:side], dq[side:])
            dq_ref[at, :] = dq * (HEAD_WIDTH ** -0.5)
            return carry

        lax.fori_loop(0, nparts, step, 0)

        block = pl.ds(c * rows, rows)
        dk, dv = dk_ref[block, :], dv_ref[block, :]
        other = jnp.where(
            keyed, dk + pltpu.roll(dk, HEAD_WIDTH, 1), dv + pltpu.roll(dv, HEAD_WIDTH, 1)
        )
        take_turn.wait()
        cosine, sine = turn[:, :LANES], turn[:, LANES:]
        mixes[c, :, :LANES] = turned(dq_ref[...], cosine, -sine).astype(BF)
        mixes[c, :, LANES:] = turned(
            other, jnp.where(keyed, cosine, 1.0), jnp.where(keyed, -sine, 0.0)
        ).astype(BF)

        @pl.when(me != c)
        def _(c=c):
            home_copy(c).start()

    if shards < 8:
        for h, m in first_takes + late_takes:
            going.take(h, m)
    for h in range(2):
        for m in span(going.orders[h][:-1]):
            going.incoming(h, m ^ going.orders[h][-1]).wait_recv()

    landed[me] = mixes[me]
    if near:
        columns[me] = columns_ref[...]
    else:
        keep = pltpu.make_async_copy(columns_ref, columns.at[me], isem.at[3])
        keep.start()
        keep.wait()
    for take in takes:
        take.wait()
    own_mask = own_mask_ref[...].astype(F32)
    x = x_ref[...].astype(F32)
    r1 = lax.rsqrt(jnp.mean(x * x, axis=1, keepdims=True) + EPSILON)
    gain = gain_row(small_ref[...], 16)
    normed = (x * r1 * gain).astype(BF)
    for m in range(1, shards):
        pltpu.make_async_remote_copy(
            src_ref=mixes.at[0],
            dst_ref=landed.at[me ^ m],
            send_sem=msend.at[0],
            recv_sem=mrecv.at[me ^ m],
            device_id={"fsdp": me ^ m},
            device_id_type=MESH,
        ).wait_recv()
    query_grad, normed_grad = [], jnp.zeros((rows, MODEL_WIDTH), F32)
    for s in range(shards):
        if near:
            weight = columns[s]
        else:
            fetch = pltpu.make_async_copy(columns.at[s], near_columns, isem.at[3])
            fetch.start()
            fetch.wait()
            weight = near_columns[...]
        normed_grad = normed_grad + dot(landed[s], weight, 1, 1)
        query = landed[s, :, :LANES]
        if heads == 2:
            query_grad.append(query)
        elif s % 2 == 0:
            then = pltpu.roll(landed[s + 1, :, :LANES].astype(F32), HEAD_WIDTH, 1)
            query_grad.append(jnp.where(keyed, query.astype(F32), then).astype(BF))

    def pair_of(head):
        pair = jnp.zeros((rows, LANES), F32)
        for s in range(head * share, (head + 1) * share):
            pair = pair + landed[s, :, LANES:].astype(F32)
        return pair

    keys_grad, values_grad = [], []
    for head in range(0, KEY_VALUE_HEADS, 2):
        one, two = pair_of(head), pair_of(head + 1)
        keys_grad.append(jnp.where(keyed, one, pltpu.roll(two, HEAD_WIDTH, 1)).astype(BF))
        values_grad.append(jnp.where(keyed, pltpu.roll(one, HEAD_WIDTH, 1), two).astype(BF))
    whole = [jnp.concatenate(part, axis=1) for part in (query_grad, keys_grad, values_grad)]
    seconds = (wide_ref[0], kv_ref[0], kv_ref[1])
    firsts = []
    for s in range(3):
        firsts.append((dot(whole[s], seconds[s], 1, 1) * own_mask).astype(BF))
        normed_grad = normed_grad + dot(firsts[s], factors_ref[s], 1, 1)

    packed, share_rows = [], late_part.shape[1]
    gfirst = dot(normed, jnp.concatenate(firsts, axis=1), 0, 0).astype(BF)
    packed += [gfirst[:, s * LANES : (s + 1) * LANES] for s in range(3)]
    for s in range(3):
        second = dot(low[:, s * LANES : (s + 1) * LANES], whole[s], 0, 0).astype(BF)
        packed += [second[:, j : j + LANES] for j in range(0, second.shape[1], LANES)]
    pack(late_part, packed, share_rows)
    late.next()
    w1 = gain * normed_grad
    xgrad_ref[...] = (
        hgrad_ref[...] + r1 * w1 - x * (r1 * r1 * r1) * jnp.mean(w1 * x, axis=1, keepdims=True)
    )
    late.next(2)
    layer = base_ref[...]
    if near:
        for k in range(3, levels + 1):
            out_level(k)
        layer = layer + outs[me].astype(F32)
    layer_ref[...] = layer.astype(layer_ref.dtype)
    late.next(99)

    for m in range(1, shards):
        head_copy(m).wait_send()
    for c in range(shards):

        @pl.when(me != c)
        def _(c=c):
            home_copy(c).wait_send()

    going.finish()
    if near:
        leaving.finish()


def pieces_of(first, size, share):
    parts, done = [], 0
    while done < size:
        block, row = divmod(first + done, share)
        length = min(size - done, share - row)
        parts.append((block, row, done, length))
        done += length
    return parts


def pack(target, arrays, share):
    first = 0
    for array in arrays:
        for block, row, done, length in pieces_of(first, array.shape[0], share):
            target[block, row : row + length, :] = array[done : done + length]
        first += array.shape[0]
    total = target.shape[0] * share
    for block, row, _, length in pieces_of(first, total - first, share):
        target[block, row : row + length, :] = jnp.zeros((length, LANES), BF)


def unpack(source, first, size):
    parts = pieces_of(first, size, source.shape[1])
    parts = [source[block, row : row + length, :] for block, row, _, length in parts]
    return parts[0] if len(parts) == 1 else jnp.concatenate(parts, axis=0)


def unpack_kernel(late_out, early_out, gfactor_ref, gdown_ref, gwide_ref, gkv_ref, gff_ref, groute_ref):
    def read(source, first, size):
        return unpack(source, first, size).astype(F32)

    for s in range(3):
        gfactor_ref[s] = read(late_out, s * MODEL_WIDTH, MODEL_WIDTH)
        gfactor_ref[3 + s] = read(early_out, s * MODEL_WIDTH, MODEL_WIDTH)
    gfactor_ref[6] = read(early_out, 3 * MODEL_WIDTH, MODEL_WIDTH)
    edge = 4 * MODEL_WIDTH
    gdown_ref[...] = read(early_out, edge, HIDDEN_UNITS)
    edge += HIDDEN_UNITS
    for s in range(2):
        for j in range(4):
            gff_ref[s, :, j * LANES : (j + 1) * LANES] = read(early_out, edge, STACKED)
            edge += STACKED
    for s in range(2):
        for j in range(8):
            gwide_ref[1 + s, :, j * LANES : (j + 1) * LANES] = read(early_out, edge, STACKED)
            edge += STACKED
    groute_ref[...] = read(early_out, edge, STACKED)
    edge = 3 * MODEL_WIDTH
    for j in range(8):
        gwide_ref[0, :, j * LANES : (j + 1) * LANES] = read(late_out, edge, STACKED)
        edge += STACKED
    for s in range(2):
        for j in range(4):
            gkv_ref[s, :, j * LANES : (j + 1) * LANES] = read(late_out, edge, STACKED)
            edge += STACKED

def unpack_all(late, early):
    return pl.pallas_call(
        unpack_kernel,
        out_shape=(
            jax.ShapeDtypeStruct((7, MODEL_WIDTH, STACKED), F32),
            jax.ShapeDtypeStruct((HIDDEN_UNITS, STACKED), F32),
            jax.ShapeDtypeStruct((3, STACKED, MODEL_WIDTH), F32),
            jax.ShapeDtypeStruct((2, STACKED, HIDDEN_UNITS), F32),
            jax.ShapeDtypeStruct((2, STACKED, HIDDEN_UNITS), F32),
            jax.ShapeDtypeStruct((STACKED, LANES), F32),
        ),
        in_specs=[IN_VMEM] * 2,
        out_specs=(IN_VMEM,) * 6,
        compiler_params=pltpu.CompilerParams(vmem_limit_bytes=40 << 20),
        name="unpack_all",
    )(late, early)


def leave(to_heads, q, k, v, att, columns, x, small, factors, wide, kv_second, hgrad, base, low, turn, mask, outs, identity):
    shards, groups = lax.axis_size("fsdp"), lax.axis_size("dp")
    rows = x.shape[0]
    near = shards <= 8
    total = shards * rows
    return pl.pallas_call(
        functools.partial(leave_kernel, shards, groups),
        out_shape=(
            jax.ShapeDtypeStruct((rows, MODEL_WIDTH), BF if near else F32),
            jax.ShapeDtypeStruct((rows, MODEL_WIDTH), F32),
            jax.ShapeDtypeStruct((shards, total_length(LATE) // shards, LANES), BF),
            jax.ShapeDtypeStruct((16, LANES) if near else (shards, MODEL_WIDTH, 2 * LANES), BF),
        ),
        in_specs=[IN_VMEM] * 13 + [ANYWHERE] * 4,
        out_specs=(IN_VMEM, IN_VMEM, IN_VMEM, ANYWHERE),
        scratch_shapes=[
            pltpu.VMEM((shards, rows, LANES), BF),
            pltpu.VMEM((total, LANES), F32),
            pltpu.VMEM((total, LANES), F32),
            pltpu.VMEM((rows, LANES), F32),
            pltpu.VMEM((shards, rows, 2 * LANES), BF),
            pltpu.VMEM((shards, rows, 2 * LANES), BF),
            pltpu.VMEM((shards, MODEL_WIDTH, 2 * LANES) if near else (MODEL_WIDTH, 2 * LANES), BF),
            pltpu.VMEM((rows, 3 * STACKED), BF),
            pltpu.VMEM((rows, 2 * LANES), F32),
            pltpu.VMEM((rows, STACKED), BF),
            pltpu.VMEM((shards, rows, MODEL_WIDTH) if near else (2, 32, LANES), BF),
            pltpu.VMEM((2, shards - 1, rows // 2, MODEL_WIDTH) if near else (2, 2, 32, LANES), BF),
        ]
        + [pltpu.SemaphoreType.DMA((shards,))] * 4
        + pair_of_sems(shards) * 2
        + [pltpu.SemaphoreType.DMA((4,))]
        + total_scratch(shards, groups, total_length(LATE))[1:],
        compiler_params=remote(identity, 62),
        name="leave",
    )(to_heads, q, k, v, att, columns, x, small, factors, wide, kv_second, hgrad, base, low, turn, mask, outs)


def local(
    tokens,
    cotangent,
    lengths,
    adapter_index,
    routes,
    deal,
    norm_gain_pair,
    query_weight,
    key_weight,
    value_weight,
    output_weight_transposed,
    router_weight,
    expert_input_weight,
    expert_output_weight,
    factors,
    down_first,
    wide,
    kv_second,
    hidden_second,
    router_second,
):
    shards = lax.axis_size("fsdp")
    groups = lax.axis_size("dp")
    rows = tokens.shape[0]
    total = rows * shards
    heads = HEADS // shards
    share = max(1, shards // KEY_VALUE_HEADS)
    me = lax.axis_index("fsdp")

    padded = ((0, 0), (0, rows - lengths.shape[1]))
    meta = jnp.concatenate(
        [
            routes.T,
            jnp.pad(lengths, padded),
            jnp.pad(adapter_index, padded),
            jnp.zeros((6, rows), jnp.int32),
        ],
        axis=0,
    )
    small = jnp.concatenate(
        [
            router_weight,
            norm_gain_pair,
            jnp.zeros((router_weight.shape[0], LANES - EXPERT_COUNT - 2), BF),
        ],
        axis=1,
    )
    qkv, low_all, group_mask, small, meta, columns, turn = enter(
        deal,
        tokens,
        query_weight,
        key_weight,
        value_weight,
        small,
        meta,
        factors,
        wide,
        kv_second,
        1,
    )
    win = expert_input_weight.reshape(MODEL_WIDTH, -1)
    wout = expert_output_weight.reshape(MODEL_WIDTH, -1)
    out_weight = lax.all_gather(output_weight_transposed, ("dp", "fsdp"), axis=0, tiled=True)
    mine, attended, q_kept, k_kept, v_kept, all_grad = attend(meta, qkv, cotangent, heads, 5)
    router2 = jnp.pad(router_second, ((0, 0), (0, LANES - EXPERT_COUNT)))
    (
        base,
        out_part,
        hidden_grad,
        to_heads,
        early,
    ) = middle(
        mine,
        tokens,
        small,
        meta,
        group_mask,
        out_weight,
        factors,
        wide,
        router2,
        hidden_second,
        down_first,
        all_grad,
        win,
        wout,
        6,
    )
    early_sum = lax.psum(early, ("dp", "fsdp"))
    layer_out, input_grad, late, _ = leave(
        to_heads,
        q_kept,
        k_kept,
        v_kept,
        attended,
        columns,
        tokens,
        small,
        factors,
        wide,
        kv_second,
        hidden_grad,
        base,
        low_all,
        turn,
        group_mask,
        out_part,
        7,
    )
    if shards > 8:
        layer_out = (layer_out + scatter(out_part, "fsdp", 8).astype(F32)).astype(BF)
    g_factors, g_down, g_wide, g_kv, g_ff, g_route = unpack_all(late, early_sum)
    return (
        layer_out,
        input_grad,
        g_factors,
        g_down,
        g_wide,
        g_kv,
        g_ff,
        g_route[:, :EXPERT_COUNT],
    )


def solution(mesh):
    rows = P(("dp", "fsdp"), None)
    placed = (
        (rows, rows, P("dp", None), P("dp", None), rows, P())
        + (rows,) * 6
        + (P(None, "fsdp", None),) * 2
        + (P(),) * 6
    )
    return jax.shard_map(
        local,
        mesh=mesh,
        in_specs=placed,
        out_specs=(rows, rows) + (P(),) * 6,
        check_vma=False,
    )
```

```python
import functools
import math

import jax
import jax.numpy as jnp
import numpy as np
from jax import lax
from jax.experimental import pallas as pl
from jax.experimental.pallas import tpu as pltpu
from jax.sharding import PartitionSpec as P

MODEL_WIDTH = 1024
HEADS = 16
KEY_VALUE_HEADS = 8
HEAD_WIDTH = 64
HIDDEN_UNITS = 512
TOPK = 8
EXPERT_COUNT = 16
ADAPTER_COUNT = 8
ADAPTER_RANK = 16
STACKED = ADAPTER_COUNT * ADAPTER_RANK

EPSILON = 1e-06
ROPE_BASE = 10000.0
MASKED = -1e30
LANES = 128
PART = 128
NSEQ = 4

BF = jnp.bfloat16
F32 = jnp.float32
MESH = pl.DeviceIdType.MESH


def dot(a, b, ca=1, cb=0):
    return lax.dot_general(a, b, (((ca,), (cb,)), ((), ())), preferred_element_type=F32)


def splits(v):
    hi = v.astype(BF).astype(F32)
    rest = v - hi
    mid = rest.astype(BF).astype(F32)
    return hi, mid, rest - mid


def lane_of(shape):
    return lax.broadcasted_iota(jnp.int32, shape, len(shape) - 1)


def row_of(shape):
    return lax.broadcasted_iota(jnp.int32, shape, 0)


def bits_of(count):
    return [1 << k for k in range(count.bit_length() - 1)]


def orders_of(count):
    bits = bits_of(count)
    far = bits[1:]
    cut = (len(far) + 1) // 2
    return (far + bits[:1], far[cut:] + far[:cut] + bits[:1])


def span(bits):
    masks = [0]
    for bit in bits:
        masks = masks + [m ^ bit for m in masks]
    return masks


def greet(meetings):
    barrier = pltpu.get_barrier_semaphore()
    count = 0
    for axis, me, masks in meetings:
        for mask in masks:
            pl.semaphore_signal(
                barrier, inc=1, device_id={axis: me ^ mask}, device_id_type=MESH
            )
            count += 1
    pl.semaphore_wait(barrier, count)


class Gather:
    def __init__(self, axis, count, own, store, sems):
        self.axis, self.count, self.own, self.store = axis, count, own, store
        self.sends, self.recvs = sems
        self.me = lax.axis_index(axis)
        self.orders = orders_of(count)
        self.half = store.shape[1] // 2

    def copy(self, h, mask, bit):
        rows = pl.ds(h * self.half, self.half)
        there = self.store.at[self.me ^ mask, rows]
        return pltpu.make_async_remote_copy(
            src_ref=self.own.at[rows] if mask == 0 else there,
            dst_ref=there,
            send_sem=self.sends.at[h, mask ^ bit],
            recv_sem=self.recvs.at[h, mask ^ bit],
            device_id={self.axis: self.me ^ bit},
            device_id_type=MESH,
        )

    def incoming(self, h, mask):
        there = self.store.at[self.me ^ mask, pl.ds(h * self.half, self.half)]
        return pltpu.make_async_remote_copy(
            src_ref=there,
            dst_ref=there,
            send_sem=self.sends.at[h, mask],
            recv_sem=self.recvs.at[h, mask],
            device_id={self.axis: self.me ^ mask},
            device_id_type=MESH,
        )

    def start(self):
        for k in range(len(self.orders[0])):
            for h in range(2):
                self.copy(h, 0, self.orders[h][k]).start()

    def take(self, h, mask):
        order = self.orders[h]
        self.incoming(h, mask).wait_recv()
        k = max(i for i, bit in enumerate(order) if mask & bit)
        for bit in order[k + 1 :]:
            self.copy(h, mask, bit).start()

    def halves(self):
        early, late = [], []
        for k in range(len(self.orders[0]) - 1):
            for s in range(1 << k):
                for h in range(2):
                    mask = self.orders[h][k] ^ span(self.orders[h][:k])[s]
                    (late if self.count == 8 and k == 1 and s else early).append((h, mask))
        return early, late

    def stage(self, k):
        for s in range(1 << k):
            for h in range(2):
                order = self.orders[h]
                mask = order[k] ^ span(order[:k])[s]
                self.incoming(h, mask).wait_recv()
                for bit in order[k + 1 :]:
                    self.copy(h, mask, bit).start()

    def held(self, k):
        sets = [set(span(order[: k + 1])) for order in self.orders]
        return sets[0] & sets[1]

    def stages(self):
        for k in range(len(self.orders[0])):
            self.stage(k)

    def finish(self):
        for h in range(2):
            for mask in range(1, self.count):
                self.incoming(h, mask).wait_send()


class Scatter:
    def __init__(self, axis, count, part, land, sems):
        self.axis, self.count, self.part, self.land = axis, count, part, land
        self.sends, self.recvs = sems
        self.me = lax.axis_index(axis)
        self.orders = [order[::-1] for order in orders_of(count)]
        self.half = part.shape[1] // 2

    def depth(self, h, mask):
        for k, bit in enumerate(self.orders[h]):
            if mask & bit:
                return k
        return len(self.orders[h])

    def copy(self, h, mask):
        bit = self.orders[h][self.depth(h, mask)]
        return pltpu.make_async_remote_copy(
            src_ref=self.part.at[self.me ^ mask, pl.ds(h * self.half, self.half)],
            dst_ref=self.land.at[h, mask - 1],
            send_sem=self.sends.at[h, mask],
            recv_sem=self.recvs.at[h, mask],
            device_id={self.axis: self.me ^ bit},
            device_id_type=MESH,
        )

    def reduce(self, h, mask):
        depth = self.depth(h, mask)
        sources = [mask ^ bit for bit in self.orders[h][:depth]]
        for source in sources:
            self.copy(h, source).wait_recv()
        if sources:
            step = math.gcd(self.half, 64)
            mine = self.me ^ mask

            def add(c, carry):
                here = pl.ds(pl.multiple_of(c * step, step), step)
                at = pl.ds(pl.multiple_of(h * self.half + c * step, step), step)
                total = self.part[mine, at].astype(F32)
                for source in sources:
                    total = total + self.land[h, source - 1, here].astype(F32)
                self.part[mine, at] = total.astype(BF)
                return carry

            lax.fori_loop(0, self.half // step, add, 0)
        if mask:
            self.copy(h, mask).start()

    def run(self):
        for k in range(len(self.orders[0]) + 1):
            for mask in range(self.count):
                for h in range(2):
                    if self.depth(h, mask) == k:
                        self.reduce(h, mask)

    def finish(self):
        for h in range(2):
            for mask in range(1, self.count):
                self.copy(h, mask).wait_send()


def pair_of_sems(count):
    return [pltpu.SemaphoreType.DMA((2, count)), pltpu.SemaphoreType.DMA((2, count))]


ANYWHERE = pl.BlockSpec(memory_space=pl.ANY)
IN_VMEM = pl.BlockSpec(memory_space=pltpu.VMEM)


def remote(identity, limit=48):
    return pltpu.CompilerParams(
        collective_id=identity, has_side_effects=True, vmem_limit_bytes=limit << 20
    )


def scatter_kernel(axis, count, given, total, part, land, sends, recvs, local_sem):
    me = lax.axis_index(axis)
    take = pltpu.make_async_copy(given, part, local_sem)
    take.start()
    greet([(axis, me, bits_of(count))])
    moving = Scatter(axis, count, part, land, (sends, recvs))
    take.wait()
    moving.run()
    total[...] = part[me]
    moving.finish()


def scatter(blocks, axis, identity):
    count, rows, columns = blocks.shape
    return pl.pallas_call(
        functools.partial(scatter_kernel, axis, count),
        out_shape=jax.ShapeDtypeStruct((rows, columns), BF),
        in_specs=[ANYWHERE],
        out_specs=IN_VMEM,
        scratch_shapes=[
            pltpu.VMEM(blocks.shape, BF),
            pltpu.VMEM((2, count - 1, rows // 2, columns), BF),
        ]
        + pair_of_sems(count)
        + [pltpu.SemaphoreType.DMA(())],
        compiler_params=remote(identity, 56),
        name="scatter",
    )(blocks)


def attend_kernel(
    shards,
    near,
    heads,
    meta_ref,
    qkv_ref,
    cot_ref,
    mine_ref,
    out_ref,
    q_ref,
    k_ref,
    v_ref,
    cots_ref,
    gsend,
    grecv,
    asend,
    arecv,
    keep_sem,
):
    me = lax.axis_index("fsdp")
    total = qkv_ref.shape[0]
    nseq = NSEQ
    keep = pltpu.make_async_copy(cot_ref, cots_ref.at[me], keep_sem)
    keep.start()
    greet([("fsdp", me, range(1, shards))])
    going = Gather("fsdp", shards, cot_ref, cots_ref, (gsend, grecv))
    going.start()
    early, late = going.halves()
    edges = [jnp.zeros((1, 1), jnp.int32)]
    for s in range(nseq):
        edges.append(edges[-1] + meta_ref[8:9, s : s + 1])
    half = HEAD_WIDTH
    side = PART

    def prepare(i, carry):
        at = pl.ds(pl.multiple_of(i * side, side), side)
        low = lane_of((side, LANES)) < half
        lane = lane_of((side, LANES))
        row = row_of((side, LANES)) + i * side
        seq = jnp.zeros((side, LANES), jnp.bool_)
        for s in range(nseq):
            seq = seq | ((lane == s) & (row >= edges[s]) & (row < edges[s + 1]))
        queries = qkv_ref[at, 0:LANES].astype(F32) * (HEAD_WIDTH ** -0.5)
        pair = qkv_ref[at, LANES : 2 * LANES].astype(F32)
        swapped = pltpu.roll(pair, half, 1)
        marks = jnp.where(seq, 1.0, 0.0).astype(BF)
        for h in range(heads):
            mine = jnp.where(low if h == 0 else ~low, queries, 0.0).astype(BF)
            q_ref[i, h * side : (h + 1) * side, 0:LANES] = mine
            q_ref[i, h * side : (h + 1) * side, LANES : 2 * LANES] = marks
        k_ref[at, 0:LANES] = jnp.where(low, pair, swapped).astype(BF)
        far = jnp.where(lane < nseq, jnp.where(seq, 0.0, MASKED), 0.0)
        k_ref[at, LANES : 2 * LANES] = jnp.where(
            (lane >= nseq) & (lane < nseq + 3), 1.0, far
        ).astype(BF)
        v_ref[at, 0:LANES] = jnp.where(low, swapped, pair).astype(BF)
        v_ref[at, LANES : 2 * LANES] = jnp.ones((side, LANES), BF)
        return carry

    lax.fori_loop(0, total // side, prepare, 0)

    rows = 3 * side

    def place(ref, source):
        if near:
            return ref.at[:, pl.ds(pl.multiple_of(source * LANES, LANES), LANES)]
        return ref.at[source]

    def home_copy(target):
        return pltpu.make_async_remote_copy(
            src_ref=out_ref.at[pl.ds(target * rows, rows)],
            dst_ref=place(mine_ref, me),
            send_sem=asend.at[target],
            recv_sem=arecv.at[me],
            device_id={"fsdp": target},
            device_id_type=MESH,
        )

    low = lane_of((rows, LANES)) < half
    lane = lane_of((rows, LANES))
    visible = lane_of((rows, rows)) <= row_of((rows, rows))
    for i in range(total // rows):
        keys = (i + 1) * rows
        at = pl.ds(i * rows, rows)
        mixed = []
        for h in range(heads):
            mine = pl.ds(h * side, side)
            queries = jnp.concatenate([q_ref[3 * i + u, mine, :] for u in range(3)], axis=0)
            scores = dot(queries, k_ref[0:keys, :], 1, 1)
            final = jnp.where(visible, scores[:, keys - rows :], MASKED)
            if i:
                scores = jnp.concatenate([scores[:, : keys - rows], final], axis=1)
            else:
                scores = final
            top = jnp.max(scores, axis=1, keepdims=True)
            weights = jnp.exp(scores - top).astype(BF)
            acc = dot(weights, v_ref[0:keys, :])
            weight = acc[:, LANES:]
            mixed.append(acc[:, :LANES] / weight)
            hi, mid, lo = splits(-(top + jnp.log(weight)))
            marks = queries[:, LANES:].astype(F32)
            marks = jnp.where(lane == nseq, hi, marks)
            marks = jnp.where(lane == nseq + 1, mid, marks)
            marks = jnp.where(lane == nseq + 2, lo, marks).astype(BF)
            for u in range(3):
                q_ref[3 * i + u, mine, LANES:] = marks[u * side : (u + 1) * side]
        value = mixed[0] if heads == 1 else jnp.where(low, mixed[0], mixed[1])
        out_ref[at, :] = value.astype(BF)

        @pl.when(me != i)
        def _(i=i):
            home_copy(i).start()

        if i == shards - 2:
            for h, m in early:
                going.take(h, m)

    place(mine_ref, me)[...] = out_ref[pl.ds(pl.multiple_of(me * rows, rows), rows), :]
    for h, m in late:
        going.take(h, m)
    for m in range(1, shards):
        pltpu.make_async_remote_copy(
            src_ref=out_ref.at[pl.ds(0, rows)],
            dst_ref=place(mine_ref, me ^ m),
            send_sem=asend.at[0],
            recv_sem=arecv.at[me ^ m],
            device_id={"fsdp": me ^ m},
            device_id_type=MESH,
        ).wait_recv()
    for i in range(shards):

        @pl.when(me != i)
        def _(i=i):
            home_copy(i).wait_send()

    for h in range(2):
        for m in span(going.orders[h][:-1]):
            going.incoming(h, m ^ going.orders[h][-1]).wait_recv()
    going.finish()
    keep.wait()


def attend(meta, qkv, cot, heads, identity):
    shards = lax.axis_size("fsdp")
    near = shards <= 8
    total = qkv.shape[0]
    rows = total // shards
    return pl.pallas_call(
        functools.partial(attend_kernel, shards, near, heads),
        out_shape=(
            jax.ShapeDtypeStruct((rows, MODEL_WIDTH) if near else (shards, rows, LANES), BF),
            jax.ShapeDtypeStruct((total, LANES), BF),
            jax.ShapeDtypeStruct((total // PART, heads * PART, 2 * LANES), BF),
            jax.ShapeDtypeStruct((total, 2 * LANES), BF),
            jax.ShapeDtypeStruct((total, 2 * LANES), BF),
            jax.ShapeDtypeStruct((shards,) + cot.shape, BF),
        ),
        in_specs=[IN_VMEM, IN_VMEM, ANYWHERE],
        out_specs=(IN_VMEM,) * 5 + (ANYWHERE,),
        scratch_shapes=pair_of_sems(shards)
        + [pltpu.SemaphoreType.DMA((shards,))] * 2
        + [pltpu.SemaphoreType.DMA(())],
        compiler_params=remote(identity, 60),
        name="attend",
    )(meta, qkv, cot)


def sequences(meta, first, rows, heads_of):
    row = row_of((rows, LANES)) + first
    start = jnp.zeros((1, 1), jnp.int32)
    picked = [jnp.zeros((rows, LANES), part[0].dtype) for part in heads_of]
    for s in range(len(heads_of[0])):
        inside = row >= start
        picked = [jnp.where(inside, part[s], value) for part, value in zip(heads_of, picked)]
        start = start + meta[8:9, s : s + 1]
    return picked


def turned(tensor, cosine, sine):
    lower = lane_of(tensor.shape) % HEAD_WIDTH < HEAD_WIDTH // 2
    other = jnp.where(lower, pltpu.roll(tensor, LANES - 32, 1), pltpu.roll(tensor, 32, 1))
    return tensor * cosine + other * sine


def head_columns(wide, narrow, pick_wide, pick_narrow, heads):
    low = lane_of((1, LANES)) < HEAD_WIDTH
    queries = wide
    if heads == 1:
        queries = jnp.where(low, jnp.where(pick_wide, pltpu.roll(wide, HEAD_WIDTH, 1), wide), 0.0)
    keys, values = narrow
    keys = jnp.where(pick_narrow, pltpu.roll(keys, HEAD_WIDTH, 1), keys)
    values = jnp.where(pick_narrow, values, pltpu.roll(values, HEAD_WIDTH, 1))
    return queries, jnp.where(low, keys, values)


def enter_kernel(
    shards,
    groups,
    deal_ref,
    x_ref,
    wq_ref,
    wk_ref,
    wv_ref,
    small_ref,
    meta_ref,
    factors_ref,
    wide_ref,
    kv_ref,
    cos_ref,
    sin_ref,
    freq_ref,
    qkv_ref,
    low_ref,
    mask_ref,
    small_out,
    meta_out,
    columns_out,
    turn_ref,
    xs,
    slices,
    weights,
    metas,
    merged,
    second,
    xsend,
    xrecv,
    wsend,
    wrecv,
    zsend,
    zrecv,
    msend,
    mrecv,
):
    me, plane = lax.axis_index("fsdp"), lax.axis_index("dp")
    heads = HEADS // shards
    share = max(1, shards // KEY_VALUE_HEADS)
    rows = x_ref.shape[0]
    part = wq_ref.shape[0]
    order = [mask for mask in range(1, shards)]

    for f in range(shards):
        chunk = f * heads * HEAD_WIDTH // LANES
        head = f // share
        pair = head // 2
        queries, others = head_columns(
            wq_ref[:, chunk * LANES : (chunk + 1) * LANES].astype(F32),
            (
                wk_ref[:, pair * LANES : (pair + 1) * LANES].astype(F32),
                wv_ref[:, pair * LANES : (pair + 1) * LANES].astype(F32),
            ),
            f % 2 == 1,
            head % 2 == 1,
            heads,
        )
        slices[f, :, 0:LANES] = queries.astype(BF)
        slices[f, :, LANES : 2 * LANES] = others.astype(BF)
        slices[f, :, 2 * LANES :] = small_ref[...]
    metas[plane] = meta_ref[...]

    greet([("fsdp", me, order), ("dp", plane, range(1, groups))])

    moving = Gather("fsdp", shards, x_ref, xs, (xsend, xrecv))
    plane_rows = shards * part

    def column_copy(mask):
        return pltpu.make_async_remote_copy(
            src_ref=slices.at[me ^ mask],
            dst_ref=weights.at[plane, me],
            send_sem=wsend.at[mask],
            recv_sem=wrecv.at[mask],
            device_id={"fsdp": me ^ mask},
            device_id_type=MESH,
        )

    def plane_copy(mask):
        return pltpu.make_async_remote_copy(
            src_ref=weights.at[plane],
            dst_ref=weights.at[plane],
            send_sem=zsend.at[mask],
            recv_sem=zrecv.at[mask],
            device_id={"dp": plane ^ mask},
            device_id_type=MESH,
        )

    def meta_copy(mask):
        return pltpu.make_async_remote_copy(
            src_ref=meta_ref,
            dst_ref=metas.at[plane],
            send_sem=msend.at[mask],
            recv_sem=mrecv.at[mask],
            device_id={"dp": plane ^ mask},
            device_id_type=MESH,
        )

    for mask in order:
        column_copy(mask).start()
    for mask in range(1, groups):
        meta_copy(mask).start()
    moving.start()
    weights[plane, me] = slices[me]

    half = HEAD_WIDTH
    at = pl.ds(pl.multiple_of(me * heads * half // LANES * LANES, LANES), LANES)
    head = me // share
    pair_at = pl.ds(pl.multiple_of(head // 2 * LANES, LANES), LANES)
    queries, others = head_columns(
        wide_ref[0, :, at].astype(F32),
        (kv_ref[0, :, pair_at].astype(F32), kv_ref[1, :, pair_at].astype(F32)),
        me % 2 == 1,
        head % 2 == 1,
        heads,
    )
    low_lane = lane_of((STACKED, LANES)) < half
    second[...] = jnp.zeros(second.shape, BF)
    second[0:STACKED, 0:LANES] = queries.astype(BF)
    second[STACKED : 2 * STACKED, LANES:] = jnp.where(low_lane, others, 0.0).astype(BF)
    second[2 * STACKED :, LANES:] = jnp.where(low_lane, 0.0, others).astype(BF)

    for mask in order:
        column_copy(mask).wait_recv()
    for mask in range(1, groups):
        plane_copy(mask).start()
    for mask in range(1, groups):
        meta_copy(mask).wait_recv()
    dealt = jnp.int32(0)
    for g in range(groups):
        dealt = dealt + jnp.where(deal_ref[g] == plane, g, 0)
    meta = jnp.zeros(meta_ref.shape, jnp.int32)
    for g in range(groups):
        meta = jnp.where(dealt == g, metas[g], meta)
    meta_out[...] = meta
    moving.stage(0)
    for mask in range(1, groups):
        plane_copy(mask).wait_recv()

    for g in range(groups):
        for f in range(shards):
            here = pl.ds((g * shards + f) * part, part)
            block = weights[g, f]
            small_out[here, :] = block[:, 2 * LANES :]
            merged[here, 0 : 2 * LANES] = block[:, : 2 * LANES]
            columns_out[here, :] = block[:, : 2 * LANES]
    for s in range(3):
        merged[:, (2 + s) * LANES : (3 + s) * LANES] = factors_ref[s]
    gain = gain_row(small_out[...], 16)

    nseq = NSEQ
    lanes = lane_of((1, LANES))
    starts, first = [], jnp.zeros((1, 1), jnp.int32)
    for s in range(nseq):
        starts.append(first)
        first = first + meta[8:9, s : s + 1]
    angles = [start.astype(F32) * freq_ref[...] for start in starts]
    start_cos = [jnp.cos(angle) for angle in angles]
    start_sin = [jnp.sin(angle) for angle in angles]
    adapters = [jnp.broadcast_to(meta[9:10, s : s + 1], (1, LANES)) for s in range(nseq)]
    keyed = lanes < half
    sign = jnp.where(lanes % half < half // 2, -1.0, 1.0)

    def compute(mask):
        block = me ^ mask
        at = pl.ds(pl.multiple_of(block * rows, rows), rows)
        x = x_ref[...] if mask == 0 else xs[block]
        full = x.astype(F32)
        r1 = lax.rsqrt(jnp.mean(full * full, axis=1, keepdims=True) + EPSILON)
        product = dot((full * r1 * gain).astype(BF), merged[...])
        base_cos, base_sin, pick = sequences(
            meta, block * rows, rows, (start_cos, start_sin, adapters)
        )
        masked = lane_of((rows, LANES)) // ADAPTER_RANK == pick
        mask_ref[at, :] = jnp.where(masked, 1.0, 0.0).astype(BF)
        lows = [
            jnp.where(masked, product[:, (2 + s) * LANES : (3 + s) * LANES], 0.0).astype(BF)
            for s in range(3)
        ]
        lows = jnp.concatenate(lows, axis=1)
        low_ref[at, :] = lows
        product = product[:, : 2 * LANES] + dot(lows, second[...])
        row_cos, row_sin = cos_ref[at, :], sin_ref[at, :]
        cosine = row_cos * base_cos + row_sin * base_sin
        sine = (row_sin * base_cos - row_cos * base_sin) * sign
        turn_ref[at, :LANES] = cosine
        turn_ref[at, LANES:] = sine
        qkv_ref[at, :LANES] = turned(product[:, :LANES], cosine, sine).astype(BF)
        others = product[:, LANES:]
        qkv_ref[at, LANES:] = turned(
            others, jnp.where(keyed, cosine, 1.0), jnp.where(keyed, sine, 0.0)
        ).astype(BF)

    compute(0)
    for h in range(2):
        moving.take(h, 1)
    compute(1)
    early, late = moving.halves()
    for h, m in early:
        if m not in (moving.orders[h][0],):
            moving.take(h, m)
    whole = [m for m in range(2, shards, 2) if all((h, m) in early for h in range(2))]
    for m in whole:
        compute(m)
    for m in whole:
        for h in range(2):
            moving.take(h, m + 1)
        compute(m + 1)
    for h, m in late:
        moving.take(h, m)
    rest = [m for m in range(2, shards, 2) if m not in whole]
    for m in rest:
        compute(m)
    for m in rest:
        for h in range(2):
            moving.take(h, m + 1)
        compute(m + 1)
    moving.finish()
    for mask in order:
        column_copy(mask).wait_send()
    for mask in range(1, groups):
        plane_copy(mask).wait_send()
        meta_copy(mask).wait_send()


def enter(deal, x, wq, wk, wv, small, meta, factors, wide, kv_second, identity):
    shards, groups = lax.axis_size("fsdp"), lax.axis_size("dp")
    rows, part = x.shape[0], wq.shape[0]
    total = rows * shards
    half = HEAD_WIDTH // 2
    frequency = ROPE_BASE ** (-np.arange(half, dtype=np.float64) / half)
    frequency = frequency.astype(np.float32)
    angles = np.arange(total, dtype=np.float64)[:, None] * frequency.astype(np.float64)[None, :]
    cosine = jnp.asarray(np.tile(np.cos(angles).astype(np.float32), (1, 4)))
    sine = jnp.asarray(np.tile(np.sin(angles).astype(np.float32), (1, 4)))
    frequency = jnp.asarray(np.tile(frequency, 4)[None, :])
    return pl.pallas_call(
        functools.partial(enter_kernel, shards, groups),
        out_shape=(
            jax.ShapeDtypeStruct((total, 2 * LANES), BF),
            jax.ShapeDtypeStruct((total, 3 * STACKED), BF),
            jax.ShapeDtypeStruct((total, STACKED), BF),
            jax.ShapeDtypeStruct((MODEL_WIDTH, LANES), BF),
            jax.ShapeDtypeStruct(meta.shape, jnp.int32),
            jax.ShapeDtypeStruct((MODEL_WIDTH, 2 * LANES), BF),
            jax.ShapeDtypeStruct((total, 2 * LANES), F32),
        ),
        in_specs=[pl.BlockSpec(memory_space=pltpu.SMEM)] + [IN_VMEM] * 12,
        out_specs=(IN_VMEM,) * 7,
        scratch_shapes=[
            pltpu.VMEM((shards, rows, MODEL_WIDTH), BF),
            pltpu.VMEM((shards, part, 3 * LANES), BF),
            pltpu.VMEM((groups, shards, part, 3 * LANES), BF),
            pltpu.VMEM((groups,) + meta.shape, jnp.int32),
            pltpu.VMEM((MODEL_WIDTH, 2 * LANES + 3 * STACKED), BF),
            pltpu.VMEM((3 * STACKED, 2 * LANES), BF),
        ]
        + pair_of_sems(shards)
        + [pltpu.SemaphoreType.DMA((shards,))] * 2
        + [pltpu.SemaphoreType.DMA((groups,))] * 4,
        compiler_params=remote(identity, 60),
        name="enter",
    )(deal, x, wq, wk, wv, small, meta, factors, wide, kv_second, cosine, sine, frequency)


def gain_row(small, lane):
    pick = jnp.where(lane_of((8, LANES)) == lane, 1.0, 0.0).astype(BF)
    return dot(pick, small, 1, 1)[0:1, :]


def turn_of(step, shards):
    if shards == 8:
        return step + step // 4 * (1 - 2 * (step % 2))
    late = (step + shards - 4) // shards
    return step + late * (shards + 3 - 2 * step)


def scatter_plan(moving, shards):
    place = {turn_of(t, shards): t for t in range(shards)}
    sent, plan = {}, []
    for t in range(shards):
        now = []
        for mask in range(1, shards):
            for h in range(2):
                sources = [mask ^ bit for bit in moving.orders[h][: moving.depth(h, mask)]]
                ready = all((h, s) in sent and sent[h, s] < t for s in sources)
                if (h, mask) not in sent and place[mask] <= t and ready:
                    now.append((h, mask))
        for item in now:
            sent[item] = t
        plan.append(now)
    rest = [(h, m) for m in range(1, shards) for h in range(2) if (h, m) not in sent]
    rest.sort(key=lambda item: moving.depth(*item))
    return plan, rest + [(0, 0), (1, 0)]


def experts_block(first_expert, n2, side, grad, mask, win, wout, wide_down, hid, down, spread, fold):
    rows = n2.shape[0]
    width = HIDDEN_UNITS
    lane = lane_of((rows, LANES))
    lows = dot(side, spread[:, : 2 * STACKED])
    low_gate = (lows[:, :STACKED] * mask).astype(BF)
    low_up = (lows[:, STACKED:] * mask).astype(BF)
    lift_gate = dot(low_gate, hid[0])
    lift_up = dot(low_up, hid[1])
    down_grad = (dot(grad, wide_down, 1, 1) * mask).astype(BF)
    from_down = dot(down_grad, down[...], 1, 1)
    side_full = side.astype(F32)
    total_inner = jnp.zeros((rows, width), F32)
    total_gate = jnp.zeros((rows, width), F32)
    total_up = jnp.zeros((rows, width), F32)
    extra = jnp.zeros((rows, LANES), F32)
    gated_parts, slope_parts = [], []
    for e in range(win.shape[1] // (2 * width)):
        name = first_expert + e
        at_high, at_low = lane == name, lane == name + EXPERT_COUNT
        gate = jnp.sum(jnp.where(at_high | at_low, side_full, 0.0), axis=1, keepdims=True)
        first = 2 * e * width
        pre_gate = dot(n2, win[:, first : first + width]) + lift_gate
        pre_up = dot(n2, win[:, first + width : first + 2 * width]) + lift_up
        pulled = dot(grad, wout[:, e * width : (e + 1) * width]) + from_down
        squashed = jax.nn.sigmoid(pre_gate)
        active = pre_gate * squashed
        inner = active * pre_up
        gate_grad = jnp.sum(inner * pulled, axis=1, keepdims=True)
        high = gate_grad.astype(BF).astype(F32)
        extra = extra + jnp.where(at_high, high, 0.0) + jnp.where(at_low, gate_grad - high, 0.0)
        gated = inner * gate
        pulled = pulled * gate
        grad_gate = pulled * pre_up * (squashed + active * (1.0 - squashed))
        grad_up = pulled * active
        gated_parts.append(gated.astype(BF))
        slope_parts += [grad_gate.astype(BF), grad_up.astype(BF)]
        total_inner = total_inner + gated
        total_gate = total_gate + grad_gate
        total_up = total_up + grad_up
    out = dot(jnp.concatenate(gated_parts, axis=1), wout[...], 1, 1)
    back = dot(jnp.concatenate(slope_parts, axis=1), win[...], 1, 1)
    total_inner = total_inner.astype(BF)
    total_gate = total_gate.astype(BF)
    total_up = total_up.astype(BF)
    shrunk = jnp.concatenate(
        [
            (dot(total_gate, hid[0], 1, 1) * mask).astype(BF),
            (dot(total_up, hid[1], 1, 1) * mask).astype(BF),
            (dot(total_inner, down[...]) * mask).astype(BF),
        ],
        axis=1,
    )
    extra = extra + dot(shrunk, fold[...])
    sums = (
        dot(total_inner, down_grad, 0, 0),
        dot(low_gate, total_gate, 0, 0),
        dot(low_up, total_up, 0, 0),
    )
    return out.astype(BF), back.astype(BF), extra.astype(BF), sums


def middle_kernel(
    shards,
    mine_ref,
    x_ref,
    small_ref,
    meta_ref,
    mask_ref,
    wo_ref,
    factors_ref,
    wide_ref,
    router2_ref,
    hid_ref,
    down_ref,
    spread_ref,
    fold_ref,
    cots_ref,
    win_ref,
    wout_ref,
    base_ref,
    outs_ref,
    hgrad_ref,
    heads_ref,
    early_ref,
    *scratch,
):
    near = shards <= 8
    store, block_in, scratch = (scratch[0], None, scratch[1:]) if near else (scratch[0], scratch[1], scratch[2:])
    middle_body(
        shards,
        near,
        (
            mine_ref,
            x_ref,
                    small_ref,
            meta_ref,
            mask_ref,
            wo_ref,
            factors_ref,
            wide_ref,
            router2_ref,
            hid_ref,
            down_ref,
            spread_ref,
            fold_ref,
            cots_ref,
            win_ref,
            wout_ref,
        ),
        (
            base_ref,
            outs_ref,
            hgrad_ref,
            heads_ref,
            early_ref,
        ),
        store,
        block_in,
        *scratch,
    )


def middle_body(
    shards,
    near,
    given,
    results,
    store,
    block_in,
    own_in,
    part,
    land,
    win,
    wout,
    cots,
    outs,
    attended,
    factors,
    gdown_ref,
    ghid_ref,
    gsend,
    grecv,
    ssend,
    srecv,
    wsem,
    csem,
    osem,
    bsem,
):
    (
        mine_ref,
        x_ref,
            small_ref,
        meta_ref,
        mask_ref,
        wo_ref,
        factors_ref,
        wide_ref,
        router2_ref,
        hid_ref,
        down_ref,
        spread_ref,
        fold_ref,
        cots_ref,
        win_ref,
        wout_ref,
    ) = given
    (
        base_ref,
        outs_ref,
        hgrad_ref,
        heads_ref,
        early_ref,
    ) = results
    me = lax.axis_index("fsdp")
    rows = x_ref.shape[0]
    if near:
        own_in = store.at[me]
    width = MODEL_WIDTH
    heads = HEADS // shards
    lane = lane_of((rows, LANES))
    loads = [
        pltpu.make_async_copy(win_ref, win, wsem.at[0]),
        pltpu.make_async_copy(wout_ref, wout, wsem.at[1]),
    ]
    fetch_factors = pltpu.make_async_copy(factors_ref.at[pl.ds(3, 4)], factors, wsem.at[2])
    fetch_factors.start()
    for load in loads:
        load.start()

    def cot_copy(step):
        return pltpu.make_async_copy(
            cots_ref.at[me ^ turn_of(step, shards)], cots.at[step % 2], csem.at[step % 2]
        )

    cot_copy(0).start()
    greet([("fsdp", me, bits_of(shards))])

    if near:
        attended = mine_ref
    else:
        for s in range(0, shards, 2):
            second = pltpu.roll(mine_ref[s + 1].astype(F32), HEAD_WIDTH, 1)
            both = jnp.where(lane < HEAD_WIDTH, mine_ref[s].astype(F32), second)
            attended[:, s // 2 * LANES : (s // 2 + 1) * LANES] = both.astype(BF)
    own = pl.ds(pl.multiple_of(me * rows, rows), rows)
    mask = mask_ref[own, :].astype(F32)
    small = small_ref[...]
    gain = gain_row(small, 17)
    fetch_factors.wait()
    out_low = (dot(attended[...], factors[3]) * mask).astype(BF)
    hidden = (
        x_ref[...].astype(F32) + dot(attended[...], wo_ref[...], 1, 1) + dot(out_low, wide_ref[1])
    )
    base_ref[...] = hidden
    r2 = lax.rsqrt(jnp.mean(hidden * hidden, axis=1, keepdims=True) + EPSILON)
    n2 = (hidden * r2 * gain).astype(BF)
    own_in[:, :width] = n2
    lows = [(dot(n2, factors[s]) * mask).astype(BF) for s in range(3)]
    logits = dot(n2, small) + dot(lows[0], router2_ref[...])
    named = jnp.zeros((LANES, rows), jnp.bool_)
    for k in range(TOPK):
        named = named | (row_of((LANES, rows)) == meta_ref[k : k + 1, :])
    eye = jnp.where(row_of((LANES, LANES)) == lane_of((LANES, LANES)), 1.0, 0.0).astype(BF)
    picked = dot(jnp.where(named, 1.0, 0.0).astype(BF), eye, 0, 0) > 0.5
    peak = jnp.max(jnp.where(picked, logits, MASKED), axis=1, keepdims=True)
    lifted = jnp.where(picked, jnp.exp(jnp.where(picked, logits, peak) - peak), 0.0)
    gates = lifted / jnp.sum(lifted, axis=1, keepdims=True)
    high = gates.astype(BF).astype(F32)
    shrunk = dot(jnp.concatenate(lows[1:], axis=1), fold_ref[: 2 * STACKED, :])
    side = high + pltpu.roll(gates - high, EXPERT_COUNT, 1) + shrunk
    own_in[:, width:] = side.astype(BF)

    going = Gather("fsdp", shards, own_in, store, (gsend, grecv))
    coming = Scatter("fsdp", shards, part, land, (ssend, srecv))
    going.start()
    for load in loads:
        load.wait()

    early, late = going.halves()
    plan, rest = scatter_plan(coming, shards)
    first_expert = me * (EXPERT_COUNT // shards)

    def out_copy(at):
        return pltpu.make_async_copy(outs, outs_ref.at[me ^ turn_of(at, shards)], osem.at[0])

    def step(t, carry):
        turn = turn_of(t, shards)
        block = me ^ turn
        slot = t % 2

        @pl.when(t == 2)
        def _():
            for h, m in early:
                going.take(h, m)

        @pl.when(t == 4)
        def _():
            for h, m in late:
                going.take(h, m)

        for k in range(shards):
            m = turn_of(k, shards)
            if m % 2:

                @pl.when(t == k)
                def _(m=m):
                    for h in range(2):
                        going.take(h, m)

        @pl.when(t + 1 < shards)
        def _():
            cot_copy(t + 1).start()

        cot_copy(t).wait()

        @pl.when(t >= 1)
        def _():
            out_copy(t - 1).wait()

        block_rows = pl.ds(pl.multiple_of(block * rows, rows), rows)
        if near:
            here = store.at[block]
        else:
            here = block_in

            @pl.when(t == 0)
            def _():
                block_in[...] = own_in[...]

            @pl.when(t != 0)
            def _():
                fetch = pltpu.make_async_copy(store.at[block], block_in, bsem)
                fetch.start()
                fetch.wait()

        out, back, extra, sums = experts_block(
            first_expert,
            here[:, :width],
            here[:, width:],
            cots[slot],
            mask_ref[block_rows, :].astype(F32),
            win,
            wout,
            wide_ref[2],
            hid_ref,
            down_ref,
            spread_ref,
            fold_ref,
        )
        outs[...] = out
        out_copy(t).start()
        part[block, :, :width] = back
        part[block, :, width:] = extra

        @pl.when(t == 0)
        def _():
            gdown_ref[...] = sums[0]
            ghid_ref[0] = sums[1]
            ghid_ref[1] = sums[2]

        @pl.when(t != 0)
        def _():
            gdown_ref[...] += sums[0]
            ghid_ref[0] += sums[1]
            ghid_ref[1] += sums[2]

        for k in range(shards):
            if plan[k]:

                @pl.when(t == k)
                def _(k=k):
                    for h, m in plan[k]:
                        coming.reduce(h, m)

        return carry

    lax.fori_loop(0, shards, step, 0)
    out_copy(shards - 1).wait()
    cot_load = pltpu.make_async_copy(cots_ref.at[me], cots.at[0], csem.at[0])
    cot_load.start()
    for h, m in rest:
        coming.reduce(h, m)
    cot_load.wait()

    hidden = base_ref[...]
    mask = mask_ref[own, :].astype(F32)
    r2 = lax.rsqrt(jnp.mean(hidden * hidden, axis=1, keepdims=True) + EPSILON)
    n2 = own_in[:, :width]
    cot = cots[0]
    grad = cot.astype(F32)
    extra = part[me, :, width:]
    extra_full = extra.astype(F32)
    gate_grad = extra_full + pltpu.roll(extra_full, LANES - EXPERT_COUNT, 1)
    logit_grad = gates * (gate_grad - jnp.sum(gates * gate_grad, axis=1, keepdims=True))
    logit_grad = jnp.where(lane < EXPERT_COUNT, logit_grad, 0.0).astype(BF)
    wider = dot(extra, spread_ref[...])
    second_grad = [
        (dot(logit_grad, router2_ref[...], 1, 1) * mask).astype(BF),
        (wider[:, :STACKED] * mask).astype(BF),
        (wider[:, STACKED : 2 * STACKED] * mask).astype(BF),
    ]
    down_low = (wider[:, 2 * STACKED :] * mask).astype(BF)
    base_ref[...] = hidden + dot(down_low, wide_ref[2])
    n2_grad = part[me, :, :width].astype(F32) + dot(logit_grad, small, 1, 1)
    for s in range(3):
        n2_grad = n2_grad + dot(second_grad[s], factors[s], 1, 1)
    w2 = gain * n2_grad
    hidden_grad = grad + r2 * w2 - hidden * (r2 * r2 * r2) * jnp.mean(w2 * hidden, axis=1, keepdims=True)
    hgrad_ref[...] = hidden_grad
    out_grad = hidden_grad.astype(BF)
    out_low_grad = (dot(out_grad, wide_ref[1], 1, 1) * mask).astype(BF)
    attended_grad = dot(out_grad, wo_ref[...]) + dot(out_low_grad, factors[3], 1, 1)
    for s in range(shards):
        if heads == 2:
            heads_ref[s] = attended_grad[:, s * LANES : (s + 1) * LANES].astype(BF)
        else:
            pair = attended_grad[:, s // 2 * LANES : (s // 2 + 1) * LANES]
            if s % 2:
                pair = pltpu.roll(pair, HEAD_WIDTH, 1)
            heads_ref[s] = jnp.where(lane < HEAD_WIDTH, pair, 0.0).astype(BF)
    gsecond = dot(n2, jnp.concatenate(second_grad, axis=1), 0, 0).astype(BF)
    packed = [gsecond[:, s * LANES : (s + 1) * LANES] for s in range(3)]
    packed.append(dot(attended[...], out_low_grad, 0, 0).astype(BF))
    packed.append(gdown_ref[...].astype(BF))
    for s in range(2):
        packed += [ghid_ref[s, :, j : j + LANES].astype(BF) for j in range(0, HIDDEN_UNITS, LANES)]
    for one, two in ((out_low, out_grad), (down_low, cot)):
        product = dot(one, two, 0, 0).astype(BF)
        packed += [product[:, j : j + LANES] for j in range(0, MODEL_WIDTH, LANES)]
    packed.append(dot(lows[0], logit_grad, 0, 0).astype(BF))
    pack(early_ref, packed, early_ref.shape[1])
    going.finish()
    coming.finish()


def middle(mine, x, small, meta, mask, wo, factors, wide, router2, hid, down, cots, win, wout, identity):
    shards = lax.axis_size("fsdp")
    rows = x.shape[0]
    side = MODEL_WIDTH + LANES
    source = np.arange(LANES)
    place = np.arange(STACKED) % ADAPTER_RANK
    spread = np.concatenate([source[:, None] == o + place[None, :] for o in (32, 48, 64)], axis=1)
    fold = np.concatenate([source[None, :] == o + place[:, None] for o in (32, 48, 64)], axis=0)
    spread, fold = jnp.asarray(spread, BF), jnp.asarray(fold, BF)
    gathered = (shards, rows, side)
    near = shards <= 8
    results = pl.pallas_call(
        functools.partial(middle_kernel, shards),
        out_shape=(
            jax.ShapeDtypeStruct((rows, MODEL_WIDTH), F32),
            jax.ShapeDtypeStruct((shards, rows, MODEL_WIDTH), BF),
            jax.ShapeDtypeStruct((rows, MODEL_WIDTH), F32),
            jax.ShapeDtypeStruct((shards, rows, LANES), BF),
            jax.ShapeDtypeStruct((shards, total_length(EARLY) // shards, LANES), BF),
        )
        + (() if near else (jax.ShapeDtypeStruct(gathered, BF),)),
        in_specs=[IN_VMEM] * 6 + [ANYWHERE] + [IN_VMEM] * 6 + [ANYWHERE] * 3,
        out_specs=(IN_VMEM, ANYWHERE) + (IN_VMEM,) * 3 + (() if near else (ANYWHERE,)),
        scratch_shapes=[
            pltpu.VMEM(gathered if near else gathered[1:], BF),
            pltpu.VMEM((16, LANES) if near else gathered[1:], BF),
            pltpu.VMEM((shards, rows, side), BF),
            pltpu.VMEM((2, shards - 1, rows // 2, side), BF),
            pltpu.VMEM(win.shape, BF),
            pltpu.VMEM(wout.shape, BF),
            pltpu.VMEM((2, rows, MODEL_WIDTH), BF),
            pltpu.VMEM((rows, MODEL_WIDTH), BF),
            pltpu.VMEM((16, LANES) if near else (rows, MODEL_WIDTH), BF),
            pltpu.VMEM((4, MODEL_WIDTH, STACKED), BF),
            pltpu.VMEM((HIDDEN_UNITS, STACKED), F32),
            pltpu.VMEM((2, STACKED, HIDDEN_UNITS), F32),
        ]
        + pair_of_sems(shards) * 2
        + [pltpu.SemaphoreType.DMA((3,))] * 3
        + [pltpu.SemaphoreType.DMA(())],
        compiler_params=remote(identity, 62),
        name="middle",
    )(mine, x, small, meta, mask, wo, factors, wide, router2, hid, down, spread, fold, cots, win, wout)
    return results[:5]


class Total:
    def __init__(self, shards, groups, out, part, land, zpart, zland, zall, sems):
        self.me, self.plane = lax.axis_index("fsdp"), lax.axis_index("dp")
        self.groups, self.out, self.part, self.zpart, self.zall = groups, out, part, zpart, zall
        self.down = Scatter("fsdp", shards, part, land, sems[0:2])
        self.across = Scatter("dp", groups, zpart, zland, sems[2:4])
        self.back = Gather("dp", groups, zall.at[self.plane], zall, sems[4:6])
        self.up = Gather("fsdp", shards, out.at[self.me], out, sems[6:8])
        self.steps = [lambda k=k: self.level(self.down, k) for k in range(len(bits_of(shards)))]
        self.steps.append(self.turn)
        self.steps += [lambda k=k: self.level(self.across, k) for k in range(1, len(bits_of(groups)))]
        self.steps.append(self.turn_back)
        for k in range(len(bits_of(groups)) - 1):
            self.steps.append(lambda k=k: self.back.stage(k))
        self.steps.append(self.rise)
        for k in range(len(bits_of(shards))):
            self.steps.append(lambda k=k: self.up.stage(k))
        self.steps.append(self.finish)

    def level(self, moving, k):
        for mask in range(moving.count):
            for h in range(2):
                if moving.depth(h, mask) == k:
                    moving.reduce(h, mask)

    def turn(self):
        self.level(self.down, len(self.down.orders[0]))
        piece = self.zpart.shape[1]
        for g in range(self.groups):
            self.zpart[g] = self.part[self.me, pl.ds(g * piece, piece)]
        self.level(self.across, 0)

    def turn_back(self):
        self.level(self.across, len(self.across.orders[0]))
        self.zall[self.plane] = self.zpart[self.plane]
        self.back.start()

    def rise(self):
        self.back.stage(len(bits_of(self.groups)) - 1)
        piece = self.zpart.shape[1]
        for g in range(self.groups):
            self.out[self.me, pl.ds(g * piece, piece)] = self.zall[g]
        self.up.start()

    def finish(self):
        self.down.finish()
        self.across.finish()
        self.back.finish()
        self.up.finish()

    def next(self, count=1):
        for _ in range(count):
            if self.steps:
                self.steps.pop(0)()


def total_scratch(shards, groups, length):
    share = length // shards
    piece = share // groups
    return [
        pltpu.VMEM((shards, share, LANES), BF),
        pltpu.VMEM((shards, share, LANES), BF),
        pltpu.VMEM((2, shards - 1, share // 2, LANES), BF),
        pltpu.VMEM((groups, piece, LANES), BF),
        pltpu.VMEM((2, groups - 1, piece // 2, LANES), BF),
        pltpu.VMEM((groups, piece, LANES), BF),
    ] + pair_of_sems(shards) + pair_of_sems(groups) * 2 + pair_of_sems(shards)


def total_length(length):
    unit = lax.axis_size("fsdp") * lax.axis_size("dp") * 2 * 16
    return -(-length // unit) * unit


EARLY = 5 * MODEL_WIDTH + HIDDEN_UNITS + 2 * MODEL_WIDTH + STACKED
LATE = 5 * MODEL_WIDTH


def leave_kernel(
    shards,
    groups,
    heads_ref,
    q_ref,
    k_ref,
    v_ref,
    att_ref,
    columns_ref,
    x_ref,
    small_ref,
    factors_ref,
    wide_ref,
    kv_ref,
    hgrad_ref,
    base_ref,
    low_ref,
    turn_ref,
    mask_ref,
    outs_ref,
    layer_ref,
    xgrad_ref,
    late_out,
    columns,
    grads,
    dk_ref,
    dv_ref,
    dq_ref,
    mixes,
    landed,
    near_columns,
    low,
    turn,
    own_mask_ref,
    outs,
    out_land,
    asend,
    arecv,
    msend,
    mrecv,
    gsend,
    grecv,
    osend,
    orecv,
    isem,
    *sums,
):
    me, plane = lax.axis_index("fsdp"), lax.axis_index("dp")
    rows = x_ref.shape[0]
    heads = HEADS // shards
    share = max(1, shards // KEY_VALUE_HEADS)
    side = PART
    cols = heads * side
    nparts = rows // side
    late_part = sums[0]
    near = shards <= 8
    columns = near_columns if near else columns
    own_rows = pl.ds(pl.multiple_of(me * rows, rows), rows)
    takes = [
        pltpu.make_async_copy(mask_ref.at[own_rows], own_mask_ref, isem.at[1]),
        pltpu.make_async_copy(low_ref.at[own_rows], low, isem.at[2]),
    ]
    for take in takes:
        take.start()
    if near:
        take_outs = pltpu.make_async_copy(outs_ref, outs, isem.at[3])
        take_outs.start()
    greet([("fsdp", me, range(1, shards)), ("dp", plane, bits_of(groups))])

    def head_copy(mask):
        return pltpu.make_async_remote_copy(
            src_ref=heads_ref.at[me ^ mask],
            dst_ref=grads.at[me],
            send_sem=asend.at[mask],
            recv_sem=arecv.at[me],
            device_id={"fsdp": me ^ mask},
            device_id_type=MESH,
        )

    def home_copy(target):
        return pltpu.make_async_remote_copy(
            src_ref=mixes.at[target],
            dst_ref=landed.at[me],
            send_sem=msend.at[target],
            recv_sem=mrecv.at[me],
            device_id={"fsdp": target},
            device_id_type=MESH,
        )

    for m in range(shards - 1, 0, -1):
        head_copy(m).start()
    grads[me] = heads_ref[me]
    dk_ref[...] = jnp.zeros(dk_ref.shape, F32)
    dv_ref[...] = jnp.zeros(dv_ref.shape, F32)

    going = Gather("fsdp", shards, columns_ref, columns, (gsend, grecv))
    late = Total(shards, groups, late_out, *sums[:5], sums[5:])

    if near:
        leaving = Scatter("fsdp", shards, outs, out_land, (osend, orecv))
        levels = len(leaving.orders[0])

        def out_level(k):
            for m in range(shards):
                for h in range(2):
                    if leaving.depth(h, m) == k:
                        leaving.reduce(h, m)

        take_outs.wait()
        out_level(0)

    low_lane = lane_of((side, LANES)) < HEAD_WIDTH
    lane = lane_of((side, LANES))
    keyed = lane_of((rows, LANES)) < HEAD_WIDTH
    first_takes, late_takes = going.halves()

    for c in reversed(range(shards)):
        take_turn = pltpu.make_async_copy(turn_ref.at[pl.ds(c * rows, rows)], turn, isem.at[0])
        take_turn.start()

        @pl.when(me != c)
        def _(c=c):
            pltpu.make_async_remote_copy(
                src_ref=heads_ref.at[c],
                dst_ref=grads.at[c],
                send_sem=asend.at[0],
                recv_sem=arecv.at[c],
                device_id={"fsdp": c},
                device_id_type=MESH,
            ).wait_recv()

        if c == shards - 1:
            going.start()
        if c == shards - 4:
            for h, m in first_takes:
                going.take(h, m)
        if c == shards - 6:
            for h, m in late_takes:
                going.take(h, m)
        if near and shards - 1 - c in (2, 4):
            out_level((shards - 1 - c) // 2)
        keys = (c + 1) * rows

        def step(u, carry, c=c, keys=keys):
            at = pl.ds(pl.multiple_of(u * side, side), side)
            grad = grads[c, at, :].astype(F32)
            both = grad * att_ref[pl.ds(pl.multiple_of(c * rows + u * side, side), side), :].astype(F32)
            stack = []
            for h in range(heads):
                mine = low_lane if h == 0 else ~low_lane
                delta = jnp.sum(jnp.where(mine, both, 0.0), axis=1, keepdims=True)
                hi, mid, lo = splits(-delta)
                extra = jnp.where(lane == 0, hi, jnp.where(lane == 1, mid, jnp.where(lane == 2, lo, 0.0)))
                stack.append(
                    jnp.concatenate([jnp.where(mine, grad, 0.0).astype(BF), extra.astype(BF)], axis=1)
                )
            do = jnp.concatenate(stack, axis=0) if heads > 1 else stack[0]
            queries = q_ref[c * nparts + u]
            weights = jnp.exp(dot(k_ref[0:keys, :], queries, 1, 1))
            seen = row_of((rows, cols)) <= lane_of((rows, cols)) % side + u * side
            final = jnp.where(seen, weights[keys - rows :], 0.0)
            weights = jnp.concatenate([weights[: keys - rows], final], axis=0) if c else final
            slope = (weights * dot(v_ref[0:keys, :], do, 1, 1)).astype(BF)
            dv_ref[0:keys, :] += dot(weights.astype(BF), do[:, :LANES])
            dk_ref[0:keys, :] += dot(slope, queries[:, :LANES])
            dq = dot(slope, k_ref[0:keys, :LANES], 0, 0)
            dq = dq if heads == 1 else jnp.where(low_lane, dq[:side], dq[side:])
            dq_ref[at, :] = dq * (HEAD_WIDTH ** -0.5)
            return carry

        lax.fori_loop(0, nparts, step, 0)

        block = pl.ds(c * rows, rows)
        dk, dv = dk_ref[block, :], dv_ref[block, :]
        other = jnp.where(
            keyed, dk + pltpu.roll(dk, HEAD_WIDTH, 1), dv + pltpu.roll(dv, HEAD_WIDTH, 1)
        )
        take_turn.wait()
        cosine, sine = turn[:, :LANES], turn[:, LANES:]
        mixes[c, :, :LANES] = turned(dq_ref[...], cosine, -sine).astype(BF)
        mixes[c, :, LANES:] = turned(
            other, jnp.where(keyed, cosine, 1.0), jnp.where(keyed, -sine, 0.0)
        ).astype(BF)

        @pl.when(me != c)
        def _(c=c):
            home_copy(c).start()

    if shards < 8:
        for h, m in first_takes + late_takes:
            going.take(h, m)
    for h in range(2):
        for m in span(going.orders[h][:-1]):
            going.incoming(h, m ^ going.orders[h][-1]).wait_recv()

    landed[me] = mixes[me]
    if near:
        columns[me] = columns_ref[...]
    else:
        keep = pltpu.make_async_copy(columns_ref, columns.at[me], isem.at[3])
        keep.start()
        keep.wait()
    for take in takes:
        take.wait()
    own_mask = own_mask_ref[...].astype(F32)
    x = x_ref[...].astype(F32)
    r1 = lax.rsqrt(jnp.mean(x * x, axis=1, keepdims=True) + EPSILON)
    gain = gain_row(small_ref[...], 16)
    normed = (x * r1 * gain).astype(BF)
    for m in range(1, shards):
        pltpu.make_async_remote_copy(
            src_ref=mixes.at[0],
            dst_ref=landed.at[me ^ m],
            send_sem=msend.at[0],
            recv_sem=mrecv.at[me ^ m],
            device_id={"fsdp": me ^ m},
            device_id_type=MESH,
        ).wait_recv()
    query_grad, normed_grad = [], jnp.zeros((rows, MODEL_WIDTH), F32)
    for s in range(shards):
        if near:
            weight = columns[s]
        else:
            fetch = pltpu.make_async_copy(columns.at[s], near_columns, isem.at[3])
            fetch.start()
            fetch.wait()
            weight = near_columns[...]
        normed_grad = normed_grad + dot(landed[s], weight, 1, 1)
        query = landed[s, :, :LANES]
        if heads == 2:
            query_grad.append(query)
        elif s % 2 == 0:
            then = pltpu.roll(landed[s + 1, :, :LANES].astype(F32), HEAD_WIDTH, 1)
            query_grad.append(jnp.where(keyed, query.astype(F32), then).astype(BF))

    def pair_of(head):
        pair = jnp.zeros((rows, LANES), F32)
        for s in range(head * share, (head + 1) * share):
            pair = pair + landed[s, :, LANES:].astype(F32)
        return pair

    keys_grad, values_grad = [], []
    for head in range(0, KEY_VALUE_HEADS, 2):
        one, two = pair_of(head), pair_of(head + 1)
        keys_grad.append(jnp.where(keyed, one, pltpu.roll(two, HEAD_WIDTH, 1)).astype(BF))
        values_grad.append(jnp.where(keyed, pltpu.roll(one, HEAD_WIDTH, 1), two).astype(BF))
    whole = [jnp.concatenate(part, axis=1) for part in (query_grad, keys_grad, values_grad)]
    seconds = (wide_ref[0], kv_ref[0], kv_ref[1])
    firsts = []
    for s in range(3):
        firsts.append((dot(whole[s], seconds[s], 1, 1) * own_mask).astype(BF))
        normed_grad = normed_grad + dot(firsts[s], factors_ref[s], 1, 1)

    packed, share_rows = [], late_part.shape[1]
    gfirst = dot(normed, jnp.concatenate(firsts, axis=1), 0, 0).astype(BF)
    packed += [gfirst[:, s * LANES : (s + 1) * LANES] for s in range(3)]
    for s in range(3):
        second = dot(low[:, s * LANES : (s + 1) * LANES], whole[s], 0, 0).astype(BF)
        packed += [second[:, j : j + LANES] for j in range(0, second.shape[1], LANES)]
    pack(late_part, packed, share_rows)
    late.next()
    w1 = gain * normed_grad
    xgrad_ref[...] = (
        hgrad_ref[...] + r1 * w1 - x * (r1 * r1 * r1) * jnp.mean(w1 * x, axis=1, keepdims=True)
    )
    late.next(2)
    layer = base_ref[...]
    if near:
        for k in range(3, levels + 1):
            out_level(k)
        layer = layer + outs[me].astype(F32)
    layer_ref[...] = layer.astype(layer_ref.dtype)
    late.next(99)

    for m in range(1, shards):
        head_copy(m).wait_send()
    for c in range(shards):

        @pl.when(me != c)
        def _(c=c):
            home_copy(c).wait_send()

    going.finish()
    if near:
        leaving.finish()


def pieces_of(first, size, share):
    parts, done = [], 0
    while done < size:
        block, row = divmod(first + done, share)
        length = min(size - done, share - row)
        parts.append((block, row, done, length))
        done += length
    return parts


def pack(target, arrays, share):
    first = 0
    for array in arrays:
        for block, row, done, length in pieces_of(first, array.shape[0], share):
            target[block, row : row + length, :] = array[done : done + length]
        first += array.shape[0]
    total = target.shape[0] * share
    for block, row, _, length in pieces_of(first, total - first, share):
        target[block, row : row + length, :] = jnp.zeros((length, LANES), BF)


def unpack(source, first, size):
    parts = pieces_of(first, size, source.shape[1])
    parts = [source[block, row : row + length, :] for block, row, _, length in parts]
    return parts[0] if len(parts) == 1 else jnp.concatenate(parts, axis=0)


def unpack_kernel(late_out, early_out, gfactor_ref, gdown_ref, gwide_ref, gkv_ref, gff_ref, groute_ref):
    def read(source, first, size):
        return unpack(source, first, size).astype(F32)

    for s in range(3):
        gfactor_ref[s] = read(late_out, s * MODEL_WIDTH, MODEL_WIDTH)
        gfactor_ref[3 + s] = read(early_out, s * MODEL_WIDTH, MODEL_WIDTH)
    gfactor_ref[6] = read(early_out, 3 * MODEL_WIDTH, MODEL_WIDTH)
    edge = 4 * MODEL_WIDTH
    gdown_ref[...] = read(early_out, edge, HIDDEN_UNITS)
    edge += HIDDEN_UNITS
    for s in range(2):
        for j in range(4):
            gff_ref[s, :, j * LANES : (j + 1) * LANES] = read(early_out, edge, STACKED)
            edge += STACKED
    for s in range(2):
        for j in range(8):
            gwide_ref[1 + s, :, j * LANES : (j + 1) * LANES] = read(early_out, edge, STACKED)
            edge += STACKED
    groute_ref[...] = read(early_out, edge, STACKED)
    edge = 3 * MODEL_WIDTH
    for j in range(8):
        gwide_ref[0, :, j * LANES : (j + 1) * LANES] = read(late_out, edge, STACKED)
        edge += STACKED
    for s in range(2):
        for j in range(4):
            gkv_ref[s, :, j * LANES : (j + 1) * LANES] = read(late_out, edge, STACKED)
            edge += STACKED

def unpack_all(late, early):
    return pl.pallas_call(
        unpack_kernel,
        out_shape=(
            jax.ShapeDtypeStruct((7, MODEL_WIDTH, STACKED), F32),
            jax.ShapeDtypeStruct((HIDDEN_UNITS, STACKED), F32),
            jax.ShapeDtypeStruct((3, STACKED, MODEL_WIDTH), F32),
            jax.ShapeDtypeStruct((2, STACKED, HIDDEN_UNITS), F32),
            jax.ShapeDtypeStruct((2, STACKED, HIDDEN_UNITS), F32),
            jax.ShapeDtypeStruct((STACKED, LANES), F32),
        ),
        in_specs=[IN_VMEM] * 2,
        out_specs=(IN_VMEM,) * 6,
        compiler_params=pltpu.CompilerParams(vmem_limit_bytes=40 << 20),
        name="unpack_all",
    )(late, early)


def leave(to_heads, q, k, v, att, columns, x, small, factors, wide, kv_second, hgrad, base, low, turn, mask, outs, identity):
    shards, groups = lax.axis_size("fsdp"), lax.axis_size("dp")
    rows = x.shape[0]
    near = shards <= 8
    total = shards * rows
    return pl.pallas_call(
        functools.partial(leave_kernel, shards, groups),
        out_shape=(
            jax.ShapeDtypeStruct((rows, MODEL_WIDTH), BF if near else F32),
            jax.ShapeDtypeStruct((rows, MODEL_WIDTH), F32),
            jax.ShapeDtypeStruct((shards, total_length(LATE) // shards, LANES), BF),
            jax.ShapeDtypeStruct((16, LANES) if near else (shards, MODEL_WIDTH, 2 * LANES), BF),
        ),
        in_specs=[IN_VMEM] * 13 + [ANYWHERE] * 4,
        out_specs=(IN_VMEM, IN_VMEM, IN_VMEM, ANYWHERE),
        scratch_shapes=[
            pltpu.VMEM((shards, rows, LANES), BF),
            pltpu.VMEM((total, LANES), F32),
            pltpu.VMEM((total, LANES), F32),
            pltpu.VMEM((rows, LANES), F32),
            pltpu.VMEM((shards, rows, 2 * LANES), BF),
            pltpu.VMEM((shards, rows, 2 * LANES), BF),
            pltpu.VMEM((shards, MODEL_WIDTH, 2 * LANES) if near else (MODEL_WIDTH, 2 * LANES), BF),
            pltpu.VMEM((rows, 3 * STACKED), BF),
            pltpu.VMEM((rows, 2 * LANES), F32),
            pltpu.VMEM((rows, STACKED), BF),
            pltpu.VMEM((shards, rows, MODEL_WIDTH) if near else (2, 32, LANES), BF),
            pltpu.VMEM((2, shards - 1, rows // 2, MODEL_WIDTH) if near else (2, 2, 32, LANES), BF),
        ]
        + [pltpu.SemaphoreType.DMA((shards,))] * 4
        + pair_of_sems(shards) * 2
        + [pltpu.SemaphoreType.DMA((4,))]
        + total_scratch(shards, groups, total_length(LATE))[1:],
        compiler_params=remote(identity, 62),
        name="leave",
    )(to_heads, q, k, v, att, columns, x, small, factors, wide, kv_second, hgrad, base, low, turn, mask, outs)


def local(
    tokens,
    cotangent,
    lengths,
    adapter_index,
    routes,
    deal,
    norm_gain_pair,
    query_weight,
    key_weight,
    value_weight,
    output_weight_transposed,
    router_weight,
    expert_input_weight,
    expert_output_weight,
    factors,
    down_first,
    wide,
    kv_second,
    hidden_second,
    router_second,
):
    shards = lax.axis_size("fsdp")
    groups = lax.axis_size("dp")
    rows = tokens.shape[0]
    total = rows * shards
    heads = HEADS // shards
    share = max(1, shards // KEY_VALUE_HEADS)
    me = lax.axis_index("fsdp")

    padded = ((0, 0), (0, rows - lengths.shape[1]))
    meta = jnp.concatenate(
        [
            routes.T,
            jnp.pad(lengths, padded),
            jnp.pad(adapter_index, padded),
            jnp.zeros((6, rows), jnp.int32),
        ],
        axis=0,
    )
    small = jnp.concatenate(
        [
            router_weight,
            norm_gain_pair,
            jnp.zeros((router_weight.shape[0], LANES - EXPERT_COUNT - 2), BF),
        ],
        axis=1,
    )
    qkv, low_all, group_mask, small, meta, columns, turn = enter(
        deal,
        tokens,
        query_weight,
        key_weight,
        value_weight,
        small,
        meta,
        factors,
        wide,
        kv_second,
        1,
    )
    win = expert_input_weight.reshape(MODEL_WIDTH, -1)
    wout = expert_output_weight.reshape(MODEL_WIDTH, -1)
    out_weight = lax.all_gather(output_weight_transposed, ("dp", "fsdp"), axis=0, tiled=True)
    mine, attended, q_kept, k_kept, v_kept, all_grad = attend(meta, qkv, cotangent, heads, 5)
    router2 = jnp.pad(router_second, ((0, 0), (0, LANES - EXPERT_COUNT)))
    (
        base,
        out_part,
        hidden_grad,
        to_heads,
        early,
    ) = middle(
        mine,
        tokens,
        small,
        meta,
        group_mask,
        out_weight,
        factors,
        wide,
        router2,
        hidden_second,
        down_first,
        all_grad,
        win,
        wout,
        6,
    )
    early_sum = lax.psum(early, ("dp", "fsdp"))
    layer_out, input_grad, late, _ = leave(
        to_heads,
        q_kept,
        k_kept,
        v_kept,
        attended,
        columns,
        tokens,
        small,
        factors,
        wide,
        kv_second,
        hidden_grad,
        base,
        low_all,
        turn,
        group_mask,
        out_part,
        7,
    )
    if shards > 8:
        layer_out = (layer_out + scatter(out_part, "fsdp", 8).astype(F32)).astype(BF)
    g_factors, g_down, g_wide, g_kv, g_ff, g_route = unpack_all(late, early_sum)
    return (
        layer_out,
        input_grad,
        g_factors,
        g_down,
        g_wide,
        g_kv,
        g_ff,
        g_route[:, :EXPERT_COUNT],
    )


def solution(mesh):
    rows = P(("dp", "fsdp"), None)
    placed = (
        (rows, rows, P("dp", None), P("dp", None), rows, P())
        + (rows,) * 6
        + (P(None, "fsdp", None),) * 2
        + (P(),) * 6
    )
    return jax.shard_map(
        local,
        mesh=mesh,
        in_specs=placed,
        out_specs=(rows, rows) + (P(),) * 6,
        check_vma=False,
    )
```
